32 devices in a mesh: dp: 16 (over z, x, core), mp: 2 (over y).
Axes of the slice: x: 2, y: 2, z: 4, core: 2. Of those that a mesh axis runs over, the one named last changes fastest.
Arguments:
- hidden_in: bfloat16 [32, 512, 768], P('dp', 'mp'), may hold values from -6 to 6
- cotangent: bfloat16 [32, 512, 768], P('dp', 'mp'), may hold values from -6 to 6
- segment_ids: int32 [32, 512], P('dp'), may hold values from 0 to 7, as said below
- clip_ranges: int32 [2, 4], replicated, may hold values from 1 to 3
- w_qkv: bfloat16 [2, 3, 768, 768], P(None, None, None, 'mp'), may hold values from -0.21875 to 0.21875
- bias_qv: float32 [2, 2, 768], P(None, None, 'mp'), may hold values from -1.2 to 1.2
- w_out: bfloat16 [2, 768, 768], P(None, 'mp'), may hold values from -0.875 to 0.875
- vector_bias: float32 [2, 4, 768], replicated, may hold values from -1.2 to 1.2
- ln_gain: float32 [2, 2, 768], replicated, may hold values from 0.5 to 1.5
- w_up: bfloat16 [2, 768, 3072], replicated, may hold values from -0.21875 to 0.21875
- bias_up: float32 [2, 3072], replicated, may hold values from -1.2 to 1.2
- w_down: bfloat16 [2, 3072, 768], replicated, may hold values from -0.109375 to 0.109375
Outputs:
- hidden_out: bfloat16 [32, 512, 768], P('dp', 'mp')
- grad_input: float32 [32, 512, 768], P('dp', 'mp')
- grad_qkv: float32 [2, 12, 147456], P(None, 'mp', 'dp')
- grad_bias_qv: float32 [2, 2, 768], P(None, None, 'mp')
- grad_out: float32 [2, 12, 49152], P(None, 'mp', 'dp')
- grad_vector_bias: float32 [2, 4, 768], replicated
- grad_ln_gain: float32 [2, 2, 768], replicated
- grad_up: float32 [2, 2359296], P(None, 'dp')
- grad_bias_up: float32 [2, 3072], replicated
- grad_down: float32 [2, 2359296], P(None, 'dp')
The draws below stay inside these ranges and needn't reach their ends.
Inputs may be any that keep to these rules, and one draw needn't show every extreme that they name: `segment_ids`: in each row the ids start at 0, never fall, and rise by one at each of 7 distinct positions; none of these lies within 64 positions of the row's middle, so one example spans both halves of every row.
All inputs are finite; a program needn't handle non-finite values.
Results may differ from the reference program's by a relative error of at most 0.023.
Values may be sent and summed in bfloat16 or wider, within the bound.
No kernel may reach another device: no remote copies, remote signals or barrier semaphores. Data moves between devices by JAX's collectives and lax.ppermute only.
A program may use at most 256 MiB of HBM per device.

```python
from functools import partial
import jax
import jax.numpy as jnp
import numpy as np
from jax import lax

D = 768
HEADS = 12
HEAD = 64
FF = 3072
SEQ = 512
SEGS = 8
LAYERS = 2
ROWS = 32


def draw_segment_ids(key, part):
    key = jax.random.fold_in(key, 7)
    middle = SEQ // 2
    margin = SEQ // 8
    candidates = jnp.asarray(np.array([place for place in range(1, SEQ) if place < middle - margin or place >= middle + margin], dtype=np.int32))
    row_keys = jax.random.split(key, ROWS)
    places = jnp.arange(SEQ, dtype=jnp.int32)

    def one_row(row_key):
        picked = jax.random.permutation(row_key, candidates)[:SEGS - 1]
        return jnp.sum((places[:, None] >= picked[None, :]).astype(jnp.int32), axis=1)
    return jax.vmap(one_row)(row_keys).astype(jnp.int32)


def plant(values, stream_key, smallest, largest):
    dims = values.shape
    spot = [jax.random.randint(jax.random.fold_in(stream_key, axis), (), 0, dims[axis]) for axis in range(len(dims))]
    values = values.at[tuple(spot)].set(smallest)
    longest = dims.index(max(dims))
    spot[longest] = (spot[longest] + 1) % dims[longest]
    return values.at[tuple(spot)].set(largest)


def block_scale(key, shape, cuts, smallest, high):
    def one(dim, blocks):
        heights = jax.random.uniform(jax.random.fold_in(jax.random.fold_in(key, 6), dim), (blocks,), jnp.float32, smallest / len(cuts), high / len(cuts))
        return jnp.repeat(jnp.exp(heights), shape[dim] // blocks).reshape((-1,) + (1,) * (len(shape) - dim - 1))

    loudness = one(*cuts[0])
    for cut in cuts[1:]:
        loudness = loudness * one(*cut)
    return loudness


def bell_draw(rng, extent, deviation, reach, cuts=(), kind=jnp.bfloat16):
    drawn = deviation * jax.random.normal(rng, extent, jnp.float32)
    if cuts:
        drawn = drawn * block_scale(rng, extent, cuts, -0.22, 0.18)
    return jnp.clip(drawn, -reach, reach).astype(kind)


def setup_inputs(seed: int = 0) -> dict:
    key_of = jax.random.split(jax.random.key(seed), 13)
    hidden_in = bell_draw(key_of[0], (ROWS, SEQ, D), 1.0, 6.0, ((0, 16), (1, 2)))
    cotangent = bell_draw(key_of[1], (ROWS, SEQ, D), 1.0, 6.0, ((0, 16), (1, 2)))
    segment_ids = draw_segment_ids(jax.random.fold_in(key_of[12], 71), 0)
    clip_ranges = plant(jax.random.randint(key_of[3], (LAYERS, 4), 1, 4), jax.random.fold_in(key_of[3], 1), 1, 3).astype(jnp.int32)
    w_qkv = bell_draw(key_of[4], (LAYERS, 3, D, D), D ** -0.5, 0.21875, ((3, 2),))
    bias_qv = bell_draw(key_of[5], (LAYERS, 2, D), 0.2, 1.2, ((2, 2),), jnp.float32)
    w_out = bell_draw(key_of[6], (LAYERS, D, D), (D // 16) ** -0.5, 0.875, ((1, 2),))
    vector_bias = bell_draw(key_of[7], (LAYERS, 4, D), 0.2, 1.2, (), jnp.float32)
    ln_gain = jnp.clip(1.0 + 0.1 * jax.random.normal(key_of[8], (LAYERS, 2, D), jnp.float32), 0.5, 1.5)
    w_up = bell_draw(key_of[9], (LAYERS, D, FF), D ** -0.5, 0.21875)
    bias_up = bell_draw(key_of[10], (LAYERS, FF), 0.2, 1.2, (), jnp.float32)
    w_down = bell_draw(key_of[11], (LAYERS, FF, D), FF ** -0.5, 0.109375)
    return {"hidden_in": hidden_in, "cotangent": cotangent, "segment_ids": segment_ids, "clip_ranges": clip_ranges, "w_qkv": w_qkv, "bias_qv": bias_qv, "w_out": w_out, "vector_bias": vector_bias, "ln_gain": ln_gain, "w_up": w_up, "bias_up": bias_up, "w_down": w_down}


@jax.custom_vjp
def low(v):
    return lax.optimization_barrier(v.astype(jnp.bfloat16)).astype(jnp.float32)

@jax.custom_vjp
def low_back(v):
    return v

def low_keep(v):
    return (low(v), None)

def low_pass(kept, grad):
    return (grad,)

def back_keep(v):
    return (v, None)

def back_low(kept, grad):
    return (low(grad),)
low.defvjp(low_keep, low_pass)
low_back.defvjp(back_keep, back_low)
epsilon = 1e-06
highest = lax.Precision.HIGHEST

def layer_norm(entries, gain_vec, shift_vec):
    centred = entries - lax.optimization_barrier(jnp.mean(entries, axis=-1, keepdims=True))
    spread = lax.optimization_barrier(jnp.mean(centred * centred, axis=-1, keepdims=True))
    return centred * lax.rsqrt(spread + epsilon) * gain_vec + shift_vec

def clipped(entries, clip_limit):
    return clip_limit * jnp.tanh(entries / clip_limit)

def row_attention(pieces):
    queries, key_rows, value_rows, segment_row = pieces
    same_doc = segment_row[:, None] == segment_row[None, :]
    score_scale = HEAD ** (-0.5)
    scores = low_back(jnp.einsum('qhd,khd->hqk', queries, key_rows, precision=highest) * score_scale)
    masked = jnp.where(same_doc[None], scores, -1e+30)
    weights = low(jax.nn.softmax(masked, axis=-1))
    context = jnp.einsum('hqk,khd->qhd', weights, value_rows, precision=highest)
    return context.reshape(context.shape[0], HEADS * HEAD)

def forward(hidden, w_qkv, bias_qv, w_out, vector_bias, ln_gain, w_up, bias_up, w_down, segment_ids=None, clip_bounds=None):
    for layer_index in range(LAYERS):
        quant_in = low(clipped(hidden, clip_bounds[layer_index, 0]))
        projected = jnp.einsum('rsd,pde->prse', quant_in, w_qkv[layer_index], precision=highest)
        queries = low(low_back(projected[0] + bias_qv[layer_index, 0]))
        key_rows = low(low_back(projected[1]))
        value_rows = low(low_back(projected[2] + bias_qv[layer_index, 1]))
        head_shape = (ROWS, SEQ, HEADS, HEAD)
        context = lax.map(jax.checkpoint(row_attention), (queries.reshape(head_shape), key_rows.reshape(head_shape), value_rows.reshape(head_shape), segment_ids))
        context = low_back(context)
        quant_ctx = low(clipped(context, clip_bounds[layer_index, 1]))
        attn_out = low_back(jnp.einsum('rsc,cd->rsd', quant_ctx, w_out[layer_index], precision=highest) + vector_bias[layer_index, 0])
        normed = layer_norm(hidden + attn_out, ln_gain[layer_index, 0], vector_bias[layer_index, 1])
        quant_ff = low(clipped(normed, clip_bounds[layer_index, 2]))
        inner_pre = low_back(jnp.einsum('rsd,df->rsf', quant_ff, w_up[layer_index], precision=highest) + bias_up[layer_index])
        quant_act = low(clipped(jax.nn.gelu(inner_pre, approximate=False), clip_bounds[layer_index, 3]))
        branch = low_back(jnp.einsum('rsf,fd->rsd', quant_act, w_down[layer_index], precision=highest) + vector_bias[layer_index, 2])
        hidden = layer_norm(normed + branch, ln_gain[layer_index, 1], vector_bias[layer_index, 3])
    return hidden

def reference(hidden_in, cotangent, segment_ids, clip_ranges, w_qkv, bias_qv, w_out, vector_bias, ln_gain, w_up, bias_up, w_down):
    floats = [array_in.astype(jnp.float32) for array_in in (hidden_in, w_qkv, bias_qv, w_out, vector_bias, ln_gain, w_up, bias_up, w_down)]
    clip_bounds = clip_ranges.astype(jnp.float32)
    runner = partial(forward, segment_ids=segment_ids, clip_bounds=clip_bounds)
    output, pullback = jax.vjp(runner, *floats)
    grads = pullback(cotangent.astype(jnp.float32))
    grad_input, grad_wqkv, grad_bqv, grad_wout, grad_vec, grad_gain, grad_wup, grad_bup, grad_wdown = grads
    grad_qkv = grad_wqkv.reshape(LAYERS, 3, D, HEADS, HEAD).transpose(0, 3, 1, 2, 4).reshape(LAYERS, HEADS, 3 * D * HEAD)
    grad_out = grad_wout.reshape(LAYERS, HEADS, HEAD * D)
    return (output.astype(jnp.bfloat16), grad_input, grad_qkv, grad_bqv, grad_out, grad_vec, grad_gain, grad_wup.reshape(LAYERS, D * FF), grad_bup, grad_wdown.reshape(LAYERS, FF * D))
```

```python
import functools

import jax
import jax.numpy as jnp
from jax import lax
from jax.experimental import pallas as pl
from jax.experimental.pallas import tpu as pltpu
from jax.sharding import PartitionSpec as P

HEAD = 64
PAIR = 2 * HEAD
EPS = 1e-06
BIG = -1e30
INV_SQRT2 = 0.7071067811865476
INV_SQRT2PI = 0.3989422804014327

f32 = jnp.float32
bf16 = jnp.bfloat16
MIB = 1024 * 1024

NT = (((1,), (1,)), ((), ()))
TN = (((0,), (0,)), ((), ()))


def dot(lhs, rhs, dims=(((1,), (0,)), ((), ()))):
    return lax.dot_general(lhs, rhs, dims, preferred_element_type=f32)


def whole(*shape):
    return pl.BlockSpec(shape, lambda *_: (0,) * len(shape))


def params(mib):
    return pltpu.CompilerParams(vmem_limit_bytes=mib * MIB)


def cost(flops, moved):
    return pl.CostEstimate(flops=int(flops), bytes_accessed=int(moved), transcendentals=0)


def shape(dims, dtype):
    return jax.ShapeDtypeStruct(dims, dtype)


def head_mask(head, value):
    lane = lax.broadcasted_iota(jnp.int32, (1, PAIR), 1)
    return jnp.where((lane // HEAD) == head, value, 0.0).astype(bf16)


def attn_fwd_kernel(a_ref, w_ref, b_ref, sq_ref, sk_ref, q_ref, k_ref, v_ref, c_ref, lse_ref):
    seq = a_ref.shape[0]
    act = a_ref[...]
    both = dot(act, jnp.concatenate([w_ref[0], w_ref[1]], axis=1))
    query = (both[:, :PAIR] + b_ref[0:1, :]).astype(bf16)
    key = both[:, PAIR:].astype(bf16)
    value = dot(act, w_ref[2]) + b_ref[1:2, :]
    value_t = value.T.astype(bf16)
    q_ref[...] = query
    k_ref[...] = key
    v_ref[...] = value.astype(bf16)
    key_ext = jnp.concatenate([key, sk_ref[...]], axis=1)
    parts = []
    ones = jnp.ones((16, seq), bf16)
    for head in range(2):
        query_ext = jnp.concatenate([query * head_mask(head, HEAD**-0.5), sq_ref[...]], axis=1)
        scores = dot(key_ext, query_ext, NT)
        top = jnp.max(scores, axis=0, keepdims=True)
        weights = jnp.exp(scores - top).astype(bf16)
        summed = dot(
            jnp.concatenate([value_t[head * HEAD : (head + 1) * HEAD], ones], axis=0), weights
        )
        total = summed[HEAD : HEAD + 1]
        parts.append(summed[:HEAD] * (1.0 / total))
        lse_ref[0, head : head + 1, :] = top + jnp.log(total)
    c_ref[...] = jnp.concatenate(parts, axis=0).T


def attn_fwd(act, weights, bias, seg_q, seg_k):
    seq, width = act.shape
    cols = weights.shape[2]
    steps = cols // PAIR
    block = pl.BlockSpec((seq, PAIR), lambda t: (0, t))
    return pl.pallas_call(
        attn_fwd_kernel,
        grid=(steps,),
        in_specs=[
            whole(seq, width),
            pl.BlockSpec((3, width, PAIR), lambda t: (0, 0, t)),
            pl.BlockSpec((2, PAIR), lambda t: (0, t)),
            whole(seq, PAIR),
            whole(seq, PAIR),
        ],
        out_specs=[block, block, block, block, pl.BlockSpec((1, 8, seq), lambda t: (t, 0, 0))],
        out_shape=[
            shape((seq, cols), bf16),
            shape((seq, cols), bf16),
            shape((seq, cols), bf16),
            shape((seq, cols), f32),
            shape((steps, 8, seq), f32),
        ],
        compiler_params=params(24),
        cost_estimate=cost(6 * seq * width * cols + 16 * seq * seq * cols, 5 * MIB),
        name="attn_fwd",
    )(act, weights, bias, seg_q, seg_k)


def norm_rows(entries):
    centred = entries - jnp.mean(entries, axis=-1, keepdims=True)
    spread = jnp.mean(centred * centred, axis=-1, keepdims=True)
    rate = lax.rsqrt(spread + EPS)
    return centred * rate, rate


def ff_fwd_kernel(
    last, clip_ref, x_ref, co_ref, ct_ref, wo_ref, wt_ref, vec_ref, gain_ref, up_ref, bup_ref,
    down_ref, cq_ref, hat1_ref, rate1_ref, u_ref, g_ref, slope_ref, hat2_ref, rate2_ref, *rest
):
    acc_ref = rest[-1]
    step = pl.program_id(0)
    seq = x_ref.shape[0]
    half = co_ref.shape[1]
    rows = 64
    ctx_limit, ff_limit, act_limit = clip_ref[1], clip_ref[2], clip_ref[3]
    next_limit = clip_ref[4]

    @pl.when(step == 0)
    def _():
        inv = 1.0 / ctx_limit
        cq_ref[:, :half] = (ctx_limit * jnp.tanh(co_ref[...] * inv)).astype(bf16)
        cq_ref[:, half:] = (ctx_limit * jnp.tanh(ct_ref[...] * inv)).astype(bf16)
        acc_ref[...] = dot(cq_ref[:, :half], wo_ref[...]) + dot(cq_ref[:, half:], wt_ref[...])

        def body(i, carry):
            at = pl.ds(pl.multiple_of(i * rows, rows), rows)
            hat, rate = norm_rows(x_ref[at, :].astype(f32) + (acc_ref[at, :] + vec_ref[0:1, :]))
            hat1_ref[at, :] = hat
            rate1_ref[at, :] = jnp.broadcast_to(rate, (rows, 128))
            normed = hat * gain_ref[0:1, :] + vec_ref[1:2, :]
            u_ref[at, :] = (ff_limit * jnp.tanh(normed * (1.0 / ff_limit))).astype(bf16)
            acc_ref[at, :] = normed + vec_ref[2:3, :]
            return carry

        lax.fori_loop(0, seq // rows, body, 0)

    inv_act = 1.0 / act_limit
    chunk = up_ref.shape[1]
    sub = 256
    total = None
    for part in range(chunk // sub):
        cols = slice(part * sub, (part + 1) * sub)
        pre = dot(u_ref[...], up_ref[:, cols]) + bup_ref[:, cols]
        cdf = 0.5 * lax.erf(pre * INV_SQRT2) + 0.5
        pdf = jnp.exp(pre * pre * -0.5) * INV_SQRT2PI
        bent = jnp.tanh(pre * cdf * inv_act)
        out = (act_limit * bent).astype(bf16)
        g_ref[:, cols] = out
        slope_ref[:, cols] = ((1.0 - bent * bent) * (cdf + pre * pdf)).astype(bf16)
        term = dot(out, down_ref[cols, :])
        total = term if total is None else total + term
    acc_ref[...] += total

    @pl.when(step == pl.num_programs(0) - 1)
    def _():
        def body(i, carry):
            at = pl.ds(pl.multiple_of(i * rows, rows), rows)
            hat, rate = norm_rows(acc_ref[at, :])
            hat2_ref[at, :] = hat
            rate2_ref[at, :] = jnp.broadcast_to(rate, (rows, 128))
            new = hat * gain_ref[1:2, :] + vec_ref[3:4, :]
            if last:
                rest[0][at, :] = new.astype(bf16)
            else:
                rest[0][at, :] = new
                rest[1][at, :] = (next_limit * jnp.tanh(new * (1.0 / next_limit))).astype(bf16)
            return carry

        lax.fori_loop(0, seq // rows, body, 0)


def ff_fwd(last, clips, x, ctx_own, ctx_oth, wo_own, wo_oth, vec, gain, w_up, b_up, w_down):
    seq, width = x.shape
    half = ctx_own.shape[1]
    hidden = w_up.shape[1]
    chunk = 512
    steps = hidden // chunk
    tile = pl.BlockSpec((seq, chunk), lambda t: (0, t))
    full = whole(seq, width)
    outs = [
        (full, shape((seq, width), bf16)),
        (full, shape((seq, width), f32)),
        (whole(seq, 128), shape((seq, 128), f32)),
        (full, shape((seq, width), bf16)),
        (tile, shape((seq, hidden), bf16)),
        (tile, shape((seq, hidden), bf16)),
        (full, shape((seq, width), f32)),
        (whole(seq, 128), shape((seq, 128), f32)),
    ]
    if last:
        outs.append((full, shape((seq, width), bf16)))
    else:
        outs.append((full, shape((seq, width), f32)))
        outs.append((full, shape((seq, width), bf16)))
    return pl.pallas_call(
        functools.partial(ff_fwd_kernel, last),
        grid=(steps,),
        in_specs=[
            pl.BlockSpec(memory_space=pltpu.SMEM),
            full,
            whole(seq, half),
            whole(seq, half),
            whole(half, width),
            whole(half, width),
            whole(*vec.shape),
            whole(*gain.shape),
            pl.BlockSpec((width, chunk), lambda t: (0, t)),
            pl.BlockSpec((1, chunk), lambda t: (0, t)),
            pl.BlockSpec((chunk, width), lambda t: (t, 0)),
        ],
        out_specs=[spec for spec, _ in outs],
        out_shape=[out for _, out in outs],
        scratch_shapes=[pltpu.VMEM((seq, width), f32)],
        compiler_params=params(48),
        cost_estimate=cost(4 * seq * width * hidden * 2, 20 * MIB),
        name="ff_fwd",
    )(clips, x, ctx_own, ctx_oth, wo_own, wo_oth, vec, gain, w_up, b_up, w_down)


def norm_back(grad, hat, rate, gain):
    scaled = grad * gain
    mean = jnp.mean(scaled, axis=-1, keepdims=True)
    lean = jnp.mean(scaled * hat, axis=-1, keepdims=True)
    return rate * (scaled - mean - hat * lean)


def ff_bwd_kernel(
    core_ref, clip_ref, dx_ref, hat2_ref, rate2_ref, hat1_ref, rate1_ref, vec_ref, gain_ref,
    slope_ref, up_ref, down_ref, wo_ref, wt_ref, co_ref, ct_ref,
    zk_ref, zs_ref, fk_ref, fs_ref, ok_ref, os_ref, dy_ref, dco_ref, dct_ref, small_ref, bup_ref,
    df_ref, de_ref, du_ref,
):
    step = pl.program_id(0)
    steps = pl.num_programs(0)
    seq, width = dx_ref.shape
    half = width // 2
    rows = 64
    count = seq // rows
    core = core_ref[0]
    mine = pl.ds(pl.multiple_of(core * half, 128), half)
    other = pl.ds(pl.multiple_of((1 - core) * half, 128), half)
    zero = jnp.zeros((1, width), f32)
    ctx_limit, ff_limit = clip_ref[1], clip_ref[2]

    @pl.when(step == 0)
    def _():
        def body(i, carry):
            gain_sum, shift_sum, branch_sum = carry
            at = pl.ds(pl.multiple_of(i * rows, rows), rows)
            grad = dx_ref[at, :].astype(f32)
            hat = hat2_ref[at, :]
            de = norm_back(grad, hat, rate2_ref[at, 0:1], gain_ref[1:2, :])
            df = de.astype(bf16)
            de_ref[at, :] = de
            df_ref[at, :] = df
            return (
                gain_sum + jnp.sum(grad * hat, axis=0, keepdims=True),
                shift_sum + jnp.sum(grad, axis=0, keepdims=True),
                branch_sum + jnp.sum(df.astype(f32), axis=0, keepdims=True),
            )

        gain_sum, shift_sum, branch_sum = lax.fori_loop(0, count, body, (zero, zero, zero))
        small_ref[2:3, :] = branch_sum
        small_ref[3:4, :] = shift_sum
        small_ref[5:6, :] = gain_sum
        fk_ref[...] = df_ref[:, mine]
        fs_ref[...] = df_ref[:, other]
        du_ref[...] = jnp.zeros_like(du_ref)

    chunk = up_ref.shape[1]
    sub = 256
    total = None
    for part in range(chunk // sub):
        cols = slice(part * sub, (part + 1) * sub)
        dz = dot(df_ref[...], down_ref[cols, :], NT) * slope_ref[:, cols].astype(f32)
        low = dz.astype(bf16)
        bup_ref[:, cols] = jnp.sum(low.astype(f32), axis=0, keepdims=True)

        @pl.when(step < steps // 2)
        def _():
            zk_ref[:, pl.ds(pl.multiple_of(step * chunk + part * sub, 128), sub)] = low

        @pl.when(step >= steps // 2)
        def _():
            place = (step - steps // 2) * chunk + part * sub
            zs_ref[:, pl.ds(pl.multiple_of(place, 128), sub)] = low

        term = dot(low, up_ref[:, cols], NT)
        total = term if total is None else total + term
    du_ref[...] += total

    @pl.when(step == steps - 1)
    def _():
        def body(i, carry):
            gain_sum, shift_sum, out_sum = carry
            at = pl.ds(pl.multiple_of(i * rows, rows), rows)
            hat = hat1_ref[at, :]
            normed = hat * gain_ref[0:1, :] + vec_ref[1:2, :]
            bent = jnp.tanh(normed * (1.0 / ff_limit))
            grad = de_ref[at, :] + du_ref[at, :] * (1.0 - bent * bent)
            dy = norm_back(grad, hat, rate1_ref[at, 0:1], gain_ref[0:1, :])
            low = dy.astype(bf16)
            dy_ref[at, :] = dy
            df_ref[at, :] = low
            return (
                gain_sum + jnp.sum(grad * hat, axis=0, keepdims=True),
                shift_sum + jnp.sum(grad, axis=0, keepdims=True),
                out_sum + jnp.sum(low.astype(f32), axis=0, keepdims=True),
            )

        gain_sum, shift_sum, out_sum = lax.fori_loop(0, count, body, (zero, zero, zero))
        small_ref[0:1, :] = out_sum
        small_ref[1:2, :] = shift_sum
        small_ref[4:5, :] = gain_sum
        small_ref[6:8, :] = jnp.zeros((2, width), f32)
        ok_ref[...] = df_ref[:, mine]
        os_ref[...] = df_ref[:, other]
        inv = 1.0 / ctx_limit
        for w_ref, ctx_ref, out_ref in ((wo_ref, co_ref, dco_ref), (wt_ref, ct_ref, dct_ref)):
            bent = jnp.tanh(ctx_ref[...] * inv)
            grad = dot(df_ref[...], w_ref[...], NT)
            out_ref[...] = (grad * (1.0 - bent * bent)).astype(bf16)


def ff_bwd(
    core, clips, dx, hat2, rate2, hat1, rate1, vec, gain, slope, w_up, w_down, wo_own, wo_oth,
    ctx_own, ctx_oth,
):
    seq, width = dx.shape
    half = ctx_own.shape[1]
    hidden = w_up.shape[1]
    chunk = 512
    steps = hidden // chunk
    span = steps // 2

    def place(t, core_ref):
        first = t < span
        return jnp.where(first, core_ref[0] * span + t, (1 - core_ref[0]) * span + t - span)

    full = whole(seq, width)
    part = whole(seq, width // 2)
    outs = [
        (whole(seq, hidden // 2), shape((seq, hidden // 2), bf16)),
        (whole(seq, hidden // 2), shape((seq, hidden // 2), bf16)),
        (part, shape((seq, width // 2), bf16)),
        (part, shape((seq, width // 2), bf16)),
        (part, shape((seq, width // 2), bf16)),
        (part, shape((seq, width // 2), bf16)),
        (full, shape((seq, width), f32)),
        (whole(seq, half), shape((seq, half), bf16)),
        (whole(seq, half), shape((seq, half), bf16)),
        (whole(8, width), shape((8, width), f32)),
        (pl.BlockSpec((1, chunk), lambda t, core: (0, place(t, core))), shape((1, hidden), f32)),
    ]
    return pl.pallas_call(
        ff_bwd_kernel,
        grid_spec=pltpu.PrefetchScalarGridSpec(
            num_scalar_prefetch=1,
            grid=(steps,),
            in_specs=[
                pl.BlockSpec(memory_space=pltpu.SMEM),
                full,
                full,
                whole(seq, 128),
                full,
                whole(seq, 128),
                whole(*vec.shape),
                whole(*gain.shape),
                pl.BlockSpec((seq, chunk), lambda t, core: (0, place(t, core))),
                pl.BlockSpec((width, chunk), lambda t, core: (0, place(t, core))),
                pl.BlockSpec((chunk, width), lambda t, core: (place(t, core), 0)),
                whole(half, width),
                whole(half, width),
                whole(seq, half),
                whole(seq, half),
            ],
            out_specs=[spec for spec, _ in outs],
            scratch_shapes=[
                pltpu.VMEM((seq, width), bf16),
                pltpu.VMEM((seq, width), f32),
                pltpu.VMEM((seq, width), f32),
            ],
        ),
        out_shape=[out for _, out in outs],
        compiler_params=params(52),
        cost_estimate=cost(4 * seq * width * hidden * 2, 20 * MIB),
        name="ff_bwd",
    )(
        core, clips, dx, hat2, rate2, hat1, rate1, vec, gain, slope, w_up, w_down, wo_own, wo_oth,
        ctx_own, ctx_oth,
    )


def attn_bwd_half(q_ref, k_ref, v_ref, c_ref, lse_ref, dc_ref, seg_q, seg_k):
    query, key, value, grad = q_ref[...], k_ref[...], v_ref[...], dc_ref[...]
    key_ext = jnp.concatenate([key, seg_k], axis=1)
    key_t = key.astype(f32).T.astype(bf16)
    product_t = (grad.astype(f32) * c_ref[...]).T
    d_key = d_value = None
    d_query_t = []
    for head in range(2):
        scaled = query * head_mask(head, HEAD**-0.5)
        scores = dot(key_ext, jnp.concatenate([scaled, seg_q], axis=1), NT)
        probs = jnp.exp(scores - lse_ref[0, head : head + 1, :])
        grad_head = grad * head_mask(head, 1.0)
        d_probs = dot(value, grad_head, NT)
        delta = jnp.sum(product_t[head * HEAD : (head + 1) * HEAD], axis=0, keepdims=True)
        d_scores = (probs * (d_probs - delta)).astype(bf16)
        term_v = dot(probs.astype(bf16), grad_head)
        term_k = dot(d_scores, scaled)
        d_value = term_v if d_value is None else d_value + term_v
        d_key = term_k if d_key is None else d_key + term_k
        d_query_t.append(dot(key_t[head * HEAD : (head + 1) * HEAD], d_scores))
    d_query = jnp.concatenate(d_query_t, axis=0).T * HEAD**-0.5
    return d_query.astype(bf16), d_key.astype(bf16), d_value.astype(bf16)


def attn_bwd_kernel(
    clip_ref, x_ref, dy_ref, sq_ref, sk_ref,
    qo_ref, ko_ref, vo_ref, co_ref, lo_ref, dco_ref, wo_ref,
    qt_ref, kt_ref, vt_ref, ct_ref, lt_ref, dct_ref, wt_ref,
    dqo_ref, dko_ref, dvo_ref, dqt_ref, dkt_ref, dvt_ref, bo_ref, bt_ref, dx_ref, acc_ref,
):
    step = pl.program_id(0)
    seq = x_ref.shape[0]
    rows = 64
    own = attn_bwd_half(qo_ref, ko_ref, vo_ref, co_ref, lo_ref, dco_ref, sq_ref[...], sk_ref[...])
    oth = attn_bwd_half(qt_ref, kt_ref, vt_ref, ct_ref, lt_ref, dct_ref, sq_ref[...], sk_ref[...])
    dqo_ref[...], dko_ref[...], dvo_ref[...] = own
    dqt_ref[...], dkt_ref[...], dvt_ref[...] = oth
    for out_ref, grads in ((bo_ref, own), (bt_ref, oth)):
        out_ref[0:1, :] = jnp.sum(grads[0].astype(f32), axis=0, keepdims=True)
        out_ref[1:2, :] = jnp.sum(grads[2].astype(f32), axis=0, keepdims=True)
        out_ref[2:8, :] = jnp.zeros((6, PAIR), f32)
    total = None
    for which in range(3):
        term = dot(
            jnp.concatenate([own[which], oth[which]], axis=1),
            jnp.concatenate([wo_ref[which], wt_ref[which]], axis=1),
            NT,
        )
        total = term if total is None else total + term

    @pl.when(step == 0)
    def _():
        acc_ref[...] = total

    @pl.when(step > 0)
    def _():
        acc_ref[...] += total

    @pl.when(step == pl.num_programs(0) - 1)
    def _():
        inv = 1.0 / clip_ref[0]

        def body(i, carry):
            at = pl.ds(pl.multiple_of(i * rows, rows), rows)
            bent = jnp.tanh(x_ref[at, :].astype(f32) * inv)
            dx_ref[at, :] = dy_ref[at, :] + acc_ref[at, :] * (1.0 - bent * bent)
            return carry

        lax.fori_loop(0, seq // rows, body, 0)


def attn_bwd(clips, x, dy, seg_q, seg_k, own, oth):
    seq, width = x.shape
    cols = own[0].shape[1]
    steps = cols // PAIR
    block = pl.BlockSpec((seq, PAIR), lambda t: (0, t))
    half_specs = [
        block,
        block,
        block,
        block,
        pl.BlockSpec((1, 8, seq), lambda t: (t, 0, 0)),
        block,
        pl.BlockSpec((3, width, PAIR), lambda t: (0, 0, t)),
    ]
    return pl.pallas_call(
        attn_bwd_kernel,
        grid=(steps,),
        in_specs=[
            pl.BlockSpec(memory_space=pltpu.SMEM),
            whole(seq, width),
            whole(seq, width),
            whole(seq, PAIR),
            whole(seq, PAIR),
        ]
        + half_specs * 2,
        out_specs=[block] * 6
        + [pl.BlockSpec((8, PAIR), lambda t: (0, t))] * 2
        + [whole(seq, width)],
        out_shape=[shape((seq, cols), bf16)] * 6
        + [shape((8, cols), f32)] * 2
        + [shape((seq, width), f32)],
        scratch_shapes=[pltpu.VMEM((seq, width), f32)],
        compiler_params=params(40),
        cost_estimate=cost(14 * seq * width * width + 40 * seq * seq * width, 14 * MIB),
        name="attn_bwd",
    )(clips, x, dy, seg_q, seg_k, *own, *oth)


def w_ff_kernel(um_ref, uo_ref, zm_ref, zo_ref, gm_ref, go_ref, fm_ref, fo_ref, out_ref, ut_ref):
    step = pl.program_id(0)
    chips, _, lanes = out_ref.shape
    seq, width = um_ref.shape
    tall = width // chips
    quarters = pl.num_programs(0)

    @pl.when(step == 0)
    def _():
        ut_ref[:, :seq] = um_ref[...].T
        ut_ref[:, seq:] = uo_ref[...].T

    grad_up = dot(ut_ref[:, :seq], zm_ref[...]) + dot(ut_ref[:, seq:], zo_ref[...])
    grad_up = grad_up.astype(bf16)
    for chip in range(chips):
        at = pl.ds(pl.multiple_of(step * tall, 16), tall)
        out_ref[chip, at, :] = grad_up[chip * tall : (chip + 1) * tall]
    start = out_ref.shape[1] // 2
    span = start
    per = gm_ref.shape[1] // span
    for part in range(per):
        cols = slice(part * span, (part + 1) * span)
        grad_down = dot(gm_ref[:, cols], fm_ref[...], TN) + dot(go_ref[:, cols], fo_ref[...], TN)
        out_ref[step * per + part, start:, :] = grad_down.astype(bf16)


def w_ff(chips, u_mine, u_core, dz_mine, dz_core, g_mine, g_core, df_mine, df_core):
    seq, width = u_mine.shape
    hidden = g_mine.shape[1]
    lanes = width // 2
    steps = dz_mine.shape[1] // lanes
    tall = 2 * (hidden // chips)
    z_block = pl.BlockSpec((seq, lanes), lambda t: (0, t))
    g_block = pl.BlockSpec((seq, hidden // steps), lambda t: (0, t))
    return pl.pallas_call(
        w_ff_kernel,
        grid=(steps,),
        in_specs=[
            whole(seq, width),
            whole(seq, width),
            z_block,
            z_block,
            g_block,
            g_block,
            whole(seq, lanes),
            whole(seq, lanes),
        ],
        out_specs=whole(chips, tall, lanes),
        out_shape=shape((chips, tall, lanes), bf16),
        scratch_shapes=[pltpu.VMEM((width, 2 * seq), bf16)],
        compiler_params=params(40),
        cost_estimate=cost(4 * seq * width * hidden, 17 * MIB),
        name="w_ff",
    )(u_mine, u_core, dz_mine, dz_core, g_mine, g_core, df_mine, df_core)


def w_att_kernel(
    core_ref, a_ref, dqo_ref, dko_ref, dvo_ref, dqt_ref, dkt_ref, dvt_ref,
    cm_ref, cc_ref, dom_ref, doc_ref,
    keep_o_ref, keep_t_ref, send_o_ref, send_t_ref, out_o_ref, out_t_ref, at_ref, spare_ref,
):
    width = a_ref.shape[1]
    chips, tall, cols = keep_o_ref.shape
    core = core_ref[0]
    piece = 48
    per = tall // piece
    at_ref[...] = a_ref[...].T
    sides = (
        ((dqo_ref, dko_ref, dvo_ref), keep_o_ref, send_o_ref),
        ((dqt_ref, dkt_ref, dvt_ref), keep_t_ref, send_t_ref),
    )
    for grads, keep_ref, send_ref in sides:
        for which in range(3):
            result = dot(at_ref[...], grads[which][...]).astype(bf16)
            for j in range(width // piece):
                index = which * (width // piece) + j
                block, sub = index // per, index % per
                spare_ref[block % 2, block // 2, sub * piece : (sub + 1) * piece, :] = result[
                    j * piece : (j + 1) * piece
                ]
        keep_ref[...] = spare_ref[core]
        send_ref[...] = spare_ref[1 - core]
    half = width // 2
    heads = half // HEAD
    for base, out_ref in ((0, out_o_ref), (half, out_t_ref)):
        result = dot(cm_ref[:, base : base + half], dom_ref[...], TN) + dot(
            cc_ref[:, base : base + half], doc_ref[...], TN
        )
        for chip in range(chips):
            for pair in range(heads // 2):
                first = (2 * pair) * HEAD + 8 * chip
                second = first + HEAD
                out_ref[chip, pair * 16 : (pair + 1) * 16, :] = jnp.concatenate(
                    [result[first : first + 8], result[second : second + 8]], axis=0
                ).astype(bf16)


def w_att(chips, core, act, d_own, d_oth, cq_mine, cq_core, do_mine, do_core):
    seq, width = act.shape
    cols = width // 2
    tall = 3 * width // (2 * chips)
    vmem = pl.BlockSpec(memory_space=pltpu.VMEM)
    outs = [shape((chips, tall, cols), bf16)] * 4 + [
        shape((chips, cols // chips, cols), bf16)
    ] * 2
    return pl.pallas_call(
        w_att_kernel,
        in_specs=[pl.BlockSpec(memory_space=pltpu.SMEM)] + [vmem] * 11,
        out_specs=[vmem] * 6,
        out_shape=outs,
        scratch_shapes=[
            pltpu.VMEM((width, seq), bf16),
            pltpu.VMEM((2, chips, tall, cols), bf16),
        ],
        compiler_params=params(40),
        cost_estimate=cost(8 * seq * width * width, 12 * MIB),
        name="w_att",
    )(core, act, *d_own, *d_oth, cq_mine, cq_core, do_mine, do_core)


def local(
    hidden_in, cotangent, segment_ids, clip_ranges, w_qkv, bias_qv, w_out, vector_bias, ln_gain,
    w_up, bias_up, w_down,
):
    layers = w_qkv.shape[0]
    row_count, half_seq, width = hidden_in.shape
    seq = segment_ids.shape[1]
    cols = w_qkv.shape[3]
    heads = cols // HEAD
    hidden = w_up.shape[2]
    dp_count = lax.axis_size("dp")
    assert lax.axis_size("mp") == 2 and row_count == 2 and seq == 2 * half_seq
    bits = dp_count.bit_length() - 1
    assert dp_count == 1 << bits and bits >= 1
    chips = dp_count // 2
    side = lax.axis_index("mp")
    place = lax.axis_index("dp")
    core = place % 2
    core_arr = core.reshape(1).astype(jnp.int32)

    def over_mp(value):
        return lax.ppermute(value, "mp", [(0, 1), (1, 0)])

    def over_bit(value, bit):
        return lax.ppermute(value, "dp", [(i, i ^ (1 << bit)) for i in range(dp_count)])

    def over_core(value):
        return over_bit(value, 0)

    def pick(value, index, axis):
        return lax.dynamic_index_in_dim(value, index, axis, keepdims=False)

    def ordered(index, mine, theirs, axis):
        first = jnp.where(index == 0, mine, theirs)
        second = jnp.where(index == 0, theirs, mine)
        return jnp.concatenate([first, second], axis=axis)

    def after(value, *earlier):
        return lax.optimization_barrier((value,) + earlier)[0]

    def gather_row(array, hold=()):
        return jnp.concatenate(
            [pick(array, side, 0), over_mp(after(pick(array, 1 - side, 0), *hold))], axis=0
        )

    x = gather_row(hidden_in)
    bias_oth = over_mp(bias_qv)
    limits = clip_ranges.astype(f32)
    clips = [
        jnp.concatenate([limits[i], limits[min(i + 1, layers - 1), :1]]) for i in range(layers)
    ]
    seg_row = pick(segment_ids, side, 0).reshape(2, half_seq)
    seg_row = jnp.concatenate([pick(seg_row, side, 0), pick(seg_row, 1 - side, 0)])
    same = seg_row[:, None] == jnp.arange(PAIR, dtype=seg_row.dtype)[None, :]
    used = (jnp.arange(PAIR) < seq)[None, :]
    seg_q = jnp.where(same, BIG, 0.0).astype(bf16)
    seg_k = jnp.where(same, 0.0, 1.0).astype(bf16) * used.astype(bf16)

    def fetch(weight, axis, hold):
        pieces = weight.shape[axis] // 2
        sent = lax.dynamic_slice_in_dim(weight, core * pieces, pieces, axis)
        got = over_mp(after(sent, hold))
        return ordered(core, got, over_core(got), axis)

    hold = x
    wq_oth, wo_oth = [], []
    for layer in range(layers):
        wq_oth.append(fetch(w_qkv[layer], 1, hold))
        wo_oth.append(fetch(w_out[layer], 0, hold))
        hold = wq_oth[-1][0, :8, :128]
    dx = gather_row(cotangent, (hold,))

    r0 = limits[0, 0]
    act = (r0 * jnp.tanh(x.astype(f32) / r0)).astype(bf16)
    stored = []
    for layer in range(layers):
        last = layer == layers - 1
        own = attn_fwd(act, w_qkv[layer], bias_qv[layer], seg_q, seg_k)
        oth = attn_fwd(act, wq_oth[layer], bias_oth[layer], seg_q, seg_k)
        outs = ff_fwd(
            last, clips[layer], x, own[3], oth[3], w_out[layer], wo_oth[layer],
            vector_bias[layer], ln_gain[layer], w_up[layer], bias_up[layer][None], w_down[layer],
        )
        cq, hat1, rate1, u, g, slope, hat2, rate2 = outs[:8]
        shared = over_core(cq), over_core(u), over_core(g)
        stored.append((x, act, own, oth, cq, hat1, rate1, u, g, slope, hat2, rate2, shared))
        if last:
            hidden_row = outs[8]
        else:
            x, act = outs[8], outs[9]

    def spread_row(row, theirs):
        mine = row[None, :half_seq]
        return ordered(side, mine, theirs[None].astype(row.dtype), 0)

    hidden_out = spread_row(hidden_row, over_mp(hidden_row[half_seq:]))

    fast = chips == 8 and width == 768 and hidden == 3072 and cols == 384

    def reduce_stage(value, bit, axis, dtype=bf16):
        mybit = (place >> bit) & 1
        keep = pick(value, mybit, axis)
        sent = pick(value, 1 - mybit, axis)
        got = over_bit(sent, bit)
        return (keep.astype(f32) + got.astype(f32)).astype(dtype)

    qkv_list, out_list, up_list, down_list, small_list = [], [], [], [], []
    for layer in reversed(range(layers)):
        x, act, own, oth, cq, hat1, rate1, u, g, slope, hat2, rate2, shared = stored[layer]
        (
            dz_keep, dz_send, df_keep, df_send, do_keep, do_send, dy, dc_own, dc_oth, small, d_bup,
        ) = ff_bwd(
            core_arr, clips[layer], dx, hat2, rate2, hat1, rate1, vector_bias[layer],
            ln_gain[layer], slope, w_up[layer], w_down[layer], w_out[layer], wo_oth[layer],
            own[3], oth[3],
        )
        outs = attn_bwd(
            clips[layer], x, dy, seg_q, seg_k,
            (*own, dc_own, w_qkv[layer]), (*oth, dc_oth, wq_oth[layer]),
        )
        d_own, d_oth = outs[:3], outs[3:6]
        dx = outs[8]
        d_bias = ordered(side, outs[6][:2], outs[7][:2], 1)
        small_list.append(
            jnp.concatenate([d_bias, small[:6], d_bup.reshape(-1, width)], axis=0)
        )
        if fast:
            cq_core, u_core, g_core = shared
            packed = w_ff(
                chips, u, u_core, dz_keep, over_core(dz_send), g, g_core, df_keep,
                over_core(df_send),
            )
            tall = packed.shape[1]
            packed = packed.reshape(2, 2, 2, tall, cols)
            packed = reduce_stage(packed, 1, 2)
            packed = reduce_stage(packed, 2, 1)
            packed = reduce_stage(packed, 3, 0)
            packed = packed.astype(f32) + over_mp(packed).astype(f32)
            share = hidden // chips
            up = packed[:share].reshape(hidden // width, 2, share // 8, cols)
            keep, sent = pick(up, core, 1), pick(up, 1 - core, 1).astype(bf16)
            up = ordered(core, keep[None], over_core(sent).astype(f32)[None], 0)
            up_list.append(up.transpose(2, 0, 1, 3).reshape(-1))
            down = packed[share:].reshape(2, share // 2, cols)
            keep, sent = pick(down, core, 0), pick(down, 1 - core, 0).astype(bf16)
            down = ordered(core, keep[:, None], over_core(sent).astype(f32)[:, None], 1)
            down_list.append(down.reshape(-1))

            keep_o, keep_t, send_o, send_t, out_o, out_t = w_att(
                chips, core_arr, act, d_own, d_oth, cq, cq_core, do_keep, over_core(do_send)
            )
            send_o, send_t = over_core(send_o), over_core(send_t)
            mine = jnp.concatenate([keep_o + send_o, out_o], axis=1)
            theirs = jnp.concatenate([keep_t + send_t, out_t], axis=1)
            packed = mine + over_mp(theirs)
            tall = packed.shape[1]
            packed = packed.reshape(2, 2, 2, tall, cols)
            packed = reduce_stage(packed, 1, 2)
            packed = reduce_stage(packed, 2, 1)
            packed = reduce_stage(packed, 3, 0, f32)
            share = keep_o.shape[1]
            qkv_list.append(
                packed[:share].reshape(share, heads, HEAD).transpose(1, 0, 2).reshape(heads, -1)
            )
            out = packed[share:].reshape(heads, 2, 4, cols)
            keep, sent = pick(out, core, 1), pick(out, 1 - core, 1).astype(bf16)
            out = ordered(core, keep[:, :, None], over_core(sent).astype(f32)[:, :, None], 2)
            out_list.append(out.reshape(heads, -1))
        else:
            dz = ordered(core, dz_keep, dz_send, 1)
            df = ordered(core, df_keep, df_send, 1)
            do = ordered(core, do_keep, do_send, 1)
            for lhs, rhs, bucket in ((u, dz, up_list), (g, df, down_list)):
                grad = dot(lhs, rhs, TN).reshape(-1)
                grad = grad + over_mp(grad)
                bucket.append(lax.psum_scatter(grad, "dp", scatter_dimension=0, tiled=True))
            sides = []
            for grads, part in ((d_own, cq[:, :cols]), (d_oth, cq[:, cols:])):
                qkv = jnp.stack([dot(act, grad, TN) for grad in grads])
                qkv = qkv.reshape(3, width, heads, HEAD).transpose(2, 0, 1, 3)
                sides.append((qkv.reshape(heads, -1), dot(part, do, TN).reshape(heads, -1)))
            for k, bucket in ((0, qkv_list), (1, out_list)):
                grad = sides[0][k] + over_mp(sides[1][k])
                bucket.append(lax.psum_scatter(grad, "dp", scatter_dimension=1, tiled=True))

    grad_input = spread_row(dx, over_mp(dx[half_seq:].astype(bf16)))
    small = jnp.stack(small_list[::-1])
    small = small + over_mp(small)
    for bit in range(bits):
        small = small + over_bit(small, bit)
    grad_bias_qv = lax.dynamic_slice_in_dim(small[:, :2], side * cols, cols, 2)
    return (
        hidden_out,
        grad_input,
        jnp.stack(qkv_list[::-1]),
        grad_bias_qv,
        jnp.stack(out_list[::-1]),
        small[:, 2:6],
        small[:, 6:8],
        jnp.stack(up_list[::-1]),
        small[:, 8:].reshape(layers, hidden),
        jnp.stack(down_list[::-1]),
    )


def solution(mesh):
    return jax.shard_map(
        local,
        mesh=mesh,
        in_specs=(
            P("dp", "mp", None),
            P("dp", "mp", None),
            P("dp", None),
            P(),
            P(None, None, None, "mp"),
            P(None, None, "mp"),
            P(None, "mp", None),
            P(),
            P(),
            P(),
            P(),
            P(),
        ),
        out_specs=(
            P("dp", "mp", None),
            P("dp", "mp", None),
            P(None, "mp", "dp"),
            P(None, None, "mp"),
            P(None, "mp", "dp"),
            P(),
            P(),
            P(None, "dp"),
            P(),
            P(None, "dp"),
        ),
        check_vma=False,
    )
```

```python
import functools

import jax
import jax.numpy as jnp
from jax import lax
from jax.experimental import pallas as pl
from jax.experimental.pallas import tpu as pltpu
from jax.sharding import PartitionSpec as P

HEAD = 64
PAIR = 2 * HEAD
EPS = 1e-06
BIG = -1e30
INV_SQRT2 = 0.7071067811865476
INV_SQRT2PI = 0.3989422804014327

f32 = jnp.float32
bf16 = jnp.bfloat16
MIB = 1024 * 1024
FF_CHUNK = 768
FF_SUB = 256

NT = (((1,), (1,)), ((), ()))
TN = (((0,), (0,)), ((), ()))


def dot(lhs, rhs, dims=(((1,), (0,)), ((), ()))):
    return lax.dot_general(lhs, rhs, dims, preferred_element_type=f32)


def whole(*dims):
    return pl.BlockSpec(dims, lambda *_: (0,) * len(dims))


def at_layer(layer, *dims):
    return pl.BlockSpec((None, *dims), lambda *_: (layer,) + (0,) * len(dims))


def smem():
    return pl.BlockSpec(memory_space=pltpu.SMEM)


class Spot:
    def __init__(self, array):
        self.array = array
        self.latest = ()


def launch(body, name, spot, hold, ins, outs, scratch=(), grid=(1,), us=3.0):
    count = len(ins)
    known = [array for array, _ in ins]
    hold = [array for array in (*hold, *spot.latest) if not any(array is k for k in known)]

    def kernel(spot_ref, *refs):
        body(spot_ref, *refs[:count], *refs[count + len(hold) :])

    in_specs = [spec for _, spec in ins] + [pl.BlockSpec(memory_space=pl.ANY)] * len(hold)
    results = pl.pallas_call(
        kernel,
        grid_spec=pltpu.PrefetchScalarGridSpec(
            num_scalar_prefetch=1,
            grid=grid,
            in_specs=in_specs,
            out_specs=[spec for spec, _ in outs],
            scratch_shapes=list(scratch),
        ),
        out_shape=[out for _, out in outs],
        compiler_params=pltpu.CompilerParams(vmem_limit_bytes=60 * MIB),
        cost_estimate=pl.CostEstimate(
            flops=int(us * 1e9), bytes_accessed=int(us * 1e6), transcendentals=0
        ),
        name=name,
    )(spot.array, *known, *hold)
    spot.latest = (results[0],)
    return results


def shape(dims, dtype):
    return jax.ShapeDtypeStruct(dims, dtype)


def head_mask(head, value):
    lane = lax.broadcasted_iota(jnp.int32, (1, PAIR), 1)
    return jnp.where((lane // HEAD) == head, value, 0.0).astype(bf16)


CORE, SIDE, AXIS_X, AXIS_Z0, AXIS_Z1 = range(5)


def enter_kernel(layer_limit, spot_ref, lim_ref, mine_ref, recv_ref, act_ref):
    limit = lim_ref[0, 0]
    inv = 1.0 / limit
    half = mine_ref.shape[0]
    act_ref[:half, :] = (limit * jnp.tanh(mine_ref[...].astype(f32) * inv)).astype(bf16)
    act_ref[half:, :] = (limit * jnp.tanh(recv_ref[...].astype(f32) * inv)).astype(bf16)


def enter(spot, limits, hidden_in, recv):
    half, width = recv.shape
    (act,) = launch(
        functools.partial(enter_kernel, 0), "enter", spot, (),
        [(limits, smem()), (hidden_in, my_row(half, width)), (recv, whole(half, width))],
        [(whole(2 * half, width), shape((2 * half, width), bf16))],
        us=3.0,
    )
    return act


def my_row(half, width):
    return pl.BlockSpec((None, half, width), lambda t, s: (s[SIDE], 0, 0))


def place_kernel(spot_ref, mine_ref, recv_ref, out_ref):
    out_ref[spot_ref[SIDE]] = mine_ref[...].astype(out_ref.dtype)
    out_ref[1 - spot_ref[SIDE]] = recv_ref[...].astype(out_ref.dtype)


def place_rows(spot, hold, mine, recv, dtype):
    half, width = mine.shape
    (out,) = launch(
        place_kernel, "place_rows", spot, hold,
        [(mine, whole(half, width)), (recv, whole(half, width))],
        [(whole(2, half, width), shape((2, half, width), dtype))],
        us=2.5
    )
    return out


def copy_kernel(spot_ref, *refs):
    count = len(refs) // 2
    for source, target in zip(refs[:count], refs[count:]):
        target[...] = source[...]


def pick_weights(spot, hold, layer, w_qkv, w_out):
    _, _, width, cols = w_qkv.shape
    rows = width // 2
    wide = w_out.shape[2] // 2
    return launch(
        copy_kernel, "pick_weights", spot, hold,
        [
            (w_qkv, pl.BlockSpec((None, 3, rows, cols), lambda t, s: (layer, 0, s[CORE], 0))),
            (w_out, pl.BlockSpec((None, cols, wide), lambda t, s: (layer, 0, s[CORE]))),
        ],
        [
            (whole(3, rows, cols), shape((3, rows, cols), bf16)),
            (whole(cols, wide), shape((cols, wide), bf16)),
        ],
        us=3.0,
    )


def relay(spot, array):
    (out,) = launch(
        copy_kernel, "relay", spot, (),
        [(a, source) for a, source, _, _ in relay_piece(array)],
        [(target, out) for _, _, target, out in relay_piece(array)],
        grid=(3,),
        us=2.5,
    )
    return out


def attn_fwd_kernel(pieces, relays, spot_ref, a_ref, *refs):
    w_refs = refs[:pieces]
    b_ref, sq_ref, sk_ref = refs[pieces : pieces + 3]
    sources = refs[pieces + 3 : pieces + 3 + relays]
    q_ref, k_ref, v_ref, c_ref, lse_ref = refs[pieces + 3 + relays : pieces + 8 + relays]
    for source, target in zip(sources, refs[pieces + 8 + relays :]):
        target[...] = source[...]
    seq, width = a_ref.shape
    share = width // pieces
    both = value = None
    for piece, w_ref in enumerate(w_refs):
        if pieces == 1:
            act = a_ref[...]
        else:
            which = jnp.where(spot_ref[CORE] == 0, piece, 1 - piece)
            act = a_ref[:, pl.ds(pl.multiple_of(which * share, 128), share)]
        term = dot(act, jnp.concatenate([w_ref[0], w_ref[1]], axis=1))
        both = term if both is None else both + term
        term = dot(act, w_ref[2])
        value = term if value is None else value + term
    query = (both[:, :PAIR] + b_ref[0:1, :]).astype(bf16)
    key = both[:, PAIR:].astype(bf16)
    value = value + b_ref[1:2, :]
    value_t = value.T.astype(bf16)
    q_ref[...] = query
    k_ref[...] = key
    v_ref[...] = value.astype(bf16)
    key_ext = jnp.concatenate([key, sk_ref[...]], axis=1)
    parts = []
    ones = jnp.ones((16, seq), bf16)
    for head in range(2):
        query_ext = jnp.concatenate([query * head_mask(head, HEAD**-0.5), sq_ref[...]], axis=1)
        scores = dot(key_ext, query_ext, NT)
        top = jnp.max(scores, axis=0, keepdims=True)
        weights = jnp.exp(scores - top).astype(bf16)
        summed = dot(
            jnp.concatenate([value_t[head * HEAD : (head + 1) * HEAD], ones], axis=0), weights
        )
        total = summed[HEAD : HEAD + 1]
        parts.append(summed[:HEAD] * (1.0 / total))
        lse_ref[0, head : head + 1, :] = top + jnp.log(total)
    c_ref[...] = jnp.concatenate(parts, axis=0).T


def weight_specs(layer, weights):
    if len(weights) == 1:
        width = weights[0].shape[2]
        return [pl.BlockSpec((None, 3, width, PAIR), lambda t, s: (layer, 0, 0, t))]
    share = weights[0].shape[1]
    return [pl.BlockSpec((3, share, PAIR), lambda t, s: (0, 0, t))] * 2


def relay_weights(layer, w_qkv, w_out):
    _, _, width, cols = w_qkv.shape
    rows, wide, deep = width // 2, w_out.shape[2] // 2, cols // 3
    return [
        (
            w_qkv,
            pl.BlockSpec((None, 1, rows, cols), lambda t, s: (layer, t, s[CORE], 0)),
            pl.BlockSpec((1, rows, cols), lambda t, s: (t, 0, 0)),
            shape((3, rows, cols), bf16),
        ),
        (
            w_out,
            pl.BlockSpec((None, deep, wide), lambda t, s: (layer, t, s[CORE])),
            pl.BlockSpec((deep, wide), lambda t, s: (t, 0)),
            shape((cols, wide), bf16),
        ),
    ]


def relay_piece(array):
    lead, *rest = array.shape
    spec = pl.BlockSpec((lead // 3, *rest), lambda t, s: (t,) + (0,) * len(rest))
    return [(array, spec, spec, shape(array.shape, array.dtype))]


def relay_row(rows):
    _, half, width = rows.shape
    wide = width // 3
    return [
        (
            rows,
            pl.BlockSpec((None, half, wide), lambda t, s: (1 - s[SIDE], 0, t)),
            pl.BlockSpec((half, wide), lambda t, s: (0, t)),
            shape((half, width), rows.dtype),
        )
    ]


def attn_fwd(spot, hold, layer, act, weights, bias, seg_q, seg_k, relays=()):
    seq, width = act.shape
    cols = bias.shape[2]
    steps = cols // PAIR
    block = pl.BlockSpec((seq, PAIR), lambda t, s: (0, t))
    return launch(
        functools.partial(attn_fwd_kernel, len(weights), len(relays)), "attn_fwd", spot, hold,
        [(act, whole(seq, width))]
        + list(zip(weights, weight_specs(layer, weights)))
        + [
            (bias, pl.BlockSpec((None, 2, PAIR), lambda t, s: (layer, 0, t))),
            (seg_q, whole(seq, PAIR)),
            (seg_k, whole(seq, PAIR)),
        ]
        + [(array, source) for array, source, _, _ in relays],
        [
            (block, shape((seq, cols), bf16)),
            (block, shape((seq, cols), bf16)),
            (block, shape((seq, cols), bf16)),
            (block, shape((seq, cols), f32)),
            (pl.BlockSpec((1, 8, seq), lambda t, s: (t, 0, 0)), shape((steps, 8, seq), f32)),
        ]
        + [(target, out) for _, _, target, out in relays],
        grid=(steps,),
        us=8.0
    )


def norm_rows(entries):
    centred = entries - jnp.mean(entries, axis=-1, keepdims=True)
    spread = jnp.mean(centred * centred, axis=-1, keepdims=True)
    rate = lax.rsqrt(spread + EPS)
    return centred * rate, rate


def ff_fwd_kernel(
    layer, last, spot_ref, lim_ref, xt_ref, xb_ref, co_ref, ct_ref, wo_ref, wy_ref, wc_ref,
    vec_ref, gain_ref, up_ref, bup_ref, down_ref, *rest
):
    if last:
        gt_ref, gb_ref, *rest = rest
    cu_ref, hat1_ref, rate1_ref, g_ref, slope_ref, *rest = rest
    acc_ref = rest[-1]
    step = pl.program_id(0)
    half_seq, width = xt_ref.shape
    half = co_ref.shape[1]
    wide = width // 2
    rows = 64
    ctx_limit, ff_limit, act_limit = lim_ref[layer, 1], lim_ref[layer, 2], lim_ref[layer, 3]

    @pl.when(step == 0)
    def _():
        inv = 1.0 / ctx_limit
        cu_ref[:, :half] = (ctx_limit * jnp.tanh(co_ref[...] * inv)).astype(bf16)
        cu_ref[:, half:width] = (ctx_limit * jnp.tanh(ct_ref[...] * inv)).astype(bf16)
        acc_ref[...] = dot(cu_ref[:, :half], wo_ref[...])
        for piece, w_ref in enumerate((wy_ref, wc_ref)):
            which = jnp.where(spot_ref[CORE] == 0, piece, 1 - piece)
            at = pl.ds(pl.multiple_of(which * wide, 128), wide)
            acc_ref[:, at] += dot(cu_ref[:, half:width], w_ref[...])

        for base, x_ref in ((0, xt_ref), (half_seq, xb_ref)):

            def body(i, carry, base=base, x_ref=x_ref):
                start = pl.multiple_of(i * rows, rows)
                at = pl.ds(base + start, rows)
                hat, rate = norm_rows(
                    x_ref[pl.ds(start, rows), :].astype(f32) + (acc_ref[at, :] + vec_ref[0:1, :])
                )
                hat1_ref[at, :] = hat
                rate1_ref[at, :] = jnp.broadcast_to(rate, (rows, 128))
                normed = hat * gain_ref[0:1, :] + vec_ref[1:2, :]
                bent = ff_limit * jnp.tanh(normed * (1.0 / ff_limit))
                cu_ref[at, width:] = bent.astype(bf16)
                acc_ref[at, :] = normed + vec_ref[2:3, :]
                return carry

            lax.fori_loop(0, half_seq // rows, body, 0)

    inv_act = 1.0 / act_limit
    chunk = up_ref.shape[1]
    sub = FF_SUB
    for part in range(chunk // sub):
        cols = slice(part * sub, (part + 1) * sub)
        pre = dot(cu_ref[:, width:], up_ref[:, cols]) + bup_ref[layer : layer + 1, cols]
        cdf = 0.5 * lax.erf(pre * INV_SQRT2) + 0.5
        pdf = jnp.exp(pre * pre * -0.5) * INV_SQRT2PI
        bent = jnp.tanh(pre * cdf * inv_act)
        g_ref[:, cols] = (act_limit * bent).astype(bf16)
        slope_ref[:, cols] = ((1.0 - bent * bent) * (cdf + pre * pdf)).astype(bf16)
    acc_ref[...] += dot(g_ref[...], down_ref[...])

    @pl.when(step == pl.num_programs(0) - 1)
    def _():
        if last:
            top_ref, bottom_ref, de_ref, df_ref, sums_ref = rest[:-1]
            sums = norm_sums(width)
            for base, out_ref, in_ref in ((0, top_ref, gt_ref), (half_seq, bottom_ref, gb_ref)):

                def body(i, carry, base=base, out_ref=out_ref, in_ref=in_ref):
                    here = pl.ds(pl.multiple_of(i * rows, rows), rows)
                    at = pl.ds(base + pl.multiple_of(i * rows, rows), rows)
                    hat, rate = norm_rows(acc_ref[at, :])
                    new = hat * gain_ref[1:2, :] + vec_ref[3:4, :]
                    out_ref[here, :] = new.astype(bf16)
                    grad = in_ref[here, :].astype(f32)
                    return leave_norm(grad, hat, rate, gain_ref, at, de_ref, df_ref, carry)

                sums = lax.fori_loop(0, half_seq // rows, body, sums)
            store_sums(sums, sums_ref)
        else:
            hat2_ref, rate2_ref, new_ref, act_ref = rest[:-1]
            limit = lim_ref[layer + 1, 0]

            def body(i, carry):
                at = pl.ds(pl.multiple_of(i * rows, rows), rows)
                hat, rate = norm_rows(acc_ref[at, :])
                hat2_ref[at, :] = hat
                rate2_ref[at, :] = jnp.broadcast_to(rate, (rows, 128))
                new = hat * gain_ref[1:2, :] + vec_ref[3:4, :]
                new_ref[at, :] = new
                act_ref[at, :] = (limit * jnp.tanh(new * (1.0 / limit))).astype(bf16)
                return carry

            lax.fori_loop(0, 2 * half_seq // rows, body, 0)


def norm_back(grad, hat, rate, gain):
    scaled = grad * gain
    mean = jnp.mean(scaled, axis=-1, keepdims=True)
    lean = jnp.mean(scaled * hat, axis=-1, keepdims=True)
    return rate * (scaled - mean - hat * lean)


def norm_sums(width):
    return (jnp.zeros((1, width), f32),) * 3


def leave_norm(grad, hat, rate, gain_ref, at, de_ref, df_ref, sums):
    de = norm_back(grad, hat, rate, gain_ref[1:2, :])
    df = de.astype(bf16)
    de_ref[at, :] = de
    df_ref[at, :] = df
    return (
        sums[0] + jnp.sum(df.astype(f32), axis=0, keepdims=True),
        sums[1] + jnp.sum(grad, axis=0, keepdims=True),
        sums[2] + jnp.sum(grad * hat, axis=0, keepdims=True),
    )


def store_sums(sums, sums_ref):
    sums_ref[...] = jnp.zeros_like(sums_ref)
    sums_ref[2:3, :] = sums[0]
    sums_ref[3:4, :] = sums[1]
    sums_ref[5:6, :] = sums[2]


def norm_outs(seq, width):
    return [
        (whole(seq, width), shape((seq, width), f32)),
        (whole(seq, width), shape((seq, width), bf16)),
        (whole(8, width), shape((8, width), f32)),
    ]


def halves(pair, half, width):
    if len(pair) == 1:
        return [
            (pair[0], pl.BlockSpec((half, width), lambda *_: (0, 0))),
            (pair[0], pl.BlockSpec((half, width), lambda *_: (1, 0))),
        ]
    first = my_row(half, width) if pair[0].ndim == 3 else whole(half, width)
    return [(pair[0], first), (pair[1], whole(half, width))]


def ff_fwd(
    spot, hold, layer, last, limits, x, ctx_own, ctx_oth, w_out, wo_oth, vec, gain, w_up, b_up,
    w_down, cot=None
):
    seq, half = ctx_own.shape
    width, hidden = w_up.shape[1:]
    chunk = FF_CHUNK
    steps = hidden // chunk
    tile = pl.BlockSpec((seq, chunk), lambda t, s: (0, t))
    full = whole(seq, width)
    outs = [
        (whole(seq, 2 * width), shape((seq, 2 * width), bf16)),
        (full, shape((seq, width), f32)),
        (whole(seq, 128), shape((seq, 128), f32)),
        (tile, shape((seq, hidden), bf16)),
        (tile, shape((seq, hidden), bf16)),
    ]
    if last:
        outs += [(whole(seq // 2, width), shape((seq // 2, width), bf16))] * 2
        outs += norm_outs(seq, width)
    else:
        outs += [
            (full, shape((seq, width), f32)),
            (whole(seq, 128), shape((seq, 128), f32)),
            (full, shape((seq, width), f32)),
            (full, shape((seq, width), bf16)),
        ]
    return launch(
        functools.partial(ff_fwd_kernel, layer, last), "ff_fwd", spot, hold,
        [(limits, smem())]
        + halves(x, seq // 2, width)
        + [
            (ctx_own, whole(seq, half)),
            (ctx_oth, whole(seq, half)),
            (w_out, at_layer(layer, half, width)),
            (wo_oth[0], whole(half, width // 2)),
            (wo_oth[1], whole(half, width // 2)),
            (vec, at_layer(layer, *vec.shape[1:])),
            (gain, at_layer(layer, *gain.shape[1:])),
            (w_up, pl.BlockSpec((None, width, chunk), lambda t, s: (layer, 0, t))),
            (b_up, pl.BlockSpec((b_up.shape[0], chunk), lambda t, s: (0, t))),
            (w_down, pl.BlockSpec((None, chunk, width), lambda t, s: (layer, t, 0))),
        ]
        + (halves(cot, seq // 2, width) if last else []),
        outs,
        scratch=[pltpu.VMEM((seq, width), f32)],
        grid=(steps,),
        us=21.0
    )


def ff_bwd_kernel(
    layer, spot_ref, lim_ref, de_ref, fin_ref, hat1_ref, rate1_ref, vec_ref, gain_ref, slope_ref,
    up_ref, down_ref, wo_ref, wy_ref, wc_ref, co_ref, ct_ref,
    zk_ref, ok_ref, os_ref, dy_ref, dco_ref, dct_ref, small_ref, bup_ref,
    do_ref, du_ref, dz_ref,
):
    step = pl.program_id(0)
    steps = pl.num_programs(0)
    seq, width = de_ref.shape
    half = width // 2
    rows = 64
    core = spot_ref[CORE]
    mine = pl.ds(pl.multiple_of(core * half, 128), half)
    other = pl.ds(pl.multiple_of((1 - core) * half, 128), half)
    zero = jnp.zeros((1, width), f32)
    ctx_limit, ff_limit = lim_ref[layer, 1], lim_ref[layer, 2]

    chunk = up_ref.shape[1]
    sub = FF_SUB
    for part in range(chunk // sub):
        cols = slice(part * sub, (part + 1) * sub)
        dz = dot(fin_ref[...], down_ref[cols, :], NT) * slope_ref[:, cols].astype(f32)
        low = dz.astype(bf16)
        bup_ref[:, cols] = jnp.sum(low.astype(f32), axis=0, keepdims=True)
        dz_ref[:, cols] = low
    term = dot(dz_ref[...], up_ref[...], NT)

    @pl.when(step == 0)
    def _():
        du_ref[...] = term

    @pl.when(step > 0)
    def _():
        du_ref[...] += term

    @pl.when(step < steps // 2)
    def _():
        zk_ref[:, pl.ds(pl.multiple_of(step * chunk, 128), chunk)] = dz_ref[...]

    @pl.when(step == steps - 1)
    def _():
        def body(i, carry):
            gain_sum, shift_sum, out_sum = carry
            at = pl.ds(pl.multiple_of(i * rows, rows), rows)
            hat = hat1_ref[at, :]
            normed = hat * gain_ref[0:1, :] + vec_ref[1:2, :]
            bent = jnp.tanh(normed * (1.0 / ff_limit))
            grad = de_ref[at, :] + du_ref[at, :] * (1.0 - bent * bent)
            dy = norm_back(grad, hat, rate1_ref[at, 0:1], gain_ref[0:1, :])
            low = dy.astype(bf16)
            dy_ref[at, :] = dy
            do_ref[at, :] = low
            return (
                gain_sum + jnp.sum(grad * hat, axis=0, keepdims=True),
                shift_sum + jnp.sum(grad, axis=0, keepdims=True),
                out_sum + jnp.sum(low.astype(f32), axis=0, keepdims=True),
            )

        sums = lax.fori_loop(0, seq // rows, body, (zero, zero, zero))
        small_ref[...] = jnp.zeros_like(small_ref)
        small_ref[0:1, :] = sums[2]
        small_ref[1:2, :] = sums[1]
        small_ref[4:5, :] = sums[0]
        ok_ref[...] = do_ref[:, mine]
        os_ref[...] = do_ref[:, other]
        inv = 1.0 / ctx_limit
        bent = jnp.tanh(co_ref[...] * inv)
        dco_ref[...] = (dot(do_ref[...], wo_ref[...], NT) * (1.0 - bent * bent)).astype(bf16)
        bent = jnp.tanh(ct_ref[...] * inv)
        grad = dot(do_ref[:, mine], wy_ref[...], NT) + dot(do_ref[:, other], wc_ref[...], NT)
        dct_ref[...] = (grad * (1.0 - bent * bent)).astype(bf16)


def ff_bwd(
    spot, hold, layer, limits, de, df, hat1, rate1, vec, gain, slope, w_up, w_down, w_out,
    wo_oth, ctx_own, ctx_oth,
):
    seq, half = ctx_own.shape
    width, hidden = w_up.shape[1:]
    chunk = FF_CHUNK
    steps = hidden // chunk
    span = steps // 2

    def place(t, s):
        return jnp.where(t < span, s[CORE] * span + t, (1 - s[CORE]) * span + t - span)

    full = whole(seq, width)
    part = whole(seq, width // 2)
    outs = [
        (whole(seq, hidden // 2), shape((seq, hidden // 2), bf16)),
        (part, shape((seq, width // 2), bf16)),
        (part, shape((seq, width // 2), bf16)),
        (full, shape((seq, width), f32)),
        (whole(seq, half), shape((seq, half), bf16)),
        (whole(seq, half), shape((seq, half), bf16)),
        (whole(8, width), shape((8, width), f32)),
        (pl.BlockSpec((1, chunk), lambda t, s: (0, place(t, s))), shape((1, hidden), f32)),
    ]
    return launch(
        functools.partial(ff_bwd_kernel, layer), "ff_bwd", spot, hold,
        [(limits, smem())]
        + [
            (de, full),
            (df, full),
            (hat1, full),
            (rate1, whole(seq, 128)),
            (vec, at_layer(layer, *vec.shape[1:])),
            (gain, at_layer(layer, *gain.shape[1:])),
            (slope, pl.BlockSpec((seq, chunk), lambda t, s: (0, place(t, s)))),
            (w_up, pl.BlockSpec((None, width, chunk), lambda t, s: (layer, 0, place(t, s)))),
            (w_down, pl.BlockSpec((None, chunk, width), lambda t, s: (layer, place(t, s), 0))),
            (w_out, at_layer(layer, half, width)),
            (wo_oth[0], whole(half, width // 2)),
            (wo_oth[1], whole(half, width // 2)),
            (ctx_own, whole(seq, half)),
            (ctx_oth, whole(seq, half)),
        ],
        outs,
        scratch=[
            pltpu.VMEM((seq, width), bf16),
            pltpu.VMEM((seq, width), f32),
            pltpu.VMEM((seq, chunk), bf16),
        ],
        grid=(steps,),
        us=20.0
    )


def attn_bwd_half(q_ref, k_ref, v_ref, c_ref, lse_ref, dc_ref, seg_q, seg_k):
    query, key, value, grad = q_ref[...], k_ref[...], v_ref[...], dc_ref[...]
    key_ext = jnp.concatenate([key, seg_k], axis=1)
    key_t = key.astype(f32).T.astype(bf16)
    product_t = (grad.astype(f32) * c_ref[...]).T
    d_key = d_value = None
    d_query_t = []
    for head in range(2):
        scaled = query * head_mask(head, HEAD**-0.5)
        scores = dot(key_ext, jnp.concatenate([scaled, seg_q], axis=1), NT)
        probs = jnp.exp(scores - lse_ref[0, head : head + 1, :])
        grad_head = grad * head_mask(head, 1.0)
        d_probs = dot(value, grad_head, NT)
        delta = jnp.sum(product_t[head * HEAD : (head + 1) * HEAD], axis=0, keepdims=True)
        d_scores = (probs * (d_probs - delta)).astype(bf16)
        term_v = dot(probs.astype(bf16), grad_head)
        term_k = dot(d_scores, scaled)
        d_value = term_v if d_value is None else d_value + term_v
        d_key = term_k if d_key is None else d_key + term_k
        d_query_t.append(dot(key_t[head * HEAD : (head + 1) * HEAD], d_scores))
    d_query = jnp.concatenate(d_query_t, axis=0).T * HEAD**-0.5
    return d_query.astype(bf16), d_key.astype(bf16), d_value.astype(bf16)


def attn_bwd_kernel(
    layer, spot_ref, lim_ref, xt_ref, xb_ref, dy_ref, sq_ref, sk_ref,
    qo_ref, ko_ref, vo_ref, co_ref, lo_ref, dco_ref,
    qt_ref, kt_ref, vt_ref, ct_ref, lt_ref, dct_ref, wo_ref, wy_ref, wc_ref, *rest
):
    if layer:
        hat_ref, rate_ref, gain_ref, *rest = rest
    dqo_ref, dko_ref, dvo_ref, dqt_ref, dkt_ref, dvt_ref, bo_ref, bt_ref, *rest = rest
    acc_ref = rest[-1]
    step = pl.program_id(0)
    half_seq, width = xt_ref.shape
    share = width // 2
    rows = 64
    own = attn_bwd_half(qo_ref, ko_ref, vo_ref, co_ref, lo_ref, dco_ref, sq_ref[...], sk_ref[...])
    oth = attn_bwd_half(qt_ref, kt_ref, vt_ref, ct_ref, lt_ref, dct_ref, sq_ref[...], sk_ref[...])
    dqo_ref[...], dko_ref[...], dvo_ref[...] = own
    dqt_ref[...], dkt_ref[...], dvt_ref[...] = oth
    for out_ref, grads in ((bo_ref, own), (bt_ref, oth)):
        out_ref[0:1, :] = jnp.sum(grads[0].astype(f32), axis=0, keepdims=True)
        out_ref[1:2, :] = jnp.sum(grads[2].astype(f32), axis=0, keepdims=True)
        out_ref[2:8, :] = jnp.zeros((6, PAIR), f32)
    joined = [jnp.concatenate([own[k], oth[k]], axis=1) for k in range(3)]
    for piece, w_ref in enumerate((wy_ref, wc_ref)):
        which = jnp.where(spot_ref[CORE] == 0, piece, 1 - piece)
        at = pl.ds(pl.multiple_of(which * share, 128), share)
        total = None
        for k in range(3):
            term = dot(joined[k], jnp.concatenate([wo_ref[k, at, :], w_ref[k]], axis=1), NT)
            total = term if total is None else total + term

        @pl.when(step == 0)
        def _():
            acc_ref[:, at] = total

        @pl.when(step > 0)
        def _():
            acc_ref[:, at] += total

    @pl.when(step == pl.num_programs(0) - 1)
    def _():
        inv = 1.0 / lim_ref[layer, 0]
        sums = norm_sums(width)
        for part, x_ref in enumerate((xt_ref, xb_ref)):

            def body(i, carry, part=part, x_ref=x_ref):
                here = pl.ds(pl.multiple_of(i * rows, rows), rows)
                at = pl.ds(part * half_seq + pl.multiple_of(i * rows, rows), rows)
                bent = jnp.tanh(x_ref[here, :].astype(f32) * inv)
                grad = dy_ref[at, :] + acc_ref[at, :] * (1.0 - bent * bent)
                if layer:
                    return leave_norm(
                        grad, hat_ref[at, :], rate_ref[at, 0:1], gain_ref, at, rest[0], rest[1],
                        carry,
                    )
                rest[part][here, :] = grad.astype(rest[part].dtype)
                return carry

            sums = lax.fori_loop(0, half_seq // rows, body, sums)
        if layer:
            store_sums(sums, rest[2])


def attn_bwd(spot, hold, layer, limits, x, dy, seg_q, seg_k, own, oth, w_qkv, wq_oth, below=()):
    seq, width = dy.shape
    cols = own[0].shape[1]
    steps = cols // PAIR
    block = pl.BlockSpec((seq, PAIR), lambda t, s: (0, t))
    half_specs = [
        block,
        block,
        block,
        block,
        pl.BlockSpec((1, 8, seq), lambda t, s: (t, 0, 0)),
        block,
    ]
    return launch(
        functools.partial(attn_bwd_kernel, layer), "attn_bwd", spot, hold,
        [(limits, smem())]
        + halves(x, seq // 2, width)
        + [(dy, whole(seq, width)), (seg_q, whole(seq, PAIR)), (seg_k, whole(seq, PAIR))]
        + list(zip(own, half_specs))
        + list(zip(oth, half_specs))
        + list(zip((w_qkv,), weight_specs(layer, (w_qkv,))))
        + list(zip(wq_oth, weight_specs(layer, wq_oth)))
        + (
            [
                (below[0], whole(seq, width)),
                (below[1], whole(seq, 128)),
                (below[2], at_layer(layer - 1, *below[2].shape[1:])),
            ]
            if layer
            else []
        ),
        [(block, shape((seq, cols), bf16))] * 6
        + [(pl.BlockSpec((8, PAIR), lambda t, s: (0, t)), shape((8, cols), f32))] * 2
        + (
            norm_outs(seq, width)
            if layer
            else [
                (whole(seq // 2, width), shape((seq // 2, width), f32)),
                (whole(seq // 2, width), shape((seq // 2, width), bf16)),
            ]
        ),
        scratch=[pltpu.VMEM((seq, width), f32)],
        grid=(steps,),
        us=18.5
    )


FF_ORDERS = (
    (AXIS_X, SIDE, AXIS_Z0, AXIS_Z1),
    (SIDE, AXIS_Z0, AXIS_X, AXIS_Z1),
    (AXIS_Z0, AXIS_X, SIDE, AXIS_Z1),
)
FF_ROWS = (144, 128, 112)
ATT_ORDERS = (
    (AXIS_X, SIDE, AXIS_Z0, AXIS_Z1),
    (SIDE, AXIS_X, AXIS_Z0, AXIS_Z1),
)
ATT_ROWS = (96, 96)
PIECE = 48


def block_of(spot_ref, order, rel):
    bit = {axis: (rel >> (3 - k)) & 1 for k, axis in enumerate(order)}
    chip = 0
    for axis in (AXIS_Z1, AXIS_Z0, AXIS_X):
        own = spot_ref[axis]
        chip = chip * 2 + (1 - own if bit[axis] else own)
    return bit[SIDE], chip


def w_ff_kernel(
    spot_ref, um_ref, uo_ref, zm_ref, so_ref, gm_ref, go_ref, fm_ref, fo_ref, down_ref, *rest
):
    outs, ut_ref, half_ref, all_ref = rest[:-3], rest[-3], rest[-2], rest[-1]
    step = pl.program_id(0)
    sides, chips, tall, lanes = all_ref.shape
    seq, width = um_ref.shape
    thin = width // chips

    @pl.when(step == 0)
    def _():
        ut_ref[:, :seq] = um_ref[...].T
        ut_ref[:, seq:] = uo_ref[...].T
        mine = pl.ds(pl.multiple_of(spot_ref[CORE] * lanes, 128), lanes)
        half_ref[0] = fm_ref[:, mine]
        half_ref[1] = fo_ref[:, mine]

    theirs = (dot(fo_ref[...], down_ref[...], NT) * so_ref[...].astype(f32)).astype(bf16)
    grad_up = dot(ut_ref[:, :seq], zm_ref[...]) + dot(ut_ref[:, seq:], theirs)
    grad_up = grad_up.astype(bf16)
    for chip in range(chips):
        at = pl.ds(pl.multiple_of((step % 2) * thin, 16), thin)
        all_ref[step // 2, chip, at, :] = grad_up[chip * thin : (chip + 1) * thin]
    base = 2 * thin
    deep = tall - base
    per = gm_ref.shape[1] // (2 * deep)
    for part in range(per):
        cols = slice(part * 2 * deep, (part + 1) * 2 * deep)
        grad_down = dot(gm_ref[:, cols], half_ref[0], TN) + dot(go_ref[:, cols], half_ref[1], TN)
        grad_down = grad_down.astype(bf16)
        for side in range(2):
            all_ref[side, step * per + part, base:, :] = grad_down[side * deep : (side + 1) * deep]

    @pl.when(step == pl.num_programs(0) - 1)
    def _():
        start = 0
        for part, (order, count) in enumerate(zip(FF_ORDERS, FF_ROWS)):
            for rel in range(16):
                side, chip = block_of(spot_ref, order, rel)
                side = 1 - spot_ref[SIDE] if side else spot_ref[SIDE]
                value = all_ref[side, chip, start : start + count, :]
                if rel < 8:
                    outs[2 * part][rel] = value
                else:
                    outs[2 * part + 1][(rel - 8) * count : (rel - 7) * count, :] = value
            start += count


def w_ff(
    spot, hold, layer, cu_mine, cu_core, dz_mine, slope_core, g_mine, g_core, df_mine, df_core,
    w_down
):
    seq, width = df_mine.shape
    lanes, hidden = width // 2, g_mine.shape[1]
    steps = dz_mine.shape[1] // lanes
    tall = hidden // 8
    g_block = pl.BlockSpec((seq, hidden // steps), lambda t, s: (0, t))
    u_block = pl.BlockSpec((seq, width), lambda *_: (0, 1))
    outs = []
    for rows in FF_ROWS:
        outs.append((whole(8, rows, lanes), shape((8, rows, lanes), bf16)))
        outs.append((whole(8 * rows, lanes), shape((8 * rows, lanes), bf16)))
    return launch(
        w_ff_kernel, "w_ff", spot, hold,
        [
            (cu_mine, u_block),
            (cu_core, u_block),
            (dz_mine, pl.BlockSpec((seq, lanes), lambda t, s: (0, t))),
            (slope_core, pl.BlockSpec((seq, lanes), lambda t, s: (0, s[CORE] * steps + t))),
            (g_mine, g_block),
            (g_core, g_block),
            (df_mine, whole(seq, width)),
            (df_core, whole(seq, width)),
            (
                w_down,
                pl.BlockSpec(
                    (None, lanes, width), lambda t, s: (layer, s[CORE] * steps + t, 0)
                ),
            ),
        ],
        outs,
        scratch=[
            pltpu.VMEM((width, 2 * seq), bf16),
            pltpu.VMEM((2, seq, lanes), bf16),
            pltpu.VMEM((2, 8, tall, lanes), bf16),
        ],
        grid=(steps,),
        us=13.5,
    )


def w_att_kernel(
    spot_ref, a_ref, dqo_ref, dko_ref, dvo_ref, dqt_ref, dkt_ref, dvt_ref,
    cm_ref, cc_ref, dom_ref, doc_ref, keep_ref, out_ref, *rest
):
    send_refs, at_ref, spare_ref = rest[:-2], rest[-2], rest[-1]
    width = a_ref.shape[1]
    _, chips, tall, cols = keep_ref.shape
    core = spot_ref[CORE]
    piece = PIECE
    per = tall // piece
    at_ref[...] = a_ref[...].T
    sides = ((dqo_ref, dko_ref, dvo_ref), (dqt_ref, dkt_ref, dvt_ref))
    for side, grads in enumerate(sides):
        for which in range(3):
            result = dot(at_ref[...], grads[which][...]).astype(bf16)
            for j in range(width // piece):
                index = which * (width // piece) + j
                block, sub = index // per, index % per
                spare_ref[block % 2, block // 2, sub * piece : (sub + 1) * piece, :] = result[
                    j * piece : (j + 1) * piece
                ]
        keep_ref[side] = spare_ref[core]
        for k, send_ref in enumerate(send_refs):
            send_ref[side] = spare_ref[1 - core, :, k * piece : (k + 1) * piece, :]
    half = width // 2
    heads = half // HEAD
    for side in range(2):
        at = slice(side * half, (side + 1) * half)
        result = dot(cm_ref[:, at], dom_ref[...], TN) + dot(cc_ref[:, at], doc_ref[...], TN)
        for chip in range(chips):
            for pair in range(heads // 2):
                first = (2 * pair) * HEAD + 8 * chip
                second = first + HEAD
                out_ref[side, chip, pair * 16 : (pair + 1) * 16, :] = jnp.concatenate(
                    [result[first : first + 8], result[second : second + 8]], axis=0
                ).astype(bf16)


def w_att(spot, hold, act, d_own, d_oth, cu_mine, cu_core, do_mine, do_core):
    seq, width = act.shape
    cols = width // 2
    chips = 8
    tall = 3 * width // (2 * chips)
    outs = [
        shape((2, chips, tall, cols), bf16),
        shape((2, chips, cols // chips, cols), bf16),
        *[shape((2, chips, PIECE, cols), bf16)] * (tall // PIECE),
    ]
    cq_block = pl.BlockSpec((seq, width), lambda *_: (0, 0))
    return launch(
        w_att_kernel, "w_att", spot, hold,
        [(array, whole(*array.shape)) for array in (act, *d_own, *d_oth)]
        + [
            (cu_mine, cq_block),
            (cu_core, cq_block),
            (do_mine, whole(seq, cols)),
            (do_core, whole(seq, cols)),
        ],
        [(whole(*out.shape), out) for out in outs],
        scratch=[pltpu.VMEM((width, seq), bf16), pltpu.VMEM((2, chips, tall, cols), bf16)],
        us=8.0,
    )


class Part:
    def __init__(self, kind, order, kept):
        self.kind, self.order, self.kept = kind, order, kept
        self.stage = 0
        self.array = self.start = None
        self.final = None

    def arrives(self, array, start):
        self.array, self.start = array, start


def pack_small(spot_ref, small_refs, out_ref):
    for layer in range(len(small_refs) // 5):
        bo_ref, bt_ref, vec_ref, sums_ref, up_ref = small_refs[5 * layer : 5 * layer + 5]
        half = bo_ref.shape[1]
        width = 2 * half
        side = spot_ref[SIDE]
        mine = pl.ds(pl.multiple_of(side * half, 128), half)
        other = pl.ds(pl.multiple_of((1 - side) * half, 128), half)
        out_ref[layer, 0:2, mine] = bo_ref[0:2, :]
        out_ref[layer, 0:2, other] = bt_ref[0:2, :]
        out_ref[layer, 2:8, :] = vec_ref[0:6, :] + sums_ref[0:6, :]
        for k in range(up_ref.shape[1] // width):
            out_ref[layer, 8 + k : 9 + k, :] = up_ref[:, k * width : (k + 1) * width]


def exchange(spot, over_axis, parts, att=None, smalls=(), pair=None, carry=None):
    ins, outs, steps = [], [], []

    def take(array):
        for k, (known, _) in enumerate(ins):
            if known is array:
                return k
        ins.append((array, whole(*array.shape)))
        return len(ins) - 1

    def give(dims, dtype=bf16):
        outs.append((whole(*dims), shape(dims, dtype)))
        return len(outs) - 1

    lanes = (parts[0].kept if parts else att[0]).shape[-1]
    sends = {}

    def room(axis, rows):
        start = sends.get(axis, 0)
        sends[axis] = start + rows
        return start

    new_parts, places = [], []
    parts = sorted(parts, key=lambda part: (part.kind != "ff", part.kept.shape[0]))
    for part in parts:
        blocks, rows, _ = part.kept.shape
        source = take(part.kept), take(part.array), part.start
        if blocks > 1:
            axis = part.order[part.stage + 1]
            start = room(axis, blocks // 2 * rows)
            steps.append(("halve", source, give((blocks // 2, rows, lanes)), axis, start))
        elif part.kind == "ff":
            axis = SIDE
            start = room(axis, rows)
            steps.append(("end", source, give((rows, lanes), f32), axis, start))
        else:
            axis = None
            start = 0
            steps.append(("end", source, give((rows, lanes), f32), None, 0))
        places.append((part, axis, start))
    if att is not None:
        source = [take(array) for array in att]
        begin = 0
        for order, rows in zip(ATT_ORDERS, ATT_ROWS):
            start = room(order[0], 8 * rows)
            kept = give((8, rows, lanes))
            steps.append(("enter", source, kept, order[0], start, order, begin, rows))
            places.append((Part("att", order, None), order[0], start))
            begin += rows
    small_out = None
    if smalls:
        source = [take(array) for small in smalls for array in small]
        width = smalls[0][2].shape[1]
        small_out = give((len(smalls), 8 + smalls[0][4].shape[1] // width, width), f32)
        steps.append(("pack", source, small_out))
    if pair is not None:
        small_out = give(pair[0].shape, f32)
        steps.append(("sum", [take(array) for array in pair], small_out))
    if carry is not None:
        small_out = give(carry.shape, carry.dtype)
        steps.append(("copy", [take(carry)], small_out))
    send_at = {axis: give((rows, lanes)) for axis, rows in sends.items()}

    def body(spot_ref, *refs):
        in_refs, out_refs = refs[: len(ins)], refs[len(ins) :]
        for what, source, out, *more in steps:
            out_ref = out_refs[out]
            if what == "halve":
                axis, start = more
                kept, got = in_refs[source[0]], in_refs[source[1]]
                base = source[2]
                half, rows, _ = out_ref.shape
                send = out_refs[send_at[axis]]
                for j in range(half):
                    at = base + j * rows
                    out_ref[j] = kept[j] + got[at : at + rows, :]
                    at += half * rows
                    send[start + j * rows : start + (j + 1) * rows, :] = (
                        kept[half + j] + got[at : at + rows, :]
                    )
            elif what == "end":
                axis, start = more
                kept, got = in_refs[source[0]], in_refs[source[1]]
                base = source[2]
                rows = out_ref.shape[0]
                total = kept[0].astype(f32) + got[base : base + rows, :].astype(f32)
                out_ref[...] = total
                if axis is not None:
                    out_refs[send_at[axis]][start : start + rows, :] = total.astype(bf16)
            elif what == "enter":
                axis, start, order, begin, rows = more
                keep, outer, *got = (in_refs[k] for k in source)
                send = out_refs[send_at[axis]]
                for rel in range(16):
                    side, chip = block_of(spot_ref, order, rel)
                    for k in range(begin // PIECE, (begin + rows) // PIECE):
                        if k < len(got):
                            at = slice(k * PIECE, (k + 1) * PIECE)
                            value = keep[side, chip, at, :] + got[k][side, chip]
                        else:
                            value = outer[side, chip]
                        done = k * PIECE - begin
                        if rel < 8:
                            out_ref[rel, done : done + PIECE, :] = value
                        else:
                            at = start + (rel - 8) * rows + done
                            send[at : at + PIECE, :] = value
            elif what == "copy":
                out_ref[...] = in_refs[source[0]][...]
            elif what == "pack":
                pack_small(spot_ref, [in_refs[k] for k in source], out_ref)
            else:
                out_ref[...] = in_refs[source[0]][...] + in_refs[source[1]][...]

    results = launch(body, "exchange", spot, (), ins, outs, us=5.0)
    arrived = {axis: over_axis(results[k], axis) for axis, k in send_at.items()}
    kept_at = [step[2] for step in steps]
    for (part, axis, start), what, out in zip(places, [step[0] for step in steps], kept_at):
        if what == "end":
            part.final = results[out]
        else:
            part.kept = results[out]
        if what != "enter":
            part.stage += 1
        if axis is not None:
            part.arrives(arrived[axis], start)
        new_parts.append(part)
    return new_parts, (None if small_out is None else results[small_out])


def finish_kernel(spot_ref, a_ref, b_ref, c_ref, got_ref, keep_ref, send_ref, both_ref):
    core, side = spot_ref[CORE], spot_ref[SIDE]
    start = 0
    for ref in (a_ref, b_ref, c_ref):
        both_ref[side, start : start + ref.shape[0], :] = ref[...]
        start += ref.shape[0]
    both_ref[1 - side] = got_ref[...].astype(f32)
    half = both_ref.shape[1] // 2
    quarter = half // 4
    for out_ref, which in ((keep_ref, core), (send_ref, 1 - core)):
        for k in range(4):
            at = pl.ds(pl.multiple_of((k % 2) * 2 * quarter + which * quarter, 16), quarter)
            out_ref[k * quarter : (k + 1) * quarter, :] = both_ref[k // 2, at, :].astype(
                out_ref.dtype
            )
        out_ref[half:, :] = both_ref[which, half:, :].astype(out_ref.dtype)


def finish_ff(spot, parts):
    rows = sum(FF_ROWS)
    lanes = parts[0].final.shape[1]
    start = parts[0].start
    got = parts[0].array
    assert start % rows == 0
    return launch(
        finish_kernel, "finish_ff", spot, (),
        [(part.final, whole(*part.final.shape)) for part in parts]
        + [(got, pl.BlockSpec((rows, lanes), lambda *_: (start // rows, 0)))],
        [(whole(rows, lanes), shape((rows, lanes), f32)), (whole(rows, lanes), shape((rows, lanes), bf16))],
        scratch=[pltpu.VMEM((2, rows, lanes), f32)],
        us=3.0,
    )


def local(
    hidden_in, cotangent, segment_ids, clip_ranges, w_qkv, bias_qv, w_out, vector_bias, ln_gain,
    w_up, bias_up, w_down,
):
    layers = w_qkv.shape[0]
    row_count, half_seq, width = hidden_in.shape
    seq = segment_ids.shape[1]
    cols = w_qkv.shape[3]
    heads = cols // HEAD
    hidden = w_up.shape[2]
    dp_count = lax.axis_size("dp")
    assert lax.axis_size("mp") == 2 and row_count == 2 and seq == 2 * half_seq
    bits = dp_count.bit_length() - 1
    assert dp_count == 1 << bits and bits >= 1
    chips = dp_count // 2
    side = lax.axis_index("mp")
    place = lax.axis_index("dp")
    core = place % 2
    spot = Spot(
        jnp.stack(
            [core, side, (place >> 1) & 1, (place >> 2) & 1, (place >> 3) & 1]
        ).astype(jnp.int32)
    )

    def over_mp(value):
        return lax.ppermute(value, "mp", [(0, 1), (1, 0)])

    def over_bit(value, bit):
        return lax.ppermute(value, "dp", [(i, i ^ (1 << bit)) for i in range(dp_count)])

    def over_core(value):
        return over_bit(value, 0)

    def over_axis(value, axis):
        return over_mp(value) if axis == SIDE else over_bit(value, axis - AXIS_X + 1)

    def pick(value, index, axis):
        return lax.dynamic_index_in_dim(value, index, axis, keepdims=False)

    def ordered(index, mine, theirs, axis):
        first = jnp.where(index == 0, mine, theirs)
        second = jnp.where(index == 0, theirs, mine)
        return jnp.concatenate([first, second], axis=axis)

    x = (hidden_in, over_mp(pick(hidden_in, 1 - side, 0)))
    bias_oth = over_mp(bias_qv)
    limits = clip_ranges.astype(f32)
    seg_row = pick(segment_ids, side, 0).reshape(2, half_seq)
    seg_row = jnp.concatenate([pick(seg_row, side, 0), pick(seg_row, 1 - side, 0)])
    same = seg_row[:, None] == jnp.arange(PAIR, dtype=seg_row.dtype)[None, :]
    seg_q = jnp.where(same, BIG, 0.0).astype(bf16)
    seg_k = jnp.where(same, 0.0, 1.0).astype(bf16)

    arrived = [over_mp(piece) for piece in pick_weights(spot, (), 0, w_qkv, w_out)]
    act = enter(spot, limits, hidden_in, x[1])
    fetched, stored = [], []
    shared = ()
    for layer in range(layers):
        last = layer == layers - 1
        relays = []
        if layer:
            relays = relay_piece(arrived[0]) + relay_piece(arrived[1])
        if last:
            relays = relays + relay_row(cotangent)
        outs = attn_fwd(spot, (), layer, act, (w_qkv,), bias_qv, seg_q, seg_k, relays)
        own, copies = outs[:5], outs[5:]
        if last:
            cot = (cotangent, over_mp(copies[-1]))
        copy = copies[0] if layer else relay(spot, arrived[0])
        wq_oth = (arrived[0], over_core(copy))
        relays = [] if layer else relay_piece(arrived[1])
        if not last:
            relays = relays + relay_weights(layer + 1, w_qkv, w_out)
        outs = attn_fwd(spot, (), layer, act, wq_oth, bias_oth, seg_q, seg_k, relays)
        oth = outs[:5]
        wo_oth = (arrived[1], over_core(copies[1] if layer else outs[5]))
        fetched.append((wq_oth, wo_oth))
        if not last:
            arrived = [over_mp(piece) for piece in outs[-2:]]
        outs = ff_fwd(
            spot, shared, layer, last, limits, x, own[3], oth[3], w_out, wo_oth, vector_bias, ln_gain,
            w_up, bias_up, w_down, cot if last else None,
        )
        cu, hat1, rate1, g, slope = outs[:5]
        shared = over_core(cu), over_core(g), over_core(slope)
        norm = None
        if last:
            hidden_mine, hidden_send, *descent = outs[5:]
        else:
            norm = outs[5:7]
        stored.append((x, act, own, oth, cu, hat1, rate1, g, slope, norm, shared))
        if not last:
            x, act = (outs[7],), outs[8]
    hidden_recv = over_mp(hidden_send)

    fast = chips == 8 and width == 768 and hidden == 3072 and cols == 384

    smalls, groups = [], {}
    flying = []
    small = None
    df_core = over_core(descent[1])
    for layer in reversed(range(layers)):
        x, act, own, oth, cu, hat1, rate1, g, slope, norm, shared = stored[layer]
        wq_oth, wo_oth = fetched[layer]
        de, df, sums = descent
        dz_keep, do_keep, do_send, dy, dc_own, dc_oth, vec, d_bup = ff_bwd(
            spot, (), layer, limits, de, df, hat1, rate1, vector_bias, ln_gain, slope, w_up,
            w_down, w_out, wo_oth, own[3], oth[3],
        )
        if fast:
            do_core = over_core(do_send)
            if flying:
                flying, _ = exchange(spot, over_axis, flying, entering)
                groups["att", layer + 1] = flying[-len(ATT_ROWS) :]
            else:
                hidden_out = place_rows(spot, (), hidden_mine, hidden_recv, bf16)
            outs = w_ff(
                spot, (), layer, cu, shared[0], dz_keep, shared[2], g, shared[1], df, df_core,
                w_down,
            )
            parts_ff = []
            for k, order in enumerate(FF_ORDERS):
                parts_ff.append(Part("ff", order, outs[2 * k]))
                parts_ff[k].arrives(over_axis(outs[2 * k + 1], order[0]), 0)
            groups["ff", layer] = parts_ff
            ending = [part for part in flying if part.stage == 2]
            if ending:
                exchange(spot, over_axis, ending)
            flying = flying + parts_ff
        below = (*stored[layer - 1][9], ln_gain) if layer else ()
        outs = attn_bwd(
            spot, (), layer, limits, x, dy, seg_q, seg_k, (*own, dc_own), (*oth, dc_oth), w_qkv,
            wq_oth, below,
        )
        d_own, d_oth = outs[:3], outs[3:6]
        smalls.insert(0, (outs[6], outs[7], vec, sums, d_bup))
        descent = outs[8:]
        if fast:
            keep, out, *send = w_att(
                spot, (), act, d_own, d_oth, cu, shared[0], do_keep, do_core
            )
            entering = keep, out, *(over_core(piece) for piece in send)
            if layer:
                flying, df = exchange(spot, over_axis, flying, carry=descent[1])
                df_core = over_core(df)
            else:
                flying, small = exchange(spot, over_axis, flying, entering, smalls)
                groups["att", 0] = flying[-len(ATT_ROWS) :]
        else:
            dz = (dot(df, w_down[layer], NT) * slope.astype(f32)).astype(bf16)
            do = ordered(core, do_keep, do_send, 1)
            total = []
            for lhs, rhs in ((cu[:, width:], dz), (g, df)):
                grad = dot(lhs, rhs, TN).reshape(-1)
                grad = grad + over_mp(grad)
                total.append(lax.psum_scatter(grad, "dp", scatter_dimension=0, tiled=True))
            groups["ff", layer] = total
            sides = []
            for grads, part in ((d_own, cu[:, :cols]), (d_oth, cu[:, cols:width])):
                qkv = jnp.stack([dot(act, grad, TN) for grad in grads])
                qkv = qkv.reshape(3, width, heads, HEAD).transpose(2, 0, 1, 3)
                sides.append((qkv.reshape(heads, -1), dot(part, do, TN).reshape(heads, -1)))
            total = []
            for k in range(2):
                grad = sides[0][k] + over_mp(sides[1][k])
                total.append(lax.psum_scatter(grad, "dp", scatter_dimension=1, tiled=True))
            groups["att", layer] = total

    row_mine, row_send = descent
    if fast:
        axes = [AXIS_X, SIDE, AXIS_Z0, AXIS_Z1]
        pair = None
        while True:
            flying = [part for part in flying if part.final is None]
            if not flying:
                break
            flying, summed = exchange(spot, over_axis, flying, pair=pair)
            small = small if summed is None else summed
            pair = (small, over_axis(small, axes.pop(0))) if axes else None
        while pair:
            small = pair[0] + pair[1]
            pair = (small, over_axis(small, axes.pop(0))) if axes else None
        grad_input = place_rows(spot, (), row_mine, over_mp(row_send), f32)
        small = small + over_core(small)
        ups, downs, qkvs, outs = [], [], [], []
        for layer in range(layers):
            keep, send = finish_ff(spot, groups["ff", layer])
            both = ordered(core, keep[None], over_core(send).astype(f32)[None], 0)
            up = both[:, : width // 4].reshape(2, 4, -1, cols)
            ups.append(up.transpose(2, 0, 1, 3).reshape(-1))
            downs.append(both[:, width // 4 :].transpose(1, 0, 2).reshape(-1))
            rows = jnp.concatenate([part.final for part in groups["att", layer]], axis=0)
            share = 3 * width // dp_count
            qkv = rows[:share].reshape(share, heads, HEAD)
            qkvs.append(qkv.transpose(1, 0, 2).reshape(heads, -1))
            outs.append(rows[share:].reshape(heads, 2, 4, cols))
        outs = jnp.stack(outs)
        keep, sent = pick(outs, core, 2), pick(outs, 1 - core, 2).astype(bf16)
        outs = ordered(core, keep[:, :, :, None], over_core(sent).astype(f32)[:, :, :, None], 3)
        grads = (
            jnp.stack(qkvs), outs.reshape(layers, heads, -1), jnp.stack(ups), jnp.stack(downs)
        )
    else:
        hidden_out = place_rows(spot, (), hidden_mine, hidden_recv, bf16)
        grad_input = place_rows(spot, (), row_mine, over_mp(row_send), f32)
        small = jnp.stack(
            [
                jnp.concatenate(
                    [ordered(side, bo[:2], bt[:2], 1), (vec + sums)[:6], up.reshape(-1, width)],
                    axis=0,
                )
                for bo, bt, vec, sums, up in smalls
            ]
        )
        small = lax.psum(small, ("dp", "mp"))
        grads = [
            jnp.stack([groups[kind, layer][k] for layer in range(layers)])
            for kind, k in (("att", 0), ("att", 1), ("ff", 0), ("ff", 1))
        ]
    grad_bias_qv = lax.dynamic_slice_in_dim(small[:, :2], side * cols, cols, 2)
    return (
        hidden_out,
        grad_input,
        grads[0],
        grad_bias_qv,
        grads[1],
        small[:, 2:6],
        small[:, 6:8],
        grads[2],
        small[:, 8:].reshape(layers, hidden),
        grads[3],
    )


def solution(mesh):
    return jax.shard_map(
        local,
        mesh=mesh,
        in_specs=(
            P("dp", "mp", None),
            P("dp", "mp", None),
            P("dp", None),
            P(),
            P(None, None, None, "mp"),
            P(None, None, "mp"),
            P(None, "mp", None),
            P(),
            P(),
            P(),
            P(),
            P(),
        ),
        out_specs=(
            P("dp", "mp", None),
            P("dp", "mp", None),
            P(None, "mp", "dp"),
            P(None, None, "mp"),
            P(None, "mp", "dp"),
            P(),
            P(),
            P(None, "dp"),
            P(),
            P(None, "dp"),
        ),
        check_vma=False,
    )
```

```python
import functools

import jax
import jax.numpy as jnp
from jax import lax
from jax.experimental import pallas as pl
from jax.experimental.pallas import tpu as pltpu
from jax.sharding import PartitionSpec as P

HEAD = 64
PAIR = 2 * HEAD
EPS = 1e-06
BIG = -1e30
INV_SQRT2 = 0.7071067811865476
INV_SQRT2PI = 0.3989422804014327

f32 = jnp.float32
bf16 = jnp.bfloat16
MIB = 1024 * 1024
FF_CHUNK = 768
FF_SUB = 256

NT = (((1,), (1,)), ((), ()))
TN = (((0,), (0,)), ((), ()))


def dot(lhs, rhs, dims=(((1,), (0,)), ((), ()))):
    return lax.dot_general(lhs, rhs, dims, preferred_element_type=f32)


def whole(*dims):
    return pl.BlockSpec(dims, lambda *_: (0,) * len(dims))


def at_layer(layer, *dims):
    return pl.BlockSpec((None, *dims), lambda *_: (layer,) + (0,) * len(dims))


def smem():
    return pl.BlockSpec(memory_space=pltpu.SMEM)


class Spot:
    def __init__(self, array):
        self.array = array
        self.latest = ()
        self.grant = 63.5


def launch(body, name, spot, hold, ins, outs, scratch=(), grid=(1,), us=3.0):
    count = len(ins)
    known = [array for array, _ in ins]
    hold = [array for array in (*hold, *spot.latest) if not any(array is k for k in known)]

    def kernel(spot_ref, *refs):
        body(spot_ref, *refs[:count], *refs[count + len(hold) :])

    in_specs = [spec for _, spec in ins] + [pl.BlockSpec(memory_space=pl.ANY)] * len(hold)
    results = pl.pallas_call(
        kernel,
        grid_spec=pltpu.PrefetchScalarGridSpec(
            num_scalar_prefetch=1,
            grid=grid,
            in_specs=in_specs,
            out_specs=[spec for spec, _ in outs],
            scratch_shapes=list(scratch),
        ),
        out_shape=[out for _, out in outs],
        compiler_params=pltpu.CompilerParams(vmem_limit_bytes=int(spot.grant * MIB)),
        cost_estimate=pl.CostEstimate(
            flops=int(us * 1e9), bytes_accessed=int(us * 1e6), transcendentals=0
        ),
        name=name,
    )(spot.array, *known, *hold)
    spot.latest = (results[0],)
    return results


def shape(dims, dtype):
    return jax.ShapeDtypeStruct(dims, dtype)


def head_mask(head, value):
    lane = lax.broadcasted_iota(jnp.int32, (1, PAIR), 1)
    return jnp.where((lane // HEAD) == head, value, 0.0).astype(bf16)


CORE, SIDE, AXIS_X, AXIS_Z0, AXIS_Z1 = range(5)


def enter_kernel(layer_limit, spot_ref, lim_ref, mine_ref, recv_ref, act_ref):
    limit = lim_ref[0, 0]
    inv = 1.0 / limit
    half = mine_ref.shape[0]
    act_ref[:half, :] = (limit * jnp.tanh(mine_ref[...].astype(f32) * inv)).astype(bf16)
    act_ref[half:, :] = (limit * jnp.tanh(recv_ref[...].astype(f32) * inv)).astype(bf16)


def enter(spot, hold, limits, hidden_in, recv):
    half, width = recv.shape
    (act,) = launch(
        functools.partial(enter_kernel, 0), "enter", spot, hold,
        [(limits, smem()), (hidden_in, my_row(half, width)), (recv, whole(half, width))],
        [(whole(2 * half, width), shape((2 * half, width), bf16))],
        us=3.0,
    )
    return act


def my_row(half, width):
    return pl.BlockSpec((None, half, width), lambda t, s: (s[SIDE], 0, 0))


def place_kernel(spot_ref, mine_ref, recv_ref, out_ref):
    out_ref[spot_ref[SIDE]] = mine_ref[...].astype(out_ref.dtype)
    out_ref[1 - spot_ref[SIDE]] = recv_ref[...].astype(out_ref.dtype)


def place_rows(spot, hold, mine, recv, dtype):
    half, width = mine.shape
    (out,) = launch(
        place_kernel, "place_rows", spot, hold,
        [(mine, whole(half, width)), (recv, whole(half, width))],
        [(whole(2, half, width), shape((2, half, width), dtype))],
        us=2.5
    )
    return out


def copy_kernel(spot_ref, *refs):
    count = len(refs) // 2
    for source, target in zip(refs[:count], refs[count:]):
        target[...] = source[...]


def pack_kernel(spot_ref, w_ref, o_ref, out_ref):
    rows = w_ref.shape[1]
    out_ref[:, :rows, :] = w_ref[...]
    out_ref[0, rows:, :] = o_ref[...]


def pack_weights(layer, w_qkv, w_out):
    _, _, width, cols = w_qkv.shape
    rows, wide, deep = width // 2, w_out.shape[2] // 2, cols // 3
    ins = [
        (w_qkv, pl.BlockSpec((None, 1, rows, cols), lambda t, s: (layer, t, s[CORE], 0))),
        (w_out, pl.BlockSpec((None, deep, wide), lambda t, s: (layer, t, s[CORE]))),
    ]
    out = (
        pl.BlockSpec((1, rows + deep, cols), lambda t, s: (t, 0, 0)),
        shape((3, rows + deep, cols), bf16),
    )
    return ins, out


def pick_weights(spot, w_qkv):
    _, _, width, cols = w_qkv.shape
    rows = width // 2
    return launch(
        copy_kernel, "pick_weights", spot, (),
        [(w_qkv, pl.BlockSpec((None, 1, rows, cols), lambda t, s: (0, t, s[CORE], 0)))],
        [(pl.BlockSpec((1, rows, cols), lambda t, s: (t, 0, 0)), shape((3, rows, cols), bf16))],
        grid=(3,),
        us=3.0,
    )[0]


def relay(spot, array, w_out):
    _, cols, width = w_out.shape
    copies = relay_piece(array) + [
        (
            w_out,
            pl.BlockSpec((None, cols // 3, width), lambda t, s: (0, t, 0)),
            pl.BlockSpec((cols // 3, width), lambda t, s: (t, 0)),
            shape((cols, width), bf16),
        )
    ]
    return launch(
        copy_kernel, "relay", spot, (),
        [(a, source) for a, source, _, _ in copies],
        [(target, out) for _, _, target, out in copies],
        grid=(3,),
        us=2.5,
    )


def attn_fwd_kernel(pieces, relays, packs, spot_ref, a_ref, *refs):
    w_refs = refs[:pieces]
    b_ref, sq_ref, sk_ref = refs[pieces : pieces + 3]
    count = pieces + 3 + relays + 2 * packs
    sources = refs[pieces + 3 : count]
    q_ref, k_ref, v_ref, c_ref, lse_ref = refs[count : count + 5]
    targets = refs[count + 5 :]
    for source, target in zip(sources[:relays], targets[:relays]):
        target[...] = source[...]
    if packs:
        pack_kernel(spot_ref, *sources[relays:], targets[relays])
    seq, width = a_ref.shape
    share = width // pieces
    both = value = None
    for piece, w_ref in enumerate(w_refs):
        if pieces == 1:
            act = a_ref[...]
        else:
            which = jnp.where(spot_ref[CORE] == 0, piece, 1 - piece)
            act = a_ref[:, pl.ds(pl.multiple_of(which * share, 128), share)]
        term = dot(act, jnp.concatenate([w_ref[0], w_ref[1]], axis=1))
        both = term if both is None else both + term
        term = dot(act, w_ref[2])
        value = term if value is None else value + term
    query = (both[:, :PAIR] + b_ref[0:1, :]).astype(bf16)
    key = both[:, PAIR:].astype(bf16)
    value = value + b_ref[1:2, :]
    value_t = value.T.astype(bf16)
    q_ref[...] = query
    k_ref[...] = key
    v_ref[...] = value.astype(bf16)
    key_ext = jnp.concatenate([key, sk_ref[...]], axis=1)
    parts = []
    ones = jnp.ones((16, seq), bf16)
    for head in range(2):
        query_ext = jnp.concatenate([query * head_mask(head, HEAD**-0.5), sq_ref[...]], axis=1)
        scores = dot(key_ext, query_ext, NT)
        top = jnp.max(scores, axis=0, keepdims=True)
        weights = jnp.exp(scores - top).astype(bf16)
        summed = dot(
            jnp.concatenate([value_t[head * HEAD : (head + 1) * HEAD], ones], axis=0), weights
        )
        total = summed[HEAD : HEAD + 1]
        parts.append(summed[:HEAD] * (1.0 / total))
        lse_ref[0, head : head + 1, :] = top + jnp.log(total)
    c_ref[...] = jnp.concatenate(parts, axis=0).T


def weight_specs(layer, weights):
    if len(weights) == 1:
        width = weights[0].shape[2]
        return [pl.BlockSpec((None, 3, width, PAIR), lambda t, s: (layer, 0, 0, t))]
    share = weights[0].shape[2]
    return [pl.BlockSpec((3, share, PAIR), lambda t, s: (0, 0, t))] * 2


def relay_piece(array):
    lead, *rest = array.shape
    spec = pl.BlockSpec((lead // 3, *rest), lambda t, s: (t,) + (0,) * len(rest))
    return [(array, spec, spec, shape(array.shape, array.dtype))]


def relay_row(rows):
    _, half, width = rows.shape
    wide = width // 3
    return [
        (
            rows,
            pl.BlockSpec((None, half, wide), lambda t, s: (1 - s[SIDE], 0, t)),
            pl.BlockSpec((half, wide), lambda t, s: (0, t)),
            shape((half, width), rows.dtype),
        )
    ]


def attn_fwd(spot, hold, layer, act, weights, bias, seg_q, seg_k, relays=(), pack=None):
    pack_ins, pack_out = pack if pack else ([], None)
    seq, width = act.shape
    cols = bias.shape[2]
    steps = cols // PAIR
    block = pl.BlockSpec((seq, PAIR), lambda t, s: (0, t))
    return launch(
        functools.partial(attn_fwd_kernel, len(weights), len(relays), 1 if pack else 0),
        "attn_fwd", spot, hold,
        [(act, whole(seq, width))]
        + list(zip(weights, weight_specs(layer, weights)))
        + [
            (bias, pl.BlockSpec((None, 2, PAIR), lambda t, s: (layer, 0, t))),
            (seg_q, whole(seq, PAIR)),
            (seg_k, whole(seq, PAIR)),
        ]
        + [(array, source) for array, source, _, _ in relays]
        + pack_ins,
        [
            (block, shape((seq, cols), bf16)),
            (block, shape((seq, cols), bf16)),
            (block, shape((seq, cols), bf16)),
            (block, shape((seq, cols), f32)),
            (pl.BlockSpec((1, 8, seq), lambda t, s: (t, 0, 0)), shape((steps, 8, seq), f32)),
        ]
        + [(target, out) for _, _, target, out in relays]
        + ([pack_out] if pack else []),
        grid=(steps,),
        us=8.0
    )


def norm_rows(entries):
    centred = entries - jnp.mean(entries, axis=-1, keepdims=True)
    spread = jnp.mean(centred * centred, axis=-1, keepdims=True)
    rate = lax.rsqrt(spread + EPS)
    return centred * rate, rate


def ff_fwd_kernel(
    layer, last, spot_ref, lim_ref, xt_ref, xb_ref, co_ref, ct_ref, wo_ref, wy_ref, wc_ref,
    vec_ref, gain_ref, up_ref, bup_ref, down_ref, *rest
):
    if last:
        gt_ref, gb_ref, *rest = rest
    cu_ref, hat1_ref, rate1_ref, g_ref, slope_ref, *rest = rest
    acc_ref = rest[-1]
    step = pl.program_id(0)
    half_seq, width = xt_ref.shape
    half = co_ref.shape[1]
    wide = width // 2
    rows = 128
    ctx_limit, ff_limit, act_limit = lim_ref[layer, 1], lim_ref[layer, 2], lim_ref[layer, 3]

    @pl.when(step == 0)
    def _():
        inv = 1.0 / ctx_limit
        cu_ref[:, :half] = (ctx_limit * jnp.tanh(co_ref[...] * inv)).astype(bf16)
        cu_ref[:, half:width] = (ctx_limit * jnp.tanh(ct_ref[...] * inv)).astype(bf16)
        acc_ref[...] = dot(cu_ref[:, :half], wo_ref[...])
        for piece, w_ref in enumerate((wy_ref, wc_ref)):
            which = jnp.where(spot_ref[CORE] == 0, piece, 1 - piece)
            at = pl.ds(pl.multiple_of(which * wide, 128), wide)
            acc_ref[:, at] += dot(cu_ref[:, half:width], w_ref[...].reshape(half, wide))

        for base, x_ref in ((0, xt_ref), (half_seq, xb_ref)):

            def body(i, carry, base=base, x_ref=x_ref):
                start = pl.multiple_of(i * rows, rows)
                at = pl.ds(base + start, rows)
                hat, rate = norm_rows(
                    x_ref[pl.ds(start, rows), :].astype(f32) + (acc_ref[at, :] + vec_ref[0:1, :])
                )
                hat1_ref[at, :] = hat
                rate1_ref[at, :] = jnp.broadcast_to(rate, (rows, 128))
                normed = hat * gain_ref[0:1, :] + vec_ref[1:2, :]
                bent = ff_limit * jnp.tanh(normed * (1.0 / ff_limit))
                cu_ref[at, width:] = bent.astype(bf16)
                acc_ref[at, :] = normed + vec_ref[2:3, :]
                return carry

            lax.fori_loop(0, half_seq // rows, body, 0)

    inv_act = 1.0 / act_limit
    chunk = up_ref.shape[1]
    sub = FF_SUB
    for part in range(chunk // sub):
        cols = slice(part * sub, (part + 1) * sub)
        pre = dot(cu_ref[:, width:], up_ref[:, cols]) + bup_ref[layer : layer + 1, cols]
        cdf = 0.5 * lax.erf(pre * INV_SQRT2) + 0.5
        pdf = jnp.exp(pre * pre * -0.5) * INV_SQRT2PI
        bent = jnp.tanh(pre * cdf * inv_act)
        g_ref[:, cols] = (act_limit * bent).astype(bf16)
        slope_ref[:, cols] = ((1.0 - bent * bent) * (cdf + pre * pdf)).astype(bf16)
    acc_ref[...] += dot(g_ref[...], down_ref[...])

    @pl.when(step == pl.num_programs(0) - 1)
    def _():
        if last:
            top_ref, bottom_ref, de_ref, df_ref, sums_ref = rest[:-1]
            sums = norm_sums(width)
            for base, out_ref, in_ref in ((0, top_ref, gt_ref), (half_seq, bottom_ref, gb_ref)):

                def body(i, carry, base=base, out_ref=out_ref, in_ref=in_ref):
                    here = pl.ds(pl.multiple_of(i * rows, rows), rows)
                    at = pl.ds(base + pl.multiple_of(i * rows, rows), rows)
                    hat, rate = norm_rows(acc_ref[at, :])
                    new = hat * gain_ref[1:2, :] + vec_ref[3:4, :]
                    out_ref[here, :] = new.astype(bf16)
                    grad = in_ref[here, :].astype(f32)
                    return leave_norm(grad, hat, rate, gain_ref, at, de_ref, df_ref, carry)

                sums = lax.fori_loop(0, half_seq // rows, body, sums)
            store_sums(sums, sums_ref)
        else:
            hat2_ref, rate2_ref, new_ref, act_ref = rest[:-1]
            limit = lim_ref[layer + 1, 0]

            def body(i, carry):
                at = pl.ds(pl.multiple_of(i * rows, rows), rows)
                hat, rate = norm_rows(acc_ref[at, :])
                hat2_ref[at, :] = hat
                rate2_ref[at, :] = jnp.broadcast_to(rate, (rows, 128))
                new = hat * gain_ref[1:2, :] + vec_ref[3:4, :]
                new_ref[at, :] = new
                act_ref[at, :] = (limit * jnp.tanh(new * (1.0 / limit))).astype(bf16)
                return carry

            lax.fori_loop(0, 2 * half_seq // rows, body, 0)


def norm_back(grad, hat, rate, gain):
    scaled = grad * gain
    mean = jnp.mean(scaled, axis=-1, keepdims=True)
    lean = jnp.mean(scaled * hat, axis=-1, keepdims=True)
    return rate * (scaled - mean - hat * lean)


def norm_sums(width):
    return (jnp.zeros((1, width), f32),) * 3


def leave_norm(grad, hat, rate, gain_ref, at, de_ref, df_ref, sums):
    de = norm_back(grad, hat, rate, gain_ref[1:2, :])
    df = de.astype(bf16)
    de_ref[at, :] = de
    df_ref[at, :] = df
    return (
        sums[0] + jnp.sum(df.astype(f32), axis=0, keepdims=True),
        sums[1] + jnp.sum(grad, axis=0, keepdims=True),
        sums[2] + jnp.sum(grad * hat, axis=0, keepdims=True),
    )


def store_sums(sums, sums_ref):
    sums_ref[...] = jnp.zeros_like(sums_ref)
    sums_ref[2:3, :] = sums[0]
    sums_ref[3:4, :] = sums[1]
    sums_ref[5:6, :] = sums[2]


def norm_outs(seq, width):
    return [
        (whole(seq, width), shape((seq, width), f32)),
        (whole(seq, width), shape((seq, width), bf16)),
        (whole(8, width), shape((8, width), f32)),
    ]


def out_shares(pieces, half, width):
    if len(pieces) == 2:
        spec = pl.BlockSpec((3, half // 3, width // 2), lambda *_: (0, 3, 0))
        return [(piece, spec) for piece in pieces]
    return [
        (pieces[0], pl.BlockSpec((half, width // 2), lambda t, s: (0, s[CORE]))),
        (pieces[0], pl.BlockSpec((half, width // 2), lambda t, s: (0, 1 - s[CORE]))),
    ]


def halves(pair, half, width):
    if len(pair) == 1:
        return [
            (pair[0], pl.BlockSpec((half, width), lambda *_: (0, 0))),
            (pair[0], pl.BlockSpec((half, width), lambda *_: (1, 0))),
        ]
    first = my_row(half, width) if pair[0].ndim == 3 else whole(half, width)
    return [(pair[0], first), (pair[1], whole(half, width))]


def ff_fwd(
    spot, hold, layer, last, limits, x, ctx_own, ctx_oth, w_out, wo_oth, vec, gain, w_up, b_up,
    w_down, cot=None
):
    seq, half = ctx_own.shape
    width, hidden = w_up.shape[1:]
    chunk = FF_CHUNK
    steps = hidden // chunk
    tile = pl.BlockSpec((seq, chunk), lambda t, s: (0, t))
    full = whole(seq, width)
    outs = [
        (whole(seq, 2 * width), shape((seq, 2 * width), bf16)),
        (full, shape((seq, width), f32)),
        (whole(seq, 128), shape((seq, 128), f32)),
        (tile, shape((seq, hidden), bf16)),
        (tile, shape((seq, hidden), bf16)),
    ]
    if last:
        outs += [(whole(seq // 2, width), shape((seq // 2, width), bf16))] * 2
        outs += norm_outs(seq, width)
    else:
        outs += [
            (full, shape((seq, width), f32)),
            (whole(seq, 128), shape((seq, 128), f32)),
            (full, shape((seq, width), f32)),
            (full, shape((seq, width), bf16)),
        ]
    return launch(
        functools.partial(ff_fwd_kernel, layer, last), "ff_fwd", spot, hold,
        [(limits, smem())]
        + halves(x, seq // 2, width)
        + [
            (ctx_own, whole(seq, half)),
            (ctx_oth, whole(seq, half)),
            (w_out, at_layer(layer, half, width)),
            *out_shares(wo_oth, half, width),
            (vec, at_layer(layer, *vec.shape[1:])),
            (gain, at_layer(layer, *gain.shape[1:])),
            (w_up, pl.BlockSpec((None, width, chunk), lambda t, s: (layer, 0, t))),
            (b_up, pl.BlockSpec((b_up.shape[0], chunk), lambda t, s: (0, t))),
            (w_down, pl.BlockSpec((None, chunk, width), lambda t, s: (layer, t, 0))),
        ]
        + (halves(cot, seq // 2, width) if last else []),
        outs,
        scratch=[pltpu.VMEM((seq, width), f32)],
        grid=(steps,),
        us=21.0
    )


def ff_bwd_kernel(
    layer, spot_ref, lim_ref, de_ref, fin_ref, hat1_ref, rate1_ref, vec_ref, gain_ref, slope_ref,
    up_ref, down_ref, wo_ref, wy_ref, wc_ref, co_ref, ct_ref,
    zk_ref, ok_ref, os_ref, dy_ref, dco_ref, dct_ref, small_ref, bup_ref,
    do_ref, du_ref, dz_ref,
):
    step = pl.program_id(0)
    steps = pl.num_programs(0)
    seq, width = de_ref.shape
    half = width // 2
    rows = 128
    core = spot_ref[CORE]
    mine = pl.ds(pl.multiple_of(core * half, 128), half)
    other = pl.ds(pl.multiple_of((1 - core) * half, 128), half)
    zero = jnp.zeros((1, width), f32)
    ctx_limit, ff_limit = lim_ref[layer, 1], lim_ref[layer, 2]

    chunk = up_ref.shape[1]
    sub = FF_SUB
    for part in range(chunk // sub):
        cols = slice(part * sub, (part + 1) * sub)
        dz = dot(fin_ref[...], down_ref[cols, :], NT) * slope_ref[:, cols].astype(f32)
        low = dz.astype(bf16)
        bup_ref[:, cols] = jnp.sum(low.astype(f32), axis=0, keepdims=True)
        dz_ref[:, cols] = low
    term = dot(dz_ref[...], up_ref[...], NT)

    @pl.when(step == 0)
    def _():
        du_ref[...] = term

    @pl.when(step > 0)
    def _():
        du_ref[...] += term

    @pl.when(step < steps // 2)
    def _():
        zk_ref[:, pl.ds(pl.multiple_of(step * chunk, 128), chunk)] = dz_ref[...]

    @pl.when(step == steps - 1)
    def _():
        def body(i, carry):
            gain_sum, shift_sum, out_sum = carry
            at = pl.ds(pl.multiple_of(i * rows, rows), rows)
            hat = hat1_ref[at, :]
            normed = hat * gain_ref[0:1, :] + vec_ref[1:2, :]
            bent = jnp.tanh(normed * (1.0 / ff_limit))
            grad = de_ref[at, :] + du_ref[at, :] * (1.0 - bent * bent)
            dy = norm_back(grad, hat, rate1_ref[at, 0:1], gain_ref[0:1, :])
            low = dy.astype(bf16)
            dy_ref[at, :] = dy
            do_ref[at, :] = low
            return (
                gain_sum + jnp.sum(grad * hat, axis=0, keepdims=True),
                shift_sum + jnp.sum(grad, axis=0, keepdims=True),
                out_sum + jnp.sum(low.astype(f32), axis=0, keepdims=True),
            )

        sums = lax.fori_loop(0, seq // rows, body, (zero, zero, zero))
        small_ref[...] = jnp.zeros_like(small_ref)
        small_ref[0:1, :] = sums[2]
        small_ref[1:2, :] = sums[1]
        small_ref[4:5, :] = sums[0]
        ok_ref[...] = do_ref[:, mine]
        os_ref[...] = do_ref[:, other]
        inv = 1.0 / ctx_limit
        bent = jnp.tanh(co_ref[...] * inv)
        dco_ref[...] = (dot(do_ref[...], wo_ref[...], NT) * (1.0 - bent * bent)).astype(bf16)
        bent = jnp.tanh(ct_ref[...] * inv)
        grad = dot(do_ref[:, mine], wy_ref[...].reshape(half, half), NT)
        grad += dot(do_ref[:, other], wc_ref[...].reshape(half, half), NT)
        dct_ref[...] = (grad * (1.0 - bent * bent)).astype(bf16)


def ff_bwd(
    spot, hold, layer, limits, de, df, hat1, rate1, vec, gain, slope, w_up, w_down, w_out,
    wo_oth, ctx_own, ctx_oth,
):
    seq, half = ctx_own.shape
    width, hidden = w_up.shape[1:]
    chunk = FF_CHUNK
    steps = hidden // chunk
    span = steps // 2

    def place(t, s):
        return jnp.where(t < span, s[CORE] * span + t, (1 - s[CORE]) * span + t - span)

    full = whole(seq, width)
    part = whole(seq, width // 2)
    outs = [
        (whole(seq, hidden // 2), shape((seq, hidden // 2), bf16)),
        (part, shape((seq, width // 2), bf16)),
        (part, shape((seq, width // 2), bf16)),
        (full, shape((seq, width), f32)),
        (whole(seq, half), shape((seq, half), bf16)),
        (whole(seq, half), shape((seq, half), bf16)),
        (whole(8, width), shape((8, width), f32)),
        (pl.BlockSpec((1, chunk), lambda t, s: (0, place(t, s))), shape((1, hidden), f32)),
    ]
    return launch(
        functools.partial(ff_bwd_kernel, layer), "ff_bwd", spot, hold,
        [(limits, smem())]
        + [
            (de, full),
            (df, full),
            (hat1, full),
            (rate1, whole(seq, 128)),
            (vec, at_layer(layer, *vec.shape[1:])),
            (gain, at_layer(layer, *gain.shape[1:])),
            (slope, pl.BlockSpec((seq, chunk), lambda t, s: (0, place(t, s)))),
            (w_up, pl.BlockSpec((None, width, chunk), lambda t, s: (layer, 0, place(t, s)))),
            (w_down, pl.BlockSpec((None, chunk, width), lambda t, s: (layer, place(t, s), 0))),
            (w_out, at_layer(layer, half, width)),
            *out_shares(wo_oth, half, width),
            (ctx_own, whole(seq, half)),
            (ctx_oth, whole(seq, half)),
        ],
        outs,
        scratch=[
            pltpu.VMEM((seq, width), bf16),
            pltpu.VMEM((seq, width), f32),
            pltpu.VMEM((seq, chunk), bf16),
        ],
        grid=(steps,),
        us=20.0
    )


def attn_bwd_half(q_ref, k_ref, v_ref, c_ref, lse_ref, dc_ref, seg_q, seg_k):
    query, key, value, grad = q_ref[...], k_ref[...], v_ref[...], dc_ref[...]
    key_ext = jnp.concatenate([key, seg_k], axis=1)
    key_t = key.astype(f32).T.astype(bf16)
    product_t = (grad.astype(f32) * c_ref[...]).T
    d_key = d_value = None
    d_query_t = []
    for head in range(2):
        scaled = query * head_mask(head, HEAD**-0.5)
        scores = dot(key_ext, jnp.concatenate([scaled, seg_q], axis=1), NT)
        probs = jnp.exp(scores - lse_ref[0, head : head + 1, :])
        grad_head = grad * head_mask(head, 1.0)
        d_probs = dot(value, grad_head, NT)
        delta = jnp.sum(product_t[head * HEAD : (head + 1) * HEAD], axis=0, keepdims=True)
        d_scores = (probs * (d_probs - delta)).astype(bf16)
        term_v = dot(probs.astype(bf16), grad_head)
        term_k = dot(d_scores, scaled)
        d_value = term_v if d_value is None else d_value + term_v
        d_key = term_k if d_key is None else d_key + term_k
        d_query_t.append(dot(key_t[head * HEAD : (head + 1) * HEAD], d_scores))
    d_query = jnp.concatenate(d_query_t, axis=0).T * HEAD**-0.5
    return d_query.astype(bf16), d_key.astype(bf16), d_value.astype(bf16)


def attn_bwd_kernel(
    layer, spot_ref, lim_ref, xt_ref, xb_ref, dy_ref, sq_ref, sk_ref,
    qo_ref, ko_ref, vo_ref, co_ref, lo_ref, dco_ref,
    qt_ref, kt_ref, vt_ref, ct_ref, lt_ref, dct_ref, wo_ref, wy_ref, wc_ref, *rest
):
    if layer:
        hat_ref, rate_ref, gain_ref, *rest = rest
    dqo_ref, dko_ref, dvo_ref, dqt_ref, dkt_ref, dvt_ref, bo_ref, bt_ref, *rest = rest
    acc_ref = rest[-1]
    step = pl.program_id(0)
    half_seq, width = xt_ref.shape
    share = width // 2
    rows = 128
    own = attn_bwd_half(qo_ref, ko_ref, vo_ref, co_ref, lo_ref, dco_ref, sq_ref[...], sk_ref[...])
    oth = attn_bwd_half(qt_ref, kt_ref, vt_ref, ct_ref, lt_ref, dct_ref, sq_ref[...], sk_ref[...])
    dqo_ref[...], dko_ref[...], dvo_ref[...] = own
    dqt_ref[...], dkt_ref[...], dvt_ref[...] = oth
    for out_ref, grads in ((bo_ref, own), (bt_ref, oth)):
        out_ref[0:1, :] = jnp.sum(grads[0].astype(f32), axis=0, keepdims=True)
        out_ref[1:2, :] = jnp.sum(grads[2].astype(f32), axis=0, keepdims=True)
        out_ref[2:8, :] = jnp.zeros((6, PAIR), f32)
    joined = [jnp.concatenate([own[k], oth[k]], axis=1) for k in range(3)]
    for piece, w_ref in enumerate((wy_ref, wc_ref)):
        which = jnp.where(spot_ref[CORE] == 0, piece, 1 - piece)
        at = pl.ds(pl.multiple_of(which * share, 128), share)
        total = None
        for k in range(3):
            term = dot(joined[k], jnp.concatenate([wo_ref[k, at, :], w_ref[k]], axis=1), NT)
            total = term if total is None else total + term

        @pl.when(step == 0)
        def _():
            acc_ref[:, at] = total

        @pl.when(step > 0)
        def _():
            acc_ref[:, at] += total

    @pl.when(step == pl.num_programs(0) - 1)
    def _():
        inv = 1.0 / lim_ref[layer, 0]
        sums = norm_sums(width)
        for part, x_ref in enumerate((xt_ref, xb_ref)):

            def body(i, carry, part=part, x_ref=x_ref):
                here = pl.ds(pl.multiple_of(i * rows, rows), rows)
                at = pl.ds(part * half_seq + pl.multiple_of(i * rows, rows), rows)
                bent = jnp.tanh(x_ref[here, :].astype(f32) * inv)
                grad = dy_ref[at, :] + acc_ref[at, :] * (1.0 - bent * bent)
                if layer:
                    return leave_norm(
                        grad, hat_ref[at, :], rate_ref[at, 0:1], gain_ref, at, rest[0], rest[1],
                        carry,
                    )
                rest[part][here, :] = grad.astype(rest[part].dtype)
                return carry

            sums = lax.fori_loop(0, half_seq // rows, body, sums)
        if layer:
            store_sums(sums, rest[2])


def attn_bwd(spot, hold, layer, limits, x, dy, seg_q, seg_k, own, oth, w_qkv, wq_oth, below=()):
    seq, width = dy.shape
    cols = own[0].shape[1]
    steps = cols // PAIR
    block = pl.BlockSpec((seq, PAIR), lambda t, s: (0, t))
    half_specs = [
        block,
        block,
        block,
        block,
        pl.BlockSpec((1, 8, seq), lambda t, s: (t, 0, 0)),
        block,
    ]
    return launch(
        functools.partial(attn_bwd_kernel, layer), "attn_bwd", spot, hold,
        [(limits, smem())]
        + halves(x, seq // 2, width)
        + [(dy, whole(seq, width)), (seg_q, whole(seq, PAIR)), (seg_k, whole(seq, PAIR))]
        + list(zip(own, half_specs))
        + list(zip(oth, half_specs))
        + list(zip((w_qkv,), weight_specs(layer, (w_qkv,))))
        + list(zip(wq_oth, weight_specs(layer, wq_oth)))
        + (
            [
                (below[0], whole(seq, width)),
                (below[1], whole(seq, 128)),
                (below[2], at_layer(layer - 1, *below[2].shape[1:])),
            ]
            if layer
            else []
        ),
        [(block, shape((seq, cols), bf16))] * 6
        + [(pl.BlockSpec((8, PAIR), lambda t, s: (0, t)), shape((8, cols), f32))] * 2
        + (
            norm_outs(seq, width)
            if layer
            else [
                (whole(seq // 2, width), shape((seq // 2, width), f32)),
                (whole(seq // 2, width), shape((seq // 2, width), bf16)),
            ]
        ),
        scratch=[pltpu.VMEM((seq, width), f32)],
        grid=(steps,),
        us=18.5
    )


FF_ORDERS = (
    (AXIS_X, SIDE, AXIS_Z0, AXIS_Z1),
    (SIDE, AXIS_Z0, AXIS_X, AXIS_Z1),
    (AXIS_Z0, AXIS_X, SIDE, AXIS_Z1),
)
FF_ROWS = (144, 128, 112)
ATT_ORDERS = (
    (AXIS_X, SIDE, AXIS_Z0, AXIS_Z1),
    (AXIS_Z0, SIDE, AXIS_X, AXIS_Z1),
)
ATT_ROWS = (96, 96)
PIECE = 48


def block_of(spot_ref, order, rel):
    bit = {axis: (rel >> (3 - k)) & 1 for k, axis in enumerate(order)}
    chip = 0
    for axis in (AXIS_Z1, AXIS_Z0, AXIS_X):
        own = spot_ref[axis]
        chip = chip * 2 + (1 - own if bit[axis] else own)
    return bit[SIDE], chip


def w_ff_kernel(
    spot_ref, um_ref, uo_ref, zm_ref, so_ref, gm_ref, go_ref, fm_ref, fo_ref, down_ref, *rest
):
    outs, ut_ref, half_ref, all_ref = rest[:-3], rest[-3], rest[-2], rest[-1]
    step = pl.program_id(0)
    sides, chips, tall, lanes = all_ref.shape
    seq, width = um_ref.shape
    thin = width // chips

    @pl.when(step == 0)
    def _():
        ut_ref[:, :seq] = um_ref[...].T
        ut_ref[:, seq:] = uo_ref[...].T
        mine = pl.ds(pl.multiple_of(spot_ref[CORE] * lanes, 128), lanes)
        half_ref[0] = fm_ref[:, mine]
        half_ref[1] = fo_ref[:, mine]

    theirs = (dot(fo_ref[...], down_ref[...], NT) * so_ref[...].astype(f32)).astype(bf16)
    grad_up = dot(ut_ref[:, :seq], zm_ref[...]) + dot(ut_ref[:, seq:], theirs)
    grad_up = grad_up.astype(bf16)
    for chip in range(chips):
        at = pl.ds(pl.multiple_of((step % 2) * thin, 16), thin)
        all_ref[step // 2, chip, at, :] = grad_up[chip * thin : (chip + 1) * thin]
    base = 2 * thin
    deep = tall - base
    per = gm_ref.shape[1] // (2 * deep)
    for part in range(per):
        cols = slice(part * 2 * deep, (part + 1) * 2 * deep)
        grad_down = dot(gm_ref[:, cols], half_ref[0], TN) + dot(go_ref[:, cols], half_ref[1], TN)
        grad_down = grad_down.astype(bf16)
        for side in range(2):
            all_ref[side, step * per + part, base:, :] = grad_down[side * deep : (side + 1) * deep]

    @pl.when(step == pl.num_programs(0) - 1)
    def _():
        start = 0
        for part, (order, count) in enumerate(zip(FF_ORDERS, FF_ROWS)):
            for rel in range(16):
                side, chip = block_of(spot_ref, order, rel)
                side = 1 - spot_ref[SIDE] if side else spot_ref[SIDE]
                value = all_ref[side, chip, start : start + count, :]
                if rel < 8:
                    outs[2 * part][rel] = value
                else:
                    outs[2 * part + 1][(rel - 8) * count : (rel - 7) * count, :] = value
            start += count


def w_ff(
    spot, hold, layer, cu_mine, cu_core, dz_mine, slope_core, g_mine, g_core, df_mine, df_core,
    w_down
):
    seq, width = df_mine.shape
    lanes, hidden = width // 2, g_mine.shape[1]
    steps = dz_mine.shape[1] // lanes
    tall = hidden // 8
    g_block = pl.BlockSpec((seq, hidden // steps), lambda t, s: (0, t))
    u_block = pl.BlockSpec((seq, width), lambda *_: (0, 1))
    outs = []
    for rows in FF_ROWS:
        outs.append((whole(8, rows, lanes), shape((8, rows, lanes), bf16)))
        outs.append((whole(8 * rows, lanes), shape((8 * rows, lanes), bf16)))
    return launch(
        w_ff_kernel, "w_ff", spot, hold,
        [
            (cu_mine, u_block),
            (cu_core, u_block),
            (dz_mine, pl.BlockSpec((seq, lanes), lambda t, s: (0, t))),
            (slope_core, pl.BlockSpec((seq, lanes), lambda t, s: (0, s[CORE] * steps + t))),
            (g_mine, g_block),
            (g_core, g_block),
            (df_mine, whole(seq, width)),
            (df_core, whole(seq, width)),
            (
                w_down,
                pl.BlockSpec(
                    (None, lanes, width), lambda t, s: (layer, s[CORE] * steps + t, 0)
                ),
            ),
        ],
        outs,
        scratch=[
            pltpu.VMEM((width, 2 * seq), bf16),
            pltpu.VMEM((2, seq, lanes), bf16),
            pltpu.VMEM((2, 8, tall, lanes), bf16),
        ],
        grid=(steps,),
        us=13.5,
    )


def w_att_kernel(
    spot_ref, a_ref, dqo_ref, dko_ref, dvo_ref, dqt_ref, dkt_ref, dvt_ref,
    cm_ref, cc_ref, dom_ref, doc_ref, keep_ref, out_ref, *rest
):
    send_refs, at_ref, spare_ref = rest[:-2], rest[-2], rest[-1]
    width = a_ref.shape[1]
    _, chips, tall, cols = keep_ref.shape
    core = spot_ref[CORE]
    piece = PIECE
    per = tall // piece
    at_ref[...] = a_ref[...].T
    sides = ((dqo_ref, dko_ref, dvo_ref), (dqt_ref, dkt_ref, dvt_ref))
    for side, grads in enumerate(sides):
        for which in range(3):
            result = dot(at_ref[...], grads[which][...]).astype(bf16)
            for j in range(width // piece):
                index = which * (width // piece) + j
                block, sub = index // per, index % per
                spare_ref[block % 2, block // 2, sub * piece : (sub + 1) * piece, :] = result[
                    j * piece : (j + 1) * piece
                ]
        keep_ref[side] = spare_ref[core]
        for k, send_ref in enumerate(send_refs):
            send_ref[side] = spare_ref[1 - core, :, k * piece : (k + 1) * piece, :]
    half = width // 2
    heads = half // HEAD
    for side in range(2):
        at = slice(side * half, (side + 1) * half)
        result = dot(cm_ref[:, at], dom_ref[...], TN) + dot(cc_ref[:, at], doc_ref[...], TN)
        for chip in range(chips):
            for pair in range(heads // 2):
                first = (2 * pair) * HEAD + 8 * chip
                second = first + HEAD
                out_ref[side, chip, pair * 16 : (pair + 1) * 16, :] = jnp.concatenate(
                    [result[first : first + 8], result[second : second + 8]], axis=0
                ).astype(bf16)


def w_att(spot, hold, act, d_own, d_oth, cu_mine, cu_core, do_mine, do_core):
    seq, width = act.shape
    cols = width // 2
    chips = 8
    tall = 3 * width // (2 * chips)
    outs = [
        shape((2, chips, tall, cols), bf16),
        shape((2, chips, cols // chips, cols), bf16),
        *[shape((2, chips, PIECE, cols), bf16)] * (tall // PIECE),
    ]
    cq_block = pl.BlockSpec((seq, width), lambda *_: (0, 0))
    return launch(
        w_att_kernel, "w_att", spot, hold,
        [(array, whole(*array.shape)) for array in (act, *d_own, *d_oth)]
        + [
            (cu_mine, cq_block),
            (cu_core, cq_block),
            (do_mine, whole(seq, cols)),
            (do_core, whole(seq, cols)),
        ],
        [(whole(*out.shape), out) for out in outs],
        scratch=[pltpu.VMEM((width, seq), bf16), pltpu.VMEM((2, chips, tall, cols), bf16)],
        us=8.0,
    )


class Part:
    def __init__(self, kind, order, kept):
        self.kind, self.order, self.kept = kind, order, kept
        self.stage = 0
        self.array = self.start = None
        self.final = None

    def arrives(self, array, start):
        self.array, self.start = array, start


def pack_small(spot_ref, small_refs, out_ref):
    for layer in range(len(small_refs) // 5):
        bo_ref, bt_ref, vec_ref, sums_ref, up_ref = small_refs[5 * layer : 5 * layer + 5]
        half = bo_ref.shape[1]
        width = 2 * half
        side = spot_ref[SIDE]
        mine = pl.ds(pl.multiple_of(side * half, 128), half)
        other = pl.ds(pl.multiple_of((1 - side) * half, 128), half)
        out_ref[layer, 0:2, mine] = bo_ref[0:2, :]
        out_ref[layer, 0:2, other] = bt_ref[0:2, :]
        out_ref[layer, 2:8, :] = vec_ref[0:6, :] + sums_ref[0:6, :]
        for k in range(up_ref.shape[1] // width):
            out_ref[layer, 8 + k : 9 + k, :] = up_ref[:, k * width : (k + 1) * width]


def exchange(spot, over_axis, parts, att=None, smalls=(), pair=None, carry=None, hold=()):
    ins, outs, steps = [], [], []

    def take(array):
        for k, (known, _) in enumerate(ins):
            if known is array:
                return k
        ins.append((array, whole(*array.shape)))
        return len(ins) - 1

    def give(dims, dtype=bf16):
        outs.append((whole(*dims), shape(dims, dtype)))
        return len(outs) - 1

    lanes = (parts[0].kept if parts else att[0]).shape[-1]
    sends = {}

    def room(axis, rows):
        start = sends.get(axis, 0)
        sends[axis] = start + rows
        return start

    new_parts, places = [], []
    parts = sorted(parts, key=lambda part: (part.kind != "ff", part.kept.shape[0]))
    for part in parts:
        blocks, rows, _ = part.kept.shape
        source = take(part.kept), take(part.array), part.start
        if blocks > 1:
            axis = part.order[part.stage + 1]
            start = room(axis, blocks // 2 * rows)
            steps.append(("halve", source, give((blocks // 2, rows, lanes)), axis, start))
        elif part.kind == "ff":
            axis = SIDE
            start = room(axis, rows)
            steps.append(("end", source, give((rows, lanes), f32), axis, start))
        else:
            axis = None
            start = 0
            steps.append(("end", source, give((rows, lanes), f32), None, 0))
        places.append((part, axis, start))
    if att is not None:
        source = [take(array) for array in att]
        begin = 0
        for order, rows in zip(ATT_ORDERS, ATT_ROWS):
            start = room(order[0], 8 * rows)
            kept = give((8, rows, lanes))
            steps.append(("enter", source, kept, order[0], start, order, begin, rows))
            places.append((Part("att", order, None), order[0], start))
            begin += rows
    small_out = None
    if smalls:
        source = [take(array) for small in smalls for array in small]
        width = smalls[0][2].shape[1]
        small_out = give((len(smalls), 8 + smalls[0][4].shape[1] // width, width), f32)
        steps.append(("pack", source, small_out))
    if pair is not None:
        small_out = give(pair[0].shape, f32)
        steps.append(("sum", [take(array) for array in pair], small_out))
    if carry is not None:
        small_out = give(carry.shape, carry.dtype)
        steps.append(("copy", [take(carry)], small_out))
    send_at = {axis: give((rows, lanes)) for axis, rows in sends.items()}

    def body(spot_ref, *refs):
        in_refs, out_refs = refs[: len(ins)], refs[len(ins) :]
        for what, source, out, *more in steps:
            out_ref = out_refs[out]
            if what == "halve":
                axis, start = more
                kept, got = in_refs[source[0]], in_refs[source[1]]
                base = source[2]
                half, rows, _ = out_ref.shape
                send = out_refs[send_at[axis]]
                for j in range(half):
                    at = base + j * rows
                    out_ref[j] = kept[j] + got[at : at + rows, :]
                    at += half * rows
                    send[start + j * rows : start + (j + 1) * rows, :] = (
                        kept[half + j] + got[at : at + rows, :]
                    )
            elif what == "end":
                axis, start = more
                kept, got = in_refs[source[0]], in_refs[source[1]]
                base = source[2]
                rows = out_ref.shape[0]
                total = kept[0].astype(f32) + got[base : base + rows, :].astype(f32)
                out_ref[...] = total
                if axis is not None:
                    out_refs[send_at[axis]][start : start + rows, :] = total.astype(bf16)
            elif what == "enter":
                axis, start, order, begin, rows = more
                keep, outer, *got = (in_refs[k] for k in source)
                send = out_refs[send_at[axis]]
                for rel in range(16):
                    side, chip = block_of(spot_ref, order, rel)
                    for k in range(begin // PIECE, (begin + rows) // PIECE):
                        if k < len(got):
                            at = slice(k * PIECE, (k + 1) * PIECE)
                            value = keep[side, chip, at, :] + got[k][side, chip]
                        else:
                            value = outer[side, chip]
                        done = k * PIECE - begin
                        if rel < 8:
                            out_ref[rel, done : done + PIECE, :] = value
                        else:
                            at = start + (rel - 8) * rows + done
                            send[at : at + PIECE, :] = value
            elif what == "copy":
                out_ref[...] = in_refs[source[0]][...]
            elif what == "pack":
                pack_small(spot_ref, [in_refs[k] for k in source], out_ref)
            else:
                out_ref[...] = in_refs[source[0]][...] + in_refs[source[1]][...]

    results = launch(body, "exchange", spot, hold, ins, outs, us=5.0)
    arrived = {axis: over_axis(results[k], axis) for axis, k in send_at.items()}
    kept_at = [step[2] for step in steps]
    for (part, axis, start), what, out in zip(places, [step[0] for step in steps], kept_at):
        if what == "end":
            part.final = results[out]
        else:
            part.kept = results[out]
        if what != "enter":
            part.stage += 1
        if axis is not None:
            part.arrives(arrived[axis], start)
        new_parts.append(part)
    return new_parts, (None if small_out is None else results[small_out])


def finish_kernel(spot_ref, a_ref, b_ref, c_ref, got_ref, keep_ref, send_ref, both_ref):
    core, side = spot_ref[CORE], spot_ref[SIDE]
    start = 0
    for ref in (a_ref, b_ref, c_ref):
        both_ref[side, start : start + ref.shape[0], :] = ref[...]
        start += ref.shape[0]
    both_ref[1 - side] = got_ref[...].astype(f32)
    half = both_ref.shape[1] // 2
    quarter = half // 4
    for out_ref, which in ((keep_ref, core), (send_ref, 1 - core)):
        for k in range(4):
            at = pl.ds(pl.multiple_of((k % 2) * 2 * quarter + which * quarter, 16), quarter)
            out_ref[k * quarter : (k + 1) * quarter, :] = both_ref[k // 2, at, :].astype(
                out_ref.dtype
            )
        out_ref[half:, :] = both_ref[which, half:, :].astype(out_ref.dtype)


def finish_ff(spot, parts):
    rows = sum(FF_ROWS)
    lanes = parts[0].final.shape[1]
    start = parts[0].start
    got = parts[0].array
    assert start % rows == 0
    return launch(
        finish_kernel, "finish_ff", spot, (),
        [(part.final, whole(*part.final.shape)) for part in parts]
        + [(got, pl.BlockSpec((rows, lanes), lambda *_: (start // rows, 0)))],
        [(whole(rows, lanes), shape((rows, lanes), f32)), (whole(rows, lanes), shape((rows, lanes), bf16))],
        scratch=[pltpu.VMEM((2, rows, lanes), f32)],
        us=3.0,
    )


def assemble_kernel(layers, spot_ref, *refs):
    up_ref, down_ref = refs[-2:]
    core = spot_ref[CORE]
    for layer in range(layers):
        keep, got = refs[2 * layer][...], refs[2 * layer + 1][...].astype(f32)
        lanes = keep.shape[1]
        half = keep.shape[0] // 2
        quarter = half // 4
        tiles = lanes // 128
        for side in range(2):
            value = jnp.where(core == side, keep, got)
            for t in range(tiles):
                cols = slice(t * 128, (t + 1) * 128)
                for k in range(4):
                    start = ((side * 4 + k) * tiles + t) * layers + layer
                    up_ref[pl.ds(start, quarter, stride=8 * tiles * layers), :] = value[
                        k * quarter : (k + 1) * quarter, cols
                    ]
                start = (side * tiles + t) * layers + layer
                down_ref[pl.ds(start, half, stride=2 * tiles * layers), :] = value[half:, cols]


def assemble(spot, pairs):
    layers = len(pairs)
    rows, lanes = pairs[0][0].shape
    dims = (rows * lanes // 128 * layers, 128)
    return launch(
        functools.partial(assemble_kernel, layers), "assemble", spot, (),
        [(array, whole(*array.shape)) for pair in pairs for array in pair],
        [(whole(*dims), shape(dims, f32))] * 2,
        us=3.0,
    )


def local(
    hidden_in, cotangent, segment_ids, clip_ranges, w_qkv, bias_qv, w_out, vector_bias, ln_gain,
    w_up, bias_up, w_down,
):
    layers = w_qkv.shape[0]
    row_count, half_seq, width = hidden_in.shape
    seq = segment_ids.shape[1]
    cols = w_qkv.shape[3]
    heads = cols // HEAD
    hidden = w_up.shape[2]
    dp_count = lax.axis_size("dp")
    assert lax.axis_size("mp") == 2 and row_count == 2 and seq == 2 * half_seq
    bits = dp_count.bit_length() - 1
    assert dp_count == 1 << bits and bits >= 1
    chips = dp_count // 2
    side = lax.axis_index("mp")
    place = lax.axis_index("dp")
    core = place % 2
    spot = Spot(
        jnp.stack(
            [core, side, (place >> 1) & 1, (place >> 2) & 1, (place >> 3) & 1]
        ).astype(jnp.int32)
    )

    def over_mp(value):
        return lax.ppermute(value, "mp", [(0, 1), (1, 0)])

    def over_bit(value, bit):
        return lax.ppermute(value, "dp", [(i, i ^ (1 << bit)) for i in range(dp_count)])

    def over_core(value):
        return over_bit(value, 0)

    def over_axis(value, axis):
        return over_mp(value) if axis == SIDE else over_bit(value, axis - AXIS_X + 1)

    def pick(value, index, axis):
        return lax.dynamic_index_in_dim(value, index, axis, keepdims=False)

    def ordered(index, mine, theirs, axis):
        first = jnp.where(index == 0, mine, theirs)
        second = jnp.where(index == 0, theirs, mine)
        return jnp.concatenate([first, second], axis=axis)

    x = (hidden_in, over_mp(pick(hidden_in, 1 - side, 0)))
    bias_oth = over_mp(bias_qv)
    limits = clip_ranges.astype(f32)
    seg_row = pick(segment_ids, side, 0).reshape(2, half_seq)
    seg_row = jnp.concatenate([pick(seg_row, side, 0), pick(seg_row, 1 - side, 0)])
    same = seg_row[:, None] == jnp.arange(PAIR, dtype=seg_row.dtype)[None, :]
    seg_q = jnp.where(same, BIG, 0.0).astype(bf16)
    seg_k = jnp.where(same, 0.0, 1.0).astype(bf16)

    arrived = over_mp(pick_weights(spot, w_qkv))
    act = enter(spot, (bias_oth,), limits, hidden_in, x[1])
    fetched, wo_oth, stored = [], [], []
    shared = ()
    for layer in range(layers):
        last = layer == layers - 1
        relays = relay_piece(arrived) if layer else []
        if last:
            relays = relays + relay_row(cotangent)
        outs = attn_fwd(spot, (), layer, act, (w_qkv,), bias_qv, seg_q, seg_k, relays)
        own, copies = outs[:5], outs[5:]
        if last:
            cot = (cotangent, over_mp(copies[-1]))
        if layer:
            copy = copies[0]
        else:
            copy, out_share = relay(spot, arrived, w_out)
        fetched.append((arrived, over_core(copy)))
        wo_oth.append(fetched[layer] if layer else (over_mp(out_share),))
        outs = attn_fwd(
            spot, (), layer, act, fetched[layer], bias_oth, seg_q, seg_k,
            pack=None if last else pack_weights(layer + 1, w_qkv, w_out),
        )
        oth = outs[:5]
        if not last:
            arrived = over_mp(outs[5])
        outs = ff_fwd(
            spot, shared, layer, last, limits, x, own[3], oth[3], w_out, wo_oth[layer], vector_bias,
            ln_gain,
            w_up, bias_up, w_down, cot if last else None,
        )
        cu, hat1, rate1, g, slope = outs[:5]
        shared = over_core(cu), over_core(g), over_core(slope)
        norm = None
        if last:
            hidden_mine, hidden_send, *descent = outs[5:]
        else:
            norm = outs[5:7]
        stored.append((x, act, own, oth, cu, hat1, rate1, g, slope, norm, shared))
        if not last:
            x, act = (outs[7],), outs[8]
    hidden_recv = over_mp(hidden_send)

    fast = chips == 8 and width == 768 and hidden == 3072 and cols == 384

    smalls, groups = [], {}
    flying = []
    small = None
    df_core = over_core(descent[1])
    for layer in reversed(range(layers)):
        x, act, own, oth, cu, hat1, rate1, g, slope, norm, shared = stored[layer]
        de, df, sums = descent
        dz_keep, do_keep, do_send, dy, dc_own, dc_oth, vec, d_bup = ff_bwd(
            spot, (), layer, limits, de, df, hat1, rate1, vector_bias, ln_gain, slope, w_up,
            w_down, w_out, wo_oth[layer], own[3], oth[3],
        )
        if fast:
            do_core = over_core(do_send)
            if flying:
                flying, _ = exchange(spot, over_axis, flying, entering)
                groups["att", layer + 1] = flying[-len(ATT_ROWS) :]
            else:
                hidden_out = place_rows(spot, (), hidden_mine, hidden_recv, bf16)
            outs = w_ff(
                spot, (), layer, cu, shared[0], dz_keep, shared[2], g, shared[1], df, df_core,
                w_down,
            )
            parts_ff = []
            for k, order in enumerate(FF_ORDERS):
                parts_ff.append(Part("ff", order, outs[2 * k]))
                parts_ff[k].arrives(over_axis(outs[2 * k + 1], order[0]), 0)
            groups["ff", layer] = parts_ff
            ending = [part for part in flying if part.stage == 2]
            if ending:
                exchange(spot, over_axis, ending)
            flying = flying + parts_ff
        below = (*stored[layer - 1][9], ln_gain) if layer else ()
        outs = attn_bwd(
            spot, (), layer, limits, x, dy, seg_q, seg_k, (*own, dc_own), (*oth, dc_oth), w_qkv,
            fetched[layer], below,
        )
        d_own, d_oth = outs[:3], outs[3:6]
        smalls.insert(0, (outs[6], outs[7], vec, sums, d_bup))
        descent = outs[8:]
        if fast:
            keep, out, *send = w_att(
                spot, (), act, d_own, d_oth, cu, shared[0], do_keep, do_core
            )
            entering = keep, out, *(over_core(piece) for piece in send)
            if layer:
                flying, df = exchange(spot, over_axis, flying, carry=descent[1])
                df_core = over_core(df)
            else:
                late = [part for part in flying if part.kind == "ff" and part.stage == 3]
                flying = [part for part in flying if part not in late]
                flying, small = exchange(
                    spot, over_axis, flying, entering, smalls,
                    hold=tuple({id(part.array): part.array for part in late}.values()),
                )
                groups["att", 0] = flying[-len(ATT_ROWS) :]
        else:
            dz = (dot(df, w_down[layer], NT) * slope.astype(f32)).astype(bf16)
            do = ordered(core, do_keep, do_send, 1)
            total = []
            for lhs, rhs in ((cu[:, width:], dz), (g, df)):
                grad = dot(lhs, rhs, TN).reshape(-1)
                grad = grad + over_mp(grad)
                total.append(lax.psum_scatter(grad, "dp", scatter_dimension=0, tiled=True))
            groups["ff", layer] = total
            sides = []
            for grads, part in ((d_own, cu[:, :cols]), (d_oth, cu[:, cols:width])):
                qkv = jnp.stack([dot(act, grad, TN) for grad in grads])
                qkv = qkv.reshape(3, width, heads, HEAD).transpose(2, 0, 1, 3)
                sides.append((qkv.reshape(heads, -1), dot(part, do, TN).reshape(heads, -1)))
            total = []
            for k in range(2):
                grad = sides[0][k] + over_mp(sides[1][k])
                total.append(lax.psum_scatter(grad, "dp", scatter_dimension=1, tiled=True))
            groups["att", layer] = total

    row_mine, row_send = descent
    if fast:
        axes = [AXIS_X, SIDE, AXIS_Z0, AXIS_Z1]
        pair = (small, over_axis(small, axes.pop(0)))
        turn = 0
        while True:
            if turn == 1:
                flying = flying + late
            flying = [part for part in flying if part.final is None]
            if not flying and turn > 1:
                break
            flying, summed = exchange(spot, over_axis, flying, pair=pair)
            small = small if summed is None else summed
            pair = (small, over_axis(small, axes.pop(0))) if axes else None
            if turn == 2:
                grad_input = place_rows(spot, (), row_mine, over_mp(row_send), f32)
                done = {k: finish_ff(spot, groups["ff", k]) for k in range(1, layers)}
            turn += 1
        while pair:
            small = pair[0] + pair[1]
            pair = (small, over_axis(small, axes.pop(0))) if axes else None
        small = small + over_core(small)
        done[0] = finish_ff(spot, groups["ff", 0])
        up, down = assemble(spot, [(done[k][0], over_core(done[k][1])) for k in range(layers)])
        up, down = (
            flat.reshape(-1, layers, 128).transpose(1, 0, 2).reshape(layers, -1)
            for flat in (up, down)
        )
        qkvs, outs = [], []
        for layer in range(layers):
            rows = jnp.concatenate([part.final for part in groups["att", layer]], axis=0)
            share = 3 * width // dp_count
            qkv = rows[:share].reshape(share, heads, HEAD)
            qkvs.append(qkv.transpose(1, 0, 2).reshape(heads, -1))
            outs.append(rows[share:].reshape(heads, 2, 4, cols))
        outs = jnp.stack(outs)
        keep, sent = pick(outs, core, 2), pick(outs, 1 - core, 2).astype(bf16)
        outs = ordered(core, keep[:, :, :, None], over_core(sent).astype(f32)[:, :, :, None], 3)
        grads = (
            jnp.stack(qkvs), outs.reshape(layers, heads, -1), up, down
        )
    else:
        hidden_out = place_rows(spot, (), hidden_mine, hidden_recv, bf16)
        grad_input = place_rows(spot, (), row_mine, over_mp(row_send), f32)
        small = jnp.stack(
            [
                jnp.concatenate(
                    [ordered(side, bo[:2], bt[:2], 1), (vec + sums)[:6], up.reshape(-1, width)],
                    axis=0,
                )
                for bo, bt, vec, sums, up in smalls
            ]
        )
        small = lax.psum(small, ("dp", "mp"))
        grads = [
            jnp.stack([groups[kind, layer][k] for layer in range(layers)])
            for kind, k in (("att", 0), ("att", 1), ("ff", 0), ("ff", 1))
        ]
    grad_bias_qv = lax.dynamic_slice_in_dim(small[:, :2], side * cols, cols, 2)
    return (
        hidden_out,
        grad_input,
        grads[0],
        grad_bias_qv,
        grads[1],
        small[:, 2:6],
        small[:, 6:8],
        grads[2],
        small[:, 8:].reshape(layers, hidden),
        grads[3],
    )


def solution(mesh):
    return jax.shard_map(
        local,
        mesh=mesh,
        in_specs=(
            P("dp", "mp", None),
            P("dp", "mp", None),
            P("dp", None),
            P(),
            P(None, None, None, "mp"),
            P(None, None, "mp"),
            P(None, "mp", None),
            P(),
            P(),
            P(),
            P(),
            P(),
        ),
        out_specs=(
            P("dp", "mp", None),
            P("dp", "mp", None),
            P(None, "mp", "dp"),
            P(None, None, "mp"),
            P(None, "mp", "dp"),
            P(),
            P(),
            P(None, "dp"),
            P(),
            P(None, "dp"),
        ),
        check_vma=False,
    )
```

```python
import functools

import jax
import jax.numpy as jnp
from jax import lax
from jax.experimental import pallas as pl
from jax.experimental.pallas import tpu as pltpu
from jax.sharding import PartitionSpec as P

HEAD = 64
PAIR = 2 * HEAD
EPS = 1e-06
BIG = -1e30
INV_SQRT2 = 0.7071067811865476
INV_SQRT2PI = 0.3989422804014327

f32 = jnp.float32
bf16 = jnp.bfloat16
MIB = 1024 * 1024
FF_CHUNK = 768
FF_SUB = 256

NT = (((1,), (1,)), ((), ()))
TN = (((0,), (0,)), ((), ()))


def dot(lhs, rhs, dims=(((1,), (0,)), ((), ()))):
    return lax.dot_general(lhs, rhs, dims, preferred_element_type=f32)


def whole(*dims):
    return pl.BlockSpec(dims, lambda *_: (0,) * len(dims))


def at_layer(layer, *dims):
    return pl.BlockSpec((None, *dims), lambda *_: (layer,) + (0,) * len(dims))


def smem():
    return pl.BlockSpec(memory_space=pltpu.SMEM)


class Spot:
    def __init__(self, array):
        self.array = array
        self.latest = ()
        self.grant = 63.5


def launch(body, name, spot, hold, ins, outs, scratch=(), grid=(1,), us=3.0):
    count = len(ins)
    known = [array for array, _ in ins]
    hold = [array for array in (*hold, *spot.latest) if not any(array is k for k in known)]

    def kernel(spot_ref, *refs):
        body(spot_ref, *refs[:count], *refs[count + len(hold) :])

    in_specs = [spec for _, spec in ins] + [pl.BlockSpec(memory_space=pl.ANY)] * len(hold)
    results = pl.pallas_call(
        kernel,
        grid_spec=pltpu.PrefetchScalarGridSpec(
            num_scalar_prefetch=1,
            grid=grid,
            in_specs=in_specs,
            out_specs=[spec for spec, _ in outs],
            scratch_shapes=list(scratch),
        ),
        out_shape=[out for _, out in outs],
        compiler_params=pltpu.CompilerParams(vmem_limit_bytes=int(spot.grant * MIB)),
        cost_estimate=pl.CostEstimate(
            flops=int(us * 1e9), bytes_accessed=int(us * 1e6), transcendentals=0
        ),
        name=name,
    )(spot.array, *known, *hold)
    spot.latest = (results[0],)
    return results


def shape(dims, dtype):
    return jax.ShapeDtypeStruct(dims, dtype)


def head_mask(head, value):
    lane = lax.broadcasted_iota(jnp.int32, (1, PAIR), 1)
    return jnp.where((lane // HEAD) == head, value, 0.0).astype(bf16)


CORE, SIDE, AXIS_X, AXIS_Z0, AXIS_Z1 = range(5)


def enter_kernel(layer_limit, spot_ref, lim_ref, mine_ref, recv_ref, act_ref):
    limit = lim_ref[0, 0]
    inv = 1.0 / limit
    half = mine_ref.shape[0]
    act_ref[:half, :] = (limit * jnp.tanh(mine_ref[...].astype(f32) * inv)).astype(bf16)
    act_ref[half:, :] = (limit * jnp.tanh(recv_ref[...].astype(f32) * inv)).astype(bf16)


def enter(spot, hold, limits, hidden_in, recv):
    half, width = recv.shape
    (act,) = launch(
        functools.partial(enter_kernel, 0), "enter", spot, hold,
        [(limits, smem()), (hidden_in, my_row(half, width)), (recv, whole(half, width))],
        [(whole(2 * half, width), shape((2 * half, width), bf16))],
        us=3.0,
    )
    return act


def my_row(half, width):
    return pl.BlockSpec((None, half, width), lambda t, s: (s[SIDE], 0, 0))


def place_kernel(spot_ref, mine_ref, recv_ref, out_ref):
    out_ref[spot_ref[SIDE]] = mine_ref[...].astype(out_ref.dtype)
    out_ref[1 - spot_ref[SIDE]] = recv_ref[...].astype(out_ref.dtype)


def place_rows(spot, hold, mine, recv, dtype):
    half, width = mine.shape
    (out,) = launch(
        place_kernel, "place_rows", spot, hold,
        [(mine, whole(half, width)), (recv, whole(half, width))],
        [(whole(2, half, width), shape((2, half, width), dtype))],
        us=2.5
    )
    return out


def copy_kernel(spot_ref, *refs):
    count = len(refs) // 2
    for source, target in zip(refs[:count], refs[count:]):
        target[...] = source[...]


def pack_kernel(spot_ref, w_ref, o_ref, out_ref):
    rows = w_ref.shape[1]
    out_ref[:, :rows, :] = w_ref[...]
    out_ref[0, rows:, :] = o_ref[...]


def pack_weights(layer, w_qkv, w_out):
    _, _, width, cols = w_qkv.shape
    rows, wide, deep = width // 2, w_out.shape[2] // 2, cols // 3
    ins = [
        (w_qkv, pl.BlockSpec((None, 1, rows, cols), lambda t, s: (layer, t, s[CORE], 0))),
        (w_out, pl.BlockSpec((None, deep, wide), lambda t, s: (layer, t, s[CORE]))),
    ]
    out = (
        pl.BlockSpec((1, rows + deep, cols), lambda t, s: (t, 0, 0)),
        shape((3, rows + deep, cols), bf16),
    )
    return ins, out


def pick_weights(spot, w_qkv):
    _, _, width, cols = w_qkv.shape
    rows = width // 2
    return launch(
        copy_kernel, "pick_weights", spot, (),
        [(w_qkv, pl.BlockSpec((None, 1, rows, cols), lambda t, s: (0, t, s[CORE], 0)))],
        [(pl.BlockSpec((1, rows, cols), lambda t, s: (t, 0, 0)), shape((3, rows, cols), bf16))],
        grid=(3,),
        us=3.0,
    )[0]


def relay(spot, array, w_out):
    _, cols, width = w_out.shape
    copies = relay_piece(array) + [
        (
            w_out,
            pl.BlockSpec((None, cols // 3, width), lambda t, s: (0, t, 0)),
            pl.BlockSpec((cols // 3, width), lambda t, s: (t, 0)),
            shape((cols, width), bf16),
        )
    ]
    return launch(
        copy_kernel, "relay", spot, (),
        [(a, source) for a, source, _, _ in copies],
        [(target, out) for _, _, target, out in copies],
        grid=(3,),
        us=2.5,
    )


def attn_fwd_kernel(pieces, relays, packs, spot_ref, a_ref, *refs):
    w_refs = refs[:pieces]
    b_ref, sq_ref, sk_ref = refs[pieces : pieces + 3]
    count = pieces + 3 + relays + 2 * packs
    sources = refs[pieces + 3 : count]
    q_ref, k_ref, v_ref, c_ref, lse_ref = refs[count : count + 5]
    targets = refs[count + 5 :]
    for source, target in zip(sources[:relays], targets[:relays]):
        target[...] = source[...]
    if packs:
        pack_kernel(spot_ref, *sources[relays:], targets[relays])
    seq, width = a_ref.shape
    share = width // pieces
    both = value = None
    for piece, w_ref in enumerate(w_refs):
        if pieces == 1:
            act = a_ref[...]
        else:
            which = jnp.where(spot_ref[CORE] == 0, piece, 1 - piece)
            act = a_ref[:, pl.ds(pl.multiple_of(which * share, 128), share)]
        term = dot(act, jnp.concatenate([w_ref[0], w_ref[1]], axis=1))
        both = term if both is None else both + term
        term = dot(act, w_ref[2])
        value = term if value is None else value + term
    query = (both[:, :PAIR] + b_ref[0:1, :]).astype(bf16)
    key = both[:, PAIR:].astype(bf16)
    value = value + b_ref[1:2, :]
    value_t = value.T.astype(bf16)
    q_ref[...] = query
    k_ref[...] = key
    v_ref[...] = value.astype(bf16)
    key_ext = jnp.concatenate([key, sk_ref[...]], axis=1)
    parts = []
    ones = jnp.ones((16, seq), bf16)
    for head in range(2):
        query_ext = jnp.concatenate([query * head_mask(head, HEAD**-0.5), sq_ref[...]], axis=1)
        scores = dot(key_ext, query_ext, NT)
        top = jnp.max(scores, axis=0, keepdims=True)
        weights = jnp.exp(scores - top).astype(bf16)
        summed = dot(
            jnp.concatenate([value_t[head * HEAD : (head + 1) * HEAD], ones], axis=0), weights
        )
        total = summed[HEAD : HEAD + 1]
        parts.append(summed[:HEAD] * (1.0 / total))
        lse_ref[0, head : head + 1, :] = top + jnp.log(total)
    c_ref[...] = jnp.concatenate(parts, axis=0).T


def weight_specs(layer, weights):
    if len(weights) == 1:
        width = weights[0].shape[2]
        return [pl.BlockSpec((None, 3, width, PAIR), lambda t, s: (layer, 0, 0, t))]
    share = weights[0].shape[2]
    return [pl.BlockSpec((3, share, PAIR), lambda t, s: (0, 0, t))] * 2


def relay_piece(array):
    lead, *rest = array.shape
    spec = pl.BlockSpec((lead // 3, *rest), lambda t, s: (t,) + (0,) * len(rest))
    return [(array, spec, spec, shape(array.shape, array.dtype))]


def relay_row(rows):
    _, half, width = rows.shape
    wide = width // 3
    return [
        (
            rows,
            pl.BlockSpec((None, half, wide), lambda t, s: (1 - s[SIDE], 0, t)),
            pl.BlockSpec((half, wide), lambda t, s: (0, t)),
            shape((half, width), rows.dtype),
        )
    ]


def attn_fwd(spot, hold, layer, act, weights, bias, seg_q, seg_k, relays=(), pack=None):
    pack_ins, pack_out = pack if pack else ([], None)
    seq, width = act.shape
    cols = bias.shape[2]
    steps = cols // PAIR
    block = pl.BlockSpec((seq, PAIR), lambda t, s: (0, t))
    return launch(
        functools.partial(attn_fwd_kernel, len(weights), len(relays), 1 if pack else 0),
        "attn_fwd", spot, hold,
        [(act, whole(seq, width))]
        + list(zip(weights, weight_specs(layer, weights)))
        + [
            (bias, pl.BlockSpec((None, 2, PAIR), lambda t, s: (layer, 0, t))),
            (seg_q, whole(seq, PAIR)),
            (seg_k, whole(seq, PAIR)),
        ]
        + [(array, source) for array, source, _, _ in relays]
        + pack_ins,
        [
            (block, shape((seq, cols), bf16)),
            (block, shape((seq, cols), bf16)),
            (block, shape((seq, cols), bf16)),
            (block, shape((seq, cols), f32)),
            (pl.BlockSpec((1, 8, seq), lambda t, s: (t, 0, 0)), shape((steps, 8, seq), f32)),
        ]
        + [(target, out) for _, _, target, out in relays]
        + ([pack_out] if pack else []),
        grid=(steps,),
        us=8.0
    )


def norm_rows(entries):
    centred = entries - jnp.mean(entries, axis=-1, keepdims=True)
    spread = jnp.mean(centred * centred, axis=-1, keepdims=True)
    rate = lax.rsqrt(spread + EPS)
    return centred * rate, rate


def ff_fwd_kernel(
    layer, last, spot_ref, lim_ref, xt_ref, xb_ref, co_ref, ct_ref, wo_ref, wy_ref, wc_ref,
    vec_ref, gain_ref, up_ref, bup_ref, down_ref, *rest
):
    if last:
        gt_ref, gb_ref, *rest = rest
    cu_ref, hat1_ref, rate1_ref, g_ref, slope_ref, *rest = rest
    acc_ref = rest[-1]
    step = pl.program_id(0)
    half_seq, width = xt_ref.shape
    half = co_ref.shape[1]
    wide = width // 2
    rows = 128
    ctx_limit, ff_limit, act_limit = lim_ref[layer, 1], lim_ref[layer, 2], lim_ref[layer, 3]

    @pl.when(step == 0)
    def _():
        inv = 1.0 / ctx_limit
        cu_ref[:, :half] = (ctx_limit * jnp.tanh(co_ref[...] * inv)).astype(bf16)
        cu_ref[:, half:width] = (ctx_limit * jnp.tanh(ct_ref[...] * inv)).astype(bf16)
        acc_ref[...] = dot(cu_ref[:, :half], wo_ref[...])
        for piece, w_ref in enumerate((wy_ref, wc_ref)):
            which = jnp.where(spot_ref[CORE] == 0, piece, 1 - piece)
            at = pl.ds(pl.multiple_of(which * wide, 128), wide)
            acc_ref[:, at] += dot(cu_ref[:, half:width], w_ref[...].reshape(half, wide))

        for base, x_ref in ((0, xt_ref), (half_seq, xb_ref)):

            def body(i, carry, base=base, x_ref=x_ref):
                start = pl.multiple_of(i * rows, rows)
                at = pl.ds(base + start, rows)
                hat, rate = norm_rows(
                    x_ref[pl.ds(start, rows), :].astype(f32) + (acc_ref[at, :] + vec_ref[0:1, :])
                )
                hat1_ref[at, :] = hat
                rate1_ref[at, :] = jnp.broadcast_to(rate, (rows, 128))
                normed = hat * gain_ref[0:1, :] + vec_ref[1:2, :]
                bent = ff_limit * jnp.tanh(normed * (1.0 / ff_limit))
                cu_ref[at, width:] = bent.astype(bf16)
                acc_ref[at, :] = normed + vec_ref[2:3, :]
                return carry

            lax.fori_loop(0, half_seq // rows, body, 0)

    inv_act = 1.0 / act_limit
    chunk = up_ref.shape[1]
    sub = FF_SUB
    for part in range(chunk // sub):
        cols = slice(part * sub, (part + 1) * sub)
        pre = dot(cu_ref[:, width:], up_ref[:, cols]) + bup_ref[layer : layer + 1, cols]
        cdf = 0.5 * lax.erf(pre * INV_SQRT2) + 0.5
        pdf = jnp.exp(pre * pre * -0.5) * INV_SQRT2PI
        bent = jnp.tanh(pre * cdf * inv_act)
        g_ref[:, cols] = (act_limit * bent).astype(bf16)
        slope_ref[:, cols] = ((1.0 - bent * bent) * (cdf + pre * pdf)).astype(bf16)
    acc_ref[...] += dot(g_ref[...], down_ref[...])

    @pl.when(step == pl.num_programs(0) - 1)
    def _():
        if last:
            top_ref, bottom_ref, de_ref, df_ref, sums_ref = rest[:-1]
            sums = norm_sums(width)
            for base, out_ref, in_ref in ((0, top_ref, gt_ref), (half_seq, bottom_ref, gb_ref)):

                def body(i, carry, base=base, out_ref=out_ref, in_ref=in_ref):
                    here = pl.ds(pl.multiple_of(i * rows, rows), rows)
                    at = pl.ds(base + pl.multiple_of(i * rows, rows), rows)
                    hat, rate = norm_rows(acc_ref[at, :])
                    new = hat * gain_ref[1:2, :] + vec_ref[3:4, :]
                    out_ref[here, :] = new.astype(bf16)
                    grad = in_ref[here, :].astype(f32)
                    return leave_norm(grad, hat, rate, gain_ref, at, de_ref, df_ref, carry)

                sums = lax.fori_loop(0, half_seq // rows, body, sums)
            store_sums(sums, sums_ref)
        else:
            hat2_ref, rate2_ref, new_ref, act_ref = rest[:-1]
            limit = lim_ref[layer + 1, 0]

            def body(i, carry):
                at = pl.ds(pl.multiple_of(i * rows, rows), rows)
                hat, rate = norm_rows(acc_ref[at, :])
                hat2_ref[at, :] = hat
                rate2_ref[at, :] = jnp.broadcast_to(rate, (rows, 128))
                new = hat * gain_ref[1:2, :] + vec_ref[3:4, :]
                new_ref[at, :] = new
                act_ref[at, :] = (limit * jnp.tanh(new * (1.0 / limit))).astype(bf16)
                return carry

            lax.fori_loop(0, 2 * half_seq // rows, body, 0)


def norm_back(grad, hat, rate, gain):
    scaled = grad * gain
    mean = jnp.mean(scaled, axis=-1, keepdims=True)
    lean = jnp.mean(scaled * hat, axis=-1, keepdims=True)
    return rate * (scaled - mean - hat * lean)


def norm_sums(width):
    return (jnp.zeros((1, width), f32),) * 3


def leave_norm(grad, hat, rate, gain_ref, at, de_ref, df_ref, sums):
    de = norm_back(grad, hat, rate, gain_ref[1:2, :])
    df = de.astype(bf16)
    de_ref[at, :] = de
    df_ref[at, :] = df
    return (
        sums[0] + jnp.sum(df.astype(f32), axis=0, keepdims=True),
        sums[1] + jnp.sum(grad, axis=0, keepdims=True),
        sums[2] + jnp.sum(grad * hat, axis=0, keepdims=True),
    )


def store_sums(sums, sums_ref):
    sums_ref[...] = jnp.zeros_like(sums_ref)
    sums_ref[2:3, :] = sums[0]
    sums_ref[3:4, :] = sums[1]
    sums_ref[5:6, :] = sums[2]


def norm_outs(seq, width):
    return [
        (whole(seq, width), shape((seq, width), f32)),
        (whole(seq, width), shape((seq, width), bf16)),
        (whole(8, width), shape((8, width), f32)),
    ]


def out_shares(pieces, half, width):
    if len(pieces) == 2:
        spec = pl.BlockSpec((3, half // 3, width // 2), lambda *_: (0, 3, 0))
        return [(piece, spec) for piece in pieces]
    return [
        (pieces[0], pl.BlockSpec((half, width // 2), lambda t, s: (0, s[CORE]))),
        (pieces[0], pl.BlockSpec((half, width // 2), lambda t, s: (0, 1 - s[CORE]))),
    ]


def halves(pair, half, width):
    if len(pair) == 1:
        return [
            (pair[0], pl.BlockSpec((half, width), lambda *_: (0, 0))),
            (pair[0], pl.BlockSpec((half, width), lambda *_: (1, 0))),
        ]
    first = my_row(half, width) if pair[0].ndim == 3 else whole(half, width)
    return [(pair[0], first), (pair[1], whole(half, width))]


def ff_fwd(
    spot, hold, layer, last, limits, x, ctx_own, ctx_oth, w_out, wo_oth, vec, gain, w_up, b_up,
    w_down, cot=None
):
    seq, half = ctx_own.shape
    width, hidden = w_up.shape[1:]
    chunk = FF_CHUNK
    steps = hidden // chunk
    tile = pl.BlockSpec((seq, chunk), lambda t, s: (0, t))
    full = whole(seq, width)
    outs = [
        (whole(seq, 2 * width), shape((seq, 2 * width), bf16)),
        (full, shape((seq, width), f32)),
        (whole(seq, 128), shape((seq, 128), f32)),
        (tile, shape((seq, hidden), bf16)),
        (tile, shape((seq, hidden), bf16)),
    ]
    if last:
        outs += [(whole(seq // 2, width), shape((seq // 2, width), bf16))] * 2
        outs += norm_outs(seq, width)
    else:
        outs += [
            (full, shape((seq, width), f32)),
            (whole(seq, 128), shape((seq, 128), f32)),
            (full, shape((seq, width), f32)),
            (full, shape((seq, width), bf16)),
        ]
    return launch(
        functools.partial(ff_fwd_kernel, layer, last), "ff_fwd", spot, hold,
        [(limits, smem())]
        + halves(x, seq // 2, width)
        + [
            (ctx_own, whole(seq, half)),
            (ctx_oth, whole(seq, half)),
            (w_out, at_layer(layer, half, width)),
            *out_shares(wo_oth, half, width),
            (vec, at_layer(layer, *vec.shape[1:])),
            (gain, at_layer(layer, *gain.shape[1:])),
            (w_up, pl.BlockSpec((None, width, chunk), lambda t, s: (layer, 0, t))),
            (b_up, pl.BlockSpec((b_up.shape[0], chunk), lambda t, s: (0, t))),
            (w_down, pl.BlockSpec((None, chunk, width), lambda t, s: (layer, t, 0))),
        ]
        + (halves(cot, seq // 2, width) if last else []),
        outs,
        scratch=[pltpu.VMEM((seq, width), f32)],
        grid=(steps,),
        us=21.0
    )


def ff_bwd_kernel(
    layer, spot_ref, lim_ref, de_ref, fin_ref, hat1_ref, rate1_ref, vec_ref, gain_ref, slope_ref,
    up_ref, down_ref, wo_ref, wy_ref, wc_ref, co_ref, ct_ref,
    zk_ref, ok_ref, os_ref, dy_ref, dco_ref, dct_ref, small_ref, bup_ref,
    do_ref, du_ref, dz_ref,
):
    step = pl.program_id(0)
    steps = pl.num_programs(0)
    seq, width = de_ref.shape
    half = width // 2
    rows = 128
    core = spot_ref[CORE]
    mine = pl.ds(pl.multiple_of(core * half, 128), half)
    other = pl.ds(pl.multiple_of((1 - core) * half, 128), half)
    zero = jnp.zeros((1, width), f32)
    ctx_limit, ff_limit = lim_ref[layer, 1], lim_ref[layer, 2]

    chunk = up_ref.shape[1]
    sub = FF_SUB
    for part in range(chunk // sub):
        cols = slice(part * sub, (part + 1) * sub)
        dz = dot(fin_ref[...], down_ref[cols, :], NT) * slope_ref[:, cols].astype(f32)
        low = dz.astype(bf16)
        bup_ref[:, cols] = jnp.sum(low.astype(f32), axis=0, keepdims=True)
        dz_ref[:, cols] = low
    term = dot(dz_ref[...], up_ref[...], NT)

    @pl.when(step == 0)
    def _():
        du_ref[...] = term

    @pl.when(step > 0)
    def _():
        du_ref[...] += term

    @pl.when(step < steps // 2)
    def _():
        zk_ref[:, pl.ds(pl.multiple_of(step * chunk, 128), chunk)] = dz_ref[...]

    @pl.when(step == steps - 1)
    def _():
        def body(i, carry):
            gain_sum, shift_sum, out_sum = carry
            at = pl.ds(pl.multiple_of(i * rows, rows), rows)
            hat = hat1_ref[at, :]
            normed = hat * gain_ref[0:1, :] + vec_ref[1:2, :]
            bent = jnp.tanh(normed * (1.0 / ff_limit))
            grad = de_ref[at, :] + du_ref[at, :] * (1.0 - bent * bent)
            dy = norm_back(grad, hat, rate1_ref[at, 0:1], gain_ref[0:1, :])
            low = dy.astype(bf16)
            dy_ref[at, :] = dy
            do_ref[at, :] = low
            return (
                gain_sum + jnp.sum(grad * hat, axis=0, keepdims=True),
                shift_sum + jnp.sum(grad, axis=0, keepdims=True),
                out_sum + jnp.sum(low.astype(f32), axis=0, keepdims=True),
            )

        sums = lax.fori_loop(0, seq // rows, body, (zero, zero, zero))
        small_ref[...] = jnp.zeros_like(small_ref)
        small_ref[0:1, :] = sums[2]
        small_ref[1:2, :] = sums[1]
        small_ref[4:5, :] = sums[0]
        ok_ref[...] = do_ref[:, mine]
        os_ref[...] = do_ref[:, other]
        inv = 1.0 / ctx_limit
        bent = jnp.tanh(co_ref[...] * inv)
        dco_ref[...] = (dot(do_ref[...], wo_ref[...], NT) * (1.0 - bent * bent)).astype(bf16)
        bent = jnp.tanh(ct_ref[...] * inv)
        grad = dot(do_ref[:, mine], wy_ref[...].reshape(half, half), NT)
        grad += dot(do_ref[:, other], wc_ref[...].reshape(half, half), NT)
        dct_ref[...] = (grad * (1.0 - bent * bent)).astype(bf16)


def ff_bwd(
    spot, hold, layer, limits, de, df, hat1, rate1, vec, gain, slope, w_up, w_down, w_out,
    wo_oth, ctx_own, ctx_oth,
):
    seq, half = ctx_own.shape
    width, hidden = w_up.shape[1:]
    chunk = FF_CHUNK
    steps = hidden // chunk
    span = steps // 2

    def place(t, s):
        return jnp.where(t < span, s[CORE] * span + t, (1 - s[CORE]) * span + t - span)

    full = whole(seq, width)
    part = whole(seq, width // 2)
    outs = [
        (whole(seq, hidden // 2), shape((seq, hidden // 2), bf16)),
        (part, shape((seq, width // 2), bf16)),
        (part, shape((seq, width // 2), bf16)),
        (full, shape((seq, width), f32)),
        (whole(seq, half), shape((seq, half), bf16)),
        (whole(seq, half), shape((seq, half), bf16)),
        (whole(8, width), shape((8, width), f32)),
        (pl.BlockSpec((1, chunk), lambda t, s: (0, place(t, s))), shape((1, hidden), f32)),
    ]
    return launch(
        functools.partial(ff_bwd_kernel, layer), "ff_bwd", spot, hold,
        [(limits, smem())]
        + [
            (de, full),
            (df, full),
            (hat1, full),
            (rate1, whole(seq, 128)),
            (vec, at_layer(layer, *vec.shape[1:])),
            (gain, at_layer(layer, *gain.shape[1:])),
            (slope, pl.BlockSpec((seq, chunk), lambda t, s: (0, place(t, s)))),
            (w_up, pl.BlockSpec((None, width, chunk), lambda t, s: (layer, 0, place(t, s)))),
            (w_down, pl.BlockSpec((None, chunk, width), lambda t, s: (layer, place(t, s), 0))),
            (w_out, at_layer(layer, half, width)),
            *out_shares(wo_oth, half, width),
            (ctx_own, whole(seq, half)),
            (ctx_oth, whole(seq, half)),
        ],
        outs,
        scratch=[
            pltpu.VMEM((seq, width), bf16),
            pltpu.VMEM((seq, width), f32),
            pltpu.VMEM((seq, chunk), bf16),
        ],
        grid=(steps,),
        us=20.0
    )


def attn_bwd_half(q_ref, k_ref, v_ref, c_ref, lse_ref, dc_ref, seg_q, seg_k):
    query, key, value, grad = q_ref[...], k_ref[...], v_ref[...], dc_ref[...]
    key_ext = jnp.concatenate([key, seg_k], axis=1)
    key_t = key.astype(f32).T.astype(bf16)
    product_t = (grad.astype(f32) * c_ref[...]).T
    d_key = d_value = None
    d_query_t = []
    for head in range(2):
        scaled = query * head_mask(head, HEAD**-0.5)
        scores = dot(key_ext, jnp.concatenate([scaled, seg_q], axis=1), NT)
        probs = jnp.exp(scores - lse_ref[0, head : head + 1, :])
        grad_head = grad * head_mask(head, 1.0)
        d_probs = dot(value, grad_head, NT)
        delta = jnp.sum(product_t[head * HEAD : (head + 1) * HEAD], axis=0, keepdims=True)
        d_scores = (probs * (d_probs - delta)).astype(bf16)
        term_v = dot(probs.astype(bf16), grad_head)
        term_k = dot(d_scores, scaled)
        d_value = term_v if d_value is None else d_value + term_v
        d_key = term_k if d_key is None else d_key + term_k
        d_query_t.append(dot(key_t[head * HEAD : (head + 1) * HEAD], d_scores))
    d_query = jnp.concatenate(d_query_t, axis=0).T * HEAD**-0.5
    return d_query.astype(bf16), d_key.astype(bf16), d_value.astype(bf16)


def attn_bwd_kernel(
    layer, spot_ref, lim_ref, xt_ref, xb_ref, dy_ref, sq_ref, sk_ref,
    qo_ref, ko_ref, vo_ref, co_ref, lo_ref, dco_ref,
    qt_ref, kt_ref, vt_ref, ct_ref, lt_ref, dct_ref, wo_ref, wy_ref, wc_ref, *rest
):
    if layer:
        hat_ref, rate_ref, gain_ref, *rest = rest
    dqo_ref, dko_ref, dvo_ref, dqt_ref, dkt_ref, dvt_ref, bo_ref, bt_ref, *rest = rest
    acc_ref = rest[-1]
    step = pl.program_id(0)
    half_seq, width = xt_ref.shape
    share = width // 2
    rows = 128
    own = attn_bwd_half(qo_ref, ko_ref, vo_ref, co_ref, lo_ref, dco_ref, sq_ref[...], sk_ref[...])
    oth = attn_bwd_half(qt_ref, kt_ref, vt_ref, ct_ref, lt_ref, dct_ref, sq_ref[...], sk_ref[...])
    dqo_ref[...], dko_ref[...], dvo_ref[...] = own
    dqt_ref[...], dkt_ref[...], dvt_ref[...] = oth
    for out_ref, grads in ((bo_ref, own), (bt_ref, oth)):
        out_ref[0:1, :] = jnp.sum(grads[0].astype(f32), axis=0, keepdims=True)
        out_ref[1:2, :] = jnp.sum(grads[2].astype(f32), axis=0, keepdims=True)
        out_ref[2:8, :] = jnp.zeros((6, PAIR), f32)
    joined = [jnp.concatenate([own[k], oth[k]], axis=1) for k in range(3)]
    for piece, w_ref in enumerate((wy_ref, wc_ref)):
        which = jnp.where(spot_ref[CORE] == 0, piece, 1 - piece)
        at = pl.ds(pl.multiple_of(which * share, 128), share)
        total = None
        for k in range(3):
            term = dot(joined[k], jnp.concatenate([wo_ref[k, at, :], w_ref[k]], axis=1), NT)
            total = term if total is None else total + term

        @pl.when(step == 0)
        def _():
            acc_ref[:, at] = total

        @pl.when(step > 0)
        def _():
            acc_ref[:, at] += total

    @pl.when(step == pl.num_programs(0) - 1)
    def _():
        inv = 1.0 / lim_ref[layer, 0]
        sums = norm_sums(width)
        for part, x_ref in enumerate((xt_ref, xb_ref)):

            def body(i, carry, part=part, x_ref=x_ref):
                here = pl.ds(pl.multiple_of(i * rows, rows), rows)
                at = pl.ds(part * half_seq + pl.multiple_of(i * rows, rows), rows)
                bent = jnp.tanh(x_ref[here, :].astype(f32) * inv)
                grad = dy_ref[at, :] + acc_ref[at, :] * (1.0 - bent * bent)
                if layer:
                    return leave_norm(
                        grad, hat_ref[at, :], rate_ref[at, 0:1], gain_ref, at, rest[0], rest[1],
                        carry,
                    )
                rest[part][here, :] = grad.astype(rest[part].dtype)
                return carry

            sums = lax.fori_loop(0, half_seq // rows, body, sums)
        if layer:
            store_sums(sums, rest[2])


def attn_bwd(spot, hold, layer, limits, x, dy, seg_q, seg_k, own, oth, w_qkv, wq_oth, below=()):
    seq, width = dy.shape
    cols = own[0].shape[1]
    steps = cols // PAIR
    block = pl.BlockSpec((seq, PAIR), lambda t, s: (0, t))
    half_specs = [
        block,
        block,
        block,
        block,
        pl.BlockSpec((1, 8, seq), lambda t, s: (t, 0, 0)),
        block,
    ]
    return launch(
        functools.partial(attn_bwd_kernel, layer), "attn_bwd", spot, hold,
        [(limits, smem())]
        + halves(x, seq // 2, width)
        + [(dy, whole(seq, width)), (seg_q, whole(seq, PAIR)), (seg_k, whole(seq, PAIR))]
        + list(zip(own, half_specs))
        + list(zip(oth, half_specs))
        + list(zip((w_qkv,), weight_specs(layer, (w_qkv,))))
        + list(zip(wq_oth, weight_specs(layer, wq_oth)))
        + (
            [
                (below[0], whole(seq, width)),
                (below[1], whole(seq, 128)),
                (below[2], at_layer(layer - 1, *below[2].shape[1:])),
            ]
            if layer
            else []
        ),
        [(block, shape((seq, cols), bf16))] * 6
        + [(pl.BlockSpec((8, PAIR), lambda t, s: (0, t)), shape((8, cols), f32))] * 2
        + (
            norm_outs(seq, width)
            if layer
            else [
                (whole(seq // 2, width), shape((seq // 2, width), f32)),
                (whole(seq // 2, width), shape((seq // 2, width), bf16)),
            ]
        ),
        scratch=[pltpu.VMEM((seq, width), f32)],
        grid=(steps,),
        us=18.5
    )


FF_ORDERS = (
    (AXIS_X, SIDE, AXIS_Z0, AXIS_Z1),
    (SIDE, AXIS_Z0, AXIS_X, AXIS_Z1),
    (AXIS_Z0, AXIS_X, SIDE, AXIS_Z1),
)
FF_ROWS = (144, 128, 112)
ATT_ORDERS = (
    (AXIS_X, SIDE, AXIS_Z0, AXIS_Z1),
    (AXIS_Z0, SIDE, AXIS_X, AXIS_Z1),
)
FIRST_ATT_ORDERS = (
    (AXIS_X, SIDE, AXIS_Z0, AXIS_Z1),
    (AXIS_Z0, AXIS_X, SIDE, AXIS_Z1),
)
ATT_ROWS = (96, 96)
PIECE = 48


def block_of(spot_ref, order, rel):
    bit = {axis: (rel >> (3 - k)) & 1 for k, axis in enumerate(order)}
    chip = 0
    for axis in (AXIS_Z1, AXIS_Z0, AXIS_X):
        own = spot_ref[axis]
        chip = chip * 2 + (1 - own if bit[axis] else own)
    return bit[SIDE], chip


def w_ff_kernel(
    spot_ref, um_ref, uo_ref, zm_ref, so_ref, gm_ref, go_ref, fm_ref, fo_ref, down_ref, *rest
):
    outs, ut_ref, half_ref, all_ref = rest[:-3], rest[-3], rest[-2], rest[-1]
    step = pl.program_id(0)
    sides, chips, tall, lanes = all_ref.shape
    seq, width = um_ref.shape
    thin = width // chips

    @pl.when(step == 0)
    def _():
        ut_ref[:, :seq] = um_ref[...].T
        ut_ref[:, seq:] = uo_ref[...].T
        mine = pl.ds(pl.multiple_of(spot_ref[CORE] * lanes, 128), lanes)
        half_ref[0] = fm_ref[:, mine]
        half_ref[1] = fo_ref[:, mine]

    theirs = (dot(fo_ref[...], down_ref[...], NT) * so_ref[...].astype(f32)).astype(bf16)
    grad_up = dot(ut_ref[:, :seq], zm_ref[...]) + dot(ut_ref[:, seq:], theirs)
    grad_up = grad_up.astype(bf16)
    for chip in range(chips):
        at = pl.ds(pl.multiple_of((step % 2) * thin, 16), thin)
        all_ref[step // 2, chip, at, :] = grad_up[chip * thin : (chip + 1) * thin]
    base = 2 * thin
    deep = tall - base
    per = gm_ref.shape[1] // (2 * deep)
    for part in range(per):
        cols = slice(part * 2 * deep, (part + 1) * 2 * deep)
        grad_down = dot(gm_ref[:, cols], half_ref[0], TN) + dot(go_ref[:, cols], half_ref[1], TN)
        grad_down = grad_down.astype(bf16)
        for side in range(2):
            all_ref[side, step * per + part, base:, :] = grad_down[side * deep : (side + 1) * deep]

    @pl.when(step == pl.num_programs(0) - 1)
    def _():
        start = 0
        for part, (order, count) in enumerate(zip(FF_ORDERS, FF_ROWS)):
            for rel in range(16):
                side, chip = block_of(spot_ref, order, rel)
                side = 1 - spot_ref[SIDE] if side else spot_ref[SIDE]
                value = all_ref[side, chip, start : start + count, :]
                if rel < 8:
                    outs[2 * part][rel] = value
                else:
                    outs[2 * part + 1][(rel - 8) * count : (rel - 7) * count, :] = value
            start += count


def w_ff(
    spot, hold, layer, cu_mine, cu_core, dz_mine, slope_core, g_mine, g_core, df_mine, df_core,
    w_down
):
    seq, width = df_mine.shape
    lanes, hidden = width // 2, g_mine.shape[1]
    steps = dz_mine.shape[1] // lanes
    tall = hidden // 8
    g_block = pl.BlockSpec((seq, hidden // steps), lambda t, s: (0, t))
    u_block = pl.BlockSpec((seq, width), lambda *_: (0, 1))
    outs = []
    for rows in FF_ROWS:
        outs.append((whole(8, rows, lanes), shape((8, rows, lanes), bf16)))
        outs.append((whole(8 * rows, lanes), shape((8 * rows, lanes), bf16)))
    return launch(
        w_ff_kernel, "w_ff", spot, hold,
        [
            (cu_mine, u_block),
            (cu_core, u_block),
            (dz_mine, pl.BlockSpec((seq, lanes), lambda t, s: (0, t))),
            (slope_core, pl.BlockSpec((seq, lanes), lambda t, s: (0, s[CORE] * steps + t))),
            (g_mine, g_block),
            (g_core, g_block),
            (df_mine, whole(seq, width)),
            (df_core, whole(seq, width)),
            (
                w_down,
                pl.BlockSpec(
                    (None, lanes, width), lambda t, s: (layer, s[CORE] * steps + t, 0)
                ),
            ),
        ],
        outs,
        scratch=[
            pltpu.VMEM((width, 2 * seq), bf16),
            pltpu.VMEM((2, seq, lanes), bf16),
            pltpu.VMEM((2, 8, tall, lanes), bf16),
        ],
        grid=(steps,),
        us=13.5,
    )


def w_att_kernel(
    spot_ref, a_ref, dqo_ref, dko_ref, dvo_ref, dqt_ref, dkt_ref, dvt_ref,
    cm_ref, cc_ref, dom_ref, doc_ref, keep_ref, out_ref, *rest
):
    send_refs, at_ref, spare_ref = rest[:-2], rest[-2], rest[-1]
    width = a_ref.shape[1]
    _, chips, tall, cols = keep_ref.shape
    core = spot_ref[CORE]
    piece = PIECE
    per = tall // piece
    at_ref[...] = a_ref[...].T
    sides = ((dqo_ref, dko_ref, dvo_ref), (dqt_ref, dkt_ref, dvt_ref))
    for side, grads in enumerate(sides):
        for which in range(3):
            result = dot(at_ref[...], grads[which][...]).astype(bf16)
            for j in range(width // piece):
                index = which * (width // piece) + j
                block, sub = index // per, index % per
                spare_ref[block % 2, block // 2, sub * piece : (sub + 1) * piece, :] = result[
                    j * piece : (j + 1) * piece
                ]
        keep_ref[side] = spare_ref[core]
        for k, send_ref in enumerate(send_refs):
            send_ref[side] = spare_ref[1 - core, :, k * piece : (k + 1) * piece, :]
    half = width // 2
    heads = half // HEAD
    for side in range(2):
        at = slice(side * half, (side + 1) * half)
        result = dot(cm_ref[:, at], dom_ref[...], TN) + dot(cc_ref[:, at], doc_ref[...], TN)
        for chip in range(chips):
            for pair in range(heads // 2):
                first = (2 * pair) * HEAD + 8 * chip
                second = first + HEAD
                out_ref[side, chip, pair * 16 : (pair + 1) * 16, :] = jnp.concatenate(
                    [result[first : first + 8], result[second : second + 8]], axis=0
                ).astype(bf16)


def w_att(spot, hold, act, d_own, d_oth, cu_mine, cu_core, do_mine, do_core):
    seq, width = act.shape
    cols = width // 2
    chips = 8
    tall = 3 * width // (2 * chips)
    outs = [
        shape((2, chips, tall, cols), bf16),
        shape((2, chips, cols // chips, cols), bf16),
        *[shape((2, chips, PIECE, cols), bf16)] * (tall // PIECE),
    ]
    cq_block = pl.BlockSpec((seq, width), lambda *_: (0, 0))
    return launch(
        w_att_kernel, "w_att", spot, hold,
        [(array, whole(*array.shape)) for array in (act, *d_own, *d_oth)]
        + [
            (cu_mine, cq_block),
            (cu_core, cq_block),
            (do_mine, whole(seq, cols)),
            (do_core, whole(seq, cols)),
        ],
        [(whole(*out.shape), out) for out in outs],
        scratch=[pltpu.VMEM((width, seq), bf16), pltpu.VMEM((2, chips, tall, cols), bf16)],
        us=8.0,
    )


class Part:
    def __init__(self, kind, order, kept):
        self.kind, self.order, self.kept = kind, order, kept
        self.stage = 0
        self.array = self.start = None
        self.final = None

    def arrives(self, array, start):
        self.array, self.start = array, start


def pack_small(spot_ref, small_refs, out_ref):
    for layer in range(len(small_refs) // 5):
        bo_ref, bt_ref, vec_ref, sums_ref, up_ref = small_refs[5 * layer : 5 * layer + 5]
        half = bo_ref.shape[1]
        width = 2 * half
        side = spot_ref[SIDE]
        mine = pl.ds(pl.multiple_of(side * half, 128), half)
        other = pl.ds(pl.multiple_of((1 - side) * half, 128), half)
        out_ref[layer, 0:2, mine] = bo_ref[0:2, :]
        out_ref[layer, 0:2, other] = bt_ref[0:2, :]
        out_ref[layer, 2:8, :] = vec_ref[0:6, :] + sums_ref[0:6, :]
        for k in range(up_ref.shape[1] // width):
            out_ref[layer, 8 + k : 9 + k, :] = up_ref[:, k * width : (k + 1) * width]


def exchange(spot, over_axis, parts, att=None, smalls=(), pair=None, carry=None, hold=()):
    ins, outs, steps = [], [], []

    def take(array):
        for k, (known, _) in enumerate(ins):
            if known is array:
                return k
        ins.append((array, whole(*array.shape)))
        return len(ins) - 1

    def give(dims, dtype=bf16):
        outs.append((whole(*dims), shape(dims, dtype)))
        return len(outs) - 1

    lanes = (parts[0].kept if parts else att[0]).shape[-1]
    sends = {}

    def room(axis, rows):
        start = sends.get(axis, 0)
        sends[axis] = start + rows
        return start

    new_parts, places = [], []
    parts = sorted(parts, key=lambda part: (part.kind != "ff", part.kept.shape[0]))
    for part in parts:
        blocks, rows, _ = part.kept.shape
        source = take(part.kept), take(part.array), part.start
        if blocks > 1:
            axis = part.order[part.stage + 1]
            start = room(axis, blocks // 2 * rows)
            steps.append(("halve", source, give((blocks // 2, rows, lanes)), axis, start))
        elif part.kind == "ff":
            axis = SIDE
            start = room(axis, rows)
            steps.append(("end", source, give((rows, lanes), f32), axis, start))
        else:
            axis = None
            start = 0
            steps.append(("end", source, give((rows, lanes), f32), None, 0))
        places.append((part, axis, start))
    if att is not None:
        source = [take(array) for array in att]
        begin = 0
        for order, rows in zip(FIRST_ATT_ORDERS if smalls else ATT_ORDERS, ATT_ROWS):
            start = room(order[0], 8 * rows)
            kept = give((8, rows, lanes))
            steps.append(("enter", source, kept, order[0], start, order, begin, rows))
            places.append((Part("att", order, None), order[0], start))
            begin += rows
    small_out = None
    if smalls:
        source = [take(array) for small in smalls for array in small]
        width = smalls[0][2].shape[1]
        small_out = give((len(smalls), 8 + smalls[0][4].shape[1] // width, width), f32)
        steps.append(("pack", source, small_out))
    if pair is not None:
        small_out = give(pair[0].shape, f32)
        steps.append(("sum", [take(array) for array in pair], small_out))
    if carry is not None:
        small_out = give(carry.shape, carry.dtype)
        steps.append(("copy", [take(carry)], small_out))
    send_at = {axis: give((rows, lanes)) for axis, rows in sends.items()}

    def body(spot_ref, *refs):
        in_refs, out_refs = refs[: len(ins)], refs[len(ins) :]
        for what, source, out, *more in steps:
            out_ref = out_refs[out]
            if what == "halve":
                axis, start = more
                kept, got = in_refs[source[0]], in_refs[source[1]]
                base = source[2]
                half, rows, _ = out_ref.shape
                send = out_refs[send_at[axis]]
                for j in range(half):
                    at = base + j * rows
                    out_ref[j] = kept[j] + got[at : at + rows, :]
                    at += half * rows
                    send[start + j * rows : start + (j + 1) * rows, :] = (
                        kept[half + j] + got[at : at + rows, :]
                    )
            elif what == "end":
                axis, start = more
                kept, got = in_refs[source[0]], in_refs[source[1]]
                base = source[2]
                rows = out_ref.shape[0]
                total = kept[0].astype(f32) + got[base : base + rows, :].astype(f32)
                out_ref[...] = total
                if axis is not None:
                    out_refs[send_at[axis]][start : start + rows, :] = total.astype(bf16)
            elif what == "enter":
                axis, start, order, begin, rows = more
                keep, outer, *got = (in_refs[k] for k in source)
                send = out_refs[send_at[axis]]
                for rel in range(16):
                    side, chip = block_of(spot_ref, order, rel)
                    for k in range(begin // PIECE, (begin + rows) // PIECE):
                        if k < len(got):
                            at = slice(k * PIECE, (k + 1) * PIECE)
                            value = keep[side, chip, at, :] + got[k][side, chip]
                        else:
                            value = outer[side, chip]
                        done = k * PIECE - begin
                        if rel < 8:
                            out_ref[rel, done : done + PIECE, :] = value
                        else:
                            at = start + (rel - 8) * rows + done
                            send[at : at + PIECE, :] = value
            elif what == "copy":
                out_ref[...] = in_refs[source[0]][...]
            elif what == "pack":
                pack_small(spot_ref, [in_refs[k] for k in source], out_ref)
            else:
                out_ref[...] = in_refs[source[0]][...] + in_refs[source[1]][...]

    results = launch(body, "exchange", spot, hold, ins, outs, us=5.0)
    arrived = {axis: over_axis(results[k], axis) for axis, k in send_at.items()}
    kept_at = [step[2] for step in steps]
    for (part, axis, start), what, out in zip(places, [step[0] for step in steps], kept_at):
        if what == "end":
            part.final = results[out]
        else:
            part.kept = results[out]
        if what != "enter":
            part.stage += 1
        if axis is not None:
            part.arrives(arrived[axis], start)
        new_parts.append(part)
    return new_parts, (None if small_out is None else results[small_out])


def finish_kernel(spot_ref, a_ref, b_ref, c_ref, got_ref, keep_ref, send_ref, both_ref):
    core, side = spot_ref[CORE], spot_ref[SIDE]
    start = 0
    for ref in (a_ref, b_ref, c_ref):
        both_ref[side, start : start + ref.shape[0], :] = ref[...]
        start += ref.shape[0]
    both_ref[1 - side] = got_ref[...].astype(f32)
    half = both_ref.shape[1] // 2
    quarter = half // 4
    for out_ref, which in ((keep_ref, core), (send_ref, 1 - core)):
        for k in range(4):
            at = pl.ds(pl.multiple_of((k % 2) * 2 * quarter + which * quarter, 16), quarter)
            out_ref[k * quarter : (k + 1) * quarter, :] = both_ref[k // 2, at, :].astype(
                out_ref.dtype
            )
        out_ref[half:, :] = both_ref[which, half:, :].astype(out_ref.dtype)


def finish_ff(spot, parts):
    rows = sum(FF_ROWS)
    lanes = parts[0].final.shape[1]
    start = parts[0].start
    got = parts[0].array
    assert start % rows == 0
    return launch(
        finish_kernel, "finish_ff", spot, (),
        [(part.final, whole(*part.final.shape)) for part in parts]
        + [(got, pl.BlockSpec((rows, lanes), lambda *_: (start // rows, 0)))],
        [(whole(rows, lanes), shape((rows, lanes), f32)), (whole(rows, lanes), shape((rows, lanes), bf16))],
        scratch=[pltpu.VMEM((2, rows, lanes), f32)],
        us=3.0,
    )


def assemble_kernel(layers, spot_ref, *refs):
    up_ref, down_ref = refs[-2:]
    core = spot_ref[CORE]
    for layer in range(layers):
        keep, got = refs[2 * layer][...], refs[2 * layer + 1][...].astype(f32)
        lanes = keep.shape[1]
        half = keep.shape[0] // 2
        quarter = half // 4
        tiles = lanes // 128
        for side in range(2):
            value = jnp.where(core == side, keep, got)
            for t in range(tiles):
                cols = slice(t * 128, (t + 1) * 128)
                for k in range(4):
                    start = ((side * 4 + k) * tiles + t) * layers + layer
                    up_ref[pl.ds(start, quarter, stride=8 * tiles * layers), :] = value[
                        k * quarter : (k + 1) * quarter, cols
                    ]
                start = (side * tiles + t) * layers + layer
                down_ref[pl.ds(start, half, stride=2 * tiles * layers), :] = value[half:, cols]


def assemble(spot, pairs):
    layers = len(pairs)
    rows, lanes = pairs[0][0].shape
    dims = (rows * lanes // 128 * layers, 128)
    return launch(
        functools.partial(assemble_kernel, layers), "assemble", spot, (),
        [(array, whole(*array.shape)) for pair in pairs for array in pair],
        [(whole(*dims), shape(dims, f32))] * 2,
        us=3.0,
    )


def local(
    hidden_in, cotangent, segment_ids, clip_ranges, w_qkv, bias_qv, w_out, vector_bias, ln_gain,
    w_up, bias_up, w_down,
):
    layers = w_qkv.shape[0]
    row_count, half_seq, width = hidden_in.shape
    seq = segment_ids.shape[1]
    cols = w_qkv.shape[3]
    heads = cols // HEAD
    hidden = w_up.shape[2]
    dp_count = lax.axis_size("dp")
    assert lax.axis_size("mp") == 2 and row_count == 2 and seq == 2 * half_seq
    bits = dp_count.bit_length() - 1
    assert dp_count == 1 << bits and bits >= 1
    chips = dp_count // 2
    side = lax.axis_index("mp")
    place = lax.axis_index("dp")
    core = place % 2
    spot = Spot(
        jnp.stack(
            [core, side, (place >> 1) & 1, (place >> 2) & 1, (place >> 3) & 1]
        ).astype(jnp.int32)
    )

    def over_mp(value):
        return lax.ppermute(value, "mp", [(0, 1), (1, 0)])

    def over_bit(value, bit):
        return lax.ppermute(value, "dp", [(i, i ^ (1 << bit)) for i in range(dp_count)])

    def over_core(value):
        return over_bit(value, 0)

    def over_axis(value, axis):
        return over_mp(value) if axis == SIDE else over_bit(value, axis - AXIS_X + 1)

    def pick(value, index, axis):
        return lax.dynamic_index_in_dim(value, index, axis, keepdims=False)

    def ordered(index, mine, theirs, axis):
        first = jnp.where(index == 0, mine, theirs)
        second = jnp.where(index == 0, theirs, mine)
        return jnp.concatenate([first, second], axis=axis)

    x = (hidden_in, over_mp(pick(hidden_in, 1 - side, 0)))
    bias_oth = over_mp(bias_qv)
    limits = clip_ranges.astype(f32)
    seg_row = pick(segment_ids, side, 0).reshape(2, half_seq)
    seg_row = jnp.concatenate([pick(seg_row, side, 0), pick(seg_row, 1 - side, 0)])
    same = seg_row[:, None] == jnp.arange(PAIR, dtype=seg_row.dtype)[None, :]
    seg_q = jnp.where(same, BIG, 0.0).astype(bf16)
    seg_k = jnp.where(same, 0.0, 1.0).astype(bf16)

    arrived = over_mp(pick_weights(spot, w_qkv))
    act = enter(spot, (bias_oth,), limits, hidden_in, x[1])
    fetched, wo_oth, stored = [], [], []
    shared = ()
    for layer in range(layers):
        last = layer == layers - 1
        relays = relay_piece(arrived) if layer else []
        if last:
            relays = relays + relay_row(cotangent)
        outs = attn_fwd(spot, (), layer, act, (w_qkv,), bias_qv, seg_q, seg_k, relays)
        own, copies = outs[:5], outs[5:]
        if last:
            cot = (cotangent, over_mp(copies[-1]))
        if layer:
            copy = copies[0]
        else:
            copy, out_share = relay(spot, arrived, w_out)
        fetched.append((arrived, over_core(copy)))
        wo_oth.append(fetched[layer] if layer else (over_mp(out_share),))
        outs = attn_fwd(
            spot, (), layer, act, fetched[layer], bias_oth, seg_q, seg_k,
            pack=None if last else pack_weights(layer + 1, w_qkv, w_out),
        )
        oth = outs[:5]
        if not last:
            arrived = over_mp(outs[5])
        outs = ff_fwd(
            spot, shared, layer, last, limits, x, own[3], oth[3], w_out, wo_oth[layer], vector_bias,
            ln_gain,
            w_up, bias_up, w_down, cot if last else None,
        )
        cu, hat1, rate1, g, slope = outs[:5]
        shared = over_core(cu), over_core(g), over_core(slope)
        norm = None
        if last:
            hidden_mine, hidden_send, *descent = outs[5:]
        else:
            norm = outs[5:7]
        stored.append((x, act, own, oth, cu, hat1, rate1, g, slope, norm, shared))
        if not last:
            x, act = (outs[7],), outs[8]
    hidden_recv = over_mp(hidden_send)

    fast = chips == 8 and width == 768 and hidden == 3072 and cols == 384

    smalls, groups = [], {}
    flying = []
    small = None
    df_core = over_core(descent[1])
    for layer in reversed(range(layers)):
        x, act, own, oth, cu, hat1, rate1, g, slope, norm, shared = stored[layer]
        de, df, sums = descent
        dz_keep, do_keep, do_send, dy, dc_own, dc_oth, vec, d_bup = ff_bwd(
            spot, (), layer, limits, de, df, hat1, rate1, vector_bias, ln_gain, slope, w_up,
            w_down, w_out, wo_oth[layer], own[3], oth[3],
        )
        if fast:
            do_core = over_core(do_send)
            if flying:
                flying, _ = exchange(spot, over_axis, flying, entering)
                groups["att", layer + 1] = flying[-len(ATT_ROWS) :]
            outs = w_ff(
                spot, (hidden_recv, do_core), layer, cu, shared[0], dz_keep, shared[2], g, shared[1], df, df_core,
                w_down,
            )
            parts_ff = []
            for k, order in enumerate(FF_ORDERS):
                parts_ff.append(Part("ff", order, outs[2 * k]))
                parts_ff[k].arrives(over_axis(outs[2 * k + 1], order[0]), 0)
            groups["ff", layer] = parts_ff
            if flying:
                exchange(spot, over_axis, flying)
            flying = flying + parts_ff
        below = (*stored[layer - 1][9], ln_gain) if layer else ()
        outs = attn_bwd(
            spot, (), layer, limits, x, dy, seg_q, seg_k, (*own, dc_own), (*oth, dc_oth), w_qkv,
            fetched[layer], below,
        )
        d_own, d_oth = outs[:3], outs[3:6]
        smalls.insert(0, (outs[6], outs[7], vec, sums, d_bup))
        descent = outs[8:]
        if fast:
            keep, out, *send = w_att(
                spot, (), act, d_own, d_oth, cu, shared[0], do_keep, do_core
            )
            entering = keep, out, *(over_core(piece) for piece in send)
            if layer:
                flying, df = exchange(spot, over_axis, flying, carry=descent[1])
                df_core = over_core(df)
            else:
                late = [part for part in flying if part.kind == "ff" and part.stage == 3]
                flying = [part for part in flying if part not in late]
                flying, small = exchange(
                    spot, over_axis, flying, entering, smalls,
                    hold=tuple({id(part.array): part.array for part in late}.values()),
                )
                groups["att", 0] = flying[-len(ATT_ROWS) :]
        else:
            dz = (dot(df, w_down[layer], NT) * slope.astype(f32)).astype(bf16)
            do = ordered(core, do_keep, do_send, 1)
            total = []
            for lhs, rhs in ((cu[:, width:], dz), (g, df)):
                grad = dot(lhs, rhs, TN).reshape(-1)
                grad = grad + over_mp(grad)
                total.append(lax.psum_scatter(grad, "dp", scatter_dimension=0, tiled=True))
            groups["ff", layer] = total
            sides = []
            for grads, part in ((d_own, cu[:, :cols]), (d_oth, cu[:, cols:width])):
                qkv = jnp.stack([dot(act, grad, TN) for grad in grads])
                qkv = qkv.reshape(3, width, heads, HEAD).transpose(2, 0, 1, 3)
                sides.append((qkv.reshape(heads, -1), dot(part, do, TN).reshape(heads, -1)))
            total = []
            for k in range(2):
                grad = sides[0][k] + over_mp(sides[1][k])
                total.append(lax.psum_scatter(grad, "dp", scatter_dimension=1, tiled=True))
            groups["att", layer] = total

    row_mine, row_send = descent
    if fast:
        axes = [AXIS_X, SIDE, AXIS_Z0, AXIS_Z1]
        pair = (small, over_axis(small, axes.pop(0)))
        turn = 0
        while True:
            if turn == 1:
                flying = flying + late
            flying = [part for part in flying if part.final is None]
            if not flying and turn > 1:
                break
            flying, summed = exchange(spot, over_axis, flying, pair=pair)
            small = small if summed is None else summed
            pair = (small, over_axis(small, axes.pop(0))) if axes else None
            if turn == 0:
                hidden_out = place_rows(spot, (), hidden_mine, hidden_recv, bf16)
            if turn == 2:
                grad_input = place_rows(spot, (), row_mine, over_mp(row_send), f32)
                done = {k: finish_ff(spot, groups["ff", k]) for k in range(1, layers)}
            turn += 1
        while pair:
            small = pair[0] + pair[1]
            pair = (small, over_axis(small, axes.pop(0))) if axes else None
        small = small + over_core(small)
        done[0] = finish_ff(spot, groups["ff", 0])
        up, down = assemble(spot, [(done[k][0], over_core(done[k][1])) for k in range(layers)])
        up, down = (
            flat.reshape(-1, layers, 128).transpose(1, 0, 2).reshape(layers, -1)
            for flat in (up, down)
        )
        qkvs, outs = [], []
        for layer in range(layers):
            rows = jnp.concatenate([part.final for part in groups["att", layer]], axis=0)
            share = 3 * width // dp_count
            qkv = rows[:share].reshape(share, heads, HEAD)
            qkvs.append(qkv.transpose(1, 0, 2).reshape(heads, -1))
            outs.append(rows[share:].reshape(heads, 2, 4, cols))
        outs = jnp.stack(outs)
        keep, sent = pick(outs, core, 2), pick(outs, 1 - core, 2).astype(bf16)
        outs = ordered(core, keep[:, :, :, None], over_core(sent).astype(f32)[:, :, :, None], 3)
        grads = (
            jnp.stack(qkvs), outs.reshape(layers, heads, -1), up, down
        )
    else:
        hidden_out = place_rows(spot, (), hidden_mine, hidden_recv, bf16)
        grad_input = place_rows(spot, (), row_mine, over_mp(row_send), f32)
        small = jnp.stack(
            [
                jnp.concatenate(
                    [ordered(side, bo[:2], bt[:2], 1), (vec + sums)[:6], up.reshape(-1, width)],
                    axis=0,
                )
                for bo, bt, vec, sums, up in smalls
            ]
        )
        small = lax.psum(small, ("dp", "mp"))
        grads = [
            jnp.stack([groups[kind, layer][k] for layer in range(layers)])
            for kind, k in (("att", 0), ("att", 1), ("ff", 0), ("ff", 1))
        ]
    grad_bias_qv = lax.dynamic_slice_in_dim(small[:, :2], side * cols, cols, 2)
    return (
        hidden_out,
        grad_input,
        grads[0],
        grad_bias_qv,
        grads[1],
        small[:, 2:6],
        small[:, 6:8],
        grads[2],
        small[:, 8:].reshape(layers, hidden),
        grads[3],
    )


def solution(mesh):
    return jax.shard_map(
        local,
        mesh=mesh,
        in_specs=(
            P("dp", "mp", None),
            P("dp", "mp", None),
            P("dp", None),
            P(),
            P(None, None, None, "mp"),
            P(None, None, "mp"),
            P(None, "mp", None),
            P(),
            P(),
            P(),
            P(),
            P(),
        ),
        out_specs=(
            P("dp", "mp", None),
            P("dp", "mp", None),
            P(None, "mp", "dp"),
            P(None, None, "mp"),
            P(None, "mp", "dp"),
            P(),
            P(),
            P(None, "dp"),
            P(),
            P(None, "dp"),
        ),
        check_vma=False,
    )
```

```python
import functools

import jax
import jax.numpy as jnp
from jax import lax
from jax.experimental import pallas as pl
from jax.experimental.pallas import tpu as pltpu
from jax.sharding import PartitionSpec as P

HEAD = 64
PAIR = 2 * HEAD
EPS = 1e-06
BIG = -1e30
INV_SQRT2 = 0.7071067811865476
INV_SQRT2PI = 0.3989422804014327

f32 = jnp.float32
bf16 = jnp.bfloat16
MIB = 1024 * 1024
FF_CHUNK = 768
FF_SUB = 256

NT = (((1,), (1,)), ((), ()))
TN = (((0,), (0,)), ((), ()))


def dot(lhs, rhs, dims=(((1,), (0,)), ((), ()))):
    return lax.dot_general(lhs, rhs, dims, preferred_element_type=f32)


def whole(*dims):
    return pl.BlockSpec(dims, lambda *_: (0,) * len(dims))


def at_layer(layer, *dims):
    return pl.BlockSpec((None, *dims), lambda *_: (layer,) + (0,) * len(dims))


def smem():
    return pl.BlockSpec(memory_space=pltpu.SMEM)


class Spot:
    def __init__(self, array):
        self.array = array
        self.latest = ()
        self.grant = 63.5


def launch(
    body, name, spot, hold, ins, outs, scratch=(), grid=(1,), us=3.0, late=(), early=()
):
    known = [array for array, _ in ins] + [array for array, _ in late]
    hold = [array for array in (*hold, *spot.latest) if not any(array is k for k in known)]
    n_in, n_late, n_early, n_out = len(ins), len(late), len(early), len(outs)
    last = grid[0] - 1
    anywhere = pl.BlockSpec(memory_space=pl.ANY)

    def kernel(spot_ref, *refs):
        groups = []
        for count in (n_in, n_late, len(hold), n_early, n_out, n_late, n_early):
            groups.append(refs[:count])
            refs = refs[count:]
        in_refs, late_refs, _, early_refs, out_refs, late_bufs, early_bufs = groups
        fetches, stores = [], []
        if n_late:
            for k, (_, layer) in enumerate(late):
                source = late_refs[k] if layer is None else late_refs[k].at[layer]
                fetches.append(pltpu.make_async_copy(source, late_bufs[k], refs[0].at[k]))
            refs = refs[1:]
        if n_early:
            for k, (_, when) in enumerate(early):
                copy = pltpu.make_async_copy(early_bufs[k], early_refs[k], refs[0].at[k])
                stores.append((copy, when))
            refs = refs[1:]
        step = pl.program_id(0)
        if fetches:

            @pl.when(step == 0)
            def _():
                for copy in fetches:
                    copy.start()

            @pl.when(step == last)
            def _():
                for copy in fetches:
                    copy.wait()

        body(spot_ref, *in_refs, *late_bufs, *early_bufs, *out_refs, *refs)
        for copy, when in stores:
            pl.when(step == when)(copy.start)
        if stores:

            @pl.when(step == last)
            def _():
                for copy, _ in stores:
                    copy.wait()

    buffers = []
    for array, layer in late:
        buffers.append(pltpu.VMEM(array.shape if layer is None else array.shape[1:], array.dtype))
    buffers += [pltpu.VMEM(out.shape, out.dtype) for out, _ in early]
    buffers += [pltpu.SemaphoreType.DMA((count,)) for count in (n_late, n_early) if count]
    results = pl.pallas_call(
        kernel,
        grid_spec=pltpu.PrefetchScalarGridSpec(
            num_scalar_prefetch=1,
            grid=grid,
            in_specs=[spec for _, spec in ins] + [anywhere] * (n_late + len(hold)),
            out_specs=[anywhere] * n_early + [spec for spec, _ in outs],
            scratch_shapes=buffers + list(scratch),
        ),
        out_shape=[out for out, _ in early] + [out for _, out in outs],
        compiler_params=pltpu.CompilerParams(vmem_limit_bytes=int(spot.grant * MIB)),
        cost_estimate=pl.CostEstimate(
            flops=int(us * 1e9), bytes_accessed=int(us * 1e6), transcendentals=0
        ),
        name=name,
    )(spot.array, *known, *hold)
    spot.latest = (results[0],)
    return results


def shape(dims, dtype):
    return jax.ShapeDtypeStruct(dims, dtype)


def head_mask(head, value):
    lane = lax.broadcasted_iota(jnp.int32, (1, PAIR), 1)
    return jnp.where((lane // HEAD) == head, value, 0.0).astype(bf16)


CORE, SIDE, AXIS_X, AXIS_Z0, AXIS_Z1 = range(5)


def enter_kernel(layer_limit, spot_ref, lim_ref, mine_ref, recv_ref, act_ref):
    limit = lim_ref[0, 0]
    inv = 1.0 / limit
    half = mine_ref.shape[0]
    act_ref[:half, :] = (limit * jnp.tanh(mine_ref[...].astype(f32) * inv)).astype(bf16)
    act_ref[half:, :] = (limit * jnp.tanh(recv_ref[...].astype(f32) * inv)).astype(bf16)


def enter(spot, hold, limits, hidden_in, recv):
    half, width = recv.shape
    (act,) = launch(
        functools.partial(enter_kernel, 0), "enter", spot, hold,
        [(limits, smem()), (hidden_in, my_row(half, width)), (recv, whole(half, width))],
        [(whole(2 * half, width), shape((2 * half, width), bf16))],
        us=3.0,
    )
    return act


def my_row(half, width):
    return pl.BlockSpec((None, half, width), lambda t, s: (s[SIDE], 0, 0))


def place_kernel(spot_ref, mine_ref, recv_ref, out_ref):
    out_ref[spot_ref[SIDE]] = mine_ref[...].astype(out_ref.dtype)
    out_ref[1 - spot_ref[SIDE]] = recv_ref[...].astype(out_ref.dtype)


def place_rows(spot, hold, mine, recv, dtype):
    half, width = mine.shape
    (out,) = launch(
        place_kernel, "place_rows", spot, hold,
        [(mine, whole(half, width)), (recv, whole(half, width))],
        [(whole(2, half, width), shape((2, half, width), dtype))],
        us=2.5
    )
    return out


def copy_kernel(spot_ref, *refs):
    count = len(refs) // 2
    for source, target in zip(refs[:count], refs[count:]):
        target[...] = source[...]


def pack_kernel(spot_ref, w_ref, o_ref, out_ref):
    rows = w_ref.shape[1]
    out_ref[:, :rows, :] = w_ref[...]
    out_ref[0, rows:, :] = o_ref[...]


def pack_weights(layer, w_qkv, w_out):
    _, _, width, cols = w_qkv.shape
    rows, wide, deep = width // 2, w_out.shape[2] // 2, cols // 3
    ins = [
        (w_qkv, pl.BlockSpec((None, 1, rows, cols), lambda t, s: (layer, t, s[CORE], 0))),
        (w_out, pl.BlockSpec((None, deep, wide), lambda t, s: (layer, t, s[CORE]))),
    ]
    out = (
        pl.BlockSpec((1, rows + deep, cols), lambda t, s: (t, 0, 0)),
        shape((3, rows + deep, cols), bf16),
    )
    return ins, out


def pick_weights(spot, w_qkv):
    _, _, width, cols = w_qkv.shape
    rows = width // 2
    return launch(
        copy_kernel, "pick_weights", spot, (),
        [(w_qkv, pl.BlockSpec((None, 1, rows, cols), lambda t, s: (0, t, s[CORE], 0)))],
        [(pl.BlockSpec((1, rows, cols), lambda t, s: (t, 0, 0)), shape((3, rows, cols), bf16))],
        grid=(3,),
        us=3.0,
    )[0]


def relay(spot, array, w_out):
    _, cols, width = w_out.shape
    copies = relay_piece(array) + [
        (
            w_out,
            pl.BlockSpec((None, cols // 3, width), lambda t, s: (0, t, 0)),
            pl.BlockSpec((cols // 3, width), lambda t, s: (t, 0)),
            shape((cols, width), bf16),
        )
    ]
    return launch(
        copy_kernel, "relay", spot, (),
        [(a, source) for a, source, _, _ in copies],
        [(target, out) for _, _, target, out in copies],
        grid=(3,),
        us=2.5,
    )


def attn_fwd_kernel(pieces, relays, packs, spot_ref, a_ref, *refs):
    w_refs = refs[:pieces]
    b_ref, sq_ref, sk_ref = refs[pieces : pieces + 3]
    count = pieces + 3 + relays + 2 * packs
    sources = refs[pieces + 3 : count]
    q_ref, k_ref, v_ref, c_ref, lse_ref = refs[count : count + 5]
    targets = refs[count + 5 :]
    for source, target in zip(sources[:relays], targets[:relays]):
        target[...] = source[...]
    if packs:
        pack_kernel(spot_ref, *sources[relays:], targets[relays])
    seq, width = a_ref.shape
    share = width // pieces
    both = value = None
    for piece, w_ref in enumerate(w_refs):
        if pieces == 1:
            act = a_ref[...]
        else:
            which = jnp.where(spot_ref[CORE] == 0, piece, 1 - piece)
            act = a_ref[:, pl.ds(pl.multiple_of(which * share, 128), share)]
        term = dot(act, jnp.concatenate([w_ref[0], w_ref[1]], axis=1))
        both = term if both is None else both + term
        term = dot(act, w_ref[2])
        value = term if value is None else value + term
    query = (both[:, :PAIR] + b_ref[0:1, :]).astype(bf16)
    key = both[:, PAIR:].astype(bf16)
    value = value + b_ref[1:2, :]
    value_t = value.T.astype(bf16)
    q_ref[...] = query
    k_ref[...] = key
    v_ref[...] = value.astype(bf16)
    key_ext = jnp.concatenate([key, sk_ref[...]], axis=1)
    parts = []
    ones = jnp.ones((16, seq), bf16)
    for head in range(2):
        query_ext = jnp.concatenate([query * head_mask(head, HEAD**-0.5), sq_ref[...]], axis=1)
        scores = dot(key_ext, query_ext, NT)
        top = jnp.max(scores, axis=0, keepdims=True)
        weights = jnp.exp(scores - top).astype(bf16)
        summed = dot(
            jnp.concatenate([value_t[head * HEAD : (head + 1) * HEAD], ones], axis=0), weights
        )
        total = summed[HEAD : HEAD + 1]
        parts.append(summed[:HEAD] * (1.0 / total))
        lse_ref[0, head : head + 1, :] = top + jnp.log(total)
    c_ref[...] = jnp.concatenate(parts, axis=0).T


def weight_specs(layer, weights):
    if len(weights) == 1:
        width = weights[0].shape[2]
        return [pl.BlockSpec((None, 3, width, PAIR), lambda t, s: (layer, 0, 0, t))]
    share = weights[0].shape[2]
    return [pl.BlockSpec((3, share, PAIR), lambda t, s: (0, 0, t))] * 2


def relay_piece(array):
    lead, *rest = array.shape
    spec = pl.BlockSpec((lead // 3, *rest), lambda t, s: (t,) + (0,) * len(rest))
    return [(array, spec, spec, shape(array.shape, array.dtype))]


def relay_row(rows):
    _, half, width = rows.shape
    wide = width // 3
    return [
        (
            rows,
            pl.BlockSpec((None, half, wide), lambda t, s: (1 - s[SIDE], 0, t)),
            pl.BlockSpec((half, wide), lambda t, s: (0, t)),
            shape((half, width), rows.dtype),
        )
    ]


def attn_fwd(spot, hold, layer, act, weights, bias, seg_q, seg_k, relays=(), pack=None):
    pack_ins, pack_out = pack if pack else ([], None)
    seq, width = act.shape
    cols = bias.shape[2]
    steps = cols // PAIR
    block = pl.BlockSpec((seq, PAIR), lambda t, s: (0, t))
    return launch(
        functools.partial(attn_fwd_kernel, len(weights), len(relays), 1 if pack else 0),
        "attn_fwd", spot, hold,
        [(act, whole(seq, width))]
        + list(zip(weights, weight_specs(layer, weights)))
        + [
            (bias, pl.BlockSpec((None, 2, PAIR), lambda t, s: (layer, 0, t))),
            (seg_q, whole(seq, PAIR)),
            (seg_k, whole(seq, PAIR)),
        ]
        + [(array, source) for array, source, _, _ in relays]
        + pack_ins,
        [
            (block, shape((seq, cols), bf16)),
            (block, shape((seq, cols), bf16)),
            (block, shape((seq, cols), bf16)),
            (block, shape((seq, cols), f32)),
            (pl.BlockSpec((1, 8, seq), lambda t, s: (t, 0, 0)), shape((steps, 8, seq), f32)),
        ]
        + [(target, out) for _, _, target, out in relays]
        + ([pack_out] if pack else []),
        grid=(steps,),
        us=8.0
    )


def norm_rows(entries):
    centred = entries - jnp.mean(entries, axis=-1, keepdims=True)
    spread = jnp.mean(centred * centred, axis=-1, keepdims=True)
    rate = lax.rsqrt(spread + EPS)
    return centred * rate, rate


def ff_fwd_kernel(
    layer, last, spot_ref, lim_ref, xt_ref, xb_ref, co_ref, ct_ref, wo_ref, wy_ref, wc_ref,
    vec_ref, gain_ref, up_ref, bup_ref, down_ref, *rest
):
    if last:
        gt_ref, gb_ref, *rest = rest
    cu_ref, hat1_ref, rate1_ref, g_ref, slope_ref, *rest = rest
    acc_ref = rest[-1]
    step = pl.program_id(0)
    half_seq, width = xt_ref.shape
    half = co_ref.shape[1]
    wide = width // 2
    rows = 256
    ctx_limit, ff_limit, act_limit = lim_ref[layer, 1], lim_ref[layer, 2], lim_ref[layer, 3]

    @pl.when(step == 0)
    def _():
        inv = 1.0 / ctx_limit
        cu_ref[:, :half] = (ctx_limit * jnp.tanh(co_ref[...] * inv)).astype(bf16)
        cu_ref[:, half:width] = (ctx_limit * jnp.tanh(ct_ref[...] * inv)).astype(bf16)
        acc_ref[...] = dot(cu_ref[:, :half], wo_ref[...])
        for piece, w_ref in enumerate((wy_ref, wc_ref)):
            which = jnp.where(spot_ref[CORE] == 0, piece, 1 - piece)
            at = pl.ds(pl.multiple_of(which * wide, 128), wide)
            acc_ref[:, at] += dot(cu_ref[:, half:width], w_ref[...].reshape(half, wide))

        for base, x_ref in ((0, xt_ref), (half_seq, xb_ref)):

            def body(i, carry, base=base, x_ref=x_ref):
                start = pl.multiple_of(i * rows, rows)
                at = pl.ds(base + start, rows)
                hat, rate = norm_rows(
                    x_ref[pl.ds(start, rows), :].astype(f32) + (acc_ref[at, :] + vec_ref[0:1, :])
                )
                hat1_ref[at, :] = hat
                rate1_ref[at, :] = jnp.broadcast_to(rate, (rows, 128))
                normed = hat * gain_ref[0:1, :] + vec_ref[1:2, :]
                bent = ff_limit * jnp.tanh(normed * (1.0 / ff_limit))
                cu_ref[at, width:] = bent.astype(bf16)
                acc_ref[at, :] = normed + vec_ref[2:3, :]
                return carry

            lax.fori_loop(0, half_seq // rows, body, 0)

    inv_act = 1.0 / act_limit
    chunk = up_ref.shape[1]
    sub = FF_SUB
    for part in range(chunk // sub):
        cols = slice(part * sub, (part + 1) * sub)
        pre = dot(cu_ref[:, width:], up_ref[:, cols]) + bup_ref[layer : layer + 1, cols]
        cdf = 0.5 * lax.erf(pre * INV_SQRT2) + 0.5
        pdf = jnp.exp(pre * pre * -0.5) * INV_SQRT2PI
        bent = jnp.tanh(pre * cdf * inv_act)
        g_ref[:, cols] = (act_limit * bent).astype(bf16)
        slope_ref[:, cols] = ((1.0 - bent * bent) * (cdf + pre * pdf)).astype(bf16)
    acc_ref[...] += dot(g_ref[...], down_ref[...])

    @pl.when(step == pl.num_programs(0) - 1)
    def _():
        if last:
            top_ref, bottom_ref, de_ref, df_ref, sums_ref = rest[:-1]
            sums = norm_sums(width)
            for base, out_ref, in_ref in ((0, top_ref, gt_ref), (half_seq, bottom_ref, gb_ref)):

                def body(i, carry, base=base, out_ref=out_ref, in_ref=in_ref):
                    here = pl.ds(pl.multiple_of(i * rows, rows), rows)
                    at = pl.ds(base + pl.multiple_of(i * rows, rows), rows)
                    hat, rate = norm_rows(acc_ref[at, :])
                    new = hat * gain_ref[1:2, :] + vec_ref[3:4, :]
                    out_ref[here, :] = new.astype(bf16)
                    grad = in_ref[here, :].astype(f32)
                    return leave_norm(grad, hat, rate, gain_ref, at, de_ref, df_ref, carry)

                sums = lax.fori_loop(0, half_seq // rows, body, sums)
            store_sums(sums, sums_ref)
        else:
            hat2_ref, rate2_ref, new_ref, act_ref = rest[:-1]
            limit = lim_ref[layer + 1, 0]

            def body(i, carry):
                at = pl.ds(pl.multiple_of(i * rows, rows), rows)
                hat, rate = norm_rows(acc_ref[at, :])
                hat2_ref[at, :] = hat
                rate2_ref[at, :] = jnp.broadcast_to(rate, (rows, 128))
                new = hat * gain_ref[1:2, :] + vec_ref[3:4, :]
                new_ref[at, :] = new
                act_ref[at, :] = (limit * jnp.tanh(new * (1.0 / limit))).astype(bf16)
                return carry

            lax.fori_loop(0, 2 * half_seq // rows, body, 0)


def norm_back(grad, hat, rate, gain):
    scaled = grad * gain
    mean = jnp.mean(scaled, axis=-1, keepdims=True)
    lean = jnp.mean(scaled * hat, axis=-1, keepdims=True)
    return rate * (scaled - mean - hat * lean)


def norm_sums(width):
    return (jnp.zeros((1, width), f32),) * 3


def leave_norm(grad, hat, rate, gain_ref, at, de_ref, df_ref, sums):
    de = norm_back(grad, hat, rate, gain_ref[1:2, :])
    df = de.astype(bf16)
    de_ref[at, :] = de
    df_ref[at, :] = df
    return (
        sums[0] + jnp.sum(df.astype(f32), axis=0, keepdims=True),
        sums[1] + jnp.sum(grad, axis=0, keepdims=True),
        sums[2] + jnp.sum(grad * hat, axis=0, keepdims=True),
    )


def store_sums(sums, sums_ref):
    sums_ref[...] = jnp.zeros_like(sums_ref)
    sums_ref[2:3, :] = sums[0]
    sums_ref[3:4, :] = sums[1]
    sums_ref[5:6, :] = sums[2]


def norm_outs(seq, width):
    return [
        (whole(seq, width), shape((seq, width), f32)),
        (whole(seq, width), shape((seq, width), bf16)),
        (whole(8, width), shape((8, width), f32)),
    ]


def out_shares(pieces, half, width):
    if len(pieces) == 2:
        spec = pl.BlockSpec((3, half // 3, width // 2), lambda *_: (0, 3, 0))
        return [(piece, spec) for piece in pieces]
    return [
        (pieces[0], pl.BlockSpec((half, width // 2), lambda t, s: (0, s[CORE]))),
        (pieces[0], pl.BlockSpec((half, width // 2), lambda t, s: (0, 1 - s[CORE]))),
    ]


def halves(pair, half, width):
    if len(pair) == 1:
        return [
            (pair[0], pl.BlockSpec((half, width), lambda *_: (0, 0))),
            (pair[0], pl.BlockSpec((half, width), lambda *_: (1, 0))),
        ]
    first = my_row(half, width) if pair[0].ndim == 3 else whole(half, width)
    return [(pair[0], first), (pair[1], whole(half, width))]


def ff_fwd(
    spot, hold, layer, last, limits, x, ctx_own, ctx_oth, w_out, wo_oth, vec, gain, w_up, b_up,
    w_down, cot=None
):
    seq, half = ctx_own.shape
    width, hidden = w_up.shape[1:]
    chunk = FF_CHUNK
    steps = hidden // chunk
    tile = pl.BlockSpec((seq, chunk), lambda t, s: (0, t))
    full = whole(seq, width)
    early = [
        (shape((seq, 2 * width), bf16), 0),
        (shape((seq, width), f32), 0),
        (shape((seq, 128), f32), 0),
    ]
    outs = [
        (tile, shape((seq, hidden), bf16)),
        (tile, shape((seq, hidden), bf16)),
    ]
    if last:
        outs += [(whole(seq // 2, width), shape((seq // 2, width), bf16))] * 2
        outs += norm_outs(seq, width)
    else:
        outs += [
            (full, shape((seq, width), f32)),
            (whole(seq, 128), shape((seq, 128), f32)),
            (full, shape((seq, width), f32)),
            (full, shape((seq, width), bf16)),
        ]
    return launch(
        functools.partial(ff_fwd_kernel, layer, last), "ff_fwd", spot, hold,
        [(limits, smem())]
        + halves(x, seq // 2, width)
        + [
            (ctx_own, whole(seq, half)),
            (ctx_oth, whole(seq, half)),
            (w_out, at_layer(layer, half, width)),
            *out_shares(wo_oth, half, width),
            (vec, at_layer(layer, *vec.shape[1:])),
            (gain, at_layer(layer, *gain.shape[1:])),
            (w_up, pl.BlockSpec((None, width, chunk), lambda t, s: (layer, 0, t))),
            (b_up, pl.BlockSpec((b_up.shape[0], chunk), lambda t, s: (0, t))),
            (w_down, pl.BlockSpec((None, chunk, width), lambda t, s: (layer, t, 0))),
        ]
        + (halves(cot, seq // 2, width) if last else []),
        outs,
        early=early,
        scratch=[pltpu.VMEM((seq, width), f32)],
        grid=(steps,),
        us=21.0
    )


def ff_bwd_kernel(
    layer, spot_ref, lim_ref, fin_ref, vec_ref, gain_ref, slope_ref, up_ref, down_ref, wy_ref,
    wc_ref, de_ref, hat1_ref, rate1_ref, wo_ref, co_ref, ct_ref,
    zk_ref, ok_ref, os_ref, dy_ref, dco_ref, dct_ref, small_ref, bup_ref,
    do_ref, du_ref, dz_ref,
):
    step = pl.program_id(0)
    steps = pl.num_programs(0)
    seq, width = de_ref.shape
    half = width // 2
    rows = 256
    core = spot_ref[CORE]
    mine = pl.ds(pl.multiple_of(core * half, 128), half)
    other = pl.ds(pl.multiple_of((1 - core) * half, 128), half)
    zero = jnp.zeros((1, width), f32)
    ctx_limit, ff_limit = lim_ref[layer, 1], lim_ref[layer, 2]

    chunk = up_ref.shape[1]
    sub = FF_SUB
    for part in range(chunk // sub):
        cols = slice(part * sub, (part + 1) * sub)
        dz = dot(fin_ref[...], down_ref[cols, :], NT) * slope_ref[:, cols].astype(f32)
        low = dz.astype(bf16)
        bup_ref[:, cols] = jnp.sum(low.astype(f32), axis=0, keepdims=True)
        dz_ref[:, cols] = low
    term = dot(dz_ref[...], up_ref[...], NT)

    @pl.when(step == 0)
    def _():
        du_ref[...] = term

    @pl.when(step > 0)
    def _():
        du_ref[...] += term

    @pl.when(step < steps // 2)
    def _():
        zk_ref[:, pl.ds(pl.multiple_of(step * chunk, 128), chunk)] = dz_ref[...]

    @pl.when(step == steps - 1)
    def _():
        def body(i, carry):
            gain_sum, shift_sum, out_sum = carry
            at = pl.ds(pl.multiple_of(i * rows, rows), rows)
            hat = hat1_ref[at, :]
            normed = hat * gain_ref[0:1, :] + vec_ref[1:2, :]
            bent = jnp.tanh(normed * (1.0 / ff_limit))
            grad = de_ref[at, :] + du_ref[at, :] * (1.0 - bent * bent)
            dy = norm_back(grad, hat, rate1_ref[at, 0:1], gain_ref[0:1, :])
            low = dy.astype(bf16)
            dy_ref[at, :] = dy
            do_ref[at, :] = low
            return (
                gain_sum + jnp.sum(grad * hat, axis=0, keepdims=True),
                shift_sum + jnp.sum(grad, axis=0, keepdims=True),
                out_sum + jnp.sum(low.astype(f32), axis=0, keepdims=True),
            )

        sums = lax.fori_loop(0, seq // rows, body, (zero, zero, zero))
        small_ref[...] = jnp.zeros_like(small_ref)
        small_ref[0:1, :] = sums[2]
        small_ref[1:2, :] = sums[1]
        small_ref[4:5, :] = sums[0]
        ok_ref[...] = do_ref[:, mine]
        os_ref[...] = do_ref[:, other]
        inv = 1.0 / ctx_limit
        bent = jnp.tanh(co_ref[...] * inv)
        dco_ref[...] = (dot(do_ref[...], wo_ref[...], NT) * (1.0 - bent * bent)).astype(bf16)
        bent = jnp.tanh(ct_ref[...] * inv)
        grad = dot(do_ref[:, mine], wy_ref[...].reshape(half, half), NT)
        grad += dot(do_ref[:, other], wc_ref[...].reshape(half, half), NT)
        dct_ref[...] = (grad * (1.0 - bent * bent)).astype(bf16)


def ff_bwd(
    spot, hold, layer, limits, de, df, hat1, rate1, vec, gain, slope, w_up, w_down, w_out,
    wo_oth, ctx_own, ctx_oth,
):
    seq, half = ctx_own.shape
    width, hidden = w_up.shape[1:]
    chunk = FF_CHUNK
    steps = hidden // chunk
    span = steps // 2

    def place(t, s):
        return jnp.where(t < span, s[CORE] * span + t, (1 - s[CORE]) * span + t - span)

    full = whole(seq, width)
    part = whole(seq, width // 2)
    outs = [
        (part, shape((seq, width // 2), bf16)),
        (part, shape((seq, width // 2), bf16)),
        (full, shape((seq, width), f32)),
        (whole(seq, half), shape((seq, half), bf16)),
        (whole(seq, half), shape((seq, half), bf16)),
        (whole(8, width), shape((8, width), f32)),
        (pl.BlockSpec((1, chunk), lambda t, s: (0, place(t, s))), shape((1, hidden), f32)),
    ]
    return launch(
        functools.partial(ff_bwd_kernel, layer), "ff_bwd", spot, hold,
        [(limits, smem())]
        + [
            (df, full),
            (vec, at_layer(layer, *vec.shape[1:])),
            (gain, at_layer(layer, *gain.shape[1:])),
            (slope, pl.BlockSpec((seq, chunk), lambda t, s: (0, place(t, s)))),
            (w_up, pl.BlockSpec((None, width, chunk), lambda t, s: (layer, 0, place(t, s)))),
            (w_down, pl.BlockSpec((None, chunk, width), lambda t, s: (layer, place(t, s), 0))),
            *out_shares(wo_oth, half, width),
        ],
        outs,
        late=[
            (de, None),
            (hat1, None),
            (rate1, None),
            (w_out, layer),
            (ctx_own, None),
            (ctx_oth, None),
        ],
        early=[(shape((seq, hidden // 2), bf16), span - 1)],
        scratch=[
            pltpu.VMEM((seq, width), bf16),
            pltpu.VMEM((seq, width), f32),
            pltpu.VMEM((seq, chunk), bf16),
        ],
        grid=(steps,),
        us=20.0
    )


def attn_bwd_half(q_ref, k_ref, v_ref, c_ref, lse_ref, dc_ref, seg_q, seg_k):
    query, key, value, grad = q_ref[...], k_ref[...], v_ref[...], dc_ref[...]
    key_ext = jnp.concatenate([key, seg_k], axis=1)
    key_t = key.astype(f32).T.astype(bf16)
    product_t = (grad.astype(f32) * c_ref[...]).T
    d_key = d_value = None
    d_query_t = []
    for head in range(2):
        scaled = query * head_mask(head, HEAD**-0.5)
        scores = dot(key_ext, jnp.concatenate([scaled, seg_q], axis=1), NT)
        probs = jnp.exp(scores - lse_ref[0, head : head + 1, :])
        grad_head = grad * head_mask(head, 1.0)
        d_probs = dot(value, grad_head, NT)
        delta = jnp.sum(product_t[head * HEAD : (head + 1) * HEAD], axis=0, keepdims=True)
        d_scores = (probs * (d_probs - delta)).astype(bf16)
        term_v = dot(probs.astype(bf16), grad_head)
        term_k = dot(d_scores, scaled)
        d_value = term_v if d_value is None else d_value + term_v
        d_key = term_k if d_key is None else d_key + term_k
        d_query_t.append(dot(key_t[head * HEAD : (head + 1) * HEAD], d_scores))
    d_query = jnp.concatenate(d_query_t, axis=0).T * HEAD**-0.5
    return d_query.astype(bf16), d_key.astype(bf16), d_value.astype(bf16)


def attn_bwd_kernel(
    layer, spot_ref, lim_ref, sq_ref, sk_ref,
    qo_ref, ko_ref, vo_ref, co_ref, lo_ref, dco_ref,
    qt_ref, kt_ref, vt_ref, ct_ref, lt_ref, dct_ref, wo_ref, wy_ref, wc_ref, *rest
):
    if layer:
        gain_ref, dy_ref, x_ref, hat_ref, rate_ref, *rest = rest
    else:
        xt_ref, xb_ref, dy_ref, *rest = rest
    dqo_ref, dko_ref, dvo_ref, dqt_ref, dkt_ref, dvt_ref, bo_ref, bt_ref, *rest = rest
    acc_ref = rest[-1]
    step = pl.program_id(0)
    seq, width = dy_ref.shape
    half_seq, share = seq // 2, width // 2
    rows = 128
    own = attn_bwd_half(qo_ref, ko_ref, vo_ref, co_ref, lo_ref, dco_ref, sq_ref[...], sk_ref[...])
    oth = attn_bwd_half(qt_ref, kt_ref, vt_ref, ct_ref, lt_ref, dct_ref, sq_ref[...], sk_ref[...])
    dqo_ref[...], dko_ref[...], dvo_ref[...] = own
    dqt_ref[...], dkt_ref[...], dvt_ref[...] = oth
    for out_ref, grads in ((bo_ref, own), (bt_ref, oth)):
        out_ref[0:1, :] = jnp.sum(grads[0].astype(f32), axis=0, keepdims=True)
        out_ref[1:2, :] = jnp.sum(grads[2].astype(f32), axis=0, keepdims=True)
        out_ref[2:8, :] = jnp.zeros((6, PAIR), f32)
    joined = [jnp.concatenate([own[k], oth[k]], axis=1) for k in range(3)]
    for piece, w_ref in enumerate((wy_ref, wc_ref)):
        which = jnp.where(spot_ref[CORE] == 0, piece, 1 - piece)
        at = pl.ds(pl.multiple_of(which * share, 128), share)
        total = None
        for k in range(3):
            term = dot(joined[k], jnp.concatenate([wo_ref[k, at, :], w_ref[k]], axis=1), NT)
            total = term if total is None else total + term

        @pl.when(step == 0)
        def _():
            acc_ref[:, at] = total

        @pl.when(step > 0)
        def _():
            acc_ref[:, at] += total

    @pl.when(step == pl.num_programs(0) - 1)
    def _():
        inv = 1.0 / lim_ref[layer, 0]
        sums = norm_sums(width)
        for part in range(2):

            def body(i, carry, part=part):
                here = pl.ds(pl.multiple_of(i * rows, rows), rows)
                at = pl.ds(part * half_seq + pl.multiple_of(i * rows, rows), rows)
                value = x_ref[at, :] if layer else (xt_ref, xb_ref)[part][here, :]
                bent = jnp.tanh(value.astype(f32) * inv)
                grad = dy_ref[at, :] + acc_ref[at, :] * (1.0 - bent * bent)
                if layer:
                    return leave_norm(
                        grad, hat_ref[at, :], rate_ref[at, 0:1], gain_ref, at, rest[0], rest[1],
                        carry,
                    )
                rest[part][here, :] = grad.astype(rest[part].dtype)
                return carry

            sums = lax.fori_loop(0, half_seq // rows, body, sums)
        if layer:
            store_sums(sums, rest[2])


def attn_bwd(spot, hold, layer, limits, x, dy, seg_q, seg_k, own, oth, w_qkv, wq_oth, below=()):
    seq, width = dy.shape
    cols = own[0].shape[1]
    steps = cols // PAIR
    block = pl.BlockSpec((seq, PAIR), lambda t, s: (0, t))
    half_specs = [
        block,
        block,
        block,
        block,
        pl.BlockSpec((1, 8, seq), lambda t, s: (t, 0, 0)),
        block,
    ]
    return launch(
        functools.partial(attn_bwd_kernel, layer), "attn_bwd", spot, hold,
        [(limits, smem())]
        + [(seg_q, whole(seq, PAIR)), (seg_k, whole(seq, PAIR))]
        + list(zip(own, half_specs))
        + list(zip(oth, half_specs))
        + list(zip((w_qkv,), weight_specs(layer, (w_qkv,))))
        + list(zip(wq_oth, weight_specs(layer, wq_oth)))
        + (
            [(below[2], at_layer(layer - 1, *below[2].shape[1:]))]
            if layer
            else halves(x, seq // 2, width)
        ),
        [(block, shape((seq, cols), bf16))] * 6
        + [(pl.BlockSpec((8, PAIR), lambda t, s: (0, t)), shape((8, cols), f32))] * 2
        + (
            norm_outs(seq, width)
            if layer
            else [
                (whole(seq // 2, width), shape((seq // 2, width), f32)),
                (whole(seq // 2, width), shape((seq // 2, width), bf16)),
            ]
        ),
        late=[(dy, None)]
        + ([(x[0], None), (below[0], None), (below[1], None)] if layer else []),
        scratch=[pltpu.VMEM((seq, width), f32)],
        grid=(steps,),
        us=18.5
    )


FF_ORDERS = (
    (AXIS_X, SIDE, AXIS_Z0, AXIS_Z1),
    (SIDE, AXIS_Z0, AXIS_X, AXIS_Z1),
    (AXIS_Z0, AXIS_X, SIDE, AXIS_Z1),
)
FF_ROWS = (144, 128, 112)
ATT_ORDERS = (
    (AXIS_X, SIDE, AXIS_Z0, AXIS_Z1),
    (AXIS_Z0, SIDE, AXIS_X, AXIS_Z1),
)
FIRST_ATT_ORDERS = (
    (AXIS_X, SIDE, AXIS_Z0, AXIS_Z1),
    (AXIS_Z0, AXIS_X, SIDE, AXIS_Z1),
)
ATT_ROWS = (96, 96)
PIECE = 48


def block_of(spot_ref, order, rel):
    bit = {axis: (rel >> (3 - k)) & 1 for k, axis in enumerate(order)}
    chip = 0
    for axis in (AXIS_Z1, AXIS_Z0, AXIS_X):
        own = spot_ref[axis]
        chip = chip * 2 + (1 - own if bit[axis] else own)
    return bit[SIDE], chip


def w_ff_kernel(
    spot_ref, um_ref, uo_ref, zm_ref, so_ref, gm_ref, go_ref, fm_ref, fo_ref, down_ref, *rest
):
    outs, ut_ref, half_ref, all_ref = rest[:-3], rest[-3], rest[-2], rest[-1]
    step = pl.program_id(0)
    sides, chips, tall, lanes = all_ref.shape
    seq, width = um_ref.shape
    thin = width // chips

    @pl.when(step == 0)
    def _():
        ut_ref[:, :seq] = um_ref[...].T
        ut_ref[:, seq:] = uo_ref[...].T
        mine = pl.ds(pl.multiple_of(spot_ref[CORE] * lanes, 128), lanes)
        half_ref[0] = fm_ref[:, mine]
        half_ref[1] = fo_ref[:, mine]

    theirs = (dot(fo_ref[...], down_ref[...], NT) * so_ref[...].astype(f32)).astype(bf16)
    grad_up = dot(ut_ref[:, :seq], zm_ref[...]) + dot(ut_ref[:, seq:], theirs)
    grad_up = grad_up.astype(bf16)
    for chip in range(chips):
        at = pl.ds(pl.multiple_of((step % 2) * thin, 16), thin)
        all_ref[step // 2, chip, at, :] = grad_up[chip * thin : (chip + 1) * thin]
    base = 2 * thin
    deep = tall - base
    per = gm_ref.shape[1] // (2 * deep)
    for part in range(per):
        cols = slice(part * 2 * deep, (part + 1) * 2 * deep)
        grad_down = dot(gm_ref[:, cols], half_ref[0], TN) + dot(go_ref[:, cols], half_ref[1], TN)
        grad_down = grad_down.astype(bf16)
        for side in range(2):
            all_ref[side, step * per + part, base:, :] = grad_down[side * deep : (side + 1) * deep]

    @pl.when(step == pl.num_programs(0) - 1)
    def _():
        start = 0
        for part, (order, count) in enumerate(zip(FF_ORDERS, FF_ROWS)):
            for rel in range(16):
                side, chip = block_of(spot_ref, order, rel)
                side = 1 - spot_ref[SIDE] if side else spot_ref[SIDE]
                value = all_ref[side, chip, start : start + count, :]
                if rel < 8:
                    outs[2 * part][rel] = value
                else:
                    outs[2 * part + 1][(rel - 8) * count : (rel - 7) * count, :] = value
            start += count


def w_ff(
    spot, hold, layer, cu_mine, cu_core, dz_mine, slope_core, g_mine, g_core, df_mine, df_core,
    w_down
):
    seq, width = df_mine.shape
    lanes, hidden = width // 2, g_mine.shape[1]
    steps = dz_mine.shape[1] // lanes
    tall = hidden // 8
    g_block = pl.BlockSpec((seq, hidden // steps), lambda t, s: (0, t))
    u_block = pl.BlockSpec((seq, width), lambda *_: (0, 1))
    outs = []
    for rows in FF_ROWS:
        outs.append((whole(8, rows, lanes), shape((8, rows, lanes), bf16)))
        outs.append((whole(8 * rows, lanes), shape((8 * rows, lanes), bf16)))
    return launch(
        w_ff_kernel, "w_ff", spot, hold,
        [
            (cu_mine, u_block),
            (cu_core, u_block),
            (dz_mine, pl.BlockSpec((seq, lanes), lambda t, s: (0, t))),
            (slope_core, pl.BlockSpec((seq, lanes), lambda t, s: (0, s[CORE] * steps + t))),
            (g_mine, g_block),
            (g_core, g_block),
            (df_mine, whole(seq, width)),
            (df_core, whole(seq, width)),
            (
                w_down,
                pl.BlockSpec(
                    (None, lanes, width), lambda t, s: (layer, s[CORE] * steps + t, 0)
                ),
            ),
        ],
        outs,
        scratch=[
            pltpu.VMEM((width, 2 * seq), bf16),
            pltpu.VMEM((2, seq, lanes), bf16),
            pltpu.VMEM((2, 8, tall, lanes), bf16),
        ],
        grid=(steps,),
        us=13.5,
    )


def w_att_kernel(
    spot_ref, a_ref, dqo_ref, dko_ref, dvo_ref, dqt_ref, dkt_ref, dvt_ref,
    cm_ref, cc_ref, dom_ref, doc_ref, keep_ref, out_ref, *rest
):
    send_refs, at_ref, spare_ref = rest[:-2], rest[-2], rest[-1]
    width = a_ref.shape[1]
    _, chips, tall, cols = keep_ref.shape
    core = spot_ref[CORE]
    piece = PIECE
    per = tall // piece
    at_ref[...] = a_ref[...].T
    sides = ((dqo_ref, dko_ref, dvo_ref), (dqt_ref, dkt_ref, dvt_ref))
    for side, grads in enumerate(sides):
        for which in range(3):
            result = dot(at_ref[...], grads[which][...]).astype(bf16)
            for j in range(width // piece):
                index = which * (width // piece) + j
                block, sub = index // per, index % per
                spare_ref[block % 2, block // 2, sub * piece : (sub + 1) * piece, :] = result[
                    j * piece : (j + 1) * piece
                ]
        keep_ref[side] = spare_ref[core]
        for k, send_ref in enumerate(send_refs):
            send_ref[side] = spare_ref[1 - core, :, k * piece : (k + 1) * piece, :]
    half = width // 2
    heads = half // HEAD
    for side in range(2):
        at = slice(side * half, (side + 1) * half)
        result = dot(cm_ref[:, at], dom_ref[...], TN) + dot(cc_ref[:, at], doc_ref[...], TN)
        for chip in range(chips):
            for pair in range(heads // 2):
                first = (2 * pair) * HEAD + 8 * chip
                second = first + HEAD
                out_ref[side, chip, pair * 16 : (pair + 1) * 16, :] = jnp.concatenate(
                    [result[first : first + 8], result[second : second + 8]], axis=0
                ).astype(bf16)


def w_att(spot, hold, act, d_own, d_oth, cu_mine, cu_core, do_mine, do_core):
    seq, width = act.shape
    cols = width // 2
    chips = 8
    tall = 3 * width // (2 * chips)
    outs = [
        shape((2, chips, tall, cols), bf16),
        shape((2, chips, cols // chips, cols), bf16),
        *[shape((2, chips, PIECE, cols), bf16)] * (tall // PIECE),
    ]
    cq_block = pl.BlockSpec((seq, width), lambda *_: (0, 0))
    return launch(
        w_att_kernel, "w_att", spot, hold,
        [(array, whole(*array.shape)) for array in (act, *d_own, *d_oth)]
        + [
            (cu_mine, cq_block),
            (cu_core, cq_block),
            (do_mine, whole(seq, cols)),
            (do_core, whole(seq, cols)),
        ],
        [(whole(*out.shape), out) for out in outs],
        scratch=[pltpu.VMEM((width, seq), bf16), pltpu.VMEM((2, chips, tall, cols), bf16)],
        us=8.0,
    )


class Part:
    def __init__(self, kind, order, kept):
        self.kind, self.order, self.kept = kind, order, kept
        self.stage = 0
        self.array = self.start = None
        self.final = None

    def arrives(self, array, start):
        self.array, self.start = array, start


def pack_small(spot_ref, small_refs, out_ref):
    for layer in range(len(small_refs) // 5):
        bo_ref, bt_ref, vec_ref, sums_ref, up_ref = small_refs[5 * layer : 5 * layer + 5]
        half = bo_ref.shape[1]
        width = 2 * half
        side = spot_ref[SIDE]
        mine = pl.ds(pl.multiple_of(side * half, 128), half)
        other = pl.ds(pl.multiple_of((1 - side) * half, 128), half)
        out_ref[layer, 0:2, mine] = bo_ref[0:2, :]
        out_ref[layer, 0:2, other] = bt_ref[0:2, :]
        out_ref[layer, 2:8, :] = vec_ref[0:6, :] + sums_ref[0:6, :]
        for k in range(up_ref.shape[1] // width):
            out_ref[layer, 8 + k : 9 + k, :] = up_ref[:, k * width : (k + 1) * width]


def exchange(spot, over_axis, parts, att=None, smalls=(), pair=None, carry=None, hold=()):
    ins, outs, steps = [], [], []

    def take(array):
        for k, (known, _) in enumerate(ins):
            if known is array:
                return k
        ins.append((array, whole(*array.shape)))
        return len(ins) - 1

    def give(dims, dtype=bf16):
        outs.append((whole(*dims), shape(dims, dtype)))
        return len(outs) - 1

    lanes = (parts[0].kept if parts else att[0]).shape[-1]
    sends = {}

    def room(axis, rows):
        start = sends.get(axis, 0)
        sends[axis] = start + rows
        return start

    new_parts, places = [], []
    parts = sorted(parts, key=lambda part: (part.kind != "ff", part.kept.shape[0]))
    for part in parts:
        blocks, rows, _ = part.kept.shape
        source = take(part.kept), take(part.array), part.start
        if blocks > 1:
            axis = part.order[part.stage + 1]
            start = room(axis, blocks // 2 * rows)
            steps.append(("halve", source, give((blocks // 2, rows, lanes)), axis, start))
        elif part.kind == "ff":
            axis = SIDE
            start = room(axis, rows)
            steps.append(("end", source, give((rows, lanes), f32), axis, start))
        else:
            axis = None
            start = 0
            steps.append(("end", source, give((rows, lanes), f32), None, 0))
        places.append((part, axis, start))
    if att is not None:
        source = [take(array) for array in att]
        begin = 0
        for order, rows in zip(FIRST_ATT_ORDERS if smalls else ATT_ORDERS, ATT_ROWS):
            start = room(order[0], 8 * rows)
            kept = give((8, rows, lanes))
            steps.append(("enter", source, kept, order[0], start, order, begin, rows))
            places.append((Part("att", order, None), order[0], start))
            begin += rows
    small_out = None
    if smalls:
        source = [take(array) for small in smalls for array in small]
        width = smalls[0][2].shape[1]
        small_out = give((len(smalls), 8 + smalls[0][4].shape[1] // width, width), f32)
        steps.append(("pack", source, small_out))
    if pair is not None:
        small_out = give(pair[0].shape, f32)
        steps.append(("sum", [take(array) for array in pair], small_out))
    if carry is not None:
        small_out = give(carry.shape, carry.dtype)
        steps.append(("copy", [take(carry)], small_out))
    send_at = {axis: give((rows, lanes)) for axis, rows in sends.items()}

    def body(spot_ref, *refs):
        in_refs, out_refs = refs[: len(ins)], refs[len(ins) :]
        for what, source, out, *more in steps:
            out_ref = out_refs[out]
            if what == "halve":
                axis, start = more
                kept, got = in_refs[source[0]], in_refs[source[1]]
                base = source[2]
                half, rows, _ = out_ref.shape
                send = out_refs[send_at[axis]]
                for j in range(half):
                    at = base + j * rows
                    out_ref[j] = kept[j] + got[at : at + rows, :]
                    at += half * rows
                    send[start + j * rows : start + (j + 1) * rows, :] = (
                        kept[half + j] + got[at : at + rows, :]
                    )
            elif what == "end":
                axis, start = more
                kept, got = in_refs[source[0]], in_refs[source[1]]
                base = source[2]
                rows = out_ref.shape[0]
                total = kept[0].astype(f32) + got[base : base + rows, :].astype(f32)
                out_ref[...] = total
                if axis is not None:
                    out_refs[send_at[axis]][start : start + rows, :] = total.astype(bf16)
            elif what == "enter":
                axis, start, order, begin, rows = more
                keep, outer, *got = (in_refs[k] for k in source)
                send = out_refs[send_at[axis]]
                for rel in range(16):
                    side, chip = block_of(spot_ref, order, rel)
                    for k in range(begin // PIECE, (begin + rows) // PIECE):
                        if k < len(got):
                            at = slice(k * PIECE, (k + 1) * PIECE)
                            value = keep[side, chip, at, :] + got[k][side, chip]
                        else:
                            value = outer[side, chip]
                        done = k * PIECE - begin
                        if rel < 8:
                            out_ref[rel, done : done + PIECE, :] = value
                        else:
                            at = start + (rel - 8) * rows + done
                            send[at : at + PIECE, :] = value
            elif what == "copy":
                out_ref[...] = in_refs[source[0]][...]
            elif what == "pack":
                pack_small(spot_ref, [in_refs[k] for k in source], out_ref)
            else:
                out_ref[...] = in_refs[source[0]][...] + in_refs[source[1]][...]

    results = launch(body, "exchange", spot, hold, ins, outs, us=5.0)
    arrived = {axis: over_axis(results[k], axis) for axis, k in send_at.items()}
    kept_at = [step[2] for step in steps]
    for (part, axis, start), what, out in zip(places, [step[0] for step in steps], kept_at):
        if what == "end":
            part.final = results[out]
        else:
            part.kept = results[out]
        if what != "enter":
            part.stage += 1
        if axis is not None:
            part.arrives(arrived[axis], start)
        new_parts.append(part)
    return new_parts, (None if small_out is None else results[small_out])


def finish_kernel(layers, spot_ref, *refs):
    core, side = spot_ref[CORE], spot_ref[SIDE]
    count = len(FF_ROWS) + 1
    both_ref = refs[-1]
    for layer in range(layers):
        *part_refs, got_ref = refs[count * layer : count * (layer + 1)]
        keep_ref, send_ref = refs[count * layers + 2 * layer : count * layers + 2 * layer + 2]
        start = 0
        for ref in part_refs:
            both_ref[side, start : start + ref.shape[0], :] = ref[...]
            start += ref.shape[0]
        both_ref[1 - side] = got_ref[...].astype(f32)
        half = both_ref.shape[1] // 2
        quarter = half // 4
        for out_ref, which in ((keep_ref, core), (send_ref, 1 - core)):
            for k in range(4):
                at = pl.ds(pl.multiple_of((k % 2) * 2 * quarter + which * quarter, 16), quarter)
                out_ref[k * quarter : (k + 1) * quarter, :] = both_ref[k // 2, at, :].astype(
                    out_ref.dtype
                )
            out_ref[half:, :] = both_ref[which, half:, :].astype(out_ref.dtype)


def finish_ff(spot, groups):
    rows = sum(FF_ROWS)
    ins, outs = [], []
    for parts in groups:
        lanes = parts[0].final.shape[1]
        block = parts[0].start // rows
        assert parts[0].start == block * rows
        ins += [(part.final, whole(*part.final.shape)) for part in parts]
        ins.append(
            (parts[0].array, pl.BlockSpec((rows, lanes), lambda *_, block=block: (block, 0)))
        )
        outs.append((whole(rows, lanes), shape((rows, lanes), f32)))
        outs.append((whole(rows, lanes), shape((rows, lanes), bf16)))
    results = launch(
        functools.partial(finish_kernel, len(groups)), "finish_ff", spot, (), ins, outs,
        scratch=[pltpu.VMEM((2, rows, lanes), f32)],
    )
    return [results[2 * k : 2 * k + 2] for k in range(len(groups))]


def assemble_kernel(layers, spot_ref, *refs):
    up_ref, down_ref = refs[-2:]
    core = spot_ref[CORE]
    for layer in range(layers):
        keep, got = refs[2 * layer][...], refs[2 * layer + 1][...].astype(f32)
        lanes = keep.shape[1]
        half = keep.shape[0] // 2
        quarter = half // 4
        tiles = lanes // 128
        for side in range(2):
            value = jnp.where(core == side, keep, got)
            for t in range(tiles):
                cols = slice(t * 128, (t + 1) * 128)
                for k in range(4):
                    start = ((side * 4 + k) * tiles + t) * layers + layer
                    up_ref[pl.ds(start, quarter, stride=8 * tiles * layers), :] = value[
                        k * quarter : (k + 1) * quarter, cols
                    ]
                start = (side * tiles + t) * layers + layer
                down_ref[pl.ds(start, half, stride=2 * tiles * layers), :] = value[half:, cols]


def assemble(spot, pairs):
    layers = len(pairs)
    rows, lanes = pairs[0][0].shape
    dims = (rows * lanes // 128 * layers, 128)
    return launch(
        functools.partial(assemble_kernel, layers), "assemble", spot, (),
        [(array, whole(*array.shape)) for pair in pairs for array in pair],
        [(whole(*dims), shape(dims, f32))] * 2,
        us=3.0,
    )


def local(
    hidden_in, cotangent, segment_ids, clip_ranges, w_qkv, bias_qv, w_out, vector_bias, ln_gain,
    w_up, bias_up, w_down,
):
    layers = w_qkv.shape[0]
    row_count, half_seq, width = hidden_in.shape
    seq = segment_ids.shape[1]
    cols = w_qkv.shape[3]
    heads = cols // HEAD
    hidden = w_up.shape[2]
    dp_count = lax.axis_size("dp")
    assert lax.axis_size("mp") == 2 and row_count == 2 and seq == 2 * half_seq
    bits = dp_count.bit_length() - 1
    assert dp_count == 1 << bits and bits >= 1
    chips = dp_count // 2
    side = lax.axis_index("mp")
    place = lax.axis_index("dp")
    core = place % 2
    spot = Spot(
        jnp.stack(
            [core, side, (place >> 1) & 1, (place >> 2) & 1, (place >> 3) & 1]
        ).astype(jnp.int32)
    )

    def over_mp(value):
        return lax.ppermute(value, "mp", [(0, 1), (1, 0)])

    def over_bit(value, bit):
        return lax.ppermute(value, "dp", [(i, i ^ (1 << bit)) for i in range(dp_count)])

    def over_core(value):
        return over_bit(value, 0)

    def over_axis(value, axis):
        return over_mp(value) if axis == SIDE else over_bit(value, axis - AXIS_X + 1)

    def pick(value, index, axis):
        return lax.dynamic_index_in_dim(value, index, axis, keepdims=False)

    def ordered(index, mine, theirs, axis):
        first = jnp.where(index == 0, mine, theirs)
        second = jnp.where(index == 0, theirs, mine)
        return jnp.concatenate([first, second], axis=axis)

    x = (hidden_in, over_mp(pick(hidden_in, 1 - side, 0)))
    bias_oth = over_mp(bias_qv)
    limits = clip_ranges.astype(f32)
    seg_row = pick(segment_ids, side, 0).reshape(2, half_seq)
    seg_row = jnp.concatenate([pick(seg_row, side, 0), pick(seg_row, 1 - side, 0)])
    same = seg_row[:, None] == jnp.arange(PAIR, dtype=seg_row.dtype)[None, :]
    seg_q = jnp.where(same, BIG, 0.0).astype(bf16)
    seg_k = jnp.where(same, 0.0, 1.0).astype(bf16)

    arrived = over_mp(pick_weights(spot, w_qkv))
    act = enter(spot, (bias_oth,), limits, hidden_in, x[1])
    fetched, wo_oth, stored = [], [], []
    shared = ()
    for layer in range(layers):
        last = layer == layers - 1
        relays = relay_piece(arrived) if layer else []
        if last:
            relays = relays + relay_row(cotangent)
        outs = attn_fwd(spot, (), layer, act, (w_qkv,), bias_qv, seg_q, seg_k, relays)
        own, copies = outs[:5], outs[5:]
        if last:
            cot = (cotangent, over_mp(copies[-1]))
        if layer:
            copy = copies[0]
        else:
            copy, out_share = relay(spot, arrived, w_out)
        fetched.append((arrived, over_core(copy)))
        wo_oth.append(fetched[layer] if layer else (over_mp(out_share),))
        outs = attn_fwd(
            spot, (), layer, act, fetched[layer], bias_oth, seg_q, seg_k,
            pack=None if last else pack_weights(layer + 1, w_qkv, w_out),
        )
        oth = outs[:5]
        if not last:
            arrived = over_mp(outs[5])
        outs = ff_fwd(
            spot, shared, layer, last, limits, x, own[3], oth[3], w_out, wo_oth[layer], vector_bias,
            ln_gain,
            w_up, bias_up, w_down, cot if last else None,
        )
        cu, hat1, rate1, g, slope = outs[:5]
        shared = over_core(cu), over_core(g), over_core(slope)
        norm = None
        if last:
            hidden_mine, hidden_send, *descent = outs[5:]
        else:
            norm = outs[5:7]
        stored.append((x, act, own, oth, cu, hat1, rate1, g, slope, norm, shared))
        if not last:
            x, act = (outs[7],), outs[8]
    hidden_recv = over_mp(hidden_send)

    fast = chips == 8 and width == 768 and hidden == 3072 and cols == 384

    smalls, groups = [], {}
    flying = []
    small = None
    df_core = over_core(descent[1])
    for layer in reversed(range(layers)):
        x, act, own, oth, cu, hat1, rate1, g, slope, norm, shared = stored[layer]
        de, df, sums = descent
        dz_keep, do_keep, do_send, dy, dc_own, dc_oth, vec, d_bup = ff_bwd(
            spot, (), layer, limits, de, df, hat1, rate1, vector_bias, ln_gain, slope, w_up,
            w_down, w_out, wo_oth[layer], own[3], oth[3],
        )
        if fast:
            do_core = over_core(do_send)
            if flying:
                flying, _ = exchange(spot, over_axis, flying, entering)
                groups["att", layer + 1] = flying[-len(ATT_ROWS) :]
            outs = w_ff(
                spot, (hidden_recv, do_core), layer, cu, shared[0], dz_keep, shared[2], g, shared[1], df, df_core,
                w_down,
            )
            parts_ff = []
            for k, order in enumerate(FF_ORDERS):
                parts_ff.append(Part("ff", order, outs[2 * k]))
                parts_ff[k].arrives(over_axis(outs[2 * k + 1], order[0]), 0)
            groups["ff", layer] = parts_ff
            if flying:
                exchange(spot, over_axis, flying)
            flying = flying + parts_ff
        below = (*stored[layer - 1][9], ln_gain) if layer else ()
        outs = attn_bwd(
            spot, (), layer, limits, x, dy, seg_q, seg_k, (*own, dc_own), (*oth, dc_oth), w_qkv,
            fetched[layer], below,
        )
        d_own, d_oth = outs[:3], outs[3:6]
        smalls.insert(0, (outs[6], outs[7], vec, sums, d_bup))
        descent = outs[8:]
        if fast:
            keep, out, *send = w_att(
                spot, (), act, d_own, d_oth, cu, shared[0], do_keep, do_core
            )
            entering = keep, out, *(over_core(piece) for piece in send)
            if layer:
                flying, df = exchange(spot, over_axis, flying, carry=descent[1])
                df_core = over_core(df)
            else:
                late = [part for part in flying if part.kind == "ff" and part.stage == 3]
                flying = [part for part in flying if part not in late]
                flying, small = exchange(
                    spot, over_axis, flying, entering, smalls,
                    hold=tuple({id(part.array): part.array for part in late}.values()),
                )
                groups["att", 0] = flying[-len(ATT_ROWS) :]
        else:
            dz = (dot(df, w_down[layer], NT) * slope.astype(f32)).astype(bf16)
            do = ordered(core, do_keep, do_send, 1)
            total = []
            for lhs, rhs in ((cu[:, width:], dz), (g, df)):
                grad = dot(lhs, rhs, TN).reshape(-1)
                grad = grad + over_mp(grad)
                total.append(lax.psum_scatter(grad, "dp", scatter_dimension=0, tiled=True))
            groups["ff", layer] = total
            sides = []
            for grads, part in ((d_own, cu[:, :cols]), (d_oth, cu[:, cols:width])):
                qkv = jnp.stack([dot(act, grad, TN) for grad in grads])
                qkv = qkv.reshape(3, width, heads, HEAD).transpose(2, 0, 1, 3)
                sides.append((qkv.reshape(heads, -1), dot(part, do, TN).reshape(heads, -1)))
            total = []
            for k in range(2):
                grad = sides[0][k] + over_mp(sides[1][k])
                total.append(lax.psum_scatter(grad, "dp", scatter_dimension=1, tiled=True))
            groups["att", layer] = total

    row_mine, row_send = descent
    if fast:
        axes = [AXIS_X, SIDE, AXIS_Z0, AXIS_Z1]
        pair = (small, over_axis(small, axes.pop(0)))
        turn = 0
        while True:
            if turn == 1:
                flying = flying + late
            flying = [part for part in flying if part.final is None]
            if not flying and turn > 1:
                break
            flying, summed = exchange(spot, over_axis, flying, pair=pair)
            small = small if summed is None else summed
            pair = (small, over_axis(small, axes.pop(0))) if axes else None
            if turn == 0:
                hidden_out = place_rows(spot, (), hidden_mine, hidden_recv, bf16)
            if turn == 2:
                grad_input = place_rows(spot, (), row_mine, over_mp(row_send), f32)
                done = finish_ff(spot, [groups["ff", k] for k in range(layers)])
                pairs = [(keep, over_core(send)) for keep, send in done]
            turn += 1
        while pair:
            small = pair[0] + pair[1]
            pair = (small, over_axis(small, axes.pop(0))) if axes else None
        small = small + over_core(small)
        up, down = assemble(spot, pairs)
        up, down = (
            flat.reshape(-1, layers, 128).transpose(1, 0, 2).reshape(layers, -1)
            for flat in (up, down)
        )
        qkvs, outs = [], []
        for layer in range(layers):
            rows = jnp.concatenate([part.final for part in groups["att", layer]], axis=0)
            share = 3 * width // dp_count
            qkv = rows[:share].reshape(share, heads, HEAD)
            qkvs.append(qkv.transpose(1, 0, 2).reshape(heads, -1))
            outs.append(rows[share:].reshape(heads, 2, 4, cols))
        outs = jnp.stack(outs)
        keep, sent = pick(outs, core, 2), pick(outs, 1 - core, 2).astype(bf16)
        outs = ordered(core, keep[:, :, :, None], over_core(sent).astype(f32)[:, :, :, None], 3)
        grads = (
            jnp.stack(qkvs), outs.reshape(layers, heads, -1), up, down
        )
    else:
        hidden_out = place_rows(spot, (), hidden_mine, hidden_recv, bf16)
        grad_input = place_rows(spot, (), row_mine, over_mp(row_send), f32)
        small = jnp.stack(
            [
                jnp.concatenate(
                    [ordered(side, bo[:2], bt[:2], 1), (vec + sums)[:6], up.reshape(-1, width)],
                    axis=0,
                )
                for bo, bt, vec, sums, up in smalls
            ]
        )
        small = lax.psum(small, ("dp", "mp"))
        grads = [
            jnp.stack([groups[kind, layer][k] for layer in range(layers)])
            for kind, k in (("att", 0), ("att", 1), ("ff", 0), ("ff", 1))
        ]
    grad_bias_qv = lax.dynamic_slice_in_dim(small[:, :2], side * cols, cols, 2)
    return (
        hidden_out,
        grad_input,
        grads[0],
        grad_bias_qv,
        grads[1],
        small[:, 2:6],
        small[:, 6:8],
        grads[2],
        small[:, 8:].reshape(layers, hidden),
        grads[3],
    )


def solution(mesh):
    return jax.shard_map(
        local,
        mesh=mesh,
        in_specs=(
            P("dp", "mp", None),
            P("dp", "mp", None),
            P("dp", None),
            P(),
            P(None, None, None, "mp"),
            P(None, None, "mp"),
            P(None, "mp", None),
            P(),
            P(),
            P(),
            P(),
            P(),
        ),
        out_specs=(
            P("dp", "mp", None),
            P("dp", "mp", None),
            P(None, "mp", "dp"),
            P(None, None, "mp"),
            P(None, "mp", "dp"),
            P(),
            P(),
            P(None, "dp"),
            P(),
            P(None, "dp"),
        ),
        check_vma=False,
    )
```

```python
import functools

import jax
import jax.numpy as jnp
from jax import lax
from jax.experimental import pallas as pl
from jax.experimental.pallas import tpu as pltpu
from jax.sharding import PartitionSpec as P

HEAD = 64
PAIR = 2 * HEAD
EPS = 1e-06
BIG = -1e30
INV_SQRT2 = 0.7071067811865476
INV_SQRT2PI = 0.3989422804014327

f32 = jnp.float32
bf16 = jnp.bfloat16
MIB = 1024 * 1024
FF_CHUNK = 768
FF_SUB = 256

NT = (((1,), (1,)), ((), ()))
TN = (((0,), (0,)), ((), ()))


def dot(lhs, rhs, dims=(((1,), (0,)), ((), ()))):
    return lax.dot_general(lhs, rhs, dims, preferred_element_type=f32)


def whole(*dims):
    return pl.BlockSpec(dims, lambda *_: (0,) * len(dims))


def at_layer(layer, *dims):
    return pl.BlockSpec((None, *dims), lambda *_: (layer,) + (0,) * len(dims))


def smem():
    return pl.BlockSpec(memory_space=pltpu.SMEM)


class Spot:
    def __init__(self, array):
        self.array = array
        self.latest = ()
        self.grant = 63.5


def launch(
    body, name, spot, hold, ins, outs, scratch=(), grid=(1,), us=3.0, late=(), early=()
):
    known = [array for array, _ in ins] + [array for array, _ in late]
    hold = [array for array in (*hold, *spot.latest) if not any(array is k for k in known)]
    n_in, n_late, n_early, n_out = len(ins), len(late), len(early), len(outs)
    last = grid[0] - 1
    anywhere = pl.BlockSpec(memory_space=pl.ANY)

    def kernel(spot_ref, *refs):
        groups = []
        for count in (n_in, n_late, len(hold), n_early, n_out, n_late, n_early):
            groups.append(refs[:count])
            refs = refs[count:]
        in_refs, late_refs, _, early_refs, out_refs, late_bufs, early_bufs = groups
        fetches, stores = [], []
        if n_late:
            for k, (_, layer) in enumerate(late):
                source = late_refs[k] if layer is None else late_refs[k].at[layer]
                fetches.append(pltpu.make_async_copy(source, late_bufs[k], refs[0].at[k]))
            refs = refs[1:]
        if n_early:
            for k, (_, when) in enumerate(early):
                copy = pltpu.make_async_copy(early_bufs[k], early_refs[k], refs[0].at[k])
                stores.append((copy, when))
            refs = refs[1:]
        step = pl.program_id(0)
        if fetches:

            @pl.when(step == 0)
            def _():
                for copy in fetches:
                    copy.start()

            @pl.when(step == last)
            def _():
                for copy in fetches:
                    copy.wait()

        body(spot_ref, *in_refs, *late_bufs, *early_bufs, *out_refs, *refs)
        for copy, when in stores:
            pl.when(step == when)(copy.start)
        if stores:

            @pl.when(step == last)
            def _():
                for copy, _ in stores:
                    copy.wait()

    buffers = []
    for array, layer in late:
        buffers.append(pltpu.VMEM(array.shape if layer is None else array.shape[1:], array.dtype))
    buffers += [pltpu.VMEM(out.shape, out.dtype) for out, _ in early]
    buffers += [pltpu.SemaphoreType.DMA((count,)) for count in (n_late, n_early) if count]
    results = pl.pallas_call(
        kernel,
        grid_spec=pltpu.PrefetchScalarGridSpec(
            num_scalar_prefetch=1,
            grid=grid,
            in_specs=[spec for _, spec in ins] + [anywhere] * (n_late + len(hold)),
            out_specs=[anywhere] * n_early + [spec for spec, _ in outs],
            scratch_shapes=buffers + list(scratch),
        ),
        out_shape=[out for out, _ in early] + [out for _, out in outs],
        compiler_params=pltpu.CompilerParams(vmem_limit_bytes=int(spot.grant * MIB)),
        cost_estimate=pl.CostEstimate(
            flops=int(us * 1e9), bytes_accessed=int(us * 1e6), transcendentals=0
        ),
        name=name,
    )(spot.array, *known, *hold)
    spot.latest = (results[0],)
    return results


def shape(dims, dtype):
    return jax.ShapeDtypeStruct(dims, dtype)


def head_mask(head, value):
    lane = lax.broadcasted_iota(jnp.int32, (1, PAIR), 1)
    return jnp.where((lane // HEAD) == head, value, 0.0).astype(bf16)


CORE, SIDE, AXIS_X, AXIS_Z0, AXIS_Z1 = range(5)


def enter_kernel(layer_limit, spot_ref, lim_ref, mine_ref, recv_ref, act_ref):
    limit = lim_ref[0, 0]
    inv = 1.0 / limit
    half = mine_ref.shape[0]
    act_ref[:half, :] = (limit * jnp.tanh(mine_ref[...].astype(f32) * inv)).astype(bf16)
    act_ref[half:, :] = (limit * jnp.tanh(recv_ref[...].astype(f32) * inv)).astype(bf16)


def enter(spot, hold, limits, hidden_in, recv):
    half, width = recv.shape
    (act,) = launch(
        functools.partial(enter_kernel, 0), "enter", spot, hold,
        [(limits, smem()), (hidden_in, my_row(half, width)), (recv, whole(half, width))],
        [(whole(2 * half, width), shape((2 * half, width), bf16))],
        us=3.0,
    )
    return act


def my_row(half, width):
    return pl.BlockSpec((None, half, width), lambda t, s: (s[SIDE], 0, 0))


def place_kernel(spot_ref, mine_ref, recv_ref, out_ref):
    out_ref[spot_ref[SIDE]] = mine_ref[...].astype(out_ref.dtype)
    out_ref[1 - spot_ref[SIDE]] = recv_ref[...].astype(out_ref.dtype)


def place_rows(spot, hold, mine, recv, dtype):
    half, width = mine.shape
    (out,) = launch(
        place_kernel, "place_rows", spot, hold,
        [(mine, whole(half, width)), (recv, whole(half, width))],
        [(whole(2, half, width), shape((2, half, width), dtype))],
        us=2.5
    )
    return out


def copy_kernel(spot_ref, *refs):
    count = len(refs) // 2
    for source, target in zip(refs[:count], refs[count:]):
        target[...] = source[...]


def pack_kernel(spot_ref, w_ref, o_ref, out_ref):
    rows = w_ref.shape[1]
    out_ref[:, :rows, :] = w_ref[...]
    out_ref[0, rows:, :] = o_ref[...]


def pack_weights(layer, w_qkv, w_out):
    _, _, width, cols = w_qkv.shape
    rows, wide, deep = width // 2, w_out.shape[2] // 2, cols // 3
    ins = [
        (w_qkv, pl.BlockSpec((None, 1, rows, cols), lambda t, s: (layer, t, s[CORE], 0))),
        (w_out, pl.BlockSpec((None, deep, wide), lambda t, s: (layer, t, s[CORE]))),
    ]
    out = (
        pl.BlockSpec((1, rows + deep, cols), lambda t, s: (t, 0, 0)),
        shape((3, rows + deep, cols), bf16),
    )
    return ins, out


def pick_weights(spot, w_qkv):
    _, _, width, cols = w_qkv.shape
    rows = width // 2
    return launch(
        copy_kernel, "pick_weights", spot, (),
        [(w_qkv, pl.BlockSpec((None, 1, rows, cols), lambda t, s: (0, t, s[CORE], 0)))],
        [(pl.BlockSpec((1, rows, cols), lambda t, s: (t, 0, 0)), shape((3, rows, cols), bf16))],
        grid=(3,),
        us=3.0,
    )[0]


def relay(spot, array, w_out):
    _, cols, width = w_out.shape
    copies = relay_piece(array) + [
        (
            w_out,
            pl.BlockSpec((None, cols // 3, width), lambda t, s: (0, t, 0)),
            pl.BlockSpec((cols // 3, width), lambda t, s: (t, 0)),
            shape((cols, width), bf16),
        )
    ]
    return launch(
        copy_kernel, "relay", spot, (),
        [(a, source) for a, source, _, _ in copies],
        [(target, out) for _, _, target, out in copies],
        grid=(3,),
        us=2.5,
    )


def attn_fwd_kernel(pieces, relays, packs, spot_ref, a_ref, *refs):
    w_refs = refs[:pieces]
    b_ref, sq_ref, sk_ref = refs[pieces : pieces + 3]
    count = pieces + 3 + relays + 2 * packs
    sources = refs[pieces + 3 : count]
    q_ref, k_ref, v_ref, c_ref, lse_ref = refs[count : count + 5]
    targets = refs[count + 5 :]
    for source, target in zip(sources[:relays], targets[:relays]):
        target[...] = source[...]
    if packs:
        pack_kernel(spot_ref, *sources[relays:], targets[relays])
    seq, width = a_ref.shape
    share = width // pieces
    both = value = None
    for piece, w_ref in enumerate(w_refs):
        if pieces == 1:
            act = a_ref[...]
        else:
            which = jnp.where(spot_ref[CORE] == 0, piece, 1 - piece)
            act = a_ref[:, pl.ds(pl.multiple_of(which * share, 128), share)]
        term = dot(act, jnp.concatenate([w_ref[0], w_ref[1]], axis=1))
        both = term if both is None else both + term
        term = dot(act, w_ref[2])
        value = term if value is None else value + term
    query = (both[:, :PAIR] + b_ref[0:1, :]).astype(bf16)
    key = both[:, PAIR:].astype(bf16)
    value = value + b_ref[1:2, :]
    value_t = value.T.astype(bf16)
    q_ref[...] = query
    k_ref[...] = key
    v_ref[...] = value.astype(bf16)
    key_ext = jnp.concatenate([key, sk_ref[...]], axis=1)
    parts = []
    ones = jnp.ones((16, seq), bf16)
    for head in range(2):
        query_ext = jnp.concatenate([query * head_mask(head, HEAD**-0.5), sq_ref[...]], axis=1)
        scores = dot(key_ext, query_ext, NT)
        top = jnp.max(scores, axis=0, keepdims=True)
        weights = jnp.exp(scores - top).astype(bf16)
        summed = dot(
            jnp.concatenate([value_t[head * HEAD : (head + 1) * HEAD], ones], axis=0), weights
        )
        total = summed[HEAD : HEAD + 1]
        parts.append(summed[:HEAD] * (1.0 / total))
        lse_ref[0, head : head + 1, :] = top + jnp.log(total)
    c_ref[...] = jnp.concatenate(parts, axis=0).T


def weight_specs(layer, weights):
    if len(weights) == 1:
        width = weights[0].shape[2]
        return [pl.BlockSpec((None, 3, width, PAIR), lambda t, s: (layer, 0, 0, t))]
    share = weights[0].shape[2]
    return [pl.BlockSpec((3, share, PAIR), lambda t, s: (0, 0, t))] * 2


def relay_piece(array):
    lead, *rest = array.shape
    spec = pl.BlockSpec((lead // 3, *rest), lambda t, s: (t,) + (0,) * len(rest))
    return [(array, spec, spec, shape(array.shape, array.dtype))]


def relay_row(rows):
    _, half, width = rows.shape
    wide = width // 3
    return [
        (
            rows,
            pl.BlockSpec((None, half, wide), lambda t, s: (1 - s[SIDE], 0, t)),
            pl.BlockSpec((half, wide), lambda t, s: (0, t)),
            shape((half, width), rows.dtype),
        )
    ]


def attn_fwd(spot, hold, layer, act, weights, bias, seg_q, seg_k, relays=(), pack=None):
    pack_ins, pack_out = pack if pack else ([], None)
    seq, width = act.shape
    cols = bias.shape[2]
    steps = cols // PAIR
    block = pl.BlockSpec((seq, PAIR), lambda t, s: (0, t))
    return launch(
        functools.partial(attn_fwd_kernel, len(weights), len(relays), 1 if pack else 0),
        "attn_fwd", spot, hold,
        [(act, whole(seq, width))]
        + list(zip(weights, weight_specs(layer, weights)))
        + [
            (bias, pl.BlockSpec((None, 2, PAIR), lambda t, s: (layer, 0, t))),
            (seg_q, whole(seq, PAIR)),
            (seg_k, whole(seq, PAIR)),
        ]
        + [(array, source) for array, source, _, _ in relays]
        + pack_ins,
        [
            (block, shape((seq, cols), bf16)),
            (block, shape((seq, cols), bf16)),
            (block, shape((seq, cols), bf16)),
            (block, shape((seq, cols), f32)),
            (pl.BlockSpec((1, 8, seq), lambda t, s: (t, 0, 0)), shape((steps, 8, seq), f32)),
        ]
        + [(target, out) for _, _, target, out in relays]
        + ([pack_out] if pack else []),
        grid=(steps,),
        us=8.0
    )


def norm_rows(entries):
    centred = entries - jnp.mean(entries, axis=-1, keepdims=True)
    spread = jnp.mean(centred * centred, axis=-1, keepdims=True)
    rate = lax.rsqrt(spread + EPS)
    return centred * rate, rate


def ff_fwd_kernel(
    layer, last, spot_ref, lim_ref, xt_ref, xb_ref, co_ref, ct_ref, wo_ref, wy_ref, wc_ref,
    vec_ref, gain_ref, up_ref, bup_ref, down_ref, *rest
):
    if last:
        gt_ref, gb_ref, *rest = rest
    cu_ref, hat1_ref, rate1_ref, g_ref, slope_ref, *rest = rest
    acc_ref = rest[-1]
    step = pl.program_id(0)
    half_seq, width = xt_ref.shape
    half = co_ref.shape[1]
    wide = width // 2
    rows = 256
    ctx_limit, ff_limit, act_limit = lim_ref[layer, 1], lim_ref[layer, 2], lim_ref[layer, 3]

    @pl.when(step == 0)
    def _():
        inv = 1.0 / ctx_limit
        cu_ref[:, :half] = (ctx_limit * jnp.tanh(co_ref[...] * inv)).astype(bf16)
        cu_ref[:, half:width] = (ctx_limit * jnp.tanh(ct_ref[...] * inv)).astype(bf16)
        acc_ref[...] = dot(cu_ref[:, :half], wo_ref[...])
        for piece, w_ref in enumerate((wy_ref, wc_ref)):
            which = jnp.where(spot_ref[CORE] == 0, piece, 1 - piece)
            at = pl.ds(pl.multiple_of(which * wide, 128), wide)
            acc_ref[:, at] += dot(cu_ref[:, half:width], w_ref[...].reshape(half, wide))

        for base, x_ref in ((0, xt_ref), (half_seq, xb_ref)):

            def body(i, carry, base=base, x_ref=x_ref):
                start = pl.multiple_of(i * rows, rows)
                at = pl.ds(base + start, rows)
                hat, rate = norm_rows(
                    x_ref[pl.ds(start, rows), :].astype(f32) + (acc_ref[at, :] + vec_ref[0:1, :])
                )
                hat1_ref[at, :] = hat
                rate1_ref[at, :] = jnp.broadcast_to(rate, (rows, 128))
                normed = hat * gain_ref[0:1, :] + vec_ref[1:2, :]
                bent = ff_limit * jnp.tanh(normed * (1.0 / ff_limit))
                cu_ref[at, width:] = bent.astype(bf16)
                acc_ref[at, :] = normed + vec_ref[2:3, :]
                return carry

            lax.fori_loop(0, half_seq // rows, body, 0)

    inv_act = 1.0 / act_limit
    chunk = up_ref.shape[1]
    sub = FF_SUB
    for part in range(chunk // sub):
        cols = slice(part * sub, (part + 1) * sub)
        pre = dot(cu_ref[:, width:], up_ref[:, cols]) + bup_ref[layer : layer + 1, cols]
        cdf = 0.5 * lax.erf(pre * INV_SQRT2) + 0.5
        pdf = jnp.exp(pre * pre * -0.5) * INV_SQRT2PI
        bent = jnp.tanh(pre * cdf * inv_act)
        g_ref[:, cols] = (act_limit * bent).astype(bf16)
        slope_ref[:, cols] = ((1.0 - bent * bent) * (cdf + pre * pdf)).astype(bf16)
    acc_ref[...] += dot(g_ref[...], down_ref[...])

    @pl.when(step == pl.num_programs(0) - 1)
    def _():
        if last:
            top_ref, bottom_ref, de_ref, df_ref, sums_ref = rest[:-1]
            sums = norm_sums(width)
            for base, out_ref, in_ref in ((0, top_ref, gt_ref), (half_seq, bottom_ref, gb_ref)):

                def body(i, carry, base=base, out_ref=out_ref, in_ref=in_ref):
                    here = pl.ds(pl.multiple_of(i * rows, rows), rows)
                    at = pl.ds(base + pl.multiple_of(i * rows, rows), rows)
                    hat, rate = norm_rows(acc_ref[at, :])
                    new = hat * gain_ref[1:2, :] + vec_ref[3:4, :]
                    out_ref[here, :] = new.astype(bf16)
                    grad = in_ref[here, :].astype(f32)
                    return leave_norm(grad, hat, rate, gain_ref, at, de_ref, df_ref, carry)

                sums = lax.fori_loop(0, half_seq // rows, body, sums)
            store_sums(sums, sums_ref)
        else:
            hat2_ref, rate2_ref, new_ref, act_ref = rest[:-1]
            limit = lim_ref[layer + 1, 0]

            def body(i, carry):
                at = pl.ds(pl.multiple_of(i * rows, rows), rows)
                hat, rate = norm_rows(acc_ref[at, :])
                hat2_ref[at, :] = hat
                rate2_ref[at, :] = jnp.broadcast_to(rate, (rows, 128))
                new = hat * gain_ref[1:2, :] + vec_ref[3:4, :]
                new_ref[at, :] = new
                act_ref[at, :] = (limit * jnp.tanh(new * (1.0 / limit))).astype(bf16)
                return carry

            lax.fori_loop(0, 2 * half_seq // rows, body, 0)


def norm_back(grad, hat, rate, gain):
    scaled = grad * gain
    mean = jnp.mean(scaled, axis=-1, keepdims=True)
    lean = jnp.mean(scaled * hat, axis=-1, keepdims=True)
    return rate * (scaled - mean - hat * lean)


def norm_sums(width):
    return (jnp.zeros((1, width), f32),) * 3


def leave_norm(grad, hat, rate, gain_ref, at, de_ref, df_ref, sums):
    de = norm_back(grad, hat, rate, gain_ref[1:2, :])
    df = de.astype(bf16)
    de_ref[at, :] = de
    df_ref[at, :] = df
    return (
        sums[0] + jnp.sum(df.astype(f32), axis=0, keepdims=True),
        sums[1] + jnp.sum(grad, axis=0, keepdims=True),
        sums[2] + jnp.sum(grad * hat, axis=0, keepdims=True),
    )


def store_sums(sums, sums_ref):
    sums_ref[...] = jnp.zeros_like(sums_ref)
    sums_ref[2:3, :] = sums[0]
    sums_ref[3:4, :] = sums[1]
    sums_ref[5:6, :] = sums[2]


def norm_outs(seq, width):
    return [
        (whole(seq, width), shape((seq, width), f32)),
        (whole(seq, width), shape((seq, width), bf16)),
        (whole(8, width), shape((8, width), f32)),
    ]


def out_shares(pieces, half, width):
    if len(pieces) == 2:
        spec = pl.BlockSpec((3, half // 3, width // 2), lambda *_: (0, 3, 0))
        return [(piece, spec) for piece in pieces]
    return [
        (pieces[0], pl.BlockSpec((half, width // 2), lambda t, s: (0, s[CORE]))),
        (pieces[0], pl.BlockSpec((half, width // 2), lambda t, s: (0, 1 - s[CORE]))),
    ]


def halves(pair, half, width):
    if len(pair) == 1:
        return [
            (pair[0], pl.BlockSpec((half, width), lambda *_: (0, 0))),
            (pair[0], pl.BlockSpec((half, width), lambda *_: (1, 0))),
        ]
    first = my_row(half, width) if pair[0].ndim == 3 else whole(half, width)
    return [(pair[0], first), (pair[1], whole(half, width))]


def ff_fwd(
    spot, hold, layer, last, limits, x, ctx_own, ctx_oth, w_out, wo_oth, vec, gain, w_up, b_up,
    w_down, cot=None
):
    seq, half = ctx_own.shape
    width, hidden = w_up.shape[1:]
    chunk = FF_CHUNK
    steps = hidden // chunk
    tile = pl.BlockSpec((seq, chunk), lambda t, s: (0, t))
    full = whole(seq, width)
    early = [
        (shape((seq, 2 * width), bf16), 0),
        (shape((seq, width), f32), 0),
        (shape((seq, 128), f32), 0),
    ]
    outs = [
        (tile, shape((seq, hidden), bf16)),
        (tile, shape((seq, hidden), bf16)),
    ]
    if last:
        outs += [(whole(seq // 2, width), shape((seq // 2, width), bf16))] * 2
        outs += norm_outs(seq, width)
    else:
        outs += [
            (full, shape((seq, width), f32)),
            (whole(seq, 128), shape((seq, 128), f32)),
            (full, shape((seq, width), f32)),
            (full, shape((seq, width), bf16)),
        ]
    return launch(
        functools.partial(ff_fwd_kernel, layer, last), "ff_fwd", spot, hold,
        [(limits, smem())]
        + halves(x, seq // 2, width)
        + [
            (ctx_own, whole(seq, half)),
            (ctx_oth, whole(seq, half)),
            (w_out, at_layer(layer, half, width)),
            *out_shares(wo_oth, half, width),
            (vec, at_layer(layer, *vec.shape[1:])),
            (gain, at_layer(layer, *gain.shape[1:])),
            (w_up, pl.BlockSpec((None, width, chunk), lambda t, s: (layer, 0, t))),
            (b_up, pl.BlockSpec((b_up.shape[0], chunk), lambda t, s: (0, t))),
            (w_down, pl.BlockSpec((None, chunk, width), lambda t, s: (layer, t, 0))),
        ]
        + (halves(cot, seq // 2, width) if last else []),
        outs,
        early=early,
        scratch=[pltpu.VMEM((seq, width), f32)],
        grid=(steps,),
        us=21.0
    )


def ff_bwd_kernel(
    layer, spot_ref, lim_ref, fin_ref, vec_ref, gain_ref, slope_ref, up_ref, down_ref, wy_ref,
    wc_ref, de_ref, hat1_ref, rate1_ref, wo_ref, co_ref, ct_ref,
    zk_ref, ok_ref, os_ref, dy_ref, dco_ref, dct_ref, small_ref, bup_ref,
    do_ref, du_ref, dz_ref,
):
    step = pl.program_id(0)
    steps = pl.num_programs(0)
    seq, width = de_ref.shape
    half = width // 2
    rows = 256
    core = spot_ref[CORE]
    mine = pl.ds(pl.multiple_of(core * half, 128), half)
    other = pl.ds(pl.multiple_of((1 - core) * half, 128), half)
    zero = jnp.zeros((1, width), f32)
    ctx_limit, ff_limit = lim_ref[layer, 1], lim_ref[layer, 2]

    chunk = up_ref.shape[1]
    sub = FF_SUB
    for part in range(chunk // sub):
        cols = slice(part * sub, (part + 1) * sub)
        dz = dot(fin_ref[...], down_ref[cols, :], NT) * slope_ref[:, cols].astype(f32)
        low = dz.astype(bf16)
        bup_ref[:, cols] = jnp.sum(low.astype(f32), axis=0, keepdims=True)
        dz_ref[:, cols] = low
    term = dot(dz_ref[...], up_ref[...], NT)

    @pl.when(step == 0)
    def _():
        du_ref[...] = term

    @pl.when(step > 0)
    def _():
        du_ref[...] += term

    @pl.when(step < steps // 2)
    def _():
        zk_ref[:, pl.ds(pl.multiple_of(step * chunk, 128), chunk)] = dz_ref[...]

    @pl.when(step == steps - 1)
    def _():
        def body(i, carry):
            gain_sum, shift_sum, out_sum = carry
            at = pl.ds(pl.multiple_of(i * rows, rows), rows)
            hat = hat1_ref[at, :]
            normed = hat * gain_ref[0:1, :] + vec_ref[1:2, :]
            bent = jnp.tanh(normed * (1.0 / ff_limit))
            grad = de_ref[at, :] + du_ref[at, :] * (1.0 - bent * bent)
            dy = norm_back(grad, hat, rate1_ref[at, 0:1], gain_ref[0:1, :])
            low = dy.astype(bf16)
            dy_ref[at, :] = dy
            do_ref[at, :] = low
            return (
                gain_sum + jnp.sum(grad * hat, axis=0, keepdims=True),
                shift_sum + jnp.sum(grad, axis=0, keepdims=True),
                out_sum + jnp.sum(low.astype(f32), axis=0, keepdims=True),
            )

        sums = lax.fori_loop(0, seq // rows, body, (zero, zero, zero))
        small_ref[...] = jnp.zeros_like(small_ref)
        small_ref[0:1, :] = sums[2]
        small_ref[1:2, :] = sums[1]
        small_ref[4:5, :] = sums[0]
        ok_ref[...] = do_ref[:, mine]
        os_ref[...] = do_ref[:, other]
        inv = 1.0 / ctx_limit
        bent = jnp.tanh(co_ref[...] * inv)
        dco_ref[...] = (dot(do_ref[...], wo_ref[...], NT) * (1.0 - bent * bent)).astype(bf16)
        bent = jnp.tanh(ct_ref[...] * inv)
        grad = dot(do_ref[:, mine], wy_ref[...].reshape(half, half), NT)
        grad += dot(do_ref[:, other], wc_ref[...].reshape(half, half), NT)
        dct_ref[...] = (grad * (1.0 - bent * bent)).astype(bf16)


def ff_bwd(
    spot, hold, layer, limits, de, df, hat1, rate1, vec, gain, slope, w_up, w_down, w_out,
    wo_oth, ctx_own, ctx_oth,
):
    seq, half = ctx_own.shape
    width, hidden = w_up.shape[1:]
    chunk = FF_CHUNK
    steps = hidden // chunk
    span = steps // 2

    def place(t, s):
        return jnp.where(t < span, s[CORE] * span + t, (1 - s[CORE]) * span + t - span)

    full = whole(seq, width)
    part = whole(seq, width // 2)
    outs = [
        (part, shape((seq, width // 2), bf16)),
        (part, shape((seq, width // 2), bf16)),
        (full, shape((seq, width), f32)),
        (whole(seq, half), shape((seq, half), bf16)),
        (whole(seq, half), shape((seq, half), bf16)),
        (whole(8, width), shape((8, width), f32)),
        (pl.BlockSpec((1, chunk), lambda t, s: (0, place(t, s))), shape((1, hidden), f32)),
    ]
    return launch(
        functools.partial(ff_bwd_kernel, layer), "ff_bwd", spot, hold,
        [(limits, smem())]
        + [
            (df, full),
            (vec, at_layer(layer, *vec.shape[1:])),
            (gain, at_layer(layer, *gain.shape[1:])),
            (slope, pl.BlockSpec((seq, chunk), lambda t, s: (0, place(t, s)))),
            (w_up, pl.BlockSpec((None, width, chunk), lambda t, s: (layer, 0, place(t, s)))),
            (w_down, pl.BlockSpec((None, chunk, width), lambda t, s: (layer, place(t, s), 0))),
            *out_shares(wo_oth, half, width),
        ],
        outs,
        late=[
            (de, None),
            (hat1, None),
            (rate1, None),
            (w_out, layer),
            (ctx_own, None),
            (ctx_oth, None),
        ],
        early=[(shape((seq, hidden // 2), bf16), span - 1)],
        scratch=[
            pltpu.VMEM((seq, width), bf16),
            pltpu.VMEM((seq, width), f32),
            pltpu.VMEM((seq, chunk), bf16),
        ],
        grid=(steps,),
        us=20.0
    )


def attn_bwd_half(q_ref, k_ref, v_ref, c_ref, lse_ref, dc_ref, seg_q, seg_k):
    query, key, value, grad = q_ref[...], k_ref[...], v_ref[...], dc_ref[...]
    key_ext = jnp.concatenate([key, seg_k], axis=1)
    key_t = key.astype(f32).T.astype(bf16)
    product_t = (grad.astype(f32) * c_ref[...]).T
    d_key = d_value = None
    d_query_t = []
    for head in range(2):
        scaled = query * head_mask(head, HEAD**-0.5)
        scores = dot(key_ext, jnp.concatenate([scaled, seg_q], axis=1), NT)
        probs = jnp.exp(scores - lse_ref[0, head : head + 1, :])
        grad_head = grad * head_mask(head, 1.0)
        d_probs = dot(value, grad_head, NT)
        delta = jnp.sum(product_t[head * HEAD : (head + 1) * HEAD], axis=0, keepdims=True)
        d_scores = (probs * (d_probs - delta)).astype(bf16)
        term_v = dot(probs.astype(bf16), grad_head)
        term_k = dot(d_scores, scaled)
        d_value = term_v if d_value is None else d_value + term_v
        d_key = term_k if d_key is None else d_key + term_k
        d_query_t.append(dot(key_t[head * HEAD : (head + 1) * HEAD], d_scores))
    d_query = jnp.concatenate(d_query_t, axis=0).T * HEAD**-0.5
    return d_query.astype(bf16), d_key.astype(bf16), d_value.astype(bf16)


def attn_bwd_kernel(
    layer, spot_ref, lim_ref, sq_ref, sk_ref,
    qo_ref, ko_ref, vo_ref, co_ref, lo_ref, dco_ref,
    qt_ref, kt_ref, vt_ref, ct_ref, lt_ref, dct_ref, wo_ref, wy_ref, wc_ref, *rest
):
    if layer:
        gain_ref, dy_ref, x_ref, hat_ref, rate_ref, *rest = rest
    else:
        xt_ref, xb_ref, dy_ref, *rest = rest
    dqo_ref, dko_ref, dvo_ref, dqt_ref, dkt_ref, dvt_ref, bo_ref, bt_ref, *rest = rest
    acc_ref = rest[-1]
    step = pl.program_id(0)
    seq, width = dy_ref.shape
    half_seq, share = seq // 2, width // 2
    rows = 128
    own = attn_bwd_half(qo_ref, ko_ref, vo_ref, co_ref, lo_ref, dco_ref, sq_ref[...], sk_ref[...])
    oth = attn_bwd_half(qt_ref, kt_ref, vt_ref, ct_ref, lt_ref, dct_ref, sq_ref[...], sk_ref[...])
    dqo_ref[...], dko_ref[...], dvo_ref[...] = own
    dqt_ref[...], dkt_ref[...], dvt_ref[...] = oth
    for out_ref, grads in ((bo_ref, own), (bt_ref, oth)):
        out_ref[0:1, :] = jnp.sum(grads[0].astype(f32), axis=0, keepdims=True)
        out_ref[1:2, :] = jnp.sum(grads[2].astype(f32), axis=0, keepdims=True)
        out_ref[2:8, :] = jnp.zeros((6, PAIR), f32)
    joined = [jnp.concatenate([own[k], oth[k]], axis=1) for k in range(3)]
    for piece, w_ref in enumerate((wy_ref, wc_ref)):
        which = jnp.where(spot_ref[CORE] == 0, piece, 1 - piece)
        at = pl.ds(pl.multiple_of(which * share, 128), share)
        total = None
        for k in range(3):
            term = dot(joined[k], jnp.concatenate([wo_ref[k, at, :], w_ref[k]], axis=1), NT)
            total = term if total is None else total + term

        @pl.when(step == 0)
        def _():
            acc_ref[:, at] = total

        @pl.when(step > 0)
        def _():
            acc_ref[:, at] += total

    @pl.when(step == pl.num_programs(0) - 1)
    def _():
        inv = 1.0 / lim_ref[layer, 0]
        sums = norm_sums(width)
        for part in range(2):

            def body(i, carry, part=part):
                here = pl.ds(pl.multiple_of(i * rows, rows), rows)
                at = pl.ds(part * half_seq + pl.multiple_of(i * rows, rows), rows)
                value = x_ref[at, :] if layer else (xt_ref, xb_ref)[part][here, :]
                bent = jnp.tanh(value.astype(f32) * inv)
                grad = dy_ref[at, :] + acc_ref[at, :] * (1.0 - bent * bent)
                if layer:
                    return leave_norm(
                        grad, hat_ref[at, :], rate_ref[at, 0:1], gain_ref, at, rest[0], rest[1],
                        carry,
                    )
                rest[part][here, :] = grad.astype(rest[part].dtype)
                return carry

            sums = lax.fori_loop(0, half_seq // rows, body, sums)
        if layer:
            store_sums(sums, rest[2])


def attn_bwd(spot, hold, layer, limits, x, dy, seg_q, seg_k, own, oth, w_qkv, wq_oth, below=()):
    seq, width = dy.shape
    cols = own[0].shape[1]
    steps = cols // PAIR
    block = pl.BlockSpec((seq, PAIR), lambda t, s: (0, t))
    half_specs = [
        block,
        block,
        block,
        block,
        pl.BlockSpec((1, 8, seq), lambda t, s: (t, 0, 0)),
        block,
    ]
    return launch(
        functools.partial(attn_bwd_kernel, layer), "attn_bwd", spot, hold,
        [(limits, smem())]
        + [(seg_q, whole(seq, PAIR)), (seg_k, whole(seq, PAIR))]
        + list(zip(own, half_specs))
        + list(zip(oth, half_specs))
        + list(zip((w_qkv,), weight_specs(layer, (w_qkv,))))
        + list(zip(wq_oth, weight_specs(layer, wq_oth)))
        + (
            [(below[2], at_layer(layer - 1, *below[2].shape[1:]))]
            if layer
            else halves(x, seq // 2, width)
        ),
        [(block, shape((seq, cols), bf16))] * 6
        + [(pl.BlockSpec((8, PAIR), lambda t, s: (0, t)), shape((8, cols), f32))] * 2
        + (
            norm_outs(seq, width)
            if layer
            else [
                (whole(seq // 2, width), shape((seq // 2, width), f32)),
                (whole(seq // 2, width), shape((seq // 2, width), bf16)),
            ]
        ),
        late=[(dy, None)]
        + ([(x[0], None), (below[0], None), (below[1], None)] if layer else []),
        scratch=[pltpu.VMEM((seq, width), f32)],
        grid=(steps,),
        us=18.5
    )


FF_ORDERS = (
    (AXIS_X, SIDE, AXIS_Z0, AXIS_Z1),
    (SIDE, AXIS_Z0, AXIS_X, AXIS_Z1),
    (AXIS_Z0, AXIS_X, SIDE, AXIS_Z1),
)
FF_ROWS = (144, 128, 112)
ATT_ORDERS = (
    (AXIS_X, SIDE, AXIS_Z0, AXIS_Z1),
    (AXIS_Z0, SIDE, AXIS_X, AXIS_Z1),
)
FIRST_ATT_ORDERS = (
    (AXIS_X, SIDE, AXIS_Z0, AXIS_Z1),
    (AXIS_Z0, AXIS_X, SIDE, AXIS_Z1),
)
ATT_ROWS = (96, 96)
PIECE = 48


def block_of(spot_ref, order, rel):
    bit = {axis: (rel >> (3 - k)) & 1 for k, axis in enumerate(order)}
    chip = 0
    for axis in (AXIS_Z1, AXIS_Z0, AXIS_X):
        own = spot_ref[axis]
        chip = chip * 2 + (1 - own if bit[axis] else own)
    return bit[SIDE], chip


def w_ff_kernel(
    spot_ref, um_ref, uo_ref, zm_ref, so_ref, gm_ref, go_ref, fm_ref, fo_ref, down_ref, *rest
):
    outs, ut_ref, half_ref, all_ref = rest[:-3], rest[-3], rest[-2], rest[-1]
    step = pl.program_id(0)
    sides, chips, tall, lanes = all_ref.shape
    seq, width = um_ref.shape
    thin = width // chips

    @pl.when(step == 0)
    def _():
        ut_ref[:, :seq] = um_ref[...].T
        ut_ref[:, seq:] = uo_ref[...].T
        mine = pl.ds(pl.multiple_of(spot_ref[CORE] * lanes, 128), lanes)
        half_ref[0] = fm_ref[:, mine]
        half_ref[1] = fo_ref[:, mine]

    theirs = (dot(fo_ref[...], down_ref[...], NT) * so_ref[...].astype(f32)).astype(bf16)
    grad_up = dot(ut_ref[:, :seq], zm_ref[...]) + dot(ut_ref[:, seq:], theirs)
    grad_up = grad_up.astype(bf16)
    for chip in range(chips):
        at = pl.ds(pl.multiple_of((step % 2) * thin, 16), thin)
        all_ref[step // 2, chip, at, :] = grad_up[chip * thin : (chip + 1) * thin]
    base = 2 * thin
    deep = tall - base
    per = gm_ref.shape[1] // (2 * deep)
    for part in range(per):
        cols = slice(part * 2 * deep, (part + 1) * 2 * deep)
        grad_down = dot(gm_ref[:, cols], half_ref[0], TN) + dot(go_ref[:, cols], half_ref[1], TN)
        grad_down = grad_down.astype(bf16)
        for side in range(2):
            all_ref[side, step * per + part, base:, :] = grad_down[side * deep : (side + 1) * deep]

    @pl.when(step == pl.num_programs(0) - 1)
    def _():
        start = 0
        for part, (order, count) in enumerate(zip(FF_ORDERS, FF_ROWS)):
            for rel in range(16):
                side, chip = block_of(spot_ref, order, rel)
                side = 1 - spot_ref[SIDE] if side else spot_ref[SIDE]
                value = all_ref[side, chip, start : start + count, :]
                if rel < 8:
                    outs[2 * part][rel] = value
                else:
                    outs[2 * part + 1][(rel - 8) * count : (rel - 7) * count, :] = value
            start += count


def w_ff(
    spot, hold, layer, cu_mine, cu_core, dz_mine, slope_core, g_mine, g_core, df_mine, df_core,
    w_down
):
    seq, width = df_mine.shape
    lanes, hidden = width // 2, g_mine.shape[1]
    steps = dz_mine.shape[1] // lanes
    tall = hidden // 8
    g_block = pl.BlockSpec((seq, hidden // steps), lambda t, s: (0, t))
    u_block = pl.BlockSpec((seq, width), lambda *_: (0, 1))
    outs = []
    for rows in FF_ROWS:
        outs.append((whole(8, rows, lanes), shape((8, rows, lanes), bf16)))
        outs.append((whole(8 * rows, lanes), shape((8 * rows, lanes), bf16)))
    return launch(
        w_ff_kernel, "w_ff", spot, hold,
        [
            (cu_mine, u_block),
            (cu_core, u_block),
            (dz_mine, pl.BlockSpec((seq, lanes), lambda t, s: (0, t))),
            (slope_core, pl.BlockSpec((seq, lanes), lambda t, s: (0, s[CORE] * steps + t))),
            (g_mine, g_block),
            (g_core, g_block),
            (df_mine, whole(seq, width)),
            (df_core, whole(seq, width)),
            (
                w_down,
                pl.BlockSpec(
                    (None, lanes, width), lambda t, s: (layer, s[CORE] * steps + t, 0)
                ),
            ),
        ],
        outs,
        scratch=[
            pltpu.VMEM((width, 2 * seq), bf16),
            pltpu.VMEM((2, seq, lanes), bf16),
            pltpu.VMEM((2, 8, tall, lanes), bf16),
        ],
        grid=(steps,),
        us=13.5,
    )


def w_att_kernel(
    spot_ref, a_ref, dqo_ref, dko_ref, dvo_ref, dqt_ref, dkt_ref, dvt_ref,
    cm_ref, cc_ref, dom_ref, doc_ref, keep_ref, out_ref, *rest
):
    send_refs, at_ref, spare_ref = rest[:-2], rest[-2], rest[-1]
    width = a_ref.shape[1]
    _, chips, tall, cols = keep_ref.shape
    core = spot_ref[CORE]
    piece = PIECE
    per = tall // piece
    at_ref[...] = a_ref[...].T
    sides = ((dqo_ref, dko_ref, dvo_ref), (dqt_ref, dkt_ref, dvt_ref))
    for side, grads in enumerate(sides):
        for which in range(3):
            result = dot(at_ref[...], grads[which][...]).astype(bf16)
            for j in range(width // piece):
                index = which * (width // piece) + j
                block, sub = index // per, index % per
                spare_ref[block % 2, block // 2, sub * piece : (sub + 1) * piece, :] = result[
                    j * piece : (j + 1) * piece
                ]
        keep_ref[side] = spare_ref[core]
        for k, send_ref in enumerate(send_refs):
            send_ref[side] = spare_ref[1 - core, :, k * piece : (k + 1) * piece, :]
    half = width // 2
    heads = half // HEAD
    for side in range(2):
        at = slice(side * half, (side + 1) * half)
        result = dot(cm_ref[:, at], dom_ref[...], TN) + dot(cc_ref[:, at], doc_ref[...], TN)
        for chip in range(chips):
            for pair in range(heads // 2):
                first = (2 * pair) * HEAD + 8 * chip
                second = first + HEAD
                out_ref[side, chip, pair * 16 : (pair + 1) * 16, :] = jnp.concatenate(
                    [result[first : first + 8], result[second : second + 8]], axis=0
                ).astype(bf16)


def w_att(spot, hold, act, d_own, d_oth, cu_mine, cu_core, do_mine, do_core):
    seq, width = act.shape
    cols = width // 2
    chips = 8
    tall = 3 * width // (2 * chips)
    outs = [
        shape((2, chips, tall, cols), bf16),
        shape((2, chips, cols // chips, cols), bf16),
        *[shape((2, chips, PIECE, cols), bf16)] * (tall // PIECE),
    ]
    cq_block = pl.BlockSpec((seq, width), lambda *_: (0, 0))
    return launch(
        w_att_kernel, "w_att", spot, hold,
        [(array, whole(*array.shape)) for array in (act, *d_own, *d_oth)]
        + [
            (cu_mine, cq_block),
            (cu_core, cq_block),
            (do_mine, whole(seq, cols)),
            (do_core, whole(seq, cols)),
        ],
        [(whole(*out.shape), out) for out in outs],
        scratch=[pltpu.VMEM((width, seq), bf16), pltpu.VMEM((2, chips, tall, cols), bf16)],
        us=8.0,
    )


class Part:
    def __init__(self, kind, order, kept):
        self.kind, self.order, self.kept = kind, order, kept
        self.stage = 0
        self.array = self.start = None
        self.final = None

    def arrives(self, array, start):
        self.array, self.start = array, start


def pack_small(spot_ref, small_refs, out_ref):
    for layer in range(len(small_refs) // 5):
        bo_ref, bt_ref, vec_ref, sums_ref, up_ref = small_refs[5 * layer : 5 * layer + 5]
        half = bo_ref.shape[1]
        width = 2 * half
        side = spot_ref[SIDE]
        mine = pl.ds(pl.multiple_of(side * half, 128), half)
        other = pl.ds(pl.multiple_of((1 - side) * half, 128), half)
        out_ref[layer, 0:2, mine] = bo_ref[0:2, :]
        out_ref[layer, 0:2, other] = bt_ref[0:2, :]
        out_ref[layer, 2:8, :] = vec_ref[0:6, :] + sums_ref[0:6, :]
        for k in range(up_ref.shape[1] // width):
            out_ref[layer, 8 + k : 9 + k, :] = up_ref[:, k * width : (k + 1) * width]


def exchange(spot, over_axis, parts, att=None, smalls=(), pair=None, carry=None, hold=()):
    anywhere = pl.BlockSpec(memory_space=pl.ANY)
    ins, outs, steps = [], [], []

    def take(array):
        for k, (known, _) in enumerate(ins):
            if known is array:
                return k
        ins.append((array, anywhere))
        return len(ins) - 1

    def give(dims, dtype=bf16):
        outs.append((anywhere, shape(dims, dtype)))
        return len(outs) - 1

    lanes = (parts[0].kept if parts else att[0]).shape[-1]
    sends = {}

    def room(axis, rows):
        start = sends.get(axis, 0)
        sends[axis] = start + rows
        return start

    new_parts, places = [], []
    parts = sorted(parts, key=lambda part: (part.kind != "ff", part.kept.shape[0]))
    for part in parts:
        blocks, rows, _ = part.kept.shape
        source = take(part.kept), take(part.array), part.start
        if blocks > 1:
            axis = part.order[part.stage + 1]
            start = room(axis, blocks // 2 * rows)
            steps.append(("halve", source, give((blocks // 2, rows, lanes)), axis, start))
        elif part.kind == "ff":
            axis = SIDE
            start = room(axis, rows)
            steps.append(("end", source, give((rows, lanes), f32), axis, start))
        else:
            axis = None
            start = 0
            steps.append(("end", source, give((rows, lanes), f32), None, 0))
        places.append((part, axis, start))
    if att is not None:
        source = [take(array) for array in att]
        begin = 0
        for order, rows in zip(FIRST_ATT_ORDERS if smalls else ATT_ORDERS, ATT_ROWS):
            start = room(order[0], 8 * rows)
            kept = give((8, rows, lanes))
            steps.append(("enter", source, kept, order[0], start, order, begin, rows))
            places.append((Part("att", order, None), order[0], start))
            begin += rows
    small_out = None
    if smalls:
        source = [take(array) for small in smalls for array in small]
        width = smalls[0][2].shape[1]
        small_out = give((len(smalls), 8 + smalls[0][4].shape[1] // width, width), f32)
        steps.append(("pack", source, small_out))
    if pair is not None:
        small_out = give(pair[0].shape, f32)
        steps.append(("sum", [take(array) for array in pair], small_out))
    if carry is not None:
        small_out = give(carry.shape, carry.dtype)
        steps.append(("copy", [take(carry)], small_out))
    send_at = {axis: give((rows, lanes)) for axis, rows in sends.items()}

    n_in, n_out = len(ins), len(outs)

    def body(spot_ref, *refs):
        groups = []
        for count in (n_in, n_out, n_in, n_out):
            groups.append(refs[:count])
            refs = refs[count:]
        in_any, out_any, in_refs, out_refs = groups
        in_sems, out_sems, send_sems = refs
        loads = [
            pltpu.make_async_copy(in_any[k], in_refs[k], in_sems.at[k]) for k in range(n_in)
        ]
        for load in loads:
            load.start()
        ready, stores = set(), []

        def store(source, target, sem):
            stores.append(pltpu.make_async_copy(source, target, sem))
            stores[-1].start()

        for number, (what, source, out, *more) in enumerate(steps):
            out_ref = out_refs[out]
            for k in source[:2] if what in ("halve", "end") else source:
                if k not in ready:
                    ready.add(k)
                    loads[k].wait()
            if what == "halve":
                axis, start = more
                kept, got = in_refs[source[0]], in_refs[source[1]]
                base = source[2]
                half, rows, _ = out_ref.shape
                send = out_refs[send_at[axis]]
                for j in range(half):
                    at = base + j * rows
                    out_ref[j] = kept[j] + got[at : at + rows, :]
                    at += half * rows
                    send[start + j * rows : start + (j + 1) * rows, :] = (
                        kept[half + j] + got[at : at + rows, :]
                    )
            elif what == "end":
                axis, start = more
                kept, got = in_refs[source[0]], in_refs[source[1]]
                base = source[2]
                rows = out_ref.shape[0]
                total = kept[0].astype(f32) + got[base : base + rows, :].astype(f32)
                out_ref[...] = total
                if axis is not None:
                    out_refs[send_at[axis]][start : start + rows, :] = total.astype(bf16)
            elif what == "enter":
                axis, start, order, begin, rows = more
                keep, outer, *got = (in_refs[k] for k in source)
                send = out_refs[send_at[axis]]
                for rel in range(16):
                    side, chip = block_of(spot_ref, order, rel)
                    for k in range(begin // PIECE, (begin + rows) // PIECE):
                        if k < len(got):
                            at = slice(k * PIECE, (k + 1) * PIECE)
                            value = keep[side, chip, at, :] + got[k][side, chip]
                        else:
                            value = outer[side, chip]
                        done = k * PIECE - begin
                        if rel < 8:
                            out_ref[rel, done : done + PIECE, :] = value
                        else:
                            at = start + (rel - 8) * rows + done
                            send[at : at + PIECE, :] = value
            elif what == "copy":
                out_ref[...] = in_refs[source[0]][...]
            elif what == "pack":
                pack_small(spot_ref, [in_refs[k] for k in source], out_ref)
            else:
                out_ref[...] = in_refs[source[0]][...] + in_refs[source[1]][...]
            store(out_ref, out_any[out], out_sems.at[out])
            if what in ("halve", "end", "enter") and more[0] is not None:
                k = send_at[more[0]]
                if what == "enter":
                    count = 8 * more[4]
                elif what == "halve":
                    count = out_ref.shape[0] * out_ref.shape[1]
                else:
                    count = out_ref.shape[0]
                at = pl.ds(more[1], count)
                store(out_refs[k].at[at, :], out_any[k].at[at, :], send_sems.at[number])
        for copy in stores:
            copy.wait()

    buffers = [pltpu.VMEM(array.shape, array.dtype) for array, _ in ins]
    buffers += [pltpu.VMEM(out.shape, out.dtype) for _, out in outs]
    buffers += [pltpu.SemaphoreType.DMA((count,)) for count in (n_in, n_out, len(steps))]
    results = launch(body, "exchange", spot, hold, ins, outs, scratch=buffers, us=5.0)
    arrived = {axis: over_axis(results[k], axis) for axis, k in send_at.items()}
    kept_at = [step[2] for step in steps]
    for (part, axis, start), what, out in zip(places, [step[0] for step in steps], kept_at):
        if what == "end":
            part.final = results[out]
        else:
            part.kept = results[out]
        if what != "enter":
            part.stage += 1
        if axis is not None:
            part.arrives(arrived[axis], start)
        new_parts.append(part)
    return new_parts, (None if small_out is None else results[small_out])


def finish_kernel(layers, spot_ref, *refs):
    core, side = spot_ref[CORE], spot_ref[SIDE]
    count = len(FF_ROWS) + 1
    both_ref = refs[-1]
    for layer in range(layers):
        *part_refs, got_ref = refs[count * layer : count * (layer + 1)]
        keep_ref, send_ref = refs[count * layers + 2 * layer : count * layers + 2 * layer + 2]
        start = 0
        for ref in part_refs:
            both_ref[side, start : start + ref.shape[0], :] = ref[...]
            start += ref.shape[0]
        both_ref[1 - side] = got_ref[...].astype(f32)
        half = both_ref.shape[1] // 2
        quarter = half // 4
        for out_ref, which in ((keep_ref, core), (send_ref, 1 - core)):
            for k in range(4):
                at = pl.ds(pl.multiple_of((k % 2) * 2 * quarter + which * quarter, 16), quarter)
                out_ref[k * quarter : (k + 1) * quarter, :] = both_ref[k // 2, at, :].astype(
                    out_ref.dtype
                )
            out_ref[half:, :] = both_ref[which, half:, :].astype(out_ref.dtype)


def finish_ff(spot, groups):
    rows = sum(FF_ROWS)
    ins, outs = [], []
    for parts in groups:
        lanes = parts[0].final.shape[1]
        block = parts[0].start // rows
        assert parts[0].start == block * rows
        ins += [(part.final, whole(*part.final.shape)) for part in parts]
        ins.append(
            (parts[0].array, pl.BlockSpec((rows, lanes), lambda *_, block=block: (block, 0)))
        )
        outs.append((whole(rows, lanes), shape((rows, lanes), f32)))
        outs.append((whole(rows, lanes), shape((rows, lanes), bf16)))
    results = launch(
        functools.partial(finish_kernel, len(groups)), "finish_ff", spot, (), ins, outs,
        scratch=[pltpu.VMEM((2, rows, lanes), f32)],
    )
    return [results[2 * k : 2 * k + 2] for k in range(len(groups))]


def assemble_kernel(layers, spot_ref, *refs):
    up_ref, down_ref, qkv_ref, tile_ref = refs[-4:]
    core = spot_ref[CORE]
    for layer in range(layers):
        keep_ref, got_ref, *att_refs = refs[(2 + len(ATT_ROWS)) * layer :][: 2 + len(ATT_ROWS)]
        keep, got = keep_ref[...], got_ref[...].astype(f32)
        lanes = keep.shape[1]
        half = keep.shape[0] // 2
        quarter = half // 4
        tiles = lanes // 128
        for side in range(2):
            value = jnp.where(core == side, keep, got)
            for t in range(tiles):
                cols = slice(t * 128, (t + 1) * 128)
                for k in range(4):
                    start = ((side * 4 + k) * tiles + t) * layers + layer
                    up_ref[pl.ds(start, quarter, stride=8 * tiles * layers), :] = value[
                        k * quarter : (k + 1) * quarter, cols
                    ]
                start = (side * tiles + t) * layers + layer
                down_ref[pl.ds(start, half, stride=2 * tiles * layers), :] = value[half:, cols]
        share = tile_ref.shape[0] // tiles
        per = share // 2
        for t in range(tiles):
            done = 0
            for ref, rows in zip(att_refs, ATT_ROWS):
                count = min(rows, share - done)
                at = t * share + done
                tile_ref[at : at + count, :] = ref[:count, t * 128 : (t + 1) * 128]
                done += count
        for t in range(tiles):
            even = tile_ref[pl.ds(t * share, per, stride=2), :]
            odd = tile_ref[pl.ds(t * share + 1, per, stride=2), :]
            for k in range(2):
                cols = slice(k * HEAD, (k + 1) * HEAD)
                start = (2 * t + k) * per * layers + layer
                qkv_ref[pl.ds(start, per, stride=layers), :] = jnp.concatenate(
                    [even[:, cols], odd[:, cols]], axis=1
                )


def assemble(spot, pairs, atts, share):
    layers = len(pairs)
    rows, lanes = pairs[0][0].shape
    dims = (rows * lanes // 128 * layers, 128)
    ins = []
    for pair, parts in zip(pairs, atts):
        for array in (*pair, *(part.final for part in parts)):
            ins.append((array, whole(*array.shape)))
    wide = (share * lanes // 128 * layers, 128)
    return launch(
        functools.partial(assemble_kernel, layers), "assemble", spot, (), ins,
        [(whole(*dims), shape(dims, f32))] * 2 + [(whole(*wide), shape(wide, f32))],
        scratch=[pltpu.VMEM((share * lanes // 128, 128), f32)],
        us=3.0,
    )


def local(
    hidden_in, cotangent, segment_ids, clip_ranges, w_qkv, bias_qv, w_out, vector_bias, ln_gain,
    w_up, bias_up, w_down,
):
    layers = w_qkv.shape[0]
    row_count, half_seq, width = hidden_in.shape
    seq = segment_ids.shape[1]
    cols = w_qkv.shape[3]
    heads = cols // HEAD
    hidden = w_up.shape[2]
    dp_count = lax.axis_size("dp")
    assert lax.axis_size("mp") == 2 and row_count == 2 and seq == 2 * half_seq
    bits = dp_count.bit_length() - 1
    assert dp_count == 1 << bits and bits >= 1
    chips = dp_count // 2
    side = lax.axis_index("mp")
    place = lax.axis_index("dp")
    core = place % 2
    spot = Spot(
        jnp.stack(
            [core, side, (place >> 1) & 1, (place >> 2) & 1, (place >> 3) & 1]
        ).astype(jnp.int32)
    )

    def over_mp(value):
        return lax.ppermute(value, "mp", [(0, 1), (1, 0)])

    def over_bit(value, bit):
        return lax.ppermute(value, "dp", [(i, i ^ (1 << bit)) for i in range(dp_count)])

    def over_core(value):
        return over_bit(value, 0)

    def over_axis(value, axis):
        return over_mp(value) if axis == SIDE else over_bit(value, axis - AXIS_X + 1)

    def pick(value, index, axis):
        return lax.dynamic_index_in_dim(value, index, axis, keepdims=False)

    def ordered(index, mine, theirs, axis):
        first = jnp.where(index == 0, mine, theirs)
        second = jnp.where(index == 0, theirs, mine)
        return jnp.concatenate([first, second], axis=axis)

    x = (hidden_in, over_mp(pick(hidden_in, 1 - side, 0)))
    bias_oth = over_mp(bias_qv)
    limits = clip_ranges.astype(f32)
    seg_row = pick(segment_ids, side, 0).reshape(2, half_seq)
    seg_row = jnp.concatenate([pick(seg_row, side, 0), pick(seg_row, 1 - side, 0)])
    same = seg_row[:, None] == jnp.arange(PAIR, dtype=seg_row.dtype)[None, :]
    seg_q = jnp.where(same, BIG, 0.0).astype(bf16)
    seg_k = jnp.where(same, 0.0, 1.0).astype(bf16)

    arrived = over_mp(pick_weights(spot, w_qkv))
    act = enter(spot, (bias_oth,), limits, hidden_in, x[1])
    fetched, wo_oth, stored = [], [], []
    shared = ()
    for layer in range(layers):
        last = layer == layers - 1
        relays = relay_piece(arrived) if layer else []
        if last:
            relays = relays + relay_row(cotangent)
        outs = attn_fwd(spot, (), layer, act, (w_qkv,), bias_qv, seg_q, seg_k, relays)
        own, copies = outs[:5], outs[5:]
        if last:
            cot = (cotangent, over_mp(copies[-1]))
        if layer:
            copy = copies[0]
        else:
            copy, out_share = relay(spot, arrived, w_out)
        fetched.append((arrived, over_core(copy)))
        wo_oth.append(fetched[layer] if layer else (over_mp(out_share),))
        outs = attn_fwd(
            spot, (), layer, act, fetched[layer], bias_oth, seg_q, seg_k,
            pack=None if last else pack_weights(layer + 1, w_qkv, w_out),
        )
        oth = outs[:5]
        if not last:
            arrived = over_mp(outs[5])
        outs = ff_fwd(
            spot, shared, layer, last, limits, x, own[3], oth[3], w_out, wo_oth[layer], vector_bias,
            ln_gain,
            w_up, bias_up, w_down, cot if last else None,
        )
        cu, hat1, rate1, g, slope = outs[:5]
        shared = over_core(cu), over_core(g), over_core(slope)
        norm = None
        if last:
            hidden_mine, hidden_send, *descent = outs[5:]
        else:
            norm = outs[5:7]
        stored.append((x, act, own, oth, cu, hat1, rate1, g, slope, norm, shared))
        if not last:
            x, act = (outs[7],), outs[8]
    hidden_recv = over_mp(hidden_send)

    fast = chips == 8 and width == 768 and hidden == 3072 and cols == 384

    smalls, groups = [], {}
    flying = []
    small = None
    df_core = over_core(descent[1])
    for layer in reversed(range(layers)):
        x, act, own, oth, cu, hat1, rate1, g, slope, norm, shared = stored[layer]
        de, df, sums = descent
        dz_keep, do_keep, do_send, dy, dc_own, dc_oth, vec, d_bup = ff_bwd(
            spot, (), layer, limits, de, df, hat1, rate1, vector_bias, ln_gain, slope, w_up,
            w_down, w_out, wo_oth[layer], own[3], oth[3],
        )
        if fast:
            do_core = over_core(do_send)
            if flying:
                flying, _ = exchange(spot, over_axis, flying, entering)
                groups["att", layer + 1] = flying[-len(ATT_ROWS) :]
            outs = w_ff(
                spot, (hidden_recv, do_core), layer, cu, shared[0], dz_keep, shared[2], g, shared[1], df, df_core,
                w_down,
            )
            parts_ff = []
            for k, order in enumerate(FF_ORDERS):
                parts_ff.append(Part("ff", order, outs[2 * k]))
                parts_ff[k].arrives(over_axis(outs[2 * k + 1], order[0]), 0)
            groups["ff", layer] = parts_ff
            if flying:
                exchange(spot, over_axis, flying)
            flying = flying + parts_ff
        below = (*stored[layer - 1][9], ln_gain) if layer else ()
        outs = attn_bwd(
            spot, (), layer, limits, x, dy, seg_q, seg_k, (*own, dc_own), (*oth, dc_oth), w_qkv,
            fetched[layer], below,
        )
        d_own, d_oth = outs[:3], outs[3:6]
        smalls.insert(0, (outs[6], outs[7], vec, sums, d_bup))
        descent = outs[8:]
        if fast:
            keep, out, *send = w_att(
                spot, (), act, d_own, d_oth, cu, shared[0], do_keep, do_core
            )
            entering = keep, out, *(over_core(piece) for piece in send)
            if layer:
                flying, df = exchange(spot, over_axis, flying, carry=descent[1])
                df_core = over_core(df)
            else:
                late = [part for part in flying if part.kind == "ff" and part.stage == 3]
                flying = [part for part in flying if part not in late]
                flying, small = exchange(
                    spot, over_axis, flying, entering, smalls,
                    hold=tuple({id(part.array): part.array for part in late}.values()),
                )
                groups["att", 0] = flying[-len(ATT_ROWS) :]
        else:
            dz = (dot(df, w_down[layer], NT) * slope.astype(f32)).astype(bf16)
            do = ordered(core, do_keep, do_send, 1)
            total = []
            for lhs, rhs in ((cu[:, width:], dz), (g, df)):
                grad = dot(lhs, rhs, TN).reshape(-1)
                grad = grad + over_mp(grad)
                total.append(lax.psum_scatter(grad, "dp", scatter_dimension=0, tiled=True))
            groups["ff", layer] = total
            sides = []
            for grads, part in ((d_own, cu[:, :cols]), (d_oth, cu[:, cols:width])):
                qkv = jnp.stack([dot(act, grad, TN) for grad in grads])
                qkv = qkv.reshape(3, width, heads, HEAD).transpose(2, 0, 1, 3)
                sides.append((qkv.reshape(heads, -1), dot(part, do, TN).reshape(heads, -1)))
            total = []
            for k in range(2):
                grad = sides[0][k] + over_mp(sides[1][k])
                total.append(lax.psum_scatter(grad, "dp", scatter_dimension=1, tiled=True))
            groups["att", layer] = total

    row_mine, row_send = descent
    if fast:
        axes = [AXIS_X, SIDE, AXIS_Z0, AXIS_Z1]
        pair = (small, over_axis(small, axes.pop(0)))
        turn = 0
        while True:
            if turn == 1:
                flying = flying + late
            flying = [part for part in flying if part.final is None]
            if not flying and turn > 1:
                break
            flying, summed = exchange(spot, over_axis, flying, pair=pair)
            small = small if summed is None else summed
            pair = (small, over_axis(small, axes.pop(0))) if axes else None
            if turn == 0:
                hidden_out = place_rows(spot, (), hidden_mine, hidden_recv, bf16)
            if turn == 2:
                grad_input = place_rows(spot, (), row_mine, over_mp(row_send), f32)
                done = finish_ff(spot, [groups["ff", k] for k in range(layers)])
                pairs = [(keep, over_core(send)) for keep, send in done]
            turn += 1
        while pair:
            small = pair[0] + pair[1]
            pair = (small, over_axis(small, axes.pop(0))) if axes else None
        small = small + over_core(small)
        share = 3 * width // dp_count
        atts = [groups["att", k] for k in range(layers)]
        up, down, qkv = assemble(spot, pairs, atts, share)
        up, down = (
            flat.reshape(-1, layers, 128).transpose(1, 0, 2).reshape(layers, -1)
            for flat in (up, down)
        )
        qkv = qkv.reshape(heads, -1, layers, 128).transpose(2, 0, 1, 3).reshape(layers, heads, -1)
        outs = []
        for parts in atts:
            rows = jnp.concatenate([part.final for part in parts], axis=0)
            outs.append(rows[share:].reshape(heads, 2, 4, cols))
        outs = jnp.stack(outs)
        keep, sent = pick(outs, core, 2), pick(outs, 1 - core, 2).astype(bf16)
        outs = ordered(core, keep[:, :, :, None], over_core(sent).astype(f32)[:, :, :, None], 3)
        grads = (
            qkv, outs.reshape(layers, heads, -1), up, down
        )
    else:
        hidden_out = place_rows(spot, (), hidden_mine, hidden_recv, bf16)
        grad_input = place_rows(spot, (), row_mine, over_mp(row_send), f32)
        small = jnp.stack(
            [
                jnp.concatenate(
                    [ordered(side, bo[:2], bt[:2], 1), (vec + sums)[:6], up.reshape(-1, width)],
                    axis=0,
                )
                for bo, bt, vec, sums, up in smalls
            ]
        )
        small = lax.psum(small, ("dp", "mp"))
        grads = [
            jnp.stack([groups[kind, layer][k] for layer in range(layers)])
            for kind, k in (("att", 0), ("att", 1), ("ff", 0), ("ff", 1))
        ]
    grad_bias_qv = lax.dynamic_slice_in_dim(small[:, :2], side * cols, cols, 2)
    return (
        hidden_out,
        grad_input,
        grads[0],
        grad_bias_qv,
        grads[1],
        small[:, 2:6],
        small[:, 6:8],
        grads[2],
        small[:, 8:].reshape(layers, hidden),
        grads[3],
    )


def solution(mesh):
    return jax.shard_map(
        local,
        mesh=mesh,
        in_specs=(
            P("dp", "mp", None),
            P("dp", "mp", None),
            P("dp", None),
            P(),
            P(None, None, None, "mp"),
            P(None, None, "mp"),
            P(None, "mp", None),
            P(),
            P(),
            P(),
            P(),
            P(),
        ),
        out_specs=(
            P("dp", "mp", None),
            P("dp", "mp", None),
            P(None, "mp", "dp"),
            P(None, None, "mp"),
            P(None, "mp", "dp"),
            P(),
            P(),
            P(None, "dp"),
            P(),
            P(None, "dp"),
        ),
        check_vma=False,
    )
```

```python
import functools

import jax
import jax.numpy as jnp
from jax import lax
from jax.experimental import pallas as pl
from jax.experimental.pallas import tpu as pltpu
from jax.sharding import PartitionSpec as P

HEAD = 64
PAIR = 2 * HEAD
EPS = 1e-06
BIG = -1e30
INV_SQRT2 = 0.7071067811865476
INV_SQRT2PI = 0.3989422804014327

f32 = jnp.float32
bf16 = jnp.bfloat16
MIB = 1024 * 1024
FF_CHUNK = 768
FF_SUB = 256

NT = (((1,), (1,)), ((), ()))
TN = (((0,), (0,)), ((), ()))


def dot(lhs, rhs, dims=(((1,), (0,)), ((), ()))):
    return lax.dot_general(lhs, rhs, dims, preferred_element_type=f32)


def whole(*dims):
    return pl.BlockSpec(dims, lambda *_: (0,) * len(dims))


def at_layer(layer, *dims):
    return pl.BlockSpec((None, *dims), lambda *_: (layer,) + (0,) * len(dims))


def smem():
    return pl.BlockSpec(memory_space=pltpu.SMEM)


class Spot:
    def __init__(self, array):
        self.array = array
        self.latest = ()
        self.grant = 63.9


def launch(
    body, name, spot, hold, ins, outs, scratch=(), grid=(1,), us=3.0, late=(), early=()
):
    known = [array for array, _ in ins] + [array for array, _ in late]
    hold = [array for array in (*hold, *spot.latest) if not any(array is k for k in known)]
    n_in, n_late, n_early, n_out = len(ins), len(late), len(early), len(outs)
    last = grid[0] - 1
    anywhere = pl.BlockSpec(memory_space=pl.ANY)

    def kernel(spot_ref, *refs):
        groups = []
        for count in (n_in, n_late, len(hold), n_early, n_out, n_late, n_early):
            groups.append(refs[:count])
            refs = refs[count:]
        in_refs, late_refs, _, early_refs, out_refs, late_bufs, early_bufs = groups
        fetches, stores = [], []
        if n_late:
            for k, (_, layer) in enumerate(late):
                source = late_refs[k] if layer is None else late_refs[k].at[layer]
                fetches.append(pltpu.make_async_copy(source, late_bufs[k], refs[0].at[k]))
            refs = refs[1:]
        if n_early:
            for k, (_, when) in enumerate(early):
                copy = pltpu.make_async_copy(early_bufs[k], early_refs[k], refs[0].at[k])
                stores.append((copy, when))
            refs = refs[1:]
        step = pl.program_id(0)
        if fetches:

            @pl.when(step == 0)
            def _():
                for copy in fetches:
                    copy.start()

            @pl.when(step == last)
            def _():
                for copy in fetches:
                    copy.wait()

        body(spot_ref, *in_refs, *late_bufs, *early_bufs, *out_refs, *refs)
        for copy, when in stores:
            pl.when(step == when)(copy.start)
        if stores:

            @pl.when(step == last)
            def _():
                for copy, _ in stores:
                    copy.wait()

    buffers = []
    for array, layer in late:
        buffers.append(pltpu.VMEM(array.shape if layer is None else array.shape[1:], array.dtype))
    buffers += [pltpu.VMEM(out.shape, out.dtype) for out, _ in early]
    buffers += [pltpu.SemaphoreType.DMA((count,)) for count in (n_late, n_early) if count]
    results = pl.pallas_call(
        kernel,
        grid_spec=pltpu.PrefetchScalarGridSpec(
            num_scalar_prefetch=1,
            grid=grid,
            in_specs=[spec for _, spec in ins] + [anywhere] * (n_late + len(hold)),
            out_specs=[anywhere] * n_early + [spec for spec, _ in outs],
            scratch_shapes=buffers + list(scratch),
        ),
        out_shape=[out for out, _ in early] + [out for _, out in outs],
        compiler_params=pltpu.CompilerParams(vmem_limit_bytes=int(spot.grant * MIB)),
        cost_estimate=pl.CostEstimate(
            flops=int(us * 1e9), bytes_accessed=int(us * 1e6), transcendentals=0
        ),
        name=name,
    )(spot.array, *known, *hold)
    spot.latest = (results[0],)
    return results


def shape(dims, dtype):
    return jax.ShapeDtypeStruct(dims, dtype)


def head_mask(head, value):
    lane = lax.broadcasted_iota(jnp.int32, (1, PAIR), 1)
    return jnp.where((lane // HEAD) == head, value, 0.0).astype(bf16)


CORE, SIDE, AXIS_X, AXIS_Z0, AXIS_Z1 = range(5)


def enter_kernel(layer_limit, spot_ref, lim_ref, mine_ref, recv_ref, act_ref):
    limit = lim_ref[0, 0]
    inv = 1.0 / limit
    half = mine_ref.shape[0]
    act_ref[:half, :] = (limit * jnp.tanh(mine_ref[...].astype(f32) * inv)).astype(bf16)
    act_ref[half:, :] = (limit * jnp.tanh(recv_ref[...].astype(f32) * inv)).astype(bf16)


def enter(spot, hold, limits, hidden_in, recv):
    half, width = recv.shape
    (act,) = launch(
        functools.partial(enter_kernel, 0), "enter", spot, hold,
        [(limits, smem()), (hidden_in, my_row(half, width)), (recv, whole(half, width))],
        [(whole(2 * half, width), shape((2 * half, width), bf16))],
        us=3.0,
    )
    return act


def my_row(half, width):
    return pl.BlockSpec((None, half, width), lambda t, s: (s[SIDE], 0, 0))


def place_kernel(spot_ref, mine_ref, recv_ref, out_ref):
    out_ref[spot_ref[SIDE]] = mine_ref[...].astype(out_ref.dtype)
    out_ref[1 - spot_ref[SIDE]] = recv_ref[...].astype(out_ref.dtype)


def place_rows(spot, hold, mine, recv, dtype):
    half, width = mine.shape
    (out,) = launch(
        place_kernel, "place_rows", spot, hold,
        [(mine, whole(half, width)), (recv, whole(half, width))],
        [(whole(2, half, width), shape((2, half, width), dtype))],
        us=2.5
    )
    return out


def copy_kernel(spot_ref, *refs):
    count = len(refs) // 2
    for source, target in zip(refs[:count], refs[count:]):
        target[...] = source[...]


def pack_kernel(spot_ref, w_ref, o_ref, out_ref):
    rows = w_ref.shape[1]
    out_ref[:, :rows, :] = w_ref[...]
    out_ref[0, rows:, :] = o_ref[...]


def pack_weights(layer, w_qkv, w_out):
    _, _, width, cols = w_qkv.shape
    rows, wide, deep = width // 2, w_out.shape[2] // 2, cols // 3
    ins = [
        (w_qkv, pl.BlockSpec((None, 1, rows, cols), lambda t, s: (layer, t, s[CORE], 0))),
        (w_out, pl.BlockSpec((None, deep, wide), lambda t, s: (layer, t, s[CORE]))),
    ]
    out = (
        pl.BlockSpec((1, rows + deep, cols), lambda t, s: (t, 0, 0)),
        shape((3, rows + deep, cols), bf16),
    )
    return ins, out


def pick_weights(spot, w_qkv):
    _, _, width, cols = w_qkv.shape
    rows = width // 2
    return launch(
        copy_kernel, "pick_weights", spot, (),
        [(w_qkv, pl.BlockSpec((None, 1, rows, cols), lambda t, s: (0, t, s[CORE], 0)))],
        [(pl.BlockSpec((1, rows, cols), lambda t, s: (t, 0, 0)), shape((3, rows, cols), bf16))],
        grid=(3,),
        us=3.0,
    )[0]


def relay(spot, array, w_out):
    _, cols, width = w_out.shape
    copies = relay_piece(array) + [
        (
            w_out,
            pl.BlockSpec((None, cols // 3, width), lambda t, s: (0, t, 0)),
            pl.BlockSpec((cols // 3, width), lambda t, s: (t, 0)),
            shape((cols, width), bf16),
        )
    ]
    return launch(
        copy_kernel, "relay", spot, (),
        [(a, source) for a, source, _, _ in copies],
        [(target, out) for _, _, target, out in copies],
        grid=(3,),
        us=2.5,
    )


def attn_fwd_kernel(pieces, relays, packs, spot_ref, a_ref, *refs):
    w_refs = refs[:pieces]
    b_ref, sq_ref, sk_ref = refs[pieces : pieces + 3]
    count = pieces + 3 + relays + 2 * packs
    sources = refs[pieces + 3 : count]
    q_ref, k_ref, v_ref, c_ref, lse_ref = refs[count : count + 5]
    targets = refs[count + 5 :]
    for source, target in zip(sources[:relays], targets[:relays]):
        target[...] = source[...]
    if packs:
        pack_kernel(spot_ref, *sources[relays:], targets[relays])
    seq, width = a_ref.shape
    share = width // pieces
    both = value = None
    for piece, w_ref in enumerate(w_refs):
        if pieces == 1:
            act = a_ref[...]
        else:
            which = jnp.where(spot_ref[CORE] == 0, piece, 1 - piece)
            act = a_ref[:, pl.ds(pl.multiple_of(which * share, 128), share)]
        term = dot(act, jnp.concatenate([w_ref[0], w_ref[1]], axis=1))
        both = term if both is None else both + term
        term = dot(act, w_ref[2])
        value = term if value is None else value + term
    query = (both[:, :PAIR] + b_ref[0:1, :]).astype(bf16)
    key = both[:, PAIR:].astype(bf16)
    value = value + b_ref[1:2, :]
    value_t = value.T.astype(bf16)
    q_ref[...] = query
    k_ref[...] = key
    v_ref[...] = value.astype(bf16)
    key_ext = jnp.concatenate([key, sk_ref[...]], axis=1)
    parts = []
    ones = jnp.ones((16, seq), bf16)
    for head in range(2):
        query_ext = jnp.concatenate([query * head_mask(head, HEAD**-0.5), sq_ref[...]], axis=1)
        scores = dot(key_ext, query_ext, NT)
        top = jnp.max(scores, axis=0, keepdims=True)
        weights = jnp.exp(scores - top).astype(bf16)
        summed = dot(
            jnp.concatenate([value_t[head * HEAD : (head + 1) * HEAD], ones], axis=0), weights
        )
        total = summed[HEAD : HEAD + 1]
        parts.append(summed[:HEAD] * (1.0 / total))
        lse_ref[0, head : head + 1, :] = top + jnp.log(total)
    c_ref[...] = jnp.concatenate(parts, axis=0).T


def weight_specs(layer, weights):
    if len(weights) == 1:
        width = weights[0].shape[2]
        return [pl.BlockSpec((None, 3, width, PAIR), lambda t, s: (layer, 0, 0, t))]
    share = weights[0].shape[2]
    return [pl.BlockSpec((3, share, PAIR), lambda t, s: (0, 0, t))] * 2


def relay_piece(array):
    lead, *rest = array.shape
    spec = pl.BlockSpec((lead // 3, *rest), lambda t, s: (t,) + (0,) * len(rest))
    return [(array, spec, spec, shape(array.shape, array.dtype))]


def relay_row(rows):
    _, half, width = rows.shape
    wide = width // 3
    return [
        (
            rows,
            pl.BlockSpec((None, half, wide), lambda t, s: (1 - s[SIDE], 0, t)),
            pl.BlockSpec((half, wide), lambda t, s: (0, t)),
            shape((half, width), rows.dtype),
        )
    ]


def attn_fwd(spot, hold, layer, act, weights, bias, seg_q, seg_k, relays=(), pack=None):
    pack_ins, pack_out = pack if pack else ([], None)
    seq, width = act.shape
    cols = bias.shape[2]
    steps = cols // PAIR
    block = pl.BlockSpec((seq, PAIR), lambda t, s: (0, t))
    return launch(
        functools.partial(attn_fwd_kernel, len(weights), len(relays), 1 if pack else 0),
        "attn_fwd", spot, hold,
        [(act, whole(seq, width))]
        + list(zip(weights, weight_specs(layer, weights)))
        + [
            (bias, pl.BlockSpec((None, 2, PAIR), lambda t, s: (layer, 0, t))),
            (seg_q, whole(seq, PAIR)),
            (seg_k, whole(seq, PAIR)),
        ]
        + [(array, source) for array, source, _, _ in relays]
        + pack_ins,
        [
            (block, shape((seq, cols), bf16)),
            (block, shape((seq, cols), bf16)),
            (block, shape((seq, cols), bf16)),
            (block, shape((seq, cols), f32)),
            (pl.BlockSpec((1, 8, seq), lambda t, s: (t, 0, 0)), shape((steps, 8, seq), f32)),
        ]
        + [(target, out) for _, _, target, out in relays]
        + ([pack_out] if pack else []),
        grid=(steps,),
        us=8.0
    )


def norm_rows(entries):
    centred = entries - jnp.mean(entries, axis=-1, keepdims=True)
    spread = jnp.mean(centred * centred, axis=-1, keepdims=True)
    rate = lax.rsqrt(spread + EPS)
    return centred * rate, rate


def ff_fwd_kernel(
    layer, last, spot_ref, lim_ref, xt_ref, xb_ref, co_ref, ct_ref, wo_ref, wy_ref, wc_ref,
    vec_ref, gain_ref, up_ref, bup_ref, down_ref, *rest
):
    if last:
        gt_ref, gb_ref, *rest = rest
    cu_ref, hat1_ref, rate1_ref, g_ref, slope_ref, *rest = rest
    acc_ref = rest[-1]
    step = pl.program_id(0)
    half_seq, width = xt_ref.shape
    half = co_ref.shape[1]
    wide = width // 2
    rows = 256
    ctx_limit, ff_limit, act_limit = lim_ref[layer, 1], lim_ref[layer, 2], lim_ref[layer, 3]

    @pl.when(step == 0)
    def _():
        inv = 1.0 / ctx_limit
        cu_ref[:, :half] = (ctx_limit * jnp.tanh(co_ref[...] * inv)).astype(bf16)
        cu_ref[:, half:width] = (ctx_limit * jnp.tanh(ct_ref[...] * inv)).astype(bf16)
        acc_ref[...] = dot(cu_ref[:, :half], wo_ref[...])
        for piece, w_ref in enumerate((wy_ref, wc_ref)):
            which = jnp.where(spot_ref[CORE] == 0, piece, 1 - piece)
            at = pl.ds(pl.multiple_of(which * wide, 128), wide)
            acc_ref[:, at] += dot(cu_ref[:, half:width], w_ref[...].reshape(half, wide))

        for base, x_ref in ((0, xt_ref), (half_seq, xb_ref)):

            def body(i, carry, base=base, x_ref=x_ref):
                start = pl.multiple_of(i * rows, rows)
                at = pl.ds(base + start, rows)
                hat, rate = norm_rows(
                    x_ref[pl.ds(start, rows), :].astype(f32) + (acc_ref[at, :] + vec_ref[0:1, :])
                )
                hat1_ref[at, :] = hat
                rate1_ref[at, :] = jnp.broadcast_to(rate, (rows, 128))
                normed = hat * gain_ref[0:1, :] + vec_ref[1:2, :]
                bent = ff_limit * jnp.tanh(normed * (1.0 / ff_limit))
                cu_ref[at, width:] = bent.astype(bf16)
                acc_ref[at, :] = normed + vec_ref[2:3, :]
                return carry

            lax.fori_loop(0, half_seq // rows, body, 0)

    inv_act = 1.0 / act_limit
    chunk = up_ref.shape[1]
    sub = FF_SUB
    for part in range(chunk // sub):
        cols = slice(part * sub, (part + 1) * sub)
        pre = dot(cu_ref[:, width:], up_ref[:, cols]) + bup_ref[layer : layer + 1, cols]
        cdf = 0.5 * lax.erf(pre * INV_SQRT2) + 0.5
        pdf = jnp.exp(pre * pre * -0.5) * INV_SQRT2PI
        bent = jnp.tanh(pre * cdf * inv_act)
        g_ref[:, cols] = (act_limit * bent).astype(bf16)
        slope_ref[:, cols] = ((1.0 - bent * bent) * (cdf + pre * pdf)).astype(bf16)
    acc_ref[...] += dot(g_ref[...], down_ref[...])

    @pl.when(step == pl.num_programs(0) - 1)
    def _():
        if last:
            top_ref, bottom_ref, de_ref, df_ref, sums_ref = rest[:-1]
            sums = norm_sums(width)
            for base, out_ref, in_ref in ((0, top_ref, gt_ref), (half_seq, bottom_ref, gb_ref)):

                def body(i, carry, base=base, out_ref=out_ref, in_ref=in_ref):
                    here = pl.ds(pl.multiple_of(i * rows, rows), rows)
                    at = pl.ds(base + pl.multiple_of(i * rows, rows), rows)
                    hat, rate = norm_rows(acc_ref[at, :])
                    new = hat * gain_ref[1:2, :] + vec_ref[3:4, :]
                    out_ref[here, :] = new.astype(bf16)
                    grad = in_ref[here, :].astype(f32)
                    return leave_norm(grad, hat, rate, gain_ref, at, de_ref, df_ref, carry)

                sums = lax.fori_loop(0, half_seq // rows, body, sums)
            store_sums(sums, sums_ref)
        else:
            hat2_ref, rate2_ref, new_ref, act_ref = rest[:-1]
            limit = lim_ref[layer + 1, 0]

            def body(i, carry):
                at = pl.ds(pl.multiple_of(i * rows, rows), rows)
                hat, rate = norm_rows(acc_ref[at, :])
                hat2_ref[at, :] = hat
                rate2_ref[at, :] = jnp.broadcast_to(rate, (rows, 128))
                new = hat * gain_ref[1:2, :] + vec_ref[3:4, :]
                new_ref[at, :] = new
                act_ref[at, :] = (limit * jnp.tanh(new * (1.0 / limit))).astype(bf16)
                return carry

            lax.fori_loop(0, 2 * half_seq // rows, body, 0)


def norm_back(grad, hat, rate, gain):
    scaled = grad * gain
    mean = jnp.mean(scaled, axis=-1, keepdims=True)
    lean = jnp.mean(scaled * hat, axis=-1, keepdims=True)
    return rate * (scaled - mean - hat * lean)


def norm_sums(width):
    return (jnp.zeros((1, width), f32),) * 3


def leave_norm(grad, hat, rate, gain_ref, at, de_ref, df_ref, sums):
    de = norm_back(grad, hat, rate, gain_ref[1:2, :])
    df = de.astype(bf16)
    de_ref[at, :] = de
    df_ref[at, :] = df
    return (
        sums[0] + jnp.sum(df.astype(f32), axis=0, keepdims=True),
        sums[1] + jnp.sum(grad, axis=0, keepdims=True),
        sums[2] + jnp.sum(grad * hat, axis=0, keepdims=True),
    )


def store_sums(sums, sums_ref):
    sums_ref[...] = jnp.zeros_like(sums_ref)
    sums_ref[2:3, :] = sums[0]
    sums_ref[3:4, :] = sums[1]
    sums_ref[5:6, :] = sums[2]


def norm_outs(seq, width):
    return [
        (whole(seq, width), shape((seq, width), f32)),
        (whole(seq, width), shape((seq, width), bf16)),
        (whole(8, width), shape((8, width), f32)),
    ]


def out_shares(pieces, half, width):
    if len(pieces) == 2:
        spec = pl.BlockSpec((3, half // 3, width // 2), lambda *_: (0, 3, 0))
        return [(piece, spec) for piece in pieces]
    return [
        (pieces[0], pl.BlockSpec((half, width // 2), lambda t, s: (0, s[CORE]))),
        (pieces[0], pl.BlockSpec((half, width // 2), lambda t, s: (0, 1 - s[CORE]))),
    ]


def halves(pair, half, width):
    if len(pair) == 1:
        return [
            (pair[0], pl.BlockSpec((half, width), lambda *_: (0, 0))),
            (pair[0], pl.BlockSpec((half, width), lambda *_: (1, 0))),
        ]
    first = my_row(half, width) if pair[0].ndim == 3 else whole(half, width)
    return [(pair[0], first), (pair[1], whole(half, width))]


def ff_fwd(
    spot, hold, layer, last, limits, x, ctx_own, ctx_oth, w_out, wo_oth, vec, gain, w_up, b_up,
    w_down, cot=None
):
    seq, half = ctx_own.shape
    width, hidden = w_up.shape[1:]
    chunk = FF_CHUNK
    steps = hidden // chunk
    tile = pl.BlockSpec((seq, chunk), lambda t, s: (0, t))
    full = whole(seq, width)
    early = [
        (shape((seq, 2 * width), bf16), 0),
        (shape((seq, width), f32), 0),
        (shape((seq, 128), f32), 0),
    ]
    outs = [
        (tile, shape((seq, hidden), bf16)),
        (tile, shape((seq, hidden), bf16)),
    ]
    if last:
        outs += [(whole(seq // 2, width), shape((seq // 2, width), bf16))] * 2
        outs += norm_outs(seq, width)
    else:
        outs += [
            (full, shape((seq, width), f32)),
            (whole(seq, 128), shape((seq, 128), f32)),
            (full, shape((seq, width), f32)),
            (full, shape((seq, width), bf16)),
        ]
    return launch(
        functools.partial(ff_fwd_kernel, layer, last), "ff_fwd", spot, hold,
        [(limits, smem())]
        + halves(x, seq // 2, width)
        + [
            (ctx_own, whole(seq, half)),
            (ctx_oth, whole(seq, half)),
            (w_out, at_layer(layer, half, width)),
            *out_shares(wo_oth, half, width),
            (vec, at_layer(layer, *vec.shape[1:])),
            (gain, at_layer(layer, *gain.shape[1:])),
            (w_up, pl.BlockSpec((None, width, chunk), lambda t, s: (layer, 0, t))),
            (b_up, pl.BlockSpec((b_up.shape[0], chunk), lambda t, s: (0, t))),
            (w_down, pl.BlockSpec((None, chunk, width), lambda t, s: (layer, t, 0))),
        ]
        + (halves(cot, seq // 2, width) if last else []),
        outs,
        early=early,
        scratch=[pltpu.VMEM((seq, width), f32)],
        grid=(steps,),
        us=21.0
    )


def ff_bwd_kernel(
    layer, spot_ref, lim_ref, fin_ref, vec_ref, gain_ref, slope_ref, up_ref, down_ref, wy_ref,
    wc_ref, de_ref, hat1_ref, rate1_ref, wo_ref, co_ref, ct_ref,
    zk_ref, ok_ref, os_ref, dy_ref, dco_ref, dct_ref, small_ref, bup_ref,
    do_ref, du_ref, dz_ref,
):
    step = pl.program_id(0)
    steps = pl.num_programs(0)
    seq, width = de_ref.shape
    half = width // 2
    rows = 256
    core = spot_ref[CORE]
    mine = pl.ds(pl.multiple_of(core * half, 128), half)
    other = pl.ds(pl.multiple_of((1 - core) * half, 128), half)
    zero = jnp.zeros((1, width), f32)
    ctx_limit, ff_limit = lim_ref[layer, 1], lim_ref[layer, 2]

    chunk = up_ref.shape[1]
    sub = FF_SUB
    for part in range(chunk // sub):
        cols = slice(part * sub, (part + 1) * sub)
        dz = dot(fin_ref[...], down_ref[cols, :], NT) * slope_ref[:, cols].astype(f32)
        low = dz.astype(bf16)
        bup_ref[:, cols] = jnp.sum(low.astype(f32), axis=0, keepdims=True)
        dz_ref[:, cols] = low
    term = dot(dz_ref[...], up_ref[...], NT)

    @pl.when(step == 0)
    def _():
        du_ref[...] = term

    @pl.when(step > 0)
    def _():
        du_ref[...] += term

    @pl.when(step < steps // 2)
    def _():
        zk_ref[:, pl.ds(pl.multiple_of(step * chunk, 128), chunk)] = dz_ref[...]

    @pl.when(step == steps - 1)
    def _():
        def body(i, carry):
            gain_sum, shift_sum, out_sum = carry
            at = pl.ds(pl.multiple_of(i * rows, rows), rows)
            hat = hat1_ref[at, :]
            normed = hat * gain_ref[0:1, :] + vec_ref[1:2, :]
            bent = jnp.tanh(normed * (1.0 / ff_limit))
            grad = de_ref[at, :] + du_ref[at, :] * (1.0 - bent * bent)
            dy = norm_back(grad, hat, rate1_ref[at, 0:1], gain_ref[0:1, :])
            low = dy.astype(bf16)
            dy_ref[at, :] = dy
            do_ref[at, :] = low
            return (
                gain_sum + jnp.sum(grad * hat, axis=0, keepdims=True),
                shift_sum + jnp.sum(grad, axis=0, keepdims=True),
                out_sum + jnp.sum(low.astype(f32), axis=0, keepdims=True),
            )

        sums = lax.fori_loop(0, seq // rows, body, (zero, zero, zero))
        small_ref[...] = jnp.zeros_like(small_ref)
        small_ref[0:1, :] = sums[2]
        small_ref[1:2, :] = sums[1]
        small_ref[4:5, :] = sums[0]
        ok_ref[...] = do_ref[:, mine]
        os_ref[...] = do_ref[:, other]
        inv = 1.0 / ctx_limit
        bent = jnp.tanh(co_ref[...] * inv)
        dco_ref[...] = (dot(do_ref[...], wo_ref[...], NT) * (1.0 - bent * bent)).astype(bf16)
        bent = jnp.tanh(ct_ref[...] * inv)
        grad = dot(do_ref[:, mine], wy_ref[...].reshape(half, half), NT)
        grad += dot(do_ref[:, other], wc_ref[...].reshape(half, half), NT)
        dct_ref[...] = (grad * (1.0 - bent * bent)).astype(bf16)


def ff_bwd(
    spot, hold, layer, limits, de, df, hat1, rate1, vec, gain, slope, w_up, w_down, w_out,
    wo_oth, ctx_own, ctx_oth,
):
    seq, half = ctx_own.shape
    width, hidden = w_up.shape[1:]
    chunk = FF_CHUNK
    steps = hidden // chunk
    span = steps // 2

    def place(t, s):
        return jnp.where(t < span, s[CORE] * span + t, (1 - s[CORE]) * span + t - span)

    full = whole(seq, width)
    part = whole(seq, width // 2)
    outs = [
        (part, shape((seq, width // 2), bf16)),
        (part, shape((seq, width // 2), bf16)),
        (full, shape((seq, width), f32)),
        (whole(seq, half), shape((seq, half), bf16)),
        (whole(seq, half), shape((seq, half), bf16)),
        (whole(8, width), shape((8, width), f32)),
        (pl.BlockSpec((1, chunk), lambda t, s: (0, place(t, s))), shape((1, hidden), f32)),
    ]
    return launch(
        functools.partial(ff_bwd_kernel, layer), "ff_bwd", spot, hold,
        [(limits, smem())]
        + [
            (df, full),
            (vec, at_layer(layer, *vec.shape[1:])),
            (gain, at_layer(layer, *gain.shape[1:])),
            (slope, pl.BlockSpec((seq, chunk), lambda t, s: (0, place(t, s)))),
            (w_up, pl.BlockSpec((None, width, chunk), lambda t, s: (layer, 0, place(t, s)))),
            (w_down, pl.BlockSpec((None, chunk, width), lambda t, s: (layer, place(t, s), 0))),
            *out_shares(wo_oth, half, width),
        ],
        outs,
        late=[
            (de, None),
            (hat1, None),
            (rate1, None),
            (w_out, layer),
            (ctx_own, None),
            (ctx_oth, None),
        ],
        early=[(shape((seq, hidden // 2), bf16), span - 1)],
        scratch=[
            pltpu.VMEM((seq, width), bf16),
            pltpu.VMEM((seq, width), f32),
            pltpu.VMEM((seq, chunk), bf16),
        ],
        grid=(steps,),
        us=20.0
    )


def attn_bwd_half(q_ref, k_ref, v_ref, c_ref, lse_ref, dc_ref, seg_q, seg_k):
    query, key, value, grad = q_ref[...], k_ref[...], v_ref[...], dc_ref[...]
    key_ext = jnp.concatenate([key, seg_k], axis=1)
    key_t = key.astype(f32).T.astype(bf16)
    product_t = (grad.astype(f32) * c_ref[...]).T
    d_key = d_value = None
    d_query_t = []
    for head in range(2):
        scaled = query * head_mask(head, HEAD**-0.5)
        scores = dot(key_ext, jnp.concatenate([scaled, seg_q], axis=1), NT)
        probs = jnp.exp(scores - lse_ref[0, head : head + 1, :])
        grad_head = grad * head_mask(head, 1.0)
        d_probs = dot(value, grad_head, NT)
        delta = jnp.sum(product_t[head * HEAD : (head + 1) * HEAD], axis=0, keepdims=True)
        d_scores = (probs * (d_probs - delta)).astype(bf16)
        term_v = dot(probs.astype(bf16), grad_head)
        term_k = dot(d_scores, scaled)
        d_value = term_v if d_value is None else d_value + term_v
        d_key = term_k if d_key is None else d_key + term_k
        d_query_t.append(dot(key_t[head * HEAD : (head + 1) * HEAD], d_scores))
    d_query = jnp.concatenate(d_query_t, axis=0).T * HEAD**-0.5
    return d_query.astype(bf16), d_key.astype(bf16), d_value.astype(bf16)


def attn_bwd_kernel(
    layer, spot_ref, lim_ref, sq_ref, sk_ref,
    qo_ref, ko_ref, vo_ref, co_ref, lo_ref, dco_ref,
    qt_ref, kt_ref, vt_ref, ct_ref, lt_ref, dct_ref, wo_ref, wy_ref, wc_ref, *rest
):
    if layer:
        gain_ref, dy_ref, x_ref, hat_ref, rate_ref, *rest = rest
    else:
        xt_ref, xb_ref, dy_ref, *rest = rest
    dqo_ref, dko_ref, dvo_ref, dqt_ref, dkt_ref, dvt_ref, bo_ref, bt_ref, *rest = rest
    acc_ref = rest[-1]
    step = pl.program_id(0)
    seq, width = dy_ref.shape
    half_seq, share = seq // 2, width // 2
    rows = 128
    own = attn_bwd_half(qo_ref, ko_ref, vo_ref, co_ref, lo_ref, dco_ref, sq_ref[...], sk_ref[...])
    oth = attn_bwd_half(qt_ref, kt_ref, vt_ref, ct_ref, lt_ref, dct_ref, sq_ref[...], sk_ref[...])
    dqo_ref[...], dko_ref[...], dvo_ref[...] = own
    dqt_ref[...], dkt_ref[...], dvt_ref[...] = oth
    for out_ref, grads in ((bo_ref, own), (bt_ref, oth)):
        out_ref[0:1, :] = jnp.sum(grads[0].astype(f32), axis=0, keepdims=True)
        out_ref[1:2, :] = jnp.sum(grads[2].astype(f32), axis=0, keepdims=True)
        out_ref[2:8, :] = jnp.zeros((6, PAIR), f32)
    joined = [jnp.concatenate([own[k], oth[k]], axis=1) for k in range(3)]
    for piece, w_ref in enumerate((wy_ref, wc_ref)):
        which = jnp.where(spot_ref[CORE] == 0, piece, 1 - piece)
        at = pl.ds(pl.multiple_of(which * share, 128), share)
        total = None
        for k in range(3):
            term = dot(joined[k], jnp.concatenate([wo_ref[k, at, :], w_ref[k]], axis=1), NT)
            total = term if total is None else total + term

        @pl.when(step == 0)
        def _():
            acc_ref[:, at] = total

        @pl.when(step > 0)
        def _():
            acc_ref[:, at] += total

    @pl.when(step == pl.num_programs(0) - 1)
    def _():
        inv = 1.0 / lim_ref[layer, 0]
        sums = norm_sums(width)
        for part in range(2):

            def body(i, carry, part=part):
                here = pl.ds(pl.multiple_of(i * rows, rows), rows)
                at = pl.ds(part * half_seq + pl.multiple_of(i * rows, rows), rows)
                value = x_ref[at, :] if layer else (xt_ref, xb_ref)[part][here, :]
                bent = jnp.tanh(value.astype(f32) * inv)
                grad = dy_ref[at, :] + acc_ref[at, :] * (1.0 - bent * bent)
                if layer:
                    return leave_norm(
                        grad, hat_ref[at, :], rate_ref[at, 0:1], gain_ref, at, rest[0], rest[1],
                        carry,
                    )
                rest[part][here, :] = grad.astype(rest[part].dtype)
                return carry

            sums = lax.fori_loop(0, half_seq // rows, body, sums)
        if layer:
            store_sums(sums, rest[2])


def attn_bwd(spot, hold, layer, limits, x, dy, seg_q, seg_k, own, oth, w_qkv, wq_oth, below=()):
    seq, width = dy.shape
    cols = own[0].shape[1]
    steps = cols // PAIR
    block = pl.BlockSpec((seq, PAIR), lambda t, s: (0, t))
    half_specs = [
        block,
        block,
        block,
        block,
        pl.BlockSpec((1, 8, seq), lambda t, s: (t, 0, 0)),
        block,
    ]
    return launch(
        functools.partial(attn_bwd_kernel, layer), "attn_bwd", spot, hold,
        [(limits, smem())]
        + [(seg_q, whole(seq, PAIR)), (seg_k, whole(seq, PAIR))]
        + list(zip(own, half_specs))
        + list(zip(oth, half_specs))
        + list(zip((w_qkv,), weight_specs(layer, (w_qkv,))))
        + list(zip(wq_oth, weight_specs(layer, wq_oth)))
        + (
            [(below[2], at_layer(layer - 1, *below[2].shape[1:]))]
            if layer
            else halves(x, seq // 2, width)
        ),
        [(block, shape((seq, cols), bf16))] * 6
        + [(pl.BlockSpec((8, PAIR), lambda t, s: (0, t)), shape((8, cols), f32))] * 2
        + (
            norm_outs(seq, width)
            if layer
            else [
                (whole(seq // 2, width), shape((seq // 2, width), f32)),
                (whole(seq // 2, width), shape((seq // 2, width), bf16)),
            ]
        ),
        late=[(dy, None)]
        + ([(x[0], None), (below[0], None), (below[1], None)] if layer else []),
        scratch=[pltpu.VMEM((seq, width), f32)],
        grid=(steps,),
        us=18.5
    )


FF_ORDERS = (
    (AXIS_X, SIDE, AXIS_Z0, AXIS_Z1),
    (SIDE, AXIS_Z0, AXIS_X, AXIS_Z1),
    (AXIS_Z0, AXIS_X, SIDE, AXIS_Z1),
)
FF_ROWS = (144, 128, 112)
ATT_ORDERS = (
    (AXIS_X, SIDE, AXIS_Z0, AXIS_Z1),
    (AXIS_Z0, SIDE, AXIS_X, AXIS_Z1),
)
FIRST_ATT_ORDERS = (
    (AXIS_X, SIDE, AXIS_Z0, AXIS_Z1),
    (AXIS_Z0, AXIS_X, SIDE, AXIS_Z1),
)
ATT_ROWS = (96, 96)
PIECE = 48


def block_of(spot_ref, order, rel):
    bit = {axis: (rel >> (3 - k)) & 1 for k, axis in enumerate(order)}
    chip = 0
    for axis in (AXIS_Z1, AXIS_Z0, AXIS_X):
        own = spot_ref[axis]
        chip = chip * 2 + (1 - own if bit[axis] else own)
    return bit[SIDE], chip


def w_ff_kernel(
    spot_ref, um_ref, uo_ref, zm_ref, so_ref, gm_ref, go_ref, fm_ref, fo_ref, down_ref, *rest
):
    outs, ut_ref, half_ref, all_ref = rest[:-3], rest[-3], rest[-2], rest[-1]
    step = pl.program_id(0)
    sides, chips, tall, lanes = all_ref.shape
    seq, width = um_ref.shape
    thin = width // chips

    @pl.when(step == 0)
    def _():
        ut_ref[:, :seq] = um_ref[...].T
        ut_ref[:, seq:] = uo_ref[...].T
        mine = pl.ds(pl.multiple_of(spot_ref[CORE] * lanes, 128), lanes)
        half_ref[0] = fm_ref[:, mine]
        half_ref[1] = fo_ref[:, mine]

    theirs = (dot(fo_ref[...], down_ref[...], NT) * so_ref[...].astype(f32)).astype(bf16)
    grad_up = dot(ut_ref[:, :seq], zm_ref[...]) + dot(ut_ref[:, seq:], theirs)
    grad_up = grad_up.astype(bf16)
    for chip in range(chips):
        at = pl.ds(pl.multiple_of((step % 2) * thin, 16), thin)
        all_ref[step // 2, chip, at, :] = grad_up[chip * thin : (chip + 1) * thin]
    base = 2 * thin
    deep = tall - base
    per = gm_ref.shape[1] // (2 * deep)
    for part in range(per):
        cols = slice(part * 2 * deep, (part + 1) * 2 * deep)
        grad_down = dot(gm_ref[:, cols], half_ref[0], TN) + dot(go_ref[:, cols], half_ref[1], TN)
        grad_down = grad_down.astype(bf16)
        for side in range(2):
            all_ref[side, step * per + part, base:, :] = grad_down[side * deep : (side + 1) * deep]

    @pl.when(step == pl.num_programs(0) - 1)
    def _():
        start = 0
        for part, (order, count) in enumerate(zip(FF_ORDERS, FF_ROWS)):
            for rel in range(16):
                side, chip = block_of(spot_ref, order, rel)
                side = 1 - spot_ref[SIDE] if side else spot_ref[SIDE]
                value = all_ref[side, chip, start : start + count, :]
                if rel < 8:
                    outs[2 * part][rel] = value
                else:
                    outs[2 * part + 1][(rel - 8) * count : (rel - 7) * count, :] = value
            start += count


def w_ff(
    spot, hold, layer, cu_mine, cu_core, dz_mine, slope_core, g_mine, g_core, df_mine, df_core,
    w_down
):
    seq, width = df_mine.shape
    lanes, hidden = width // 2, g_mine.shape[1]
    steps = dz_mine.shape[1] // lanes
    tall = hidden // 8
    g_block = pl.BlockSpec((seq, hidden // steps), lambda t, s: (0, t))
    u_block = pl.BlockSpec((seq, width), lambda *_: (0, 1))
    outs = []
    for rows in FF_ROWS:
        outs.append((whole(8, rows, lanes), shape((8, rows, lanes), bf16)))
        outs.append((whole(8 * rows, lanes), shape((8 * rows, lanes), bf16)))
    return launch(
        w_ff_kernel, "w_ff", spot, hold,
        [
            (cu_mine, u_block),
            (cu_core, u_block),
            (dz_mine, pl.BlockSpec((seq, lanes), lambda t, s: (0, t))),
            (slope_core, pl.BlockSpec((seq, lanes), lambda t, s: (0, s[CORE] * steps + t))),
            (g_mine, g_block),
            (g_core, g_block),
            (df_mine, whole(seq, width)),
            (df_core, whole(seq, width)),
            (
                w_down,
                pl.BlockSpec(
                    (None, lanes, width), lambda t, s: (layer, s[CORE] * steps + t, 0)
                ),
            ),
        ],
        outs,
        scratch=[
            pltpu.VMEM((width, 2 * seq), bf16),
            pltpu.VMEM((2, seq, lanes), bf16),
            pltpu.VMEM((2, 8, tall, lanes), bf16),
        ],
        grid=(steps,),
        us=13.5,
    )


def w_att_kernel(
    spot_ref, a_ref, dqo_ref, dko_ref, dvo_ref, dqt_ref, dkt_ref, dvt_ref,
    cm_ref, cc_ref, dom_ref, doc_ref, keep_ref, out_ref, *rest
):
    send_refs, at_ref, spare_ref = rest[:-2], rest[-2], rest[-1]
    width = a_ref.shape[1]
    _, chips, tall, cols = keep_ref.shape
    core = spot_ref[CORE]
    piece = PIECE
    per = tall // piece
    at_ref[...] = a_ref[...].T
    sides = ((dqo_ref, dko_ref, dvo_ref), (dqt_ref, dkt_ref, dvt_ref))
    for side, grads in enumerate(sides):
        for which in range(3):
            result = dot(at_ref[...], grads[which][...]).astype(bf16)
            for j in range(width // piece):
                index = which * (width // piece) + j
                block, sub = index // per, index % per
                spare_ref[block % 2, block // 2, sub * piece : (sub + 1) * piece, :] = result[
                    j * piece : (j + 1) * piece
                ]
        keep_ref[side] = spare_ref[core]
        for k, send_ref in enumerate(send_refs):
            send_ref[side] = spare_ref[1 - core, :, k * piece : (k + 1) * piece, :]
    half = width // 2
    heads = half // HEAD
    for side in range(2):
        at = slice(side * half, (side + 1) * half)
        result = dot(cm_ref[:, at], dom_ref[...], TN) + dot(cc_ref[:, at], doc_ref[...], TN)
        for chip in range(chips):
            for pair in range(heads // 2):
                first = (2 * pair) * HEAD + 8 * chip
                second = first + HEAD
                out_ref[side, chip, pair * 16 : (pair + 1) * 16, :] = jnp.concatenate(
                    [result[first : first + 8], result[second : second + 8]], axis=0
                ).astype(bf16)


def w_att(spot, hold, act, d_own, d_oth, cu_mine, cu_core, do_mine, do_core):
    seq, width = act.shape
    cols = width // 2
    chips = 8
    tall = 3 * width // (2 * chips)
    outs = [
        shape((2, chips, tall, cols), bf16),
        shape((2, chips, cols // chips, cols), bf16),
        *[shape((2, chips, PIECE, cols), bf16)] * (tall // PIECE),
    ]
    cq_block = pl.BlockSpec((seq, width), lambda *_: (0, 0))
    return launch(
        w_att_kernel, "w_att", spot, hold,
        [(array, whole(*array.shape)) for array in (act, *d_own, *d_oth)]
        + [
            (cu_mine, cq_block),
            (cu_core, cq_block),
            (do_mine, whole(seq, cols)),
            (do_core, whole(seq, cols)),
        ],
        [(whole(*out.shape), out) for out in outs],
        scratch=[pltpu.VMEM((width, seq), bf16), pltpu.VMEM((2, chips, tall, cols), bf16)],
        us=8.0,
    )


class Part:
    def __init__(self, kind, order, kept):
        self.kind, self.order, self.kept = kind, order, kept
        self.stage = 0
        self.array = self.start = None
        self.final = None

    def arrives(self, array, start):
        self.array, self.start = array, start


def pack_small(spot_ref, small_refs, out_ref):
    for layer in range(len(small_refs) // 5):
        bo_ref, bt_ref, vec_ref, sums_ref, up_ref = small_refs[5 * layer : 5 * layer + 5]
        half = bo_ref.shape[1]
        width = 2 * half
        side = spot_ref[SIDE]
        mine = pl.ds(pl.multiple_of(side * half, 128), half)
        other = pl.ds(pl.multiple_of((1 - side) * half, 128), half)
        out_ref[layer, 0:2, mine] = bo_ref[0:2, :]
        out_ref[layer, 0:2, other] = bt_ref[0:2, :]
        out_ref[layer, 2:8, :] = vec_ref[0:6, :] + sums_ref[0:6, :]
        for k in range(up_ref.shape[1] // width):
            out_ref[layer, 8 + k : 9 + k, :] = up_ref[:, k * width : (k + 1) * width]


def exchange(spot, over_axis, parts, att=None, smalls=(), pair=None, carry=None, hold=()):
    anywhere = pl.BlockSpec(memory_space=pl.ANY)
    ins, outs, steps = [], [], []

    def take(array):
        for k, (known, _) in enumerate(ins):
            if known is array:
                return k
        ins.append((array, anywhere))
        return len(ins) - 1

    def give(dims, dtype=bf16):
        outs.append((anywhere, shape(dims, dtype)))
        return len(outs) - 1

    lanes = (parts[0].kept if parts else att[0]).shape[-1]
    sends = {}

    def room(axis, rows):
        start = sends.get(axis, 0)
        sends[axis] = start + rows
        return start

    new_parts, places = [], []
    parts = sorted(parts, key=lambda part: (part.kind != "ff", part.kept.shape[0]))
    for part in parts:
        blocks, rows, _ = part.kept.shape
        source = take(part.kept), take(part.array), part.start
        if blocks > 1:
            axis = part.order[part.stage + 1]
            start = room(axis, blocks // 2 * rows)
            steps.append(("halve", source, give((blocks // 2, rows, lanes)), axis, start))
        elif part.kind == "ff":
            axis = SIDE
            start = room(axis, rows)
            steps.append(("end", source, give((rows, lanes), f32), axis, start))
        else:
            axis = None
            start = 0
            steps.append(("end", source, give((rows, lanes), f32), None, 0))
        places.append((part, axis, start))
    if att is not None:
        source = [take(array) for array in att]
        begin = 0
        for order, rows in zip(FIRST_ATT_ORDERS if smalls else ATT_ORDERS, ATT_ROWS):
            start = room(order[0], 8 * rows)
            kept = give((8, rows, lanes))
            steps.append(("enter", source, kept, order[0], start, order, begin, rows))
            places.append((Part("att", order, None), order[0], start))
            begin += rows
    small_out = None
    if smalls:
        source = [take(array) for small in smalls for array in small]
        width = smalls[0][2].shape[1]
        small_out = give((len(smalls), 8 + smalls[0][4].shape[1] // width, width), f32)
        steps.append(("pack", source, small_out))
    if pair is not None:
        small_out = give(pair[0].shape, f32)
        steps.append(("sum", [take(array) for array in pair], small_out))
    if carry is not None:
        small_out = give(carry.shape, carry.dtype)
        steps.append(("copy", [take(carry)], small_out))
    send_at = {axis: give((rows, lanes)) for axis, rows in sends.items()}

    n_in, n_out = len(ins), len(outs)

    def body(spot_ref, *refs):
        groups = []
        for count in (n_in, n_out, n_in, n_out):
            groups.append(refs[:count])
            refs = refs[count:]
        in_any, out_any, in_refs, out_refs = groups
        in_sems, out_sems, send_sems = refs
        loads = [
            pltpu.make_async_copy(in_any[k], in_refs[k], in_sems.at[k]) for k in range(n_in)
        ]
        for load in loads:
            load.start()
        ready, stores = set(), []

        def store(source, target, sem):
            stores.append(pltpu.make_async_copy(source, target, sem))
            stores[-1].start()

        for number, (what, source, out, *more) in enumerate(steps):
            out_ref = out_refs[out]
            for k in source[:2] if what in ("halve", "end") else source:
                if k not in ready:
                    ready.add(k)
                    loads[k].wait()
            if what == "halve":
                axis, start = more
                kept, got = in_refs[source[0]], in_refs[source[1]]
                base = source[2]
                half, rows, _ = out_ref.shape
                send = out_refs[send_at[axis]]
                for j in range(half):
                    at = base + j * rows
                    out_ref[j] = kept[j] + got[at : at + rows, :]
                    at += half * rows
                    send[start + j * rows : start + (j + 1) * rows, :] = (
                        kept[half + j] + got[at : at + rows, :]
                    )
            elif what == "end":
                axis, start = more
                kept, got = in_refs[source[0]], in_refs[source[1]]
                base = source[2]
                rows = out_ref.shape[0]
                total = kept[0].astype(f32) + got[base : base + rows, :].astype(f32)
                out_ref[...] = total
                if axis is not None:
                    out_refs[send_at[axis]][start : start + rows, :] = total.astype(bf16)
            elif what == "enter":
                axis, start, order, begin, rows = more
                keep, outer, *got = (in_refs[k] for k in source)
                send = out_refs[send_at[axis]]
                for rel in range(16):
                    side, chip = block_of(spot_ref, order, rel)
                    for k in range(begin // PIECE, (begin + rows) // PIECE):
                        if k < len(got):
                            at = slice(k * PIECE, (k + 1) * PIECE)
                            value = keep[side, chip, at, :] + got[k][side, chip]
                        else:
                            value = outer[side, chip]
                        done = k * PIECE - begin
                        if rel < 8:
                            out_ref[rel, done : done + PIECE, :] = value
                        else:
                            at = start + (rel - 8) * rows + done
                            send[at : at + PIECE, :] = value
            elif what == "copy":
                out_ref[...] = in_refs[source[0]][...]
            elif what == "pack":
                pack_small(spot_ref, [in_refs[k] for k in source], out_ref)
            else:
                out_ref[...] = in_refs[source[0]][...] + in_refs[source[1]][...]
            store(out_ref, out_any[out], out_sems.at[out])
            if what in ("halve", "end", "enter") and more[0] is not None:
                k = send_at[more[0]]
                if what == "enter":
                    count = 8 * more[4]
                elif what == "halve":
                    count = out_ref.shape[0] * out_ref.shape[1]
                else:
                    count = out_ref.shape[0]
                at = pl.ds(more[1], count)
                store(out_refs[k].at[at, :], out_any[k].at[at, :], send_sems.at[number])
        for copy in stores:
            copy.wait()

    buffers = [pltpu.VMEM(array.shape, array.dtype) for array, _ in ins]
    buffers += [pltpu.VMEM(out.shape, out.dtype) for _, out in outs]
    buffers += [pltpu.SemaphoreType.DMA((count,)) for count in (n_in, n_out, len(steps))]
    results = launch(body, "exchange", spot, hold, ins, outs, scratch=buffers, us=5.0)
    arrived = {axis: over_axis(results[k], axis) for axis, k in send_at.items()}
    kept_at = [step[2] for step in steps]
    for (part, axis, start), what, out in zip(places, [step[0] for step in steps], kept_at):
        if what == "end":
            part.final = results[out]
        else:
            part.kept = results[out]
        if what != "enter":
            part.stage += 1
        if axis is not None:
            part.arrives(arrived[axis], start)
        new_parts.append(part)
    return new_parts, (None if small_out is None else results[small_out])


def finish_kernel(layers, spot_ref, *refs):
    core, side = spot_ref[CORE], spot_ref[SIDE]
    count = len(FF_ROWS) + 1
    both_ref = refs[-1]
    for layer in range(layers):
        *part_refs, got_ref = refs[count * layer : count * (layer + 1)]
        keep_ref, send_ref = refs[count * layers + 2 * layer : count * layers + 2 * layer + 2]
        start = 0
        for ref in part_refs:
            both_ref[side, start : start + ref.shape[0], :] = ref[...]
            start += ref.shape[0]
        both_ref[1 - side] = got_ref[...].astype(f32)
        half = both_ref.shape[1] // 2
        quarter = half // 4
        for out_ref, which in ((keep_ref, core), (send_ref, 1 - core)):
            for k in range(4):
                at = pl.ds(pl.multiple_of((k % 2) * 2 * quarter + which * quarter, 16), quarter)
                out_ref[k * quarter : (k + 1) * quarter, :] = both_ref[k // 2, at, :].astype(
                    out_ref.dtype
                )
            out_ref[half:, :] = both_ref[which, half:, :].astype(out_ref.dtype)


def finish_ff(spot, groups):
    rows = sum(FF_ROWS)
    ins, outs = [], []
    for parts in groups:
        lanes = parts[0].final.shape[1]
        block = parts[0].start // rows
        assert parts[0].start == block * rows
        ins += [(part.final, whole(*part.final.shape)) for part in parts]
        ins.append(
            (parts[0].array, pl.BlockSpec((rows, lanes), lambda *_, block=block: (block, 0)))
        )
        outs.append((whole(rows, lanes), shape((rows, lanes), f32)))
        outs.append((whole(rows, lanes), shape((rows, lanes), bf16)))
    results = launch(
        functools.partial(finish_kernel, len(groups)), "finish_ff", spot, (), ins, outs,
        scratch=[pltpu.VMEM((2, rows, lanes), f32)],
    )
    return [results[2 * k : 2 * k + 2] for k in range(len(groups))]


def assemble_kernel(layers, spot_ref, *refs):
    up_ref, down_ref, qkv_ref, tile_ref = refs[-4:]
    core = spot_ref[CORE]
    for layer in range(layers):
        keep_ref, got_ref, *att_refs = refs[(2 + len(ATT_ROWS)) * layer :][: 2 + len(ATT_ROWS)]
        keep, got = keep_ref[...], got_ref[...].astype(f32)
        lanes = keep.shape[1]
        half = keep.shape[0] // 2
        quarter = half // 4
        tiles = lanes // 128
        for side in range(2):
            value = jnp.where(core == side, keep, got)
            for t in range(tiles):
                cols = slice(t * 128, (t + 1) * 128)
                for k in range(4):
                    start = ((side * 4 + k) * tiles + t) * layers + layer
                    up_ref[pl.ds(start, quarter, stride=8 * tiles * layers), :] = value[
                        k * quarter : (k + 1) * quarter, cols
                    ]
                start = (side * tiles + t) * layers + layer
                down_ref[pl.ds(start, half, stride=2 * tiles * layers), :] = value[half:, cols]
        share = tile_ref.shape[0] // tiles
        per = share // 2
        for t in range(tiles):
            done = 0
            for ref, rows in zip(att_refs, ATT_ROWS):
                count = min(rows, share - done)
                at = t * share + done
                tile_ref[at : at + count, :] = ref[:count, t * 128 : (t + 1) * 128]
                done += count
        for t in range(tiles):
            even = tile_ref[pl.ds(t * share, per, stride=2), :]
            odd = tile_ref[pl.ds(t * share + 1, per, stride=2), :]
            for k in range(2):
                cols = slice(k * HEAD, (k + 1) * HEAD)
                start = (2 * t + k) * per * layers + layer
                qkv_ref[pl.ds(start, per, stride=layers), :] = jnp.concatenate(
                    [even[:, cols], odd[:, cols]], axis=1
                )


def assemble(spot, pairs, atts, share):
    layers = len(pairs)
    rows, lanes = pairs[0][0].shape
    dims = (rows * lanes // 128 * layers, 128)
    ins = []
    for pair, parts in zip(pairs, atts):
        for array in (*pair, *(part.final for part in parts)):
            ins.append((array, whole(*array.shape)))
    wide = (share * lanes // 128 * layers, 128)
    return launch(
        functools.partial(assemble_kernel, layers), "assemble", spot, (), ins,
        [(whole(*dims), shape(dims, f32))] * 2 + [(whole(*wide), shape(wide, f32))],
        scratch=[pltpu.VMEM((share * lanes // 128, 128), f32)],
        us=3.0,
    )


def local(
    hidden_in, cotangent, segment_ids, clip_ranges, w_qkv, bias_qv, w_out, vector_bias, ln_gain,
    w_up, bias_up, w_down,
):
    layers = w_qkv.shape[0]
    row_count, half_seq, width = hidden_in.shape
    seq = segment_ids.shape[1]
    cols = w_qkv.shape[3]
    heads = cols // HEAD
    hidden = w_up.shape[2]
    dp_count = lax.axis_size("dp")
    assert lax.axis_size("mp") == 2 and row_count == 2 and seq == 2 * half_seq
    bits = dp_count.bit_length() - 1
    assert dp_count == 1 << bits and bits >= 1
    chips = dp_count // 2
    side = lax.axis_index("mp")
    place = lax.axis_index("dp")
    core = place % 2
    spot = Spot(
        jnp.stack(
            [core, side, (place >> 1) & 1, (place >> 2) & 1, (place >> 3) & 1]
        ).astype(jnp.int32)
    )

    def over_mp(value):
        return lax.ppermute(value, "mp", [(0, 1), (1, 0)])

    def over_bit(value, bit):
        return lax.ppermute(value, "dp", [(i, i ^ (1 << bit)) for i in range(dp_count)])

    def over_core(value):
        return over_bit(value, 0)

    def over_axis(value, axis):
        return over_mp(value) if axis == SIDE else over_bit(value, axis - AXIS_X + 1)

    def pick(value, index, axis):
        return lax.dynamic_index_in_dim(value, index, axis, keepdims=False)

    def ordered(index, mine, theirs, axis):
        first = jnp.where(index == 0, mine, theirs)
        second = jnp.where(index == 0, theirs, mine)
        return jnp.concatenate([first, second], axis=axis)

    x = (hidden_in, over_mp(pick(hidden_in, 1 - side, 0)))
    bias_oth = over_mp(bias_qv)
    limits = clip_ranges.astype(f32)
    seg_row = pick(segment_ids, side, 0).reshape(2, half_seq)
    seg_row = jnp.concatenate([pick(seg_row, side, 0), pick(seg_row, 1 - side, 0)])
    same = seg_row[:, None] == jnp.arange(PAIR, dtype=seg_row.dtype)[None, :]
    seg_q = jnp.where(same, BIG, 0.0).astype(bf16)
    seg_k = jnp.where(same, 0.0, 1.0).astype(bf16)

    arrived = over_mp(pick_weights(spot, w_qkv))
    act = enter(spot, (bias_oth,), limits, hidden_in, x[1])
    fetched, wo_oth, stored = [], [], []
    shared = ()
    for layer in range(layers):
        last = layer == layers - 1
        relays = relay_piece(arrived) if layer else []
        if last:
            relays = relays + relay_row(cotangent)
        outs = attn_fwd(spot, (), layer, act, (w_qkv,), bias_qv, seg_q, seg_k, relays)
        own, copies = outs[:5], outs[5:]
        if last:
            cot = (cotangent, over_mp(copies[-1]))
        if layer:
            copy = copies[0]
        else:
            copy, out_share = relay(spot, arrived, w_out)
        fetched.append((arrived, over_core(copy)))
        wo_oth.append(fetched[layer] if layer else (over_mp(out_share),))
        outs = attn_fwd(
            spot, (), layer, act, fetched[layer], bias_oth, seg_q, seg_k,
            pack=None if last else pack_weights(layer + 1, w_qkv, w_out),
        )
        oth = outs[:5]
        if not last:
            arrived = over_mp(outs[5])
        outs = ff_fwd(
            spot, shared, layer, last, limits, x, own[3], oth[3], w_out, wo_oth[layer], vector_bias,
            ln_gain,
            w_up, bias_up, w_down, cot if last else None,
        )
        cu, hat1, rate1, g, slope = outs[:5]
        shared = over_core(cu), over_core(g), over_core(slope)
        norm = None
        if last:
            hidden_mine, hidden_send, *descent = outs[5:]
        else:
            norm = outs[5:7]
        stored.append((x, act, own, oth, cu, hat1, rate1, g, slope, norm, shared))
        if not last:
            x, act = (outs[7],), outs[8]
    hidden_recv = over_mp(hidden_send)

    fast = chips == 8 and width == 768 and hidden == 3072 and cols == 384

    smalls, groups = [], {}
    flying = []
    small = None
    df_core = over_core(descent[1])
    for layer in reversed(range(layers)):
        x, act, own, oth, cu, hat1, rate1, g, slope, norm, shared = stored[layer]
        de, df, sums = descent
        dz_keep, do_keep, do_send, dy, dc_own, dc_oth, vec, d_bup = ff_bwd(
            spot, (), layer, limits, de, df, hat1, rate1, vector_bias, ln_gain, slope, w_up,
            w_down, w_out, wo_oth[layer], own[3], oth[3],
        )
        if fast:
            do_core = over_core(do_send)
            if flying:
                flying, _ = exchange(spot, over_axis, flying, entering)
                groups["att", layer + 1] = flying[-len(ATT_ROWS) :]
            outs = w_ff(
                spot, (hidden_recv, do_core), layer, cu, shared[0], dz_keep, shared[2], g, shared[1], df, df_core,
                w_down,
            )
            parts_ff = []
            for k, order in enumerate(FF_ORDERS):
                parts_ff.append(Part("ff", order, outs[2 * k]))
                parts_ff[k].arrives(over_axis(outs[2 * k + 1], order[0]), 0)
            groups["ff", layer] = parts_ff
            if flying:
                exchange(spot, over_axis, flying)
            flying = flying + parts_ff
        below = (*stored[layer - 1][9], ln_gain) if layer else ()
        outs = attn_bwd(
            spot, (), layer, limits, x, dy, seg_q, seg_k, (*own, dc_own), (*oth, dc_oth), w_qkv,
            fetched[layer], below,
        )
        d_own, d_oth = outs[:3], outs[3:6]
        smalls.insert(0, (outs[6], outs[7], vec, sums, d_bup))
        descent = outs[8:]
        if fast:
            keep, out, *send = w_att(
                spot, (), act, d_own, d_oth, cu, shared[0], do_keep, do_core
            )
            entering = keep, out, *(over_core(piece) for piece in send)
            if layer:
                flying, df = exchange(spot, over_axis, flying, carry=descent[1])
                df_core = over_core(df)
            else:
                late = [part for part in flying if part.kind == "ff" and part.stage == 3]
                flying = [part for part in flying if part not in late]
                flying, small = exchange(
                    spot, over_axis, flying, entering, smalls,
                    hold=tuple({id(part.array): part.array for part in late}.values()),
                )
                groups["att", 0] = flying[-len(ATT_ROWS) :]
        else:
            dz = (dot(df, w_down[layer], NT) * slope.astype(f32)).astype(bf16)
            do = ordered(core, do_keep, do_send, 1)
            total = []
            for lhs, rhs in ((cu[:, width:], dz), (g, df)):
                grad = dot(lhs, rhs, TN).reshape(-1)
                grad = grad + over_mp(grad)
                total.append(lax.psum_scatter(grad, "dp", scatter_dimension=0, tiled=True))
            groups["ff", layer] = total
            sides = []
            for grads, part in ((d_own, cu[:, :cols]), (d_oth, cu[:, cols:width])):
                qkv = jnp.stack([dot(act, grad, TN) for grad in grads])
                qkv = qkv.reshape(3, width, heads, HEAD).transpose(2, 0, 1, 3)
                sides.append((qkv.reshape(heads, -1), dot(part, do, TN).reshape(heads, -1)))
            total = []
            for k in range(2):
                grad = sides[0][k] + over_mp(sides[1][k])
                total.append(lax.psum_scatter(grad, "dp", scatter_dimension=1, tiled=True))
            groups["att", layer] = total

    row_mine, row_send = descent
    if fast:
        axes = [AXIS_X, SIDE, AXIS_Z0, AXIS_Z1]
        pair = (small, over_axis(small, axes.pop(0)))
        turn = 0
        while True:
            if turn == 1:
                flying = flying + late
            flying = [part for part in flying if part.final is None]
            if not flying and turn > 1:
                break
            flying, summed = exchange(spot, over_axis, flying, pair=pair)
            small = small if summed is None else summed
            pair = (small, over_axis(small, axes.pop(0))) if axes else None
            if turn == 0:
                hidden_out = place_rows(spot, (), hidden_mine, hidden_recv, bf16)
            if turn == 2:
                grad_input = place_rows(spot, (), row_mine, over_mp(row_send), f32)
                done = finish_ff(spot, [groups["ff", k] for k in range(layers)])
                pairs = [(keep, over_core(send)) for keep, send in done]
            turn += 1
        while pair:
            small = pair[0] + pair[1]
            pair = (small, over_axis(small, axes.pop(0))) if axes else None
        small = small + over_core(small)
        share = 3 * width // dp_count
        atts = [groups["att", k] for k in range(layers)]
        up, down, qkv = assemble(spot, pairs, atts, share)
        up, down = (
            flat.reshape(-1, layers, 128).transpose(1, 0, 2).reshape(layers, -1)
            for flat in (up, down)
        )
        qkv = qkv.reshape(heads, -1, layers, 128).transpose(2, 0, 1, 3).reshape(layers, heads, -1)
        outs = []
        for parts in atts:
            rows = jnp.concatenate([part.final for part in parts], axis=0)
            outs.append(rows[share:].reshape(heads, 2, 4, cols))
        outs = jnp.stack(outs)
        keep, sent = pick(outs, core, 2), pick(outs, 1 - core, 2).astype(bf16)
        outs = ordered(core, keep[:, :, :, None], over_core(sent).astype(f32)[:, :, :, None], 3)
        grads = (
            qkv, outs.reshape(layers, heads, -1), up, down
        )
    else:
        hidden_out = place_rows(spot, (), hidden_mine, hidden_recv, bf16)
        grad_input = place_rows(spot, (), row_mine, over_mp(row_send), f32)
        small = jnp.stack(
            [
                jnp.concatenate(
                    [ordered(side, bo[:2], bt[:2], 1), (vec + sums)[:6], up.reshape(-1, width)],
                    axis=0,
                )
                for bo, bt, vec, sums, up in smalls
            ]
        )
        small = lax.psum(small, ("dp", "mp"))
        grads = [
            jnp.stack([groups[kind, layer][k] for layer in range(layers)])
            for kind, k in (("att", 0), ("att", 1), ("ff", 0), ("ff", 1))
        ]
    grad_bias_qv = lax.dynamic_slice_in_dim(small[:, :2], side * cols, cols, 2)
    return (
        hidden_out,
        grad_input,
        grads[0],
        grad_bias_qv,
        grads[1],
        small[:, 2:6],
        small[:, 6:8],
        grads[2],
        small[:, 8:].reshape(layers, hidden),
        grads[3],
    )


def solution(mesh):
    return jax.shard_map(
        local,
        mesh=mesh,
        in_specs=(
            P("dp", "mp", None),
            P("dp", "mp", None),
            P("dp", None),
            P(),
            P(None, None, None, "mp"),
            P(None, None, "mp"),
            P(None, "mp", None),
            P(),
            P(),
            P(),
            P(),
            P(),
        ),
        out_specs=(
            P("dp", "mp", None),
            P("dp", "mp", None),
            P(None, "mp", "dp"),
            P(None, None, "mp"),
            P(None, "mp", "dp"),
            P(),
            P(),
            P(None, "dp"),
            P(),
            P(None, "dp"),
        ),
        check_vma=False,
    )
```
